128 devices in a mesh: rep: 32 (over z, y, core), shard: 4 (over x).
Axes of the slice: x: 4, y: 4, z: 4, core: 2. Of those that a mesh axis runs over, the one named last changes fastest.
Arguments:
- tokens: bfloat16 [32, 1024, 1280], P('rep', 'shard'), may hold values from -6 to 6
- cotangent: bfloat16 [32, 1024, 1280], P('rep', 'shard'), may hold values from -6 to 6
- ln1_gain: bfloat16 [1280], P('shard'), may hold values from 0.5 to 1.5
- ln1_bias: bfloat16 [1280], P('shard'), may hold values from -1.5 to 1.5
- w_qkv: bfloat16 [1280, 3840], P('shard'), may hold values from -0.15625 to 0.15625
- qv_bias: bfloat16 [2560], P('shard'), may hold values from -1.5 to 1.5
- w_out: bfloat16 [1280, 1280], P('shard'), may hold values from -0.625 to 0.625
- out_bias: bfloat16 [1280], P('shard'), may hold values from -1.5 to 1.5
- ln2_gain: bfloat16 [1280], P('shard'), may hold values from 0.5 to 1.5
- ln2_bias: bfloat16 [1280], P('shard'), may hold values from -1.5 to 1.5
- w_fc: bfloat16 [1280, 5120], P('shard'), may hold values from -0.15625 to 0.15625
- fc_bias: bfloat16 [5120], P('shard'), may hold values from -1.5 to 1.5
- w_proj: bfloat16 [5120, 1280], P('shard'), may hold values from -0.078125 to 0.078125
- proj_bias: bfloat16 [1280], P('shard'), may hold values from -1.5 to 1.5
Outputs:
- block_out: bfloat16 [32, 1024, 1280], P('rep', 'shard')
- grad_tokens: bfloat16 [32, 1024, 1280], P('rep', 'shard')
- grad_ln1_gain: float32 [1280], P('shard')
- grad_ln1_bias: float32 [1280], P('shard')
- grad_w_qkv: float32 [1280, 3840], P('shard')
- grad_qv_bias: float32 [2560], P('shard')
- grad_w_out: float32 [1280, 1280], P('shard')
- grad_out_bias: float32 [1280], P('shard')
- grad_ln2_gain: float32 [1280], P('shard')
- grad_ln2_bias: float32 [1280], P('shard')
- grad_w_fc: float32 [1280, 5120], P('shard')
- grad_fc_bias: float32 [5120], P('shard')
- grad_w_proj: float32 [5120, 1280], P('shard')
- grad_proj_bias: float32 [1280], P('shard')
The draws below stay inside these ranges and needn't reach their ends.
All inputs are finite; a program needn't handle non-finite values.
Results may differ from the reference program's by a relative error of at most 0.023.
Values may be sent and summed in bfloat16 or wider, within the bound.
A program may use at most 256 MiB of HBM per device.

```python
import jax
import jax.numpy as jnp
from jax import lax

D = 1280
HEAD_DIM = 64
FF = 5120
TOK_DEV = 256
LENGTH = 1024
SEQS = 32
N_SHARD = 4


def steps_of(key, shape, shards, smallest, top_value):
    def one(dim, shards_of):
        steps = jax.random.uniform(jax.random.fold_in(jax.random.fold_in(key, 6), dim), (shards_of,), jnp.float32, smallest / len(shards), top_value / len(shards))
        return jnp.repeat(jnp.exp(steps), shape[dim] // shards_of).reshape((-1,) + (1,) * (len(shape) - dim - 1))

    factor_of = one(*shards[0])
    for cut in shards[1:]:
        factor_of = factor_of * one(*cut)
    return factor_of


def bell_draw(stream_key, extent, scale, reach, cuts=(), held_as=jnp.bfloat16):
    values = scale * jax.random.normal(stream_key, extent, jnp.float32)
    if cuts:
        values = values * steps_of(stream_key, extent, cuts, -0.22, 0.18)
    return jnp.clip(values, -reach, reach).astype(held_as)


def setup_inputs(seed: int = 0) -> dict:
    keys = jax.random.split(jax.random.key(seed), 15)
    return {
        "tokens": bell_draw(keys[0], (SEQS, LENGTH, D), 1.0, 6.0, ((0, 32), (1, 4))),
        "cotangent": bell_draw(keys[1], (SEQS, LENGTH, D), 1.0, 6.0, ((0, 32), (1, 4))),
        "ln1_gain": jnp.clip(1.0 + 0.1 * jax.random.normal(keys[2], (D,), jnp.float32), 0.5, 1.5).astype(jnp.bfloat16),
        "ln1_bias": bell_draw(keys[3], (D,), 0.3, 1.5, ((0, 4),)),
        "w_qkv": bell_draw(keys[4], (D, 3 * D), D ** -0.5, 0.15625, ((0, 4),)),
        "qv_bias": bell_draw(keys[5], (2 * D,), 0.3, 1.5, ((0, 4),)),
        "w_out": bell_draw(keys[6], (D, D), (D // 16) ** -0.5, 0.625, ((0, 4),)),
        "out_bias": bell_draw(keys[7], (D,), 0.3, 1.5, ((0, 4),)),
        "ln2_gain": jnp.clip(1.0 + 0.1 * jax.random.normal(keys[8], (D,), jnp.float32), 0.5, 1.5).astype(jnp.bfloat16),
        "ln2_bias": bell_draw(keys[9], (D,), 0.3, 1.5, ((0, 4),)),
        "w_fc": bell_draw(keys[10], (D, FF), D ** -0.5, 0.15625, ((0, 4),)),
        "fc_bias": bell_draw(keys[11], (FF,), 0.3, 1.5, ((0, 4),)),
        "w_proj": bell_draw(keys[12], (FF, D), FF ** -0.5, 0.078125, ((0, 4),)),
        "proj_bias": bell_draw(keys[13], (D,), 0.3, 1.5, ((0, 4),)),
    }


@jax.custom_vjp
def low(v):
    return lax.optimization_barrier(v.astype(jnp.bfloat16)).astype(jnp.float32)

@jax.custom_vjp
def low_back(v):
    return v

def low_keep(v):
    return (low(v), None)

def low_pass(kept, grad):
    return (grad,)

def back_keep(v):
    return (v, None)

def back_low(kept, grad):
    return (low(grad),)
low.defvjp(low_keep, low_pass)
low_back.defvjp(back_keep, back_low)
eps_norm = 1e-05

def layer_norm(seq_rows, norm_gain, norm_shift):
    center = seq_rows - lax.optimization_barrier(jnp.mean(seq_rows, axis=-1, keepdims=True))
    spread = lax.optimization_barrier(jnp.mean(center * center, axis=-1, keepdims=True))
    return center * lax.rsqrt(spread + eps_norm) * norm_gain + norm_shift

def matmul(left_mat, right_mat):
    return jnp.dot(left_mat, right_mat, precision=lax.Precision.HIGHEST, preferred_element_type=jnp.float32)

def attend_block(row_start, queries, key_rows, value_rows):
    raw_scores = jnp.einsum('qhd,khd->hqk', queries, key_rows, precision=lax.Precision.HIGHEST) * HEAD_DIM ** (-0.5)
    scores = low_back(raw_scores)
    row_ids = row_start + jnp.arange(queries.shape[0], dtype=jnp.int32)
    col_ids = jnp.arange(key_rows.shape[0], dtype=jnp.int32)
    allowed = col_ids[None, :] <= row_ids[:, None]
    scores = jnp.where(allowed[None], scores, -1e+30)
    prob_low = low(jax.nn.softmax(scores, axis=-1))
    return jnp.einsum('hqk,khd->qhd', prob_low, value_rows, precision=lax.Precision.HIGHEST)

def layer_forward(seq_input, gain_one, shift_one, weight_qkv, bias_qv, weight_out, bias_out, gain_two, shift_two, weight_fc, bias_fc, weight_proj, bias_proj):
    head_count = D // HEAD_DIM
    normed_one = low(layer_norm(seq_input, gain_one, shift_one))
    bias_full = jnp.concatenate([bias_qv[:D], jnp.zeros((D,), jnp.float32), bias_qv[D:]])
    qkv_all = low_back(low(matmul(normed_one, weight_qkv) + bias_full))
    query_all = qkv_all[:, :D].reshape(N_SHARD, TOK_DEV, head_count, HEAD_DIM)
    key_all = qkv_all[:, D:2 * D].reshape(LENGTH, head_count, HEAD_DIM)
    value_all = qkv_all[:, 2 * D:].reshape(LENGTH, head_count, HEAD_DIM)
    starts = jnp.arange(N_SHARD, dtype=jnp.int32) * TOK_DEV

    def one_block(block_pair):
        return attend_block(block_pair[0], block_pair[1], key_all, value_all)
    attended = lax.map(jax.checkpoint(one_block), (starts, query_all))
    attended = low_back(low(attended.reshape(LENGTH, D)))
    branch_one = low_back(matmul(attended, weight_out) + bias_out)
    middle = seq_input + branch_one
    normed_two = low(layer_norm(middle, gain_two, shift_two))
    pre_act = low_back(matmul(normed_two, weight_fc) + bias_fc)
    act_low = low(jax.nn.gelu(pre_act, approximate=True))
    branch_two = low_back(matmul(act_low, weight_proj) + bias_proj)
    return middle + branch_two

def reference(tokens, cotangent, ln1_gain, ln1_bias, w_qkv, qv_bias, w_out, out_bias, ln2_gain, ln2_bias, w_fc, fc_bias, w_proj, proj_bias):
    params = tuple((p.astype(jnp.float32) for p in (ln1_gain, ln1_bias, w_qkv, qv_bias, w_out, out_bias, ln2_gain, ln2_bias, w_fc, fc_bias, w_proj, proj_bias)))

    def one_seq(running, seq_pair):
        seq_input, seq_grad = seq_pair
        result, pull_back = jax.vjp(layer_forward, seq_input.astype(jnp.float32), *params)
        all_grads = pull_back(seq_grad.astype(jnp.float32))
        updated = tuple((r + g for r, g in zip(running, all_grads[1:])))
        return (updated, (result.astype(jnp.bfloat16), all_grads[0].astype(jnp.bfloat16)))
    initial = tuple((jnp.zeros_like(p) for p in params))
    sums, outputs = lax.scan(one_seq, initial, (tokens, cotangent))
    return (outputs[0], outputs[1], sums[0], sums[1], sums[2], sums[3], sums[4], sums[5], sums[6], sums[7], sums[8], sums[9], sums[10], sums[11])
```

```python
import jax
import jax.numpy as jnp
from jax import lax
from jax.experimental import pallas as pl
from jax.experimental.pallas import tpu as pltpu
from jax.sharding import PartitionSpec as P

MESH = pl.DeviceIdType.MESH
F32, BF16 = jnp.float32, jnp.bfloat16


def where_am_i():
    rep = lax.axis_index("rep")
    return lax.axis_index("shard"), (rep // 2) % 4, rep // 8, rep % 2


def device_at(x, y, z, c):
    return {"rep": (z * 4 + y) * 2 + c, "shard": x}


def wrap(v):
    return lax.rem(v + 4, 4)


class Net:
    def __init__(self, send_sems, recv_sems):
        self.send_sems, self.recv_sems, self.used = send_sems, recv_sems, 0
        self.all = []

    def send(self, src, dst, target):
        copy = pltpu.make_async_remote_copy(
            src_ref=src, dst_ref=dst,
            send_sem=self.send_sems.at[self.used], recv_sem=self.recv_sems.at[self.used],
            device_id=target, device_id_type=MESH,
        )
        copy.start()
        self.used += 1
        self.all.append(copy)
        return copy

    def finish(self):
        for copy in self.all:
            copy.wait_send()


def greet(targets):
    barrier = pltpu.get_barrier_semaphore()
    for target in targets:
        pl.semaphore_signal(barrier, 1, device_id=target, device_id_type=MESH)
    pl.semaphore_wait(barrier, len(targets))


class Torus:
    def __init__(self):
        self.x, self.y, self.z, self.c = where_am_i()

    def at(self, axis, step):
        x, y, z = self.x, self.y, self.z
        if axis == "x":
            x = wrap(x + step)
        elif axis == "y":
            y = wrap(y + step)
        else:
            z = wrap(z + step)
        return device_at(x, y, z, self.c)

    def pos(self, axis):
        return {"x": self.x, "y": self.y, "z": self.z}[axis]

    def sibling(self):
        return device_at(self.x, self.y, self.z, 1 - self.c)

    def neighbours(self, axes="xyz", core=True):
        out = [self.at(a, s) for a in axes for s in (1, 2, 3)]
        return out + ([self.sibling()] if core else [])


PLANS = {
    "qkv": (320, 3840, 4, 8, 3),
    "out": (320, 1280, 4, 0, 1),
    "fc": (320, 5120, 8, 8, 4),
    "proj": (1280, 1280, 2, 1, 2),
}


def rect_of(rows, start, width, order, y, z, stage):
    if rows == 320:
        if stage == 0:
            return y * 80, 80, start + z * (width // 4), width // 4
        if order == "yz":
            return 0, 320, start + z * (width // 4), width // 4
        return y * 80, 80, start, width
    first, second = (y, z) if order == "yz" else (z, y)
    if stage == 0:
        return second * 320 + first * 80, 80, start, width
    return second * 320, 320, start, width


def part(ref, owner, rect):
    r, nr, c, nc = rect
    return ref.at[owner, pl.ds(pl.multiple_of(r, 16), nr), pl.ds(pl.multiple_of(c, 128), nc)]


def own_part(ref, rect):
    r, nr, c, nc = rect
    return ref.at[pl.ds(pl.multiple_of(r, 16), nr), pl.ds(pl.multiple_of(c, 128), nc)]


class Gather:
    def __init__(self, net, torus, name, src, full, lean):
        self.net, self.t, self.src, self.full, self.lean = net, torus, src, full, lean
        self.rows, cols, a, b, d = PLANS[name]
        half = torus.c * (cols // 2)
        self.regions = []
        at = 0
        for order, tiles in (("yz", a), ("zy", b)):
            if tiles:
                self.regions.append((order, half + at * 128, tiles * 128))
            at += tiles
        self.alone = (half + at * 128, d * 128)
        self.others = [wrap(torus.x + k) for k in (1, 2, 3)]
        self.got = {}

    def rect(self, region, stage, shift=0):
        order, start, width = region
        y, z = self.t.y, self.t.z
        axis = order[stage]
        if axis == "y":
            y = wrap(y + shift)
        else:
            z = wrap(z + shift)
        return rect_of(self.rows, start, width, order, y, z, stage)

    def start(self):
        t, net = self.t, self.net
        for i, region in enumerate(self.regions):
            rect = self.rect(region, 0)
            self.got[i, "x"] = [
                net.send(own_part(self.src, rect), part(self.full, t.x, rect), t.at("x", s)) for s in (1, 3, 2)
            ]

    def start_alone(self):
        t, net = self.t, self.net
        rect = (0, self.rows, *self.alone)
        self.got["alone"] = [
            net.send(own_part(self.src, rect), part(self.full, t.x, rect), t.at("x", s)) for s in (1, 3)
        ]

    def alone_on(self):
        t, net = self.t, self.net
        h = self.rows // 2
        one, two = self.got["alone"]
        start, width = self.alone
        whole = (0, self.rows, start, width)
        one.wait_recv()
        left = wrap(t.x - 1)
        rect = (0, h, start, width)
        a = net.send(part(self.full, left, rect), part(self.full, left, rect), t.at("x", 1))
        two.wait_recv()
        right = wrap(t.x + 1)
        rect = (h, h, start, width)
        b = net.send(part(self.full, right, rect), part(self.full, right, rect), t.at("x", 3))
        self.got["alone2"] = [a, b]
        self.got["core"] = [
            net.send(part(self.full, o, whole), part(self.full, o, whole), t.sibling()) for o in (left, right)
        ]

    def alone_end(self):
        for copy in self.got["alone2"]:
            copy.wait_recv()
        o = wrap(self.t.x + 2)
        whole = (0, self.rows, *self.alone)
        self.got["core"].append(self.net.send(part(self.full, o, whole), part(self.full, o, whole), self.t.sibling()))

    def spread(self, i, stage):
        region = self.regions[i]
        if stage == 0:
            for copy in self.got[i, "x"]:
                copy.wait_recv()
        else:
            for copy in self.got[i, 0, 2]:
                copy.wait_recv()
        axis = region[0][stage]
        rect = self.rect(region, stage)
        self.got[i, stage, 1] = [
            [self.net.send(part(self.full, o, rect), part(self.full, o, rect), self.t.at(axis, s)) for o in self.others]
            for s in (1, 3)
        ]

    def pass_on(self, i, stage):
        region = self.regions[i]
        axis = region[0][stage]
        ahead, behind = self.got[i, stage, 1]
        cut = 2 if self.lean else 1
        sent = []
        for copies, shift, to, owners in (
            (ahead, -1, 1, self.others[:cut]),
            (behind, 1, 3, self.others[cut:]),
        ):
            for copy in copies:
                copy.wait_recv()
            rect = self.rect(region, stage, shift)
            for o in owners:
                sent.append(self.net.send(part(self.full, o, rect), part(self.full, o, rect), self.t.at(axis, to)))
        self.got[i, stage, 2] = sent

    def share(self, i):
        for copy in self.got[i, 1, 2]:
            copy.wait_recv()
        order, start, width = self.regions[i]
        whole = (0, self.rows, start, width)
        for o in self.others:
            self.got["core"].append(
                self.net.send(part(self.full, o, whole), part(self.full, o, whole), self.t.sibling())
            )

    def finish(self):
        for copy in self.got["core"]:
            copy.wait_recv()


LAG = 0.5
NAMES = ("qkv", "out", "fc", "proj")


def gather_steps(gathers):
    q, o, f, p = gathers
    order = [lambda: q.start(), lambda: [g.start() for g in (o, f, p)], lambda: [g.start_alone() for g in gathers]]

    def both(g, what, *rest):
        for i in range(len(g.regions)):
            getattr(g, what)(i, *rest)

    stages = [("spread", (0,)), ("pass_on", (0,)), ("spread", (1,)), ("pass_on", (1,))]
    todo = []
    for lag, group in enumerate(((q, o), (f,), (p,))):
        for k, (what, rest) in enumerate(stages):
            todo.append((k + LAG * lag, lambda group=group, what=what, rest=rest: [both(g, what, *rest) for g in group]))
        todo.append((1 + LAG * lag, lambda group=group: [g.alone_on() for g in group]))
        todo.append((4 + LAG * lag, lambda group=group: [(both(g, "share"), g.alone_end()) for g in group]))
    order += [step for _, step in sorted(todo, key=lambda pair: pair[0])]
    return order


def gather_kernel(w_qkv, w_out, w_fc, w_proj, small, f_qkv, f_out, f_fc, f_proj, f_small, ssem, rsem, lsem, *held):
    t = Torus()
    greet(t.neighbours())
    net = Net(ssem, rsem)
    srcs, fulls = (w_qkv, w_out, w_fc, w_proj), (f_qkv, f_out, f_fc, f_proj)
    gathers = [Gather(net, t, n, s, f, i % 2) for i, (n, s, f) in enumerate(zip(NAMES, srcs, fulls))]
    smalls = [net.send(small, f_small.at[t.x], t.at("x", s)) for s in (1, 3, 2)]
    local = []
    for k, (s, f) in enumerate(zip(srcs + (small,), fulls + (f_small,))):
        local.append(pltpu.make_async_copy(s, held[k], lsem.at[k]))
        local[-1].start()
    for n, step in enumerate(gather_steps(gathers)):
        step()
        if n == 4:
            for k, f in enumerate(fulls + (f_small,)):
                local[k].wait()
                local[k] = pltpu.make_async_copy(held[k], f.at[t.x], lsem.at[k])
                local[k].start()
    for g in gathers:
        g.finish()
    for copy in smalls:
        copy.wait_recv()
    for copy in local:
        copy.wait()
    net.finish()


def gather_weights(w_qkv, w_out, w_fc, w_proj, small):
    any_space = pl.BlockSpec(memory_space=pl.ANY)
    n = 320
    srcs = (w_qkv, w_out, w_fc, w_proj, small)
    return pl.pallas_call(
        gather_kernel,
        name="gather_weights",
        out_shape=[jax.ShapeDtypeStruct((4,) + s.shape, s.dtype) for s in srcs],
        in_specs=[any_space] * 5,
        out_specs=[any_space] * 5,
        scratch_shapes=[pltpu.SemaphoreType.DMA((n,)), pltpu.SemaphoreType.DMA((n,)), pltpu.SemaphoreType.DMA((5,))]
        + [pltpu.VMEM(s.shape, s.dtype) for s in srcs],
        compiler_params=pltpu.CompilerParams(collective_id=0, has_side_effects=True),
    )(*srcs)


N_SEM_A = 64


def dot_t(a, b):
    return lax.dot_general(a, b, (((1,), (1,)), ((), ())), preferred_element_type=F32)


def causal(s, i):
    rows = lax.broadcasted_iota(jnp.int32, (256, 256), 0)
    cols = lax.broadcasted_iota(jnp.int32, (256, 256), 1)
    last = jnp.where(cols <= rows, s[:, 256 * i :], -1e30)
    return last if i == 0 else jnp.concatenate([s[:, : 256 * i], last], axis=1)


class Swap:
    def __init__(self, net, torus, parts):
        self.net, self.t, self.parts = net, torus, parts

    def pack_single(self, full, single):
        parts = self.parts
        for d in range(4):
            cols = [full[:, 1280 * k + 1024 + 64 * d : 1280 * k + 1088 + 64 * d] for k in range(parts)]
            if parts % 2:
                cols.append(jnp.zeros((256, 64), BF16))
            single[d] = jnp.concatenate(cols, axis=1)

    def out_pairs(self, full, box):
        t, net, got = self.t, self.net, []
        for p in range(2):
            sent = []
            for s in (1, 3, 2):
                d = wrap(t.x + s)
                for k in range(self.parts):
                    cols = pl.ds(pl.multiple_of(1280 * k + 256 * d + 128 * p, 128), 128)
                    sent.append(net.send(full.at[:, cols], box.at[p, k, t.x], t.at("x", s)))
            got.append(sent)
        return got

    def keep_pairs(self, full, box):
        for p in range(2):
            for k in range(self.parts):
                cols = pl.ds(pl.multiple_of(1280 * k + 256 * self.t.x + 128 * p, 128), 128)
                box[p, k, self.t.x] = full[:, cols]

    def out_single(self, single, box):
        t = self.t
        sent = [self.net.send(single.at[wrap(t.x + s)], box.at[t.x], t.at("x", s)) for s in (1, 3, 2)]
        return sent

    def back_pair(self, p, src, full):
        t, net, sent = self.t, self.net, []
        for s in (1, 3, 2):
            d = wrap(t.x + s)
            for k in range(self.parts):
                cols = pl.ds(pl.multiple_of(1280 * k + 256 * t.x + 128 * p, 128), 128)
                sent.append(net.send(src.at[d, k, p], full.at[:, cols], t.at("x", s)))
        return sent

    def keep_back(self, p, src, full):
        for k in range(self.parts):
            cols = pl.ds(pl.multiple_of(1280 * k + 256 * self.t.x + 128 * p, 128), 128)
            full[:, cols] = src[self.t.x, k, p]

    def unpack_single(self, box, full):
        for k in range(self.parts):
            cols = [box[d, :, 64 * k : 64 * k + 64] for d in range(4)]
            full[:, 1280 * k + 1024 : 1280 * (k + 1)] = jnp.concatenate(cols, axis=1)


def wait_all(copies):
    for copy in copies:
        copy.wait_recv()


def fwd_kernel(qkv, att, heads, lse, box, single, single_in, res, res_single, res_single_in, full, outs, ssem, rsem):
    t = Torus()
    greet(t.neighbours("x", core=False))
    net = Net(ssem, rsem)
    swap = Swap(net, t, 3)
    got = swap.out_pairs(qkv, box)
    swap.pack_single(qkv, single)
    got_single = swap.out_single(single, single_in)
    swap.keep_pairs(qkv, box)
    single_in[t.x] = single[t.x]
    lse[...] = jnp.zeros_like(lse)
    back = Swap(net, t, 1)
    sent = []

    def take_pair(p):
        wait_all(got[p])
        for k in range(3):
            for s in range(4):
                for j in range(2):
                    v = box[p, k, s, :, 64 * j : 64 * j + 64]
                    heads[k, 2 * p + j, 256 * s : 256 * (s + 1), :] = v * BF16(0.125) if k == 0 else v

    def take_single():
        wait_all(got_single)
        for k in range(3):
            for s in range(4):
                v = single_in[s, :, 64 * k : 64 * k + 64]
                heads[k, 4, 256 * s : 256 * (s + 1), :] = v * BF16(0.125) if k == 0 else v

    def one_head(h, j):
        lane = lax.broadcasted_iota(jnp.int32, (256, 128), 1)
        for i in range(4):
            rows = slice(256 * i, 256 * (i + 1))
            n = 256 * (i + 1)
            s = causal(dot_t(heads[0, h, rows, :], heads[1, h, :n, :]), i)
            top = jnp.max(s, axis=1, keepdims=True)
            p = jnp.exp(s - top)
            total = jnp.sum(p, axis=1, keepdims=True)
            lse[rows, :] = jnp.where(lane == h, top + jnp.log(total), lse[rows, :])
            o = jnp.dot(p.astype(BF16), heads[2, h, :n, :], preferred_element_type=F32)
            outs[j, rows, :] = (o / total).astype(BF16)

    for p in range(2):
        take_pair(p)

        def body(j, _):
            one_head(2 * p + j, j)
            return 0

        lax.fori_loop(0, 2, body, 0)
        for i in range(4):
            rows = slice(256 * i, 256 * (i + 1))
            res[i, 0, p] = jnp.concatenate([outs[0, rows, :], outs[1, rows, :]], axis=1)
        sent += back.back_pair(p, res, full)
        back.keep_back(p, res, full)
    take_single()
    one_head(4, 0)
    for i in range(4):
        res_single[i] = jnp.concatenate([outs[0, 256 * i : 256 * (i + 1), :], jnp.zeros((256, 64), BF16)], axis=1)
    sent_single = back.out_single(res_single, res_single_in)
    res_single_in[t.x] = res_single[t.x]
    wait_all(sent_single)
    back.unpack_single(res_single_in, full)
    wait_all(sent)
    att[...] = full[...]
    net.finish()


def attention(qkv):
    vm = pl.BlockSpec(memory_space=pltpu.VMEM)
    return pl.pallas_call(
        fwd_kernel,
        name="attention",
        out_shape=[
            jax.ShapeDtypeStruct((256, 1280), BF16),
            jax.ShapeDtypeStruct((3, 5, 1024, 64), BF16),
            jax.ShapeDtypeStruct((1024, 128), F32),
        ],
        in_specs=[vm],
        out_specs=[vm] * 3,
        scratch_shapes=[
            pltpu.VMEM((2, 3, 4, 256, 128), BF16),
            pltpu.VMEM((4, 256, 256), BF16),
            pltpu.VMEM((4, 256, 256), BF16),
            pltpu.VMEM((4, 1, 2, 256, 128), BF16),
            pltpu.VMEM((4, 256, 128), BF16),
            pltpu.VMEM((4, 256, 128), BF16),
            pltpu.VMEM((256, 1280), BF16),
            pltpu.VMEM((2, 1024, 64), BF16),
            pltpu.SemaphoreType.DMA((N_SEM_A,)),
            pltpu.SemaphoreType.DMA((N_SEM_A,)),
        ],
        compiler_params=pltpu.CompilerParams(collective_id=3, has_side_effects=True, vmem_limit_bytes=48 << 20),
    )(qkv)


def bwd_kernel(datt, heads, lse, gqkv, box, single, single_in, do, res, res_single, res_single_in, full, dkv, grads, ssem, rsem):
    t = Torus()
    greet(t.neighbours("x", core=False))
    net = Net(ssem, rsem)
    swap = Swap(net, t, 1)
    got = swap.out_pairs(datt, box)
    swap.pack_single(datt, single)
    got_single = swap.out_single(single, single_in)
    swap.keep_pairs(datt, box)
    single_in[t.x] = single[t.x]
    back = Swap(net, t, 3)
    sent = []

    def one_head(h, j):
        lane = lax.broadcasted_iota(jnp.int32, (256, 128), 1)
        dkv[...] = jnp.zeros_like(dkv)
        for i in range(4):
            rows = slice(256 * i, 256 * (i + 1))
            n = 256 * (i + 1)
            q, k, v, d = heads[0, h, rows, :], heads[1, h, :n, :], heads[2, h, :n, :], do[h, rows, :]
            total = jnp.sum(jnp.where(lane == h, lse[rows, :], 0.0), axis=1, keepdims=True)
            p = jnp.exp(causal(dot_t(q, k), i) - total)
            t1 = p * dot_t(d, v)
            inner = jnp.sum(t1, axis=1, keepdims=True)
            ds = (t1 - p * inner).astype(BF16)
            grads[0, j, rows, :] = (jnp.dot(ds, k, preferred_element_type=F32) * 0.125).astype(BF16)
            dkv[0, :, :n] += jnp.dot(q.T, ds, preferred_element_type=F32)
            dkv[1, :, :n] += jnp.dot(d.T, p.astype(BF16), preferred_element_type=F32)
        for k in range(2):
            grads[1 + k, j] = dkv[k].T.astype(BF16)

    for p in range(2):
        wait_all(got[p])
        for s in range(4):
            for j in range(2):
                do[2 * p + j, 256 * s : 256 * (s + 1), :] = box[p, 0, s, :, 64 * j : 64 * j + 64]

        def body(j, _):
            one_head(2 * p + j, j)
            return 0

        lax.fori_loop(0, 2, body, 0)
        for i in range(4):
            rows = slice(256 * i, 256 * (i + 1))
            for k in range(3):
                res[i, k, p] = jnp.concatenate([grads[k, 0, rows, :], grads[k, 1, rows, :]], axis=1)
        sent += back.back_pair(p, res, full)
        back.keep_back(p, res, full)
    wait_all(got_single)
    for s in range(4):
        do[4, 256 * s : 256 * (s + 1), :] = single_in[s, :, :64]
    one_head(4, 0)
    for i in range(4):
        rows = slice(256 * i, 256 * (i + 1))
        cols = [grads[k, 0, rows, :] for k in range(3)] + [jnp.zeros((256, 64), BF16)]
        res_single[i] = jnp.concatenate(cols, axis=1)
    sent_single = back.out_single(res_single, res_single_in)
    res_single_in[t.x] = res_single[t.x]
    wait_all(sent_single)
    back.unpack_single(res_single_in, full)
    wait_all(sent)
    gqkv[...] = full[...]
    net.finish()


def attention_back(datt, heads, lse):
    vm = pl.BlockSpec(memory_space=pltpu.VMEM)
    return pl.pallas_call(
        bwd_kernel,
        name="attention_back",
        out_shape=jax.ShapeDtypeStruct((256, 3840), BF16),
        in_specs=[vm] * 3,
        out_specs=vm,
        scratch_shapes=[
            pltpu.VMEM((2, 1, 4, 256, 128), BF16),
            pltpu.VMEM((4, 256, 128), BF16),
            pltpu.VMEM((4, 256, 128), BF16),
            pltpu.VMEM((5, 1024, 64), BF16),
            pltpu.VMEM((4, 3, 2, 256, 128), BF16),
            pltpu.VMEM((4, 256, 256), BF16),
            pltpu.VMEM((4, 256, 256), BF16),
            pltpu.VMEM((256, 3840), BF16),
            pltpu.VMEM((2, 64, 1024), F32),
            pltpu.VMEM((3, 2, 1024, 64), BF16),
            pltpu.SemaphoreType.DMA((N_SEM_A,)),
            pltpu.SemaphoreType.DMA((N_SEM_A,)),
        ],
        compiler_params=pltpu.CompilerParams(collective_id=4, has_side_effects=True, vmem_limit_bytes=48 << 20),
    )(datt, heads, lse)


ORDERS = ("xyz", "yzx", "zxy")


def view(ref, chosen, rows):
    return ref.at[tuple(chosen.get(a, slice(None)) for a in "xyz") + (pl.ds(*rows),)]


def leading(ref):
    return ref.shape[:-2]


def add_into(dst, *srcs):
    lead = leading(dst)
    count = 1
    for n in lead:
        count *= n

    def slab(i):
        index = []
        for n in reversed(lead):
            index.append(lax.rem(i, n))
            i = i // n
        return tuple(reversed(index))

    def body(i, _):
        at = slab(i)
        total = dst[at].astype(F32)
        for s in srcs:
            total = total + s[at].astype(F32)
        dst[at] = total.astype(BF16)
        return 0

    if count == 1 and not lead:
        total = dst[...].astype(F32)
        for s in srcs:
            total = total + s[...].astype(F32)
        dst[...] = total.astype(BF16)
    else:
        lax.fori_loop(0, count, body, 0)


def inbox_shapes(classes):
    out = []
    for (order, _, n) in classes:
        half = [2 if a == order[1] else 4 for a in "xyz" if a != order[0]]
        whole = [4, 4]
        out += [half + [n, 128]] * 2 + [whole + [n, 128]] * 2
        out += [[2, n, 128]] * 2 + [[4, n, 128]] * 2
        out += [[3, n, 128]]
    return [pltpu.VMEM(tuple(s), BF16) for s in out]


PER_CLASS = 9


class Lane:
    def __init__(self, net, torus, acc, inbox, order, row, n):
        self.net, self.t, self.acc, self.inbox, self.order = net, torus, acc, inbox, order
        self.rows = (row, n)
        self.fixed = {}
        self.got = {}

    def halves(self, phase):
        a = self.order[phase + 1]
        return [{a: pl.ds(0, 2)}, {a: pl.ds(2, 2)}]

    def box_half(self, box, phase, half):
        if phase == 1:
            return box.at[pl.ds(2 * half, 2)]
        left = [a for a in "xyz" if a != self.order[0]]
        cut = left.index(self.order[1])
        return box.at[(slice(None),) * cut + (pl.ds(2 * half, 2),)]

    def first(self, phase):
        axis = self.order[phase]
        p = self.t.pos(axis)
        h = self.halves(phase)
        b = self.inbox[4 * phase : 4 * phase + 4]
        at = lambda shift, cut: view(self.acc, {**self.fixed, axis: wrap(p + shift), **cut}, self.rows)
        up, down = self.t.at(axis, 1), self.t.at(axis, 3)
        far = [self.net.send(at(2, h[0]), b[0], up), self.net.send(at(2, h[1]), b[1], down)]
        near = [
            self.net.send(at(1, h[1]), self.box_half(b[2], phase, 1), up),
            self.net.send(at(3, h[0]), self.box_half(b[3], phase, 0), down),
        ]
        self.got[phase] = (far, near)

    def second(self, phase):
        axis = self.order[phase]
        p = self.t.pos(axis)
        h = self.halves(phase)
        b = self.inbox[4 * phase : 4 * phase + 4]
        at = lambda shift, cut: view(self.acc, {**self.fixed, axis: wrap(p + shift), **cut}, self.rows)
        up, down = self.t.at(axis, 1), self.t.at(axis, 3)
        far, near = self.got[phase]
        far[0].wait_recv()
        add_into(at(1, h[0]), b[0])
        near.append(self.net.send(at(1, h[0]), self.box_half(b[2], phase, 0), up))
        far[1].wait_recv()
        add_into(at(3, h[1]), b[1])
        near.append(self.net.send(at(3, h[1]), self.box_half(b[3], phase, 1), down))

    def third(self, phase):
        axis = self.order[phase]
        p = self.t.pos(axis)
        b = self.inbox[4 * phase : 4 * phase + 4]
        for copy in self.got[phase][1]:
            copy.wait_recv()
        self.fixed[axis] = p
        add_into(view(self.acc, self.fixed, self.rows), b[2], b[3])

    def last(self):
        axis = self.order[2]
        p = self.t.pos(axis)
        box = self.inbox[8]
        self.got[2] = [
            self.net.send(view(self.acc, {**self.fixed, axis: wrap(p + s)}, self.rows), box.at[s - 1], self.t.at(axis, s))
            for s in (1, 3, 2)
        ]

    def done(self):
        axis = self.order[2]
        for copy in self.got[2]:
            copy.wait_recv()
        self.fixed[axis] = self.t.pos(axis)
        box = self.inbox[8]
        add_into(view(self.acc, self.fixed, self.rows), box.at[0], box.at[1], box.at[2])


class Spread:
    def __init__(self, net, torus, acc, out, order, row, n, sem):
        self.net, self.t, self.out, self.order, self.rows, self.sem = net, torus, out, order, (row, n), sem
        self.own = view(acc, {"x": torus.x, "y": torus.y, "z": torus.z}, self.rows)

    def place(self, y, z):
        return self.out.at[self.t.c, y, z, pl.ds(*self.rows)]

    def band(self, v, b=slice(None)):
        y, z = (b, v) if self.order == "yz" else (v, b)
        return self.place(y, z)

    def start(self):
        t = self.t
        here = self.place(t.y, t.z)
        self.keep = pltpu.make_async_copy(self.own, here, self.sem)
        self.keep.start()
        self.first = [self.net.send(self.own, here, t.at(self.order[0], s)) for s in (1, 3, 2)]

    def second(self):
        t, axis = self.t, self.order[1]
        for copy in self.first:
            copy.wait_recv()
        self.keep.wait()
        here = self.band(t.pos(axis))
        self.near = [self.net.send(here, here, t.at(axis, s)) for s in (1, 3)]

    def third(self):
        t, axis = self.t, self.order[1]
        p = t.pos(axis)
        self.far = []
        for copy, shift, to, b in ((self.near[0], 3, 1, pl.ds(0, 2)), (self.near[1], 1, 3, pl.ds(2, 2))):
            copy.wait_recv()
            there = self.band(wrap(p + shift), b)
            self.far.append(self.net.send(there, there, t.at(axis, to)))

    def share(self):
        for copy in self.far:
            copy.wait_recv()
        whole = self.place(slice(None), slice(None))
        self.core = self.net.send(whole, whole, self.t.sibling())

    def finish(self):
        self.core.wait_recv()


def reduce_steps(lanes, spreads):
    steps = []
    for phase in (0, 1):
        for what in ("first", "second", "third"):
            if phase == 0 and what == "first":
                continue
            for lane in lanes:
                steps.append((lambda lane=lane, what=what, phase=phase: getattr(lane, what)(phase)))
    for what in ("last", "done"):
        for lane in lanes:
            steps.append(getattr(lane, what))
            if what == "done":
                steps += [s.start for owner, s in spreads if owner is lane]
    for what in ("second", "third", "share", "finish"):
        steps += [getattr(s, what) for _, s in spreads]
    return steps


def store_blocks(acc, x, first, unit, blocks, rows):
    at = 0
    for block in blocks:
        done = 0
        while done < 320:
            n = min(320 - done, rows - at % rows)
            s = at // rows
            slab = first + s
            acc[x, slab // 4, lax.rem(slab, 4), pl.ds(at % rows, n), :] = block[done : done + n]
            done += n
            at += n


GROUPS = {
    "mlp": (800, (272, 272, 272)),
    "attn": (400, (144, 144, 128)),
}


def classes_of(group):
    row, out = 0, []
    for order, n in zip(ORDERS, GROUPS[group][1]):
        out.append((order, row, n))
        row += n
    return out


def spreads_of(group):
    a, b, c = classes_of(group)
    h = c[2] // 32 * 16
    return [(0, "yz", a[1], a[2]), (1, "zy", b[1], b[2]), (2, "yz", c[1], h), (2, "zy", c[1] + h, c[2] - h)]


def scratch_of(group):
    rows = GROUPS[group][0] + 16
    return [pltpu.VMEM((4, 4, 4, rows, 128), BF16)] + inbox_shapes(classes_of(group))


def begin_reduce(group, net, torus, acc, inbox, out, sems):
    lanes = [
        Lane(net, torus, acc, inbox[PER_CLASS * k : PER_CLASS * (k + 1)], *c) for k, c in enumerate(classes_of(group))
    ]
    spreads = [
        (lanes[k], Spread(net, torus, acc, out, order, row, n, sems.at[i]))
        for i, (k, order, row, n) in enumerate(spreads_of(group))
    ]
    return lanes, spreads


def store_small(acc, total, rows):
    for x in range(4):
        for y in range(4):
            for z in range(4):
                k = y * 4 + z
                v = total[x, 16 * k : 16 * k + 16, :] if k < 2 else jnp.zeros((16, 128), F32)
                acc[x, y, z, pl.ds(rows, 16), :] = v.astype(BF16)


def product(lhs, rhs, acc, x, first, unit, rows):
    out = jnp.dot(lhs, rhs, preferred_element_type=F32).astype(BF16)
    store_blocks(acc, x, first, unit, [out[:, 128 * t : 128 * (t + 1)] for t in range(5)], rows)


N_SEM = 100


def mlp_kernel(n2t, actt, gp, cot, small, out, n2t_v, actt_v, gp_v, cot_v, small_v, ssem, rsem, lsem, acc, *inbox):
    t = Torus()
    greet(t.neighbours())
    net = Net(ssem, rsem)
    sib, c = t.sibling(), t.c
    copies, local = [], []

    def both(src, own_dst, other_dst, own_src=None):
        copies.append(net.send(src, other_dst, sib))
        k = len(local)
        local.append(pltpu.make_async_copy(src if own_src is None else own_src, own_dst, lsem.at[k]))
        local[-1].start()

    both(n2t, n2t_v.at[:, pl.ds(0, 256)], n2t_v.at[:, pl.ds(256, 256)])
    both(cot, cot_v.at[pl.ds(0, 256)], cot_v.at[pl.ds(256, 256)])
    for s in range(4):
        mine, theirs = s * 1280 + c * 640, s * 1280 + (1 - c) * 640
        both(
            gp.at[:, pl.ds(pl.multiple_of(theirs, 128), 640)],
            gp_v.at[s, pl.ds(0, 256)], gp_v.at[s, pl.ds(256, 256)],
            gp.at[:, pl.ds(pl.multiple_of(mine, 128), 640)],
        )
        both(
            actt.at[pl.ds(pl.multiple_of(theirs, 16), 640)],
            actt_v.at[pl.ds(s * 640, 640), pl.ds(0, 256)], actt_v.at[pl.ds(s * 640, 640), pl.ds(256, 256)],
            actt.at[pl.ds(pl.multiple_of(mine, 16), 640)],
        )
    both(small, small_v.at[0], small_v.at[1])
    for copy in copies:
        copy.wait_recv()
    for copy in local:
        copy.wait()
    small_v[0] = small_v[0] + small_v[1]
    store_small(acc, small_v.at[0], 800)

    def fc(i, _):
        x, s = i // 4, lax.rem(i, 4)
        product(n2t_v[pl.ds(pl.multiple_of(x * 320, 16), 320), :], gp_v[s], acc, x, s * 2, 2, 800)
        return 0

    lax.fori_loop(0, 16, fc, 0)

    def proj(i, _):
        x, sub = i // 2, lax.rem(i, 2)
        lhs = actt_v[pl.ds(pl.multiple_of(i * 320, 16), 320), :]
        for half in range(2):
            product(lhs, cot_v[:, 640 * half : 640 * (half + 1)], acc, x, 8 + sub * 4 + half * 2, 2, 800)
        return 0

    lax.fori_loop(0, 8, proj, 0)
    lanes, spreads = begin_reduce("mlp", net, t, acc, inbox, out, lsem)
    for lane in lanes:
        lane.first(0)
    for step in reduce_steps(lanes, spreads):
        step()
    net.finish()


def reduce_mlp(n2t, actt, gp, cot, small):
    anys = pl.BlockSpec(memory_space=pl.ANY)
    return pl.pallas_call(
        mlp_kernel,
        name="reduce_mlp",
        out_shape=jax.ShapeDtypeStruct((2, 4, 4, 816, 128), BF16),
        in_specs=[anys] * 5,
        out_specs=anys,
        scratch_shapes=[
            pltpu.VMEM((1280, 512), BF16),
            pltpu.VMEM((2560, 512), BF16),
            pltpu.VMEM((4, 512, 640), BF16),
            pltpu.VMEM((512, 1280), BF16),
            pltpu.VMEM((2, 4, 32, 128), F32),
            pltpu.SemaphoreType.DMA((N_SEM,)),
            pltpu.SemaphoreType.DMA((N_SEM,)),
            pltpu.SemaphoreType.DMA((16,)),
        ]
        + scratch_of("mlp"),
        compiler_params=pltpu.CompilerParams(collective_id=1, has_side_effects=True, vmem_limit_bytes=56 << 20),
    )(n2t, actt, gp, cot, small)


def attn_kernel(n1t, gqkv, attt, gb, small, out, n1t_v, gqkv_v, attt_v, gb_v, small_v, ssem, rsem, lsem, acc, *inbox):
    t = Torus()
    greet(t.neighbours())
    net = Net(ssem, rsem)
    sib, c = t.sibling(), t.c
    copies, local = [], []

    def both(src, own_dst, other_dst, own_src=None):
        copies.append(net.send(src, other_dst, sib))
        k = len(local)
        local.append(pltpu.make_async_copy(src if own_src is None else own_src, own_dst, lsem.at[k]))
        local[-1].start()

    both(n1t, n1t_v.at[:, pl.ds(0, 256)], n1t_v.at[:, pl.ds(256, 256)])
    both(attt, attt_v.at[:, pl.ds(0, 256)], attt_v.at[:, pl.ds(256, 256)])
    for s in range(3):
        mine, theirs = c * 1920 + s * 640, (1 - c) * 1920 + s * 640
        both(
            gqkv.at[:, pl.ds(pl.multiple_of(theirs, 128), 640)],
            gqkv_v.at[s, pl.ds(0, 256)], gqkv_v.at[s, pl.ds(256, 256)],
            gqkv.at[:, pl.ds(pl.multiple_of(mine, 128), 640)],
        )
    both(
        gb.at[:, pl.ds(pl.multiple_of((1 - c) * 640, 128), 640)], gb_v.at[pl.ds(0, 256)], gb_v.at[pl.ds(256, 256)],
        gb.at[:, pl.ds(pl.multiple_of(c * 640, 128), 640)],
    )
    both(small, small_v.at[0], small_v.at[1])
    for copy in copies:
        copy.wait_recv()
    for copy in local:
        copy.wait()
    small_v[0] = small_v[0] + small_v[1]
    store_small(acc, small_v.at[0], 400)

    def qkv(i, _):
        x, s = i // 3, lax.rem(i, 3)
        product(n1t_v[pl.ds(pl.multiple_of(x * 320, 16), 320), :], gqkv_v[s], acc, x, s * 4, 4, 400)
        return 0

    lax.fori_loop(0, 12, qkv, 0)

    def outp(x, _):
        product(attt_v[pl.ds(pl.multiple_of(x * 320, 16), 320), :], gb_v[...], acc, x, 12, 4, 400)
        return 0

    lax.fori_loop(0, 4, outp, 0)
    lanes, spreads = begin_reduce("attn", net, t, acc, inbox, out, lsem)
    for lane in lanes:
        lane.first(0)
    for step in reduce_steps(lanes, spreads):
        step()
    net.finish()


def reduce_attn(n1t, gqkv, attt, gb, small):
    anys = pl.BlockSpec(memory_space=pl.ANY)
    return pl.pallas_call(
        attn_kernel,
        name="reduce_attn",
        out_shape=jax.ShapeDtypeStruct((2, 4, 4, 416, 128), BF16),
        in_specs=[anys] * 5,
        out_specs=anys,
        scratch_shapes=[
            pltpu.VMEM((1280, 512), BF16),
            pltpu.VMEM((3, 512, 640), BF16),
            pltpu.VMEM((1280, 512), BF16),
            pltpu.VMEM((512, 640), BF16),
            pltpu.VMEM((2, 4, 32, 128), F32),
            pltpu.SemaphoreType.DMA((N_SEM,)),
            pltpu.SemaphoreType.DMA((N_SEM,)),
            pltpu.SemaphoreType.DMA((16,)),
        ]
        + scratch_of("attn"),
        compiler_params=pltpu.CompilerParams(collective_id=2, has_side_effects=True, vmem_limit_bytes=56 << 20),
    )(n1t, gqkv, attt, gb, small)


def unpack_mlp_kernel(src, fc, proj):
    q = pl.program_id(1)
    flat = [src[0, 0, i, :800].astype(F32) for i in range(2)]
    flat = jnp.concatenate(flat, axis=0)

    @pl.when(q < 4)
    def _():
        for k in range(5):
            fc[:, 128 * k : 128 * (k + 1)] = flat[320 * k : 320 * (k + 1)]

    @pl.when(q >= 4)
    def _():
        for k in range(5):
            proj[:, 128 * k : 128 * (k + 1)] = flat[320 * k : 320 * (k + 1)]


def unpack_mlp(packed):
    return pl.pallas_call(
        unpack_mlp_kernel,
        name="unpack_mlp",
        grid=(2, 8),
        out_shape=[jax.ShapeDtypeStruct((320, 5120), F32), jax.ShapeDtypeStruct((1280, 1280), F32)],
        in_specs=[pl.BlockSpec((1, 1, 2, 816, 128), lambda c, q: (c, q // 2, q % 2, 0, 0))],
        out_specs=[
            pl.BlockSpec((320, 640), lambda c, q: (0, jnp.where(q < 4, q * 2 + c, 6 + c))),
            pl.BlockSpec((320, 640), lambda c, q: (c * 2 + jnp.where(q < 4, 0, (q - 4) // 2), jnp.where(q < 4, 0, q % 2))),
        ],
    )(packed)


def unpack_attn_kernel(src, qkv, out):
    q = pl.program_id(1)
    flat = jnp.concatenate([src[0, 0, i, :400].astype(F32) for i in range(4)], axis=0)

    @pl.when(q < 3)
    def _():
        for k in range(5):
            qkv[:, 128 * k : 128 * (k + 1)] = flat[320 * k : 320 * (k + 1)]

    @pl.when(q == 3)
    def _():
        for k in range(5):
            out[:, 128 * k : 128 * (k + 1)] = flat[320 * k : 320 * (k + 1)]


def unpack_attn(packed):
    return pl.pallas_call(
        unpack_attn_kernel,
        name="unpack_attn",
        grid=(2, 4),
        out_shape=[jax.ShapeDtypeStruct((320, 3840), F32), jax.ShapeDtypeStruct((320, 1280), F32)],
        in_specs=[pl.BlockSpec((1, 1, 4, 416, 128), lambda c, q: (c, q, 0, 0, 0))],
        out_specs=[
            pl.BlockSpec((320, 640), lambda c, q: (0, c * 3 + jnp.minimum(q, 2))),
            pl.BlockSpec((320, 640), lambda c, q: (0, c)),
        ],
    )(packed)


def unpack_small(packed, rows, count):
    return packed[0, 0, 0:2, rows:, :].astype(F32).reshape(-1)[:count]


HEAD_DIM = 64
EPS = 1e-05
GELU_A, GELU_B = 0.7978845608028654, 0.044715


def norm(v):
    center = v - jnp.mean(v, axis=-1, keepdims=True)
    scale = lax.rsqrt(jnp.mean(center * center, axis=-1, keepdims=True) + EPS)
    return center * scale, scale


def norm_back(grad, hat, scale, gain):
    inner = grad * gain
    rows = scale * (
        inner - jnp.mean(inner, axis=-1, keepdims=True) - hat * jnp.mean(inner * hat, axis=-1, keepdims=True)
    )
    return rows, jnp.sum(grad * hat, axis=0), jnp.sum(grad, axis=0)


def dot(a, b):
    return jnp.dot(a, b, preferred_element_type=F32)


def dot_cols(a, b):
    return lax.dot_general(a, b, (((1,), (1,)), ((), ())), preferred_element_type=F32)


def small_rows(*vectors):
    flat = jnp.concatenate([v.reshape(4, -1) for v in vectors], axis=1)
    return jnp.pad(flat, ((0, 0), (0, 4096 - flat.shape[1]))).reshape(4, 32, 128)


def shards(
    tokens,
    cotangent,
    ln1_gain,
    ln1_bias,
    w_qkv,
    qv_bias,
    w_out,
    out_bias,
    ln2_gain,
    ln2_bias,
    w_fc,
    fc_bias,
    w_proj,
    proj_bias,
):
    own = (ln1_gain, ln1_bias, qv_bias, out_bias, ln2_gain, ln2_bias, fc_bias, proj_bias)
    small = jnp.concatenate(own + (jnp.zeros((256,), BF16),)).reshape(32, 128)
    f_qkv, f_out, f_fc, f_proj, f_small = gather_weights(w_qkv, w_out, w_fc, w_proj, small)
    f_qkv, f_out, f_fc, f_proj = (
        f_qkv.reshape(1280, 3840),
        f_out.reshape(1280, 1280),
        f_fc.reshape(1280, 5120),
        f_proj.reshape(5120, 1280),
    )
    f_small = f_small.reshape(4, 4096).astype(F32)
    params, at = [], 0
    for v in own:
        params.append(f_small[:, at : at + v.shape[0]].reshape(-1))
        at += v.shape[0]
    gain_one, shift_one, bias_qv, bias_out, gain_two, shift_two, bias_fc, bias_proj = params

    rows = tokens[0].astype(F32)
    hat_one, scale_one = norm(rows)
    normed_one = (hat_one * gain_one + shift_one).astype(BF16)
    bias_qkv = jnp.concatenate([bias_qv[:1280], jnp.zeros((1280,), F32), bias_qv[1280:]])
    qkv = (dot(normed_one, f_qkv) + bias_qkv).astype(BF16)
    attended, heads, lse = attention(qkv)
    middle = rows + dot(attended, f_out) + bias_out
    hat_two, scale_two = norm(middle)
    normed_two = (hat_two * gain_two + shift_two).astype(BF16)
    pre = dot(normed_two, f_fc) + bias_fc
    bend = jnp.tanh(GELU_A * (pre + GELU_B * pre * pre * pre))
    act = (0.5 * pre * (1.0 + bend)).astype(BF16)
    block_out = (middle + dot(act, f_proj) + bias_proj).astype(BF16)

    cot = cotangent[0]
    cot_rows = cot.astype(F32)
    slope = 0.5 * (1.0 + bend) + 0.5 * pre * (1.0 - bend * bend) * GELU_A * (1.0 + 3.0 * GELU_B * pre * pre)
    grad_pre = (dot_cols(cot, f_proj) * slope).astype(BF16)
    grad_two, grad_gain_two, grad_shift_two = norm_back(dot_cols(grad_pre, f_fc), hat_two, scale_two, gain_two)
    grad_middle = cot_rows + grad_two
    grad_branch = grad_middle.astype(BF16)
    small_mlp = small_rows(
        grad_gain_two, grad_shift_two, jnp.sum(grad_pre.astype(F32), axis=0), jnp.sum(cot_rows, axis=0)
    )
    packed_mlp = reduce_mlp(normed_two.T, act.T, grad_pre, cot, small_mlp)

    grad_attended = dot_cols(grad_branch, f_out).astype(BF16)
    grad_qkv = attention_back(grad_attended, heads, lse)
    grad_one, grad_gain_one, grad_shift_one = norm_back(dot_cols(grad_qkv, f_qkv), hat_one, scale_one, gain_one)
    grad_tokens = (grad_middle + grad_one).astype(BF16)
    sums = jnp.sum(grad_qkv.astype(F32), axis=0)
    small_attn = small_rows(
        grad_gain_one,
        grad_shift_one,
        jnp.concatenate([sums[:1280], sums[2560:]]),
        jnp.sum(grad_branch.astype(F32), axis=0),
    )
    packed_attn = reduce_attn(normed_one.T, grad_qkv, attended.T, grad_branch, small_attn)

    g_fc, g_proj = unpack_mlp(packed_mlp)
    g_qkv, g_out = unpack_attn(packed_attn)
    s_mlp = unpack_small(packed_mlp, 800, 2240)
    s_attn = unpack_small(packed_attn, 400, 1600)
    return (
        block_out[None],
        grad_tokens[None],
        s_attn[:320],
        s_attn[320:640],
        g_qkv,
        s_attn[640:1280],
        g_out,
        s_attn[1280:1600],
        s_mlp[:320],
        s_mlp[320:640],
        g_fc,
        s_mlp[640:1920],
        g_proj,
        s_mlp[1920:2240],
    )


def solution(mesh):
    vector, matrix, batch = P("shard"), P("shard", None), P("rep", "shard", None)
    placed = (batch, batch, vector, vector, matrix, vector, matrix, vector, vector, vector, matrix, vector, matrix, vector)
    return jax.shard_map(shards, mesh=mesh, in_specs=placed, out_specs=placed, check_vma=False)
```

```python
import jax
import jax.numpy as jnp
from jax import lax
from jax.experimental import pallas as pl
from jax.experimental.pallas import tpu as pltpu
from jax.sharding import PartitionSpec as P

MESH = pl.DeviceIdType.MESH
F32, BF16 = jnp.float32, jnp.bfloat16


def where_am_i():
    rep = lax.axis_index("rep")
    return lax.axis_index("shard"), (rep // 2) % 4, rep // 8, rep % 2


def device_at(x, y, z, c):
    return {"rep": (z * 4 + y) * 2 + c, "shard": x}


def wrap(v):
    return lax.rem(v + 4, 4)


class Net:
    def __init__(self, send_sems, recv_sems):
        self.send_sems, self.recv_sems, self.used = send_sems, recv_sems, 0
        self.all = []

    def send(self, src, dst, target):
        copy = pltpu.make_async_remote_copy(
            src_ref=src, dst_ref=dst,
            send_sem=self.send_sems.at[self.used], recv_sem=self.recv_sems.at[self.used],
            device_id=target, device_id_type=MESH,
        )
        copy.start()
        self.used += 1
        self.all.append(copy)
        return copy

    def finish(self):
        for copy in self.all:
            copy.wait_send()


def greet(targets):
    barrier = pltpu.get_barrier_semaphore()
    for target in targets:
        pl.semaphore_signal(barrier, 1, device_id=target, device_id_type=MESH)
    pl.semaphore_wait(barrier, len(targets))


class Torus:
    def __init__(self):
        self.x, self.y, self.z, self.c = where_am_i()

    def at(self, axis, step):
        x, y, z = self.x, self.y, self.z
        if axis == "x":
            x = wrap(x + step)
        elif axis == "y":
            y = wrap(y + step)
        else:
            z = wrap(z + step)
        return device_at(x, y, z, self.c)

    def pos(self, axis):
        return {"x": self.x, "y": self.y, "z": self.z}[axis]

    def sibling(self):
        return device_at(self.x, self.y, self.z, 1 - self.c)

    def neighbours(self, axes="xyz", core=True):
        out = [self.at(a, s) for a in axes for s in (1, 2, 3)]
        return out + ([self.sibling()] if core else [])


PLANS = {
    "qkv": (320, 3840, 4, 8, 3),
    "out": (320, 1280, 4, 0, 1),
    "fc": (320, 5120, 8, 8, 4),
    "proj": (1280, 1280, 2, 1, 2),
}


def rect_of(rows, start, width, order, y, z, stage):
    if rows == 320:
        if stage == 0:
            return y * 80, 80, start + z * (width // 4), width // 4
        if order == "yz":
            return 0, 320, start + z * (width // 4), width // 4
        return y * 80, 80, start, width
    first, second = (y, z) if order == "yz" else (z, y)
    if stage == 0:
        return second * 320 + first * 80, 80, start, width
    return second * 320, 320, start, width


def part(ref, owner, rect):
    r, nr, c, nc = rect
    return ref.at[owner, pl.ds(pl.multiple_of(r, 16), nr), pl.ds(pl.multiple_of(c, 128), nc)]


def own_part(ref, rect):
    r, nr, c, nc = rect
    return ref.at[pl.ds(pl.multiple_of(r, 16), nr), pl.ds(pl.multiple_of(c, 128), nc)]


class Gather:
    def __init__(self, net, torus, name, src, full, lean):
        self.net, self.t, self.src, self.full, self.lean = net, torus, src, full, lean
        self.rows, cols, a, b, d = PLANS[name]
        half = torus.c * (cols // 2)
        self.regions = []
        at = 0
        for order, tiles in (("yz", a), ("zy", b)):
            if tiles:
                self.regions.append((order, half + at * 128, tiles * 128))
            at += tiles
        self.alone = (half + at * 128, d * 128)
        self.others = [wrap(torus.x + k) for k in (1, 2, 3)]
        self.got = {}

    def rect(self, region, stage, shift=0):
        order, start, width = region
        y, z = self.t.y, self.t.z
        axis = order[stage]
        if axis == "y":
            y = wrap(y + shift)
        else:
            z = wrap(z + shift)
        return rect_of(self.rows, start, width, order, y, z, stage)

    def both(self, what, *rest):
        for i in range(len(self.regions)):
            getattr(self, what)(i, *rest)

    def start(self):
        t, net = self.t, self.net
        for i, region in enumerate(self.regions):
            rect = self.rect(region, 0)
            self.got[i, "x"] = [
                net.send(own_part(self.src, rect), part(self.full, t.x, rect), t.at("x", s)) for s in (1, 3, 2)
            ]

    def start_alone(self):
        t, net = self.t, self.net
        rect = (0, self.rows, *self.alone)
        self.got["alone"] = [
            net.send(own_part(self.src, rect), part(self.full, t.x, rect), t.at("x", s)) for s in (1, 3)
        ]

    def alone_on(self):
        t, net = self.t, self.net
        h = self.rows // 2
        one, two = self.got["alone"]
        start, width = self.alone
        whole = (0, self.rows, start, width)
        one.wait_recv()
        left = wrap(t.x - 1)
        rect = (0, h, start, width)
        a = net.send(part(self.full, left, rect), part(self.full, left, rect), t.at("x", 1))
        two.wait_recv()
        right = wrap(t.x + 1)
        rect = (h, h, start, width)
        b = net.send(part(self.full, right, rect), part(self.full, right, rect), t.at("x", 3))
        self.got["alone2"] = [a, b]
        self.got["core"] = [
            net.send(part(self.full, o, whole), part(self.full, o, whole), t.sibling()) for o in (left, right)
        ]

    def alone_end(self):
        for copy in self.got["alone2"]:
            copy.wait_recv()
        o = wrap(self.t.x + 2)
        whole = (0, self.rows, *self.alone)
        self.got["core"].append(self.net.send(part(self.full, o, whole), part(self.full, o, whole), self.t.sibling()))

    def spread(self, i, stage):
        region = self.regions[i]
        if stage == 0:
            for copy in self.got[i, "x"]:
                copy.wait_recv()
        else:
            for copy in self.got[i, 0, 2]:
                copy.wait_recv()
        axis = region[0][stage]
        rect = self.rect(region, stage)
        self.got[i, stage, 1] = [
            [self.net.send(part(self.full, o, rect), part(self.full, o, rect), self.t.at(axis, s)) for o in self.others]
            for s in (1, 3)
        ]

    def pass_on(self, i, stage):
        region = self.regions[i]
        axis = region[0][stage]
        ahead, behind = self.got[i, stage, 1]
        cut = 2 if self.lean else 1
        sent = []
        for copies, shift, to, owners in (
            (ahead, -1, 1, self.others[:cut]),
            (behind, 1, 3, self.others[cut:]),
        ):
            for copy in copies:
                copy.wait_recv()
            rect = self.rect(region, stage, shift)
            for o in owners:
                sent.append(self.net.send(part(self.full, o, rect), part(self.full, o, rect), self.t.at(axis, to)))
        self.got[i, stage, 2] = sent

    def share(self, i):
        for copy in self.got[i, 1, 2]:
            copy.wait_recv()
        order, start, width = self.regions[i]
        whole = (0, self.rows, start, width)
        for o in self.others:
            self.got["core"].append(
                self.net.send(part(self.full, o, whole), part(self.full, o, whole), self.t.sibling())
            )

    def finish(self):
        for copy in self.got["core"]:
            copy.wait_recv()


LAG = 0.5


def dot_t(a, b):
    return lax.dot_general(a, b, (((1,), (1,)), ((), ())), preferred_element_type=F32)


def causal(s, i):
    rows = lax.broadcasted_iota(jnp.int32, (256, 256), 0)
    cols = lax.broadcasted_iota(jnp.int32, (256, 256), 1)
    last = jnp.where(cols <= rows, s[:, 256 * i :], -1e30)
    return last if i == 0 else jnp.concatenate([s[:, : 256 * i], last], axis=1)


class Swap:
    def __init__(self, net, torus, parts):
        self.net, self.t, self.parts = net, torus, parts

    def pack_single(self, full, single):
        parts = self.parts
        for d in range(4):
            cols = [full[:, 1280 * k + 1024 + 64 * d : 1280 * k + 1088 + 64 * d] for k in range(parts)]
            if parts % 2:
                cols.append(jnp.zeros((256, 64), BF16))
            single[d] = jnp.concatenate(cols, axis=1)

    def out_pairs(self, full, box):
        t, net, got = self.t, self.net, []
        for p in range(2):
            sent = []
            for s in (1, 3, 2):
                d = wrap(t.x + s)
                for k in range(self.parts):
                    cols = pl.ds(pl.multiple_of(1280 * k + 256 * d + 128 * p, 128), 128)
                    sent.append(net.send(full.at[:, cols], box.at[p, k, t.x], t.at("x", s)))
            got.append(sent)
        return got

    def keep_pairs(self, full, box):
        for p in range(2):
            for k in range(self.parts):
                cols = pl.ds(pl.multiple_of(1280 * k + 256 * self.t.x + 128 * p, 128), 128)
                box[p, k, self.t.x] = full[:, cols]

    def out_single(self, single, box):
        t = self.t
        sent = [self.net.send(single.at[wrap(t.x + s)], box.at[t.x], t.at("x", s)) for s in (1, 3, 2)]
        return sent

    def back_pair(self, p, src, full):
        t, net, sent = self.t, self.net, []
        for s in (1, 3, 2):
            d = wrap(t.x + s)
            for k in range(self.parts):
                cols = pl.ds(pl.multiple_of(1280 * k + 256 * t.x + 128 * p, 128), 128)
                sent.append(net.send(src.at[d, k, p], full.at[:, cols], t.at("x", s)))
        return sent

    def keep_back(self, p, src, full):
        for k in range(self.parts):
            cols = pl.ds(pl.multiple_of(1280 * k + 256 * self.t.x + 128 * p, 128), 128)
            full[:, cols] = src[self.t.x, k, p]

    def unpack_single(self, box, full):
        for k in range(self.parts):
            cols = [box[d, :, 64 * k : 64 * k + 64] for d in range(4)]
            full[:, 1280 * k + 1024 : 1280 * (k + 1)] = jnp.concatenate(cols, axis=1)


def wait_all(copies):
    for copy in copies:
        copy.wait_recv()


EPS = 1e-05
VECTORS = ("ln1_gain", "ln1_bias", "qv_bias", "out_bias", "ln2_gain", "ln2_bias", "proj_bias", "fc_bias")
SIZES = (320, 320, 640, 320, 320, 320, 320, 1280)


def whole_vector(small, name):
    k = VECTORS.index(name)
    return jnp.concatenate([small[x, k : k + 1, : SIZES[k]] for x in range(4)], axis=1)


def dot(a, b):
    return jnp.dot(a, b, preferred_element_type=F32)


def norm(v):
    center = v - jnp.mean(v, axis=-1, keepdims=True)
    scale = lax.rsqrt(jnp.mean(center * center, axis=-1, keepdims=True) + EPS)
    return center * scale, scale


def norm_back(grad, hat, scale, gain):
    inner = grad * gain
    return scale * (
        inner - jnp.mean(inner, axis=-1, keepdims=True) - hat * jnp.mean(inner * hat, axis=-1, keepdims=True)
    )


class Forward:
    def __init__(self, net, torus, qkv, full, heads, lse, box, single, single_in, outs, res, res_single, res_single_in):
        self.net, self.t, self.qkv, self.full, self.heads, self.lse = net, torus, qkv, full, heads, lse
        self.box, self.single, self.single_in, self.outs = box, single, single_in, outs
        self.res, self.res_single, self.res_single_in = res, res_single, res_single_in
        self.swap, self.back = Swap(net, torus, 3), Swap(net, torus, 1)
        self.sent = []

    def start(self):
        t, swap = self.t, self.swap
        self.got = swap.out_pairs(self.qkv, self.box)
        swap.pack_single(self.qkv, self.single)
        self.got_single = swap.out_single(self.single, self.single_in)
        swap.keep_pairs(self.qkv, self.box)
        self.single_in[t.x] = self.single[t.x]
        self.lse[...] = jnp.zeros_like(self.lse)

    def take(self, p):
        heads = self.heads
        if p < 2:
            wait_all(self.got[p])
            for k in range(3):
                for s in range(4):
                    for j in range(2):
                        v = self.box[p, k, s, :, 64 * j : 64 * j + 64]
                        heads[k, 2 * p + j, 256 * s : 256 * (s + 1), :] = v * BF16(0.125) if k == 0 else v
            return
        wait_all(self.got_single)
        for k in range(3):
            for s in range(4):
                v = self.single_in[s, :, 64 * k : 64 * k + 64]
                heads[k, 4, 256 * s : 256 * (s + 1), :] = v * BF16(0.125) if k == 0 else v

    def head(self, h, j):
        heads, lse = self.heads, self.lse
        lane = lax.broadcasted_iota(jnp.int32, (256, 128), 1)
        for i in range(4):
            rows = slice(256 * i, 256 * (i + 1))
            n = 256 * (i + 1)
            s = causal(dot_t(heads[0, h, rows, :], heads[1, h, :n, :]), i)
            top = jnp.max(s, axis=1, keepdims=True)
            p = jnp.exp(s - top)
            total = jnp.sum(p, axis=1, keepdims=True)
            lse[rows, :] = jnp.where(lane == h, top + jnp.log(total), lse[rows, :])
            o = dot(p.astype(BF16), heads[2, h, :n, :])
            self.outs[j, rows, :] = (o / total).astype(BF16)

    def give(self, p):
        back, outs = self.back, self.outs
        for i in range(4):
            rows = slice(256 * i, 256 * (i + 1))
            if p < 2:
                self.res[i, 0, p] = jnp.concatenate([outs[0, rows, :], outs[1, rows, :]], axis=1)
            else:
                self.res_single[i] = jnp.concatenate([outs[0, rows, :], jnp.zeros((256, 64), BF16)], axis=1)
        if p < 2:
            self.sent += back.back_pair(p, self.res, self.full)
            back.keep_back(p, self.res, self.full)
        else:
            self.sent_single = back.out_single(self.res_single, self.res_single_in)
            self.res_single_in[self.t.x] = self.res_single[self.t.x]

    def finish(self):
        wait_all(self.sent_single)
        self.back.unpack_single(self.res_single_in, self.full)
        wait_all(self.sent)


def front_kernel(
    tokens, small, w_qkv, w_out, w_fc, w_proj,
    f_qkv, f_out, f_fc, f_proj, f_small, normed, att, heads, lse,
    v_qkv, h_out, h_fc, h_proj, small_all, bias, qkv, full,
    box, single, single_in, outs, res, res_single, res_single_in, ssem, rsem, lsem,
):
    t = Torus()
    greet(t.neighbours())
    net = Net(ssem, rsem)
    smalls = [net.send(small, small_all.at[t.x], t.at("x", s)) for s in (1, 3, 2)]
    q = Gather(net, t, "qkv", w_qkv, v_qkv, 0)
    o = Gather(net, t, "out", w_out, f_out, 1)
    f = Gather(net, t, "fc", w_fc, f_fc, 0)
    p = Gather(net, t, "proj", w_proj, f_proj, 1)
    q.start()
    own = pltpu.make_async_copy(w_qkv, v_qkv.at[t.x], lsem.at[0])
    own.start()
    held = [(w_out, h_out, f_out), (w_fc, h_fc, f_fc), (w_proj, h_proj, f_proj)]
    local = [pltpu.make_async_copy(s, h, lsem.at[1 + k]) for k, (s, h, _) in enumerate(held)]
    for copy in local:
        copy.start()
    f.start()
    p.start()
    o.start()
    q.start_alone()
    small_all[t.x] = small[...]
    q.both("spread", 0)
    for copy in smalls:
        copy.wait_recv()
    hat, _ = norm(tokens[...].astype(F32))
    gain, shift = whole_vector(small_all, "ln1_gain"), whole_vector(small_all, "ln1_bias")
    normed[...] = (hat * gain + shift).astype(BF16)
    k = VECTORS.index("qv_bias")
    for n in range(6):
        row = jnp.zeros((1, 640), F32) if n in (2, 3) else small_all[n if n < 2 else n - 2, k : k + 1, :640]
        bias[n, 0:1, :] = row
    f_small[...] = small_all[...]
    q.both("pass_on", 0)
    f.both("spread", 0)
    q.both("spread", 1)
    q.alone_on()
    p.both("spread", 0)
    q.both("pass_on", 1)
    f.start_alone()
    q.both("share")
    q.alone_end()
    f.both("pass_on", 0)
    q.finish()
    own.wait()
    keep = pltpu.make_async_copy(v_qkv, f_qkv, lsem.at[0])
    keep.start()
    for k, (_, h, full_w) in enumerate(held):
        local[k].wait()
        local[k] = pltpu.make_async_copy(h, full_w.at[t.x], lsem.at[1 + k])
        local[k].start()

    def columns(n, _):
        cols = pl.ds(pl.multiple_of(n * 640, 128), 640)
        w = v_qkv[:, :, cols].reshape(1280, 640)
        qkv[:, cols] = (dot(normed[...], w) + bias[n, 0:1, :]).astype(BF16)
        return 0

    lax.fori_loop(0, 6, columns, 0)
    fwd = Forward(net, t, qkv, full, heads, lse, box, single, single_in, outs, res, res_single, res_single_in)
    fwd.start()
    p.both("pass_on", 0)
    f.both("spread", 1)
    o.both("spread", 0)
    fwd.take(0)
    fwd.head(0, 0)
    p.start_alone()
    p.both("spread", 1)
    o.both("pass_on", 0)
    f.alone_on()
    fwd.head(1, 1)
    fwd.give(0)
    o.start_alone()
    o.both("spread", 1)
    fwd.take(1)
    fwd.head(2, 0)
    f.both("pass_on", 1)
    o.both("pass_on", 1)
    p.alone_on()
    fwd.head(3, 1)
    fwd.give(1)
    p.both("pass_on", 1)
    o.alone_on()
    f.alone_end()
    fwd.take(2)
    fwd.head(4, 0)
    fwd.give(2)
    f.both("share")
    o.both("share")
    o.alone_end()
    p.alone_end()
    p.both("share")
    fwd.finish()
    att[...] = full[...]
    for g in (o, f, p):
        g.finish()
    keep.wait()
    for copy in local:
        copy.wait()
    net.finish()


FRONT_SEMS = 280


def front(tokens, small, w_qkv, w_out, w_fc, w_proj):
    vm, anys = pl.BlockSpec(memory_space=pltpu.VMEM), pl.BlockSpec(memory_space=pl.ANY)
    weights = (w_qkv, w_out, w_fc, w_proj)
    return pl.pallas_call(
        front_kernel,
        name="front",
        out_shape=[jax.ShapeDtypeStruct((4,) + w.shape, BF16) for w in weights]
        + [
            jax.ShapeDtypeStruct((4, 8, 1280), F32),
            jax.ShapeDtypeStruct((256, 1280), BF16),
            jax.ShapeDtypeStruct((256, 1280), BF16),
            jax.ShapeDtypeStruct((3, 5, 1024, 64), BF16),
            jax.ShapeDtypeStruct((1024, 128), F32),
        ],
        in_specs=[vm] * 2 + [anys] * 4,
        out_specs=[anys] * 4 + [vm] * 5,
        scratch_shapes=[
            pltpu.VMEM((4, 320, 3840), BF16),
            pltpu.VMEM((320, 1280), BF16),
            pltpu.VMEM((320, 5120), BF16),
            pltpu.VMEM((1280, 1280), BF16),
            pltpu.VMEM((4, 8, 1280), F32),
            pltpu.VMEM((6, 8, 640), F32),
            pltpu.VMEM((256, 3840), BF16),
            pltpu.VMEM((256, 1280), BF16),
            pltpu.VMEM((2, 3, 4, 256, 128), BF16),
            pltpu.VMEM((4, 256, 256), BF16),
            pltpu.VMEM((4, 256, 256), BF16),
            pltpu.VMEM((2, 1024, 64), BF16),
            pltpu.VMEM((4, 1, 2, 256, 128), BF16),
            pltpu.VMEM((4, 256, 128), BF16),
            pltpu.VMEM((4, 256, 128), BF16),
            pltpu.SemaphoreType.DMA((FRONT_SEMS,)),
            pltpu.SemaphoreType.DMA((FRONT_SEMS,)),
            pltpu.SemaphoreType.DMA((4,)),
        ],
        compiler_params=pltpu.CompilerParams(collective_id=0, has_side_effects=True, vmem_limit_bytes=56 << 20),
    )(tokens, small, *weights)


GELU_A, GELU_B = 0.7978845608028654, 0.044715
FF_STEP = 640


def mlp_kernel(
    tokens, att, cot, small, w_out, w_fc, w_proj,
    block_out, n2t, actt, gp, grad_mid, grad_branch, datt, small_grad,
    n2, middle, out_acc, grad_acc, bias,
):
    j = pl.program_id(0)

    @pl.when(j == 0)
    def _():
        mid = tokens[...].astype(F32) + dot(att[...], w_out[...]) + whole_vector(small, "out_bias")
        middle[...] = mid
        hat, _ = norm(mid)
        n2[...] = (hat * whole_vector(small, "ln2_gain") + whole_vector(small, "ln2_bias")).astype(BF16)
        n2t[...] = n2[...].T
        out_acc[...] = mid + whole_vector(small, "proj_bias")
        grad_acc[...] = jnp.zeros_like(grad_acc)
        k = VECTORS.index("fc_bias")
        for x in range(4):
            for h in range(2):
                bias[2 * x + h, 0:1, :] = small[x, k : k + 1, 640 * h : 640 * (h + 1)]

    pre = dot(n2[...], w_fc[...]) + bias[j, 0:1, :]
    square = pre * pre
    bend = jnp.tanh(GELU_A * (pre + GELU_B * pre * square))
    act = (0.5 * pre * (1.0 + bend)).astype(BF16)
    actt[...] = act.T
    out_acc[...] += dot(act, w_proj[...])
    slope = 0.5 * (1.0 + bend) + (0.5 * GELU_A) * pre * (1.0 - bend * bend) * (1.0 + 3.0 * GELU_B * square)
    grad = (dot_t(cot[...], w_proj[...]) * slope).astype(BF16)
    gp[...] = grad
    grad_acc[...] += dot_t(grad, w_fc[...])
    column_sums = jnp.sum(grad.astype(F32), axis=0, keepdims=True)
    for n in range(8):
        @pl.when(j == n)
        def _():
            small_grad[4 + n // 2 : 5 + n // 2, 640 * (n % 2) : 640 * (n % 2 + 1)] = column_sums

    @pl.when(j == pl.num_programs(0) - 1)
    def _():
        block_out[...] = out_acc[...].astype(BF16)
        hat, scale = norm(middle[...])
        g = grad_acc[...]
        cot_rows = cot[...].astype(F32)
        small_grad[0:1, :] = jnp.sum(g * hat, axis=0, keepdims=True)
        small_grad[1:2, :] = jnp.sum(g, axis=0, keepdims=True)
        small_grad[2:3, :] = jnp.sum(cot_rows, axis=0, keepdims=True)
        mid = cot_rows + norm_back(g, hat, scale, whole_vector(small, "ln2_gain"))
        grad_mid[...] = mid
        branch = mid.astype(BF16)
        grad_branch[...] = branch
        small_grad[3:4, :] = jnp.sum(branch.astype(F32), axis=0, keepdims=True)
        datt[...] = dot_t(branch, w_out[...]).astype(BF16)


def mlp(tokens, att, cot, small, w_out, w_fc, w_proj):
    rows = pl.BlockSpec((256, 1280), lambda j: (0, 0))
    return pl.pallas_call(
        mlp_kernel,
        name="mlp",
        grid=(5120 // FF_STEP,),
        out_shape=[
            jax.ShapeDtypeStruct((256, 1280), BF16),
            jax.ShapeDtypeStruct((1280, 256), BF16),
            jax.ShapeDtypeStruct((5120, 256), BF16),
            jax.ShapeDtypeStruct((256, 5120), BF16),
            jax.ShapeDtypeStruct((256, 1280), F32),
            jax.ShapeDtypeStruct((256, 1280), BF16),
            jax.ShapeDtypeStruct((256, 1280), BF16),
            jax.ShapeDtypeStruct((8, 1280), F32),
        ],
        in_specs=[
            rows,
            rows,
            rows,
            pl.BlockSpec((4, 8, 1280), lambda j: (0, 0, 0)),
            pl.BlockSpec((1280, 1280), lambda j: (0, 0)),
            pl.BlockSpec((1280, FF_STEP), lambda j: (0, j)),
            pl.BlockSpec((FF_STEP, 1280), lambda j: (j, 0)),
        ],
        out_specs=[
            rows,
            pl.BlockSpec((1280, 256), lambda j: (0, 0)),
            pl.BlockSpec((FF_STEP, 256), lambda j: (j, 0)),
            pl.BlockSpec((256, FF_STEP), lambda j: (0, j)),
            rows,
            rows,
            rows,
            pl.BlockSpec((8, 1280), lambda j: (0, 0)),
        ],
        scratch_shapes=[
            pltpu.VMEM((256, 1280), BF16),
            pltpu.VMEM((256, 1280), F32),
            pltpu.VMEM((256, 1280), F32),
            pltpu.VMEM((256, 1280), F32),
            pltpu.VMEM((8, 8, 640), F32),
        ],
        compiler_params=pltpu.CompilerParams(vmem_limit_bytes=48 << 20, dimension_semantics=("arbitrary",)),
    )(tokens, att, cot, small, w_out, w_fc, w_proj)


ORDERS = ("xyz", "yzx", "zxy")


def view(ref, axes, chosen, rows):
    return ref.at[tuple(chosen.get(a, slice(None)) for a in axes) + (pl.ds(*rows),)]


def leading(ref):
    return ref.shape[:-2]


def add_into(dst, *srcs):
    lead = leading(dst)
    count = 1
    for n in lead:
        count *= n

    def slab(i):
        index = []
        for n in reversed(lead):
            index.append(lax.rem(i, n))
            i = i // n
        return tuple(reversed(index))

    def body(i, _):
        at = slab(i)
        total = dst[at].astype(F32)
        for s in srcs:
            total = total + s[at].astype(F32)
        dst[at] = total.astype(BF16)
        return 0

    if count == 1 and not lead:
        total = dst[...].astype(F32)
        for s in srcs:
            total = total + s[...].astype(F32)
        dst[...] = total.astype(BF16)
    else:
        lax.fori_loop(0, count, body, 0)


def inbox_shapes(classes, phases):
    out = []
    for order, _, n in classes:
        if 0 in phases:
            half = [2 if a == order[1] else 4 for a in "xyz" if a != order[0]]
            out += [half + [n, 128]] * 2 + [[4, 4, n, 128]] * 2
        if 1 in phases:
            out += [[2, n, 128]] * 2 + [[4, n, 128]] * 2
        if 2 in phases:
            out += [[3, n, 128]]
    return [pltpu.VMEM(tuple(s), BF16) for s in out]


def inboxes(refs, phases):
    refs, out = list(refs), []
    while refs:
        mine = {}
        for phase in phases:
            n = 1 if phase == 2 else 4
            mine[phase], refs = refs[:n], refs[n:]
        out.append(mine)
    return out


class Lane:
    def __init__(self, net, torus, acc, axes, inbox, order, row, n):
        self.net, self.t, self.acc, self.axes, self.inbox, self.order = net, torus, acc, axes, inbox, order
        self.rows, self.base = (row, n), 0
        self.fixed = {}
        self.got = {}

    def held(self):
        return view(self.acc, self.axes, self.fixed, self.rows)

    def halves(self, phase):
        a = self.order[phase + 1]
        return [{a: pl.ds(0, 2)}, {a: pl.ds(2, 2)}]

    def box_half(self, box, phase, half):
        if phase == 1:
            return box.at[pl.ds(2 * half, 2)]
        left = [a for a in "xyz" if a != self.order[0]]
        cut = left.index(self.order[1])
        return box.at[(slice(None),) * cut + (pl.ds(2 * half, 2),)]

    def first(self, phase):
        axis = self.order[phase]
        p = self.t.pos(axis)
        h = self.halves(phase)
        b = self.inbox[phase]
        at = lambda shift, cut: view(self.acc, self.axes, {**self.fixed, axis: wrap(p + shift), **cut}, self.rows)
        up, down = self.t.at(axis, 1), self.t.at(axis, 3)
        far = [self.net.send(at(2, h[0]), b[0], up), self.net.send(at(2, h[1]), b[1], down)]
        near = [
            self.net.send(at(1, h[1]), self.box_half(b[2], phase, 1), up),
            self.net.send(at(3, h[0]), self.box_half(b[3], phase, 0), down),
        ]
        self.got[phase] = (far, near)

    def second(self, phase):
        axis = self.order[phase]
        p = self.t.pos(axis)
        h = self.halves(phase)
        b = self.inbox[phase]
        at = lambda shift, cut: view(self.acc, self.axes, {**self.fixed, axis: wrap(p + shift), **cut}, self.rows)
        up, down = self.t.at(axis, 1), self.t.at(axis, 3)
        far, near = self.got[phase]
        far[0].wait_recv()
        add_into(at(1, h[0]), b[0])
        near.append(self.net.send(at(1, h[0]), self.box_half(b[2], phase, 0), up))
        far[1].wait_recv()
        add_into(at(3, h[1]), b[1])
        near.append(self.net.send(at(3, h[1]), self.box_half(b[3], phase, 1), down))

    def third(self, phase):
        axis = self.order[phase]
        p = self.t.pos(axis)
        b = self.inbox[phase]
        for copy in self.got[phase][1]:
            copy.wait_recv()
        self.fixed[axis] = p
        add_into(self.held(), b[2], b[3])

    def last(self):
        axis = self.order[2]
        p = self.t.pos(axis)
        box = self.inbox[2][0]
        self.got[2] = [
            self.net.send(view(self.acc, self.axes, {**self.fixed, axis: wrap(p + s)}, self.rows), box.at[s - 1], self.t.at(axis, s))
            for s in (1, 3, 2)
        ]

    def done(self):
        axis = self.order[2]
        for copy in self.got[2]:
            copy.wait_recv()
        self.fixed[axis] = self.t.pos(axis)
        box = self.inbox[2][0]
        add_into(self.held(), box.at[0], box.at[1], box.at[2])


class Spread:
    def __init__(self, lane, out, order, row, n, sem):
        self.net, self.t, self.out, self.order, self.rows, self.sem = lane.net, lane.t, out, order, (row, n), sem
        chosen = {a: lane.t.pos(a) for a in lane.axes}
        self.own = view(lane.acc, lane.axes, chosen, (row - lane.base, n))

    def place(self, y, z):
        return self.out.at[self.t.c, y, z, pl.ds(*self.rows)]

    def band(self, v, b=slice(None)):
        y, z = (b, v) if self.order == "yz" else (v, b)
        return self.place(y, z)

    def start(self):
        t = self.t
        here = self.place(t.y, t.z)
        self.keep = pltpu.make_async_copy(self.own, here, self.sem)
        self.keep.start()
        self.first = [self.net.send(self.own, here, t.at(self.order[0], s)) for s in (1, 3, 2)]

    def second(self):
        t, axis = self.t, self.order[1]
        for copy in self.first:
            copy.wait_recv()
        self.keep.wait()
        here = self.band(t.pos(axis))
        self.near = [self.net.send(here, here, t.at(axis, s)) for s in (1, 3)]

    def third(self):
        t, axis = self.t, self.order[1]
        p = t.pos(axis)
        self.far = []
        for copy, shift, to, b in ((self.near[0], 3, 1, pl.ds(0, 2)), (self.near[1], 1, 3, pl.ds(2, 2))):
            copy.wait_recv()
            there = self.band(wrap(p + shift), b)
            self.far.append(self.net.send(there, there, t.at(axis, to)))

    def share(self):
        for copy in self.far:
            copy.wait_recv()
        whole = self.place(slice(None), slice(None))
        self.core = self.net.send(whole, whole, self.t.sibling())

    def finish(self):
        self.core.wait_recv()


def store_blocks(acc, x, first, blocks, rows):
    at = 0
    for block in blocks:
        done = 0
        while done < 320:
            n = min(320 - done, rows - at % rows)
            s = at // rows
            slab = first + s
            acc[x, slab // 4, lax.rem(slab, 4), pl.ds(at % rows, n), :] = block[done : done + n]
            done += n
            at += n


GROUPS = {
    "mlp": (800, (272, 272, 272)),
    "attn": (400, (144, 144, 128)),
}


def classes_of(group):
    row, out = 0, []
    for order, n in zip(ORDERS, GROUPS[group][1]):
        out.append((order, row, n))
        row += n
    return out


def spreads_of(group):
    a, b, c = classes_of(group)
    h = c[2] // 32 * 16
    return [(0, "yz", a[1], a[2]), (1, "zy", b[1], b[2]), (2, "yz", c[1], h), (2, "zy", c[1] + h, c[2] - h)]


def each(items, what, *rest):
    for item in items:
        getattr(item, what)(*rest)


def spreads_for(group, lanes, out, sems):
    return [Spread(lanes[k], out, order, row, n, sems.at[i]) for i, (k, order, row, n) in enumerate(spreads_of(group))]


def row_pieces(ref, row, start, n):
    v = ref[row : row + 1, start : start + n]
    if n % 128:
        v = jnp.concatenate([v, jnp.zeros((1, 128 - n % 128), F32)], axis=1)
    return [v[:, 128 * k : 128 * (k + 1)] for k in range(v.shape[1] // 128)]


def store_small(acc, rows, slabs):
    for x in range(4):
        filled = slabs(x)
        for k in range(16):
            pieces = filled[k] if k < len(filled) else []
            if len(pieces) < 16:
                pieces = pieces + [jnp.zeros((16 - len(pieces), 128), F32)]
            acc[x, k // 4, k % 4, pl.ds(rows, 16), :] = jnp.concatenate(pieces, axis=0).astype(BF16)


def product(lhs, rhs, acc, x, first, rows):
    out = dot(lhs, rhs).astype(BF16)
    store_blocks(acc, x, first, [out[:, 128 * t : 128 * (t + 1)] for t in range(5)], rows)


class Exchange:
    def __init__(self, net, sems):
        self.net, self.sems, self.used, self.pending = net, sems, 0, []

    def send(self, src, own_dst, other_dst, sibling, own_src=None):
        copy = self.net.send(src, other_dst, sibling)
        keep = pltpu.make_async_copy(src if own_src is None else own_src, own_dst, self.sems.at[self.used])
        keep.start()
        self.used += 1
        self.pending.append((copy, keep))

    def wait(self, count):
        for copy, keep in self.pending[:count]:
            copy.wait_recv()
            keep.wait()
        self.pending = self.pending[count:]


class Backward:
    def __init__(self, net, torus, datt, full, heads, lse, box, single, single_in, do, dkv, grads, res, res_single, res_single_in):
        self.net, self.t, self.datt, self.full, self.heads, self.lse = net, torus, datt, full, heads, lse
        self.box, self.single, self.single_in, self.do, self.dkv, self.grads = box, single, single_in, do, dkv, grads
        self.res, self.res_single, self.res_single_in = res, res_single, res_single_in
        self.swap, self.back = Swap(net, torus, 1), Swap(net, torus, 3)
        self.sent = []

    def start(self):
        t, swap = self.t, self.swap
        self.got = swap.out_pairs(self.datt, self.box)
        swap.pack_single(self.datt, self.single)
        self.got_single = swap.out_single(self.single, self.single_in)
        swap.keep_pairs(self.datt, self.box)
        self.single_in[t.x] = self.single[t.x]

    def take(self, p):
        wait_all(self.got[p] if p < 2 else self.got_single)
        for s in range(4):
            rows = slice(256 * s, 256 * (s + 1))
            if p < 2:
                for j in range(2):
                    self.do[2 * p + j, rows, :] = self.box[p, 0, s, :, 64 * j : 64 * j + 64]
            else:
                self.do[4, rows, :] = self.single_in[s, :, :64]

    def head(self, h, j):
        heads, grads, dkv = self.heads, self.grads, self.dkv
        lane = lax.broadcasted_iota(jnp.int32, (256, 128), 1)
        dkv[...] = jnp.zeros_like(dkv)
        for i in range(4):
            rows = slice(256 * i, 256 * (i + 1))
            n = 256 * (i + 1)
            q, k, v, d = heads[0, h, rows, :], heads[1, h, :n, :], heads[2, h, :n, :], self.do[h, rows, :]
            total = jnp.sum(jnp.where(lane == h, self.lse[rows, :], 0.0), axis=1, keepdims=True)
            p = jnp.exp(causal(dot_t(q, k), i) - total)
            t1 = p * dot_t(d, v)
            inner = jnp.sum(t1, axis=1, keepdims=True)
            ds = (t1 - p * inner).astype(BF16)
            grads[0, j, rows, :] = (dot(ds, k) * 0.125).astype(BF16)
            dkv[0, :, :n] += dot(q.T, ds)
            dkv[1, :, :n] += dot(d.T, p.astype(BF16))
        for k in range(2):
            grads[1 + k, j] = dkv[k].T.astype(BF16)

    def give(self, p):
        grads, back = self.grads, self.back
        for i in range(4):
            rows = slice(256 * i, 256 * (i + 1))
            if p < 2:
                for k in range(3):
                    self.res[i, k, p] = jnp.concatenate([grads[k, 0, rows, :], grads[k, 1, rows, :]], axis=1)
            else:
                cols = [grads[k, 0, rows, :] for k in range(3)] + [jnp.zeros((256, 64), BF16)]
                self.res_single[i] = jnp.concatenate(cols, axis=1)
        if p < 2:
            self.sent += back.back_pair(p, self.res, self.full)
            back.keep_back(p, self.res, self.full)
        else:
            self.sent_single = back.out_single(self.res_single, self.res_single_in)
            self.res_single_in[self.t.x] = self.res_single[self.t.x]

    def finish(self):
        wait_all(self.sent_single)
        self.back.unpack_single(self.res_single_in, self.full)
        wait_all(self.sent)


def back_kernel(
    datt, heads, lse, small, n2t, actt, gp, cot,
    gqkv, part_0, part_1, part_2,
    n2t_v, actt_v, gp_v, cot_v, small_v, full,
    box, single, single_in, do, dkv, grads, res, res_single, res_single_in,
    ssem, rsem, lsem, acc, *inbox,
):
    t = Torus()
    greet(t.neighbours())
    net = Net(ssem, rsem)
    sib, c = t.sibling(), t.c
    swap = Exchange(net, lsem)
    low, high = pl.ds(0, 256), pl.ds(256, 256)
    swap.send(n2t, n2t_v.at[:, low], n2t_v.at[:, high], sib)
    for s in range(4):
        mine, theirs = (pl.ds(pl.multiple_of(s * 1280 + k * 640, 128), 640) for k in (c, 1 - c))
        swap.send(gp.at[:, theirs], gp_v.at[s, low], gp_v.at[s, high], sib, gp.at[:, mine])
    swap.send(cot, cot_v.at[low], cot_v.at[high], sib)
    for s in range(4):
        mine, theirs = (pl.ds(pl.multiple_of(s * 1280 + k * 640, 128), 640) for k in (c, 1 - c))
        to = pl.ds(s * 640, 640)
        swap.send(actt.at[theirs], actt_v.at[to, low], actt_v.at[to, high], sib, actt.at[mine])
    swap.send(small, small_v.at[0], small_v.at[1], sib)
    bwd = Backward(net, t, datt, full, heads, lse, box, single, single_in, do, dkv, grads, res, res_single, res_single_in)
    bwd.start()
    swap.wait(5)

    def fc(i, _):
        x, s = i // 4, lax.rem(i, 4)
        product(n2t_v[pl.ds(pl.multiple_of(x * 320, 16), 320), :], gp_v[s], acc, x, s * 2, 800)
        return 0

    lax.fori_loop(0, 16, fc, 0)
    swap.wait(6)

    def proj(i, _):
        x, sub = i // 2, lax.rem(i, 2)
        lhs = actt_v[pl.ds(pl.multiple_of(i * 320, 16), 320), :]
        for half in range(2):
            product(lhs, cot_v[:, 640 * half : 640 * (half + 1)], acc, x, 8 + sub * 4 + half * 2, 800)
        return 0

    lax.fori_loop(0, 8, proj, 0)
    small_v[0] = small_v[0] + small_v[1]
    total = small_v.at[0]
    store_small(
        acc, 800,
        lambda x: [
            [row for k in range(4) for row in row_pieces(total, k, 320 * x, 320)],
            row_pieces(total, 4 + x, 0, 1280),
        ],
    )
    lanes = [Lane(net, t, acc, "xyz", box_of, *k) for k, box_of in zip(classes_of("mlp"), inboxes(inbox, (0,)))]
    each(lanes, "first", 0)
    bwd.take(0)
    bwd.head(0, 0)
    bwd.head(1, 1)
    each(lanes, "second", 0)
    bwd.give(0)
    bwd.take(1)
    bwd.head(2, 0)
    bwd.head(3, 1)
    bwd.give(1)
    bwd.take(2)
    bwd.head(4, 0)
    bwd.give(2)
    keeps = []
    for k, (lane, part_k) in enumerate(zip(lanes, (part_0, part_1, part_2))):
        lane.third(0)
        keeps.append(pltpu.make_async_copy(lane.held(), part_k, lsem.at[k]))
        keeps[-1].start()
    bwd.finish()
    gqkv[...] = full[...]
    for keep in keeps:
        keep.wait()
    net.finish()


BACK_SEMS = 100


def backward(datt, heads, lse, small, n2t, actt, gp, cot):
    vm, anys = pl.BlockSpec(memory_space=pltpu.VMEM), pl.BlockSpec(memory_space=pl.ANY)
    classes = classes_of("mlp")
    return pl.pallas_call(
        back_kernel,
        name="backward",
        out_shape=[jax.ShapeDtypeStruct((256, 3840), BF16)]
        + [jax.ShapeDtypeStruct((4, 4, n, 128), BF16) for _, _, n in classes],
        in_specs=[vm] * 4 + [anys] * 4,
        out_specs=[vm] + [anys] * 3,
        scratch_shapes=[
            pltpu.VMEM((1280, 512), BF16),
            pltpu.VMEM((2560, 512), BF16),
            pltpu.VMEM((4, 512, 640), BF16),
            pltpu.VMEM((512, 1280), BF16),
            pltpu.VMEM((2, 8, 1280), F32),
            pltpu.VMEM((256, 3840), BF16),
            pltpu.VMEM((2, 1, 4, 256, 128), BF16),
            pltpu.VMEM((4, 256, 128), BF16),
            pltpu.VMEM((4, 256, 128), BF16),
            pltpu.VMEM((5, 1024, 64), BF16),
            pltpu.VMEM((2, 64, 1024), F32),
            pltpu.VMEM((3, 2, 1024, 64), BF16),
            pltpu.VMEM((4, 3, 2, 256, 128), BF16),
            pltpu.VMEM((4, 256, 256), BF16),
            pltpu.VMEM((4, 256, 256), BF16),
            pltpu.SemaphoreType.DMA((BACK_SEMS,)),
            pltpu.SemaphoreType.DMA((BACK_SEMS,)),
            pltpu.SemaphoreType.DMA((16,)),
            pltpu.VMEM((4, 4, 4, 816, 128), BF16),
        ]
        + inbox_shapes(classes, (0,)),
        compiler_params=pltpu.CompilerParams(collective_id=1, has_side_effects=True, vmem_limit_bytes=60 << 20),
    )(datt, heads, lse, small, n2t, actt, gp, cot)


def last_kernel(
    n1t, gqkv, attt, gb, small, part_0, part_1, part_2,
    out_mlp, out_attn,
    n1t_v, gqkv_v, attt_v, gb_v, small_v, ssem, rsem, lsem, acc, held_0, held_1, held_2, *inbox,
):
    t = Torus()
    greet(t.neighbours())
    net = Net(ssem, rsem)
    sib, c = t.sibling(), t.c
    swap = Exchange(net, lsem)
    low, high = pl.ds(0, 256), pl.ds(256, 256)
    swap.send(n1t, n1t_v.at[:, low], n1t_v.at[:, high], sib)
    for s in range(3):
        mine, theirs = (pl.ds(pl.multiple_of(k * 1920 + s * 640, 128), 640) for k in (c, 1 - c))
        swap.send(gqkv.at[:, theirs], gqkv_v.at[s, low], gqkv_v.at[s, high], sib, gqkv.at[:, mine])
    swap.send(attt, attt_v.at[:, low], attt_v.at[:, high], sib)
    mine, theirs = (pl.ds(pl.multiple_of(k * 640, 128), 640) for k in (c, 1 - c))
    swap.send(gb.at[:, theirs], gb_v.at[low], gb_v.at[high], sib, gb.at[:, mine])
    swap.send(small, small_v.at[0], small_v.at[1], sib)

    mlp_classes, attn_classes = classes_of("mlp"), classes_of("attn")
    parts = [
        pltpu.make_async_copy(src, dst, lsem.at[7 + k])
        for k, (src, dst) in enumerate(((part_0, held_0), (part_1, held_1), (part_2, held_2)))
    ]
    each(parts, "start")
    each(parts, "wait")
    mlp_lanes = []
    for held, box_of, (order, row, n) in zip((held_0, held_1, held_2), inboxes(inbox[:15], (1, 2)), mlp_classes):
        lane = Lane(net, t, held, "".join(a for a in "xyz" if a != order[0]), box_of, order, 0, n)
        lane.base = row
        mlp_lanes.append(lane)
    each(mlp_lanes, "first", 1)
    swap.wait(4)

    def qkv(i, _):
        x, s = i // 3, lax.rem(i, 3)
        product(n1t_v[pl.ds(pl.multiple_of(x * 320, 16), 320), :], gqkv_v[s], acc, x, s * 4, 400)
        return 0

    lax.fori_loop(0, 12, qkv, 0)
    each(mlp_lanes, "second", 1)
    swap.wait(3)

    def outp(x, _):
        product(attt_v[pl.ds(pl.multiple_of(x * 320, 16), 320), :], gb_v[...], acc, x, 12, 400)
        return 0

    lax.fori_loop(0, 4, outp, 0)
    small_v[0] = small_v[0] + small_v[1]
    total = small_v.at[0]
    store_small(
        acc, 400,
        lambda x: [
            [row for k in range(2) for row in row_pieces(total, k, 320 * x, 320)],
            row_pieces(total, 2 + x // 2, 640 * (x % 2), 640),
        ],
    )
    lanes = [Lane(net, t, acc, "xyz", box_of, *k) for k, box_of in zip(attn_classes, inboxes(inbox[15:], (0, 1, 2)))]
    mlp_spreads = spreads_for("mlp", mlp_lanes, out_mlp, lsem.at[pl.ds(0, 4)])
    spreads = spreads_for("attn", lanes, out_attn, lsem.at[pl.ds(4, 4)])
    each(lanes, "first", 0)
    each(mlp_lanes, "third", 1)
    each(mlp_lanes, "last")
    each(lanes, "second", 0)
    each(mlp_lanes, "done")
    each(mlp_spreads, "start")
    each(lanes, "third", 0)
    each(lanes, "first", 1)
    each(mlp_spreads, "second")
    each(lanes, "second", 1)
    each(mlp_spreads, "third")
    each(lanes, "third", 1)
    each(lanes, "last")
    each(lanes, "done")
    each(spreads, "start")
    each(mlp_spreads, "share")
    each(spreads, "second")
    each(spreads, "third")
    each(spreads, "share")
    each(mlp_spreads, "finish")
    each(spreads, "finish")
    net.finish()


LAST_SEMS = 160


def last(n1t, gqkv, attt, gb, small, parts):
    vm, anys = pl.BlockSpec(memory_space=pltpu.VMEM), pl.BlockSpec(memory_space=pl.ANY)
    mlp_classes, attn_classes = classes_of("mlp"), classes_of("attn")
    return pl.pallas_call(
        last_kernel,
        name="last",
        out_shape=[jax.ShapeDtypeStruct((2, 4, 4, n, 128), BF16) for n in (816, 416)],
        in_specs=[anys] * 4 + [vm] + [anys] * 3,
        out_specs=[anys] * 2,
        scratch_shapes=[
            pltpu.VMEM((1280, 512), BF16),
            pltpu.VMEM((3, 512, 640), BF16),
            pltpu.VMEM((1280, 512), BF16),
            pltpu.VMEM((512, 640), BF16),
            pltpu.VMEM((2, 8, 1280), F32),
            pltpu.SemaphoreType.DMA((LAST_SEMS,)),
            pltpu.SemaphoreType.DMA((LAST_SEMS,)),
            pltpu.SemaphoreType.DMA((16,)),
            pltpu.VMEM((4, 4, 4, 416, 128), BF16),
        ]
        + [pltpu.VMEM((4, 4, n, 128), BF16) for _, _, n in mlp_classes]
        + inbox_shapes(mlp_classes, (1, 2))
        + inbox_shapes(attn_classes, (0, 1, 2)),
        compiler_params=pltpu.CompilerParams(collective_id=2, has_side_effects=True, vmem_limit_bytes=56 << 20),
    )(n1t, gqkv, attt, gb, small, *parts)


def unpack_mlp_kernel(src, fc, proj):
    q = pl.program_id(1)
    flat = [src[0, 0, i, :800].astype(F32) for i in range(2)]
    flat = jnp.concatenate(flat, axis=0)

    @pl.when(q < 4)
    def _():
        for k in range(5):
            fc[:, 128 * k : 128 * (k + 1)] = flat[320 * k : 320 * (k + 1)]

    @pl.when(q >= 4)
    def _():
        for k in range(5):
            proj[:, 128 * k : 128 * (k + 1)] = flat[320 * k : 320 * (k + 1)]


def unpack_mlp(packed):
    return pl.pallas_call(
        unpack_mlp_kernel,
        name="unpack_mlp",
        grid=(2, 8),
        out_shape=[jax.ShapeDtypeStruct((320, 5120), F32), jax.ShapeDtypeStruct((1280, 1280), F32)],
        in_specs=[pl.BlockSpec((1, 1, 2, 816, 128), lambda c, q: (c, q // 2, q % 2, 0, 0))],
        out_specs=[
            pl.BlockSpec((320, 640), lambda c, q: (0, jnp.where(q < 4, q * 2 + c, 6 + c))),
            pl.BlockSpec((320, 640), lambda c, q: (c * 2 + jnp.where(q < 4, 0, (q - 4) // 2), jnp.where(q < 4, 0, q % 2))),
        ],
    )(packed)


def unpack_attn_kernel(src, qkv, out):
    q = pl.program_id(1)
    flat = jnp.concatenate([src[0, 0, i, :400].astype(F32) for i in range(4)], axis=0)

    @pl.when(q < 3)
    def _():
        for k in range(5):
            qkv[:, 128 * k : 128 * (k + 1)] = flat[320 * k : 320 * (k + 1)]

    @pl.when(q == 3)
    def _():
        for k in range(5):
            out[:, 128 * k : 128 * (k + 1)] = flat[320 * k : 320 * (k + 1)]


def unpack_attn(packed):
    return pl.pallas_call(
        unpack_attn_kernel,
        name="unpack_attn",
        grid=(2, 4),
        out_shape=[jax.ShapeDtypeStruct((320, 3840), F32), jax.ShapeDtypeStruct((320, 1280), F32)],
        in_specs=[pl.BlockSpec((1, 1, 4, 416, 128), lambda c, q: (c, q, 0, 0, 0))],
        out_specs=[
            pl.BlockSpec((320, 640), lambda c, q: (0, c * 3 + jnp.minimum(q, 2))),
            pl.BlockSpec((320, 640), lambda c, q: (0, c)),
        ],
    )(packed)


def small_row(packed, rows, slab, row, n):
    return packed[0, 0, slab, rows + row : rows + row + -(-n // 128), :].astype(F32).reshape(-1)[:n]


def shards(
    tokens,
    cotangent,
    ln1_gain,
    ln1_bias,
    w_qkv,
    qv_bias,
    w_out,
    out_bias,
    ln2_gain,
    ln2_bias,
    w_fc,
    fc_bias,
    w_proj,
    proj_bias,
):
    own = (ln1_gain, ln1_bias, qv_bias, out_bias, ln2_gain, ln2_bias, proj_bias, fc_bias)
    small = jnp.stack([jnp.pad(v.astype(F32), (0, 1280 - v.shape[0])) for v in own])
    f_qkv, f_out, f_fc, f_proj, f_small, normed_one, attended, heads, lse = front(
        tokens[0], small, w_qkv, w_out, w_fc, w_proj
    )
    f_qkv, f_out, f_fc, f_proj = (
        f_qkv.reshape(1280, 3840),
        f_out.reshape(1280, 1280),
        f_fc.reshape(1280, 5120),
        f_proj.reshape(5120, 1280),
    )
    block_out, n2t, actt, grad_pre, grad_middle, grad_branch, grad_attended, small_mlp = mlp(
        tokens[0], attended, cotangent[0], f_small, f_out, f_fc, f_proj
    )
    grad_qkv, *parts = backward(grad_attended, heads, lse, small_mlp, n2t, actt, grad_pre, cotangent[0])

    gain_one = f_small[:, 0, :320].reshape(-1)
    hat_one, scale_one = norm(tokens[0].astype(F32))
    grad_normed = lax.dot_general(grad_qkv, f_qkv, (((1,), (1,)), ((), ())), preferred_element_type=F32)
    grad_tokens = (grad_middle + norm_back(grad_normed, hat_one, scale_one, gain_one)).astype(BF16)
    sums = jnp.sum(grad_qkv.astype(F32), axis=0)
    zeros = jnp.zeros((1280,), F32)
    small_attn = jnp.stack(
        [jnp.sum(grad_normed * hat_one, axis=0), jnp.sum(grad_normed, axis=0), sums[:1280], sums[2560:]] + [zeros] * 4
    )
    packed_mlp, packed_attn = last(normed_one.T, grad_qkv, attended.T, grad_branch, small_attn, parts)

    g_fc, g_proj = unpack_mlp(packed_mlp)
    g_qkv, g_out = unpack_attn(packed_attn)
    return (
        block_out[None],
        grad_tokens[None],
        small_row(packed_attn, 400, 0, 0, 320),
        small_row(packed_attn, 400, 0, 3, 320),
        g_qkv,
        small_row(packed_attn, 400, 1, 0, 640),
        g_out,
        small_row(packed_mlp, 800, 0, 9, 320),
        small_row(packed_mlp, 800, 0, 0, 320),
        small_row(packed_mlp, 800, 0, 3, 320),
        g_fc,
        small_row(packed_mlp, 800, 1, 0, 1280),
        g_proj,
        small_row(packed_mlp, 800, 0, 6, 320),
    )


def solution(mesh):
    vector, matrix, batch = P("shard"), P("shard", None), P("rep", "shard", None)
    placed = (batch, batch, vector, vector, matrix, vector, matrix, vector, vector, vector, matrix, vector, matrix, vector)
    return jax.shard_map(shards, mesh=mesh, in_specs=placed, out_specs=placed, check_vma=False)
```

```python
import jax
import jax.numpy as jnp
from jax import lax
from jax.experimental import pallas as pl
from jax.experimental.pallas import tpu as pltpu
from jax.sharding import PartitionSpec as P

MESH = pl.DeviceIdType.MESH
F32, BF16 = jnp.float32, jnp.bfloat16


def where_am_i():
    rep = lax.axis_index("rep")
    return lax.axis_index("shard"), (rep // 2) % 4, rep // 8, rep % 2


def device_at(x, y, z, c):
    return {"rep": (z * 4 + y) * 2 + c, "shard": x}


def wrap(v):
    return lax.rem(v + 4, 4)


class Net:
    def __init__(self, send_sems, recv_sems):
        self.send_sems, self.recv_sems, self.used = send_sems, recv_sems, 0
        self.all = []

    def send(self, src, dst, target):
        copy = pltpu.make_async_remote_copy(
            src_ref=src, dst_ref=dst,
            send_sem=self.send_sems.at[self.used], recv_sem=self.recv_sems.at[self.used],
            device_id=target, device_id_type=MESH,
        )
        copy.start()
        self.used += 1
        self.all.append(copy)
        return copy

    def finish(self):
        for copy in self.all:
            copy.wait_send()


def wait_all(copies):
    for copy in copies:
        copy.wait_recv()


def each(items, what, *rest):
    for item in items:
        getattr(item, what)(*rest)


def greet(targets):
    barrier = pltpu.get_barrier_semaphore()
    for target in targets:
        pl.semaphore_signal(barrier, 1, device_id=target, device_id_type=MESH)
    pl.semaphore_wait(barrier, len(targets))


class Torus:
    def __init__(self):
        self.x, self.y, self.z, self.c = where_am_i()

    def at(self, axis, step):
        x, y, z = self.x, self.y, self.z
        if axis == "x":
            x = wrap(x + step)
        elif axis == "y":
            y = wrap(y + step)
        else:
            z = wrap(z + step)
        return device_at(x, y, z, self.c)

    def pos(self, axis):
        return {"x": self.x, "y": self.y, "z": self.z}[axis]

    def sibling(self):
        return device_at(self.x, self.y, self.z, 1 - self.c)

    def neighbours(self, axes="xyz", core=True):
        out = [self.at(a, s) for a in axes for s in (1, 2, 3)]
        return out + ([self.sibling()] if core else [])


PLANS = {
    "qkv": (320, 3840, 4, 8, 3),
    "out": (320, 1280, 4, 0, 1),
    "fc": (320, 5120, 8, 8, 4),
    "proj": (1280, 1280, 2, 2, 1),
}


def rect_of(rows, start, width, order, y, z, stage):
    if rows == 320:
        if stage == 0:
            return y * 80, 80, start + z * (width // 4), width // 4
        if order == "yz":
            return 0, 320, start + z * (width // 4), width // 4
        return y * 80, 80, start, width
    first, second = (y, z) if order == "yz" else (z, y)
    if stage == 0:
        return second * 320 + first * 80, 80, start, width
    return second * 320, 320, start, width


def part(ref, owner, rect):
    r, nr, c, nc = rect
    return ref.at[owner, pl.ds(pl.multiple_of(r, 16), nr), pl.ds(pl.multiple_of(c, 128), nc)]


def own_part(ref, rect):
    r, nr, c, nc = rect
    return ref.at[pl.ds(pl.multiple_of(r, 16), nr), pl.ds(pl.multiple_of(c, 128), nc)]


class Gather:
    def __init__(self, net, torus, name, src, full, lean):
        self.net, self.t, self.src, self.full, self.lean = net, torus, src, full, lean
        self.rows, cols, a, b, d = PLANS[name]
        half = torus.c * (cols // 2)
        self.regions = []
        at = 0
        for order, tiles in (("yz", a), ("zy", b)):
            if tiles:
                self.regions.append((order, half + at * 128, tiles * 128))
            at += tiles
        self.alone = (half + at * 128, d * 128)
        self.others = [wrap(torus.x + k) for k in (1, 2, 3)]
        self.got = {"core": []}

    def rect(self, region, stage, shift=0):
        order, start, width = region
        y, z = self.t.y, self.t.z
        axis = order[stage]
        if axis == "y":
            y = wrap(y + shift)
        else:
            z = wrap(z + shift)
        return rect_of(self.rows, start, width, order, y, z, stage)

    def both(self, what, *rest):
        for i in range(len(self.regions)):
            getattr(self, what)(i, *rest)

    def start(self):
        t, net = self.t, self.net
        for i, region in enumerate(self.regions):
            rect = self.rect(region, 0)
            self.got[i, "x"] = [
                net.send(own_part(self.src, rect), part(self.full, t.x, rect), t.at("x", s)) for s in (1, 3, 2)
            ]

    def start_alone(self):
        t, net = self.t, self.net
        rect = (0, self.rows, *self.alone)
        self.got["alone"] = [
            net.send(own_part(self.src, rect), part(self.full, t.x, rect), t.at("x", s)) for s in (1, 3)
        ]

    def alone_on(self):
        t, net = self.t, self.net
        h = self.rows // 2
        one, two = self.got["alone"]
        start, width = self.alone
        whole = (0, self.rows, start, width)
        one.wait_recv()
        left = wrap(t.x - 1)
        rect = (0, h, start, width)
        a = net.send(part(self.full, left, rect), part(self.full, left, rect), t.at("x", 1))
        two.wait_recv()
        right = wrap(t.x + 1)
        rect = (h, h, start, width)
        b = net.send(part(self.full, right, rect), part(self.full, right, rect), t.at("x", 3))
        self.got["alone2"] = [a, b]
        self.got["core"] += [
            net.send(part(self.full, o, whole), part(self.full, o, whole), t.sibling()) for o in (left, right)
        ]

    def alone_end(self):
        wait_all(self.got["alone2"])

    def alone_share(self):
        o = wrap(self.t.x + 2)
        whole = (0, self.rows, *self.alone)
        self.got["core"].append(self.net.send(part(self.full, o, whole), part(self.full, o, whole), self.t.sibling()))

    def spread(self, i):
        region = self.regions[i]
        wait_all(self.got[i, "x"])
        rect = self.rect(region, 0)
        self.got[i, 0] = [
            self.net.send(part(self.full, o, rect), part(self.full, o, rect), self.t.at(region[0][0], s))
            for s in (1, 3, 2)
            for o in self.others
        ]

    def widen(self, i):
        region = self.regions[i]
        wait_all(self.got[i, 0])
        rect = self.rect(region, 1)
        self.got[i, 1] = [
            [self.net.send(part(self.full, o, rect), part(self.full, o, rect), self.t.at(region[0][1], s)) for o in self.others]
            for s in (1, 3)
        ]

    def pass_on(self, i):
        region = self.regions[i]
        axis = region[0][1]
        cut = 2 if self.lean else 1
        ahead, behind = self.got[i, 1]
        sent = []
        for copies, shift, to, owners in (
            (ahead, -1, 1, self.others[:cut]),
            (behind, 1, 3, self.others[cut:]),
        ):
            wait_all(copies)
            rect = self.rect(region, 1, shift)
            for o in owners:
                sent.append(self.net.send(part(self.full, o, rect), part(self.full, o, rect), self.t.at(axis, to)))
        self.got[i, 2] = sent

    def to_sibling(self, region, shifts):
        for shift in shifts:
            rect = self.rect(region, 1, shift)
            for o in self.others:
                self.got["core"].append(
                    self.net.send(part(self.full, o, rect), part(self.full, o, rect), self.t.sibling())
                )

    def share(self, i):
        self.to_sibling(self.regions[i], (0, -1, 1))

    def arrive(self, i):
        wait_all(self.got[i, 2])

    def share_last(self, i):
        self.to_sibling(self.regions[i], (2,))

    def finish(self):
        wait_all(self.got["core"])


LAG = 0.5


def dot_t(a, b):
    return lax.dot_general(a, b, (((1,), (1,)), ((), ())), preferred_element_type=F32)


def causal(s, i):
    rows = lax.broadcasted_iota(jnp.int32, (256, 256), 0)
    cols = lax.broadcasted_iota(jnp.int32, (256, 256), 1)
    last = jnp.where(cols <= rows, s[:, 256 * i :], -1e30)
    return last if i == 0 else jnp.concatenate([s[:, : 256 * i], last], axis=1)


class Swap:
    def __init__(self, net, torus, parts):
        self.net, self.t, self.parts = net, torus, parts

    def pack_single(self, full, single):
        parts = self.parts
        for d in range(4):
            cols = [full[:, 1280 * k + 1024 + 64 * d : 1280 * k + 1088 + 64 * d] for k in range(parts)]
            if parts % 2:
                cols.append(jnp.zeros((256, 64), BF16))
            single[d] = jnp.concatenate(cols, axis=1)

    def out_pairs(self, full, box):
        t, net, got = self.t, self.net, []
        for p in range(2):
            sent = []
            for s in (1, 3, 2):
                d = wrap(t.x + s)
                for k in range(self.parts):
                    cols = pl.ds(pl.multiple_of(1280 * k + 256 * d + 128 * p, 128), 128)
                    sent.append(net.send(full.at[:, cols], box.at[p, k, t.x], t.at("x", s)))
            got.append(sent)
        return got

    def keep_pairs(self, full, box):
        for p in range(2):
            for k in range(self.parts):
                cols = pl.ds(pl.multiple_of(1280 * k + 256 * self.t.x + 128 * p, 128), 128)
                box[p, k, self.t.x] = full[:, cols]

    def out_single(self, single, box):
        t = self.t
        sent = [self.net.send(single.at[wrap(t.x + s)], box.at[t.x], t.at("x", s)) for s in (1, 3, 2)]
        return sent

    def back_pair(self, p, src, full):
        t, net, sent = self.t, self.net, []
        for s in (1, 3, 2):
            d = wrap(t.x + s)
            for k in range(self.parts):
                cols = pl.ds(pl.multiple_of(1280 * k + 256 * t.x + 128 * p, 128), 128)
                sent.append(net.send(src.at[d, k, p], full.at[:, cols], t.at("x", s)))
        return sent

    def keep_back(self, p, src, full):
        for k in range(self.parts):
            cols = pl.ds(pl.multiple_of(1280 * k + 256 * self.t.x + 128 * p, 128), 128)
            full[:, cols] = src[self.t.x, k, p]

    def unpack_single(self, box, full):
        for k in range(self.parts):
            cols = [box[d, :, 64 * k : 64 * k + 64] for d in range(4)]
            full[:, 1280 * k + 1024 : 1280 * (k + 1)] = jnp.concatenate(cols, axis=1)


EPS = 1e-05
VECTORS = ("ln1_gain", "ln1_bias", "qv_bias", "out_bias", "ln2_gain", "ln2_bias", "proj_bias", "fc_bias")
SIZES = (320, 320, 640, 320, 320, 320, 320, 1280)


def whole_vector(small, name):
    k = VECTORS.index(name)
    return jnp.concatenate([small[x, k : k + 1, : SIZES[k]] for x in range(4)], axis=1)


def dot(a, b):
    return jnp.dot(a, b, preferred_element_type=F32)


def norm(v):
    center = v - jnp.mean(v, axis=-1, keepdims=True)
    scale = lax.rsqrt(jnp.mean(center * center, axis=-1, keepdims=True) + EPS)
    return center * scale, scale


def norm_back(grad, hat, scale, gain):
    inner = grad * gain
    return scale * (
        inner - jnp.mean(inner, axis=-1, keepdims=True) - hat * jnp.mean(inner * hat, axis=-1, keepdims=True)
    )


class Forward:
    def __init__(self, net, torus, qkv, full, heads, lse, box, single, single_in, outs, res, res_single, res_single_in):
        self.net, self.t, self.qkv, self.full, self.heads, self.lse = net, torus, qkv, full, heads, lse
        self.box, self.single, self.single_in, self.outs = box, single, single_in, outs
        self.res, self.res_single, self.res_single_in = res, res_single, res_single_in
        self.swap, self.back = Swap(net, torus, 3), Swap(net, torus, 1)
        self.sent = []

    def start(self):
        t, swap = self.t, self.swap
        self.got = swap.out_pairs(self.qkv, self.box)
        swap.pack_single(self.qkv, self.single)
        self.got_single = swap.out_single(self.single, self.single_in)
        swap.keep_pairs(self.qkv, self.box)
        self.single_in[t.x] = self.single[t.x]
        self.lse[...] = jnp.zeros_like(self.lse)

    def take(self, p):
        heads = self.heads
        if p < 2:
            wait_all(self.got[p])
            for k in range(3):
                for s in range(4):
                    for j in range(2):
                        v = self.box[p, k, s, :, 64 * j : 64 * j + 64]
                        heads[k, 2 * p + j, 256 * s : 256 * (s + 1), :] = v * BF16(0.125) if k == 0 else v
            return
        wait_all(self.got_single)
        for k in range(3):
            for s in range(4):
                v = self.single_in[s, :, 64 * k : 64 * k + 64]
                heads[k, 4, 256 * s : 256 * (s + 1), :] = v * BF16(0.125) if k == 0 else v

    def head(self, h, j):
        heads, lse = self.heads, self.lse
        lane = lax.broadcasted_iota(jnp.int32, (256, 128), 1)
        for i in range(4):
            rows = slice(256 * i, 256 * (i + 1))
            n = 256 * (i + 1)
            s = causal(dot_t(heads[0, h, rows, :], heads[1, h, :n, :]), i)
            top = jnp.max(s, axis=1, keepdims=True)
            p = jnp.exp(s - top)
            total = jnp.sum(p, axis=1, keepdims=True)
            lse[rows, :] = jnp.where(lane == h, top + jnp.log(total), lse[rows, :])
            o = dot(p.astype(BF16), heads[2, h, :n, :])
            self.outs[j, rows, :] = (o / total).astype(BF16)

    def give(self, p):
        back, outs = self.back, self.outs
        for i in range(4):
            rows = slice(256 * i, 256 * (i + 1))
            if p < 2:
                self.res[i, 0, p] = jnp.concatenate([outs[0, rows, :], outs[1, rows, :]], axis=1)
            else:
                self.res_single[i] = jnp.concatenate([outs[0, rows, :], jnp.zeros((256, 64), BF16)], axis=1)
        if p < 2:
            self.sent += back.back_pair(p, self.res, self.full)
            back.keep_back(p, self.res, self.full)
        else:
            self.sent_single = back.out_single(self.res_single, self.res_single_in)
            self.res_single_in[self.t.x] = self.res_single[self.t.x]

    def finish(self):
        wait_all(self.sent_single)
        self.back.unpack_single(self.res_single_in, self.full)
        wait_all(self.sent)


def front_kernel(
    tokens, small, w_qkv, w_out, w_fc, w_proj,
    f_qkv, f_out, f_fc, f_proj, f_small, normed, att, heads, lse,
    v_qkv, h_out, h_fc, h_proj, small_all, bias, qkv, other, full,
    box, single, single_in, outs, res, res_single, res_single_in, ssem, rsem, lsem,
):
    t = Torus()
    greet(t.neighbours())
    net = Net(ssem, rsem)
    sib, c = t.sibling(), t.c
    q = Gather(net, t, "qkv", w_qkv, v_qkv, 0)
    o = Gather(net, t, "out", w_out, f_out, 1)
    f = Gather(net, t, "fc", w_fc, f_fc, 0)
    p = Gather(net, t, "proj", w_proj, f_proj, 1)
    fwd = Forward(net, t, qkv, full, heads, lse, box, single, single_in, outs, res, res_single, res_single_in)
    own = pltpu.make_async_copy(w_qkv, v_qkv.at[t.x], lsem.at[0])
    own.start()
    held = [(w_out, h_out, f_out), (w_fc, h_fc, f_fc), (w_proj, h_proj, f_proj)]
    local = [pltpu.make_async_copy(s, h, lsem.at[1 + k]) for k, (s, h, _) in enumerate(held)]
    each(local, "start")
    sent = []

    def columns(region):
        start, width = region
        cols = pl.ds(pl.multiple_of(start, 128), width)
        made = dot(normed[...].reshape(512, 1280), v_qkv[:, :, cols].reshape(1280, width)) + bias[0:1, cols]
        made = made.astype(BF16)
        qkv[:, cols] = made[:256]
        other[:, cols] = made[256:]
        sent.append(net.send(other.at[:, cols], qkv.at[:, cols], sib))

    q.start()
    p.start()
    smalls = [net.send(small, small_all.at[t.x], t.at("x", s)) for s in (1, 3, 2)]
    small_all[t.x] = small[...]
    o.start()
    q.start_alone()
    q.spread(0)
    o.start_alone()
    q.spread(1)
    p.spread(0)
    q.widen(0)
    f.start()
    q.widen(1)
    wait_all(smalls)
    hat, _ = norm(tokens[...].astype(F32))
    gain, shift = whole_vector(small_all, "ln1_gain"), whole_vector(small_all, "ln1_bias")
    normed[0] = (hat * gain + shift).astype(BF16)
    swapped = net.send(normed.at[0], normed.at[1], sib)
    p.spread(1)
    o.alone_on()
    q.alone_on()
    for n, (_, h, full_w) in enumerate(held):
        local[n].wait()
        local[n] = pltpu.make_async_copy(h, full_w.at[t.x], lsem.at[1 + n])
        local[n].start()
    p.widen(0)
    p.start_alone()
    f.start_alone()
    o.spread(0)
    q.alone_end()
    q.pass_on(1)
    f.spread(0)
    q.pass_on(0)
    o.widen(0)
    f.spread(1)
    q.share(0)
    p.widen(1)
    k = VECTORS.index("qv_bias")
    for n in (0, 1, 4, 5):
        row = small_all[n if n < 2 else n - 2, k : k + 1, :640]
        bias[0:1, 640 * n : 640 * (n + 1)] = row
    bias[0:1, 1280:2560] = jnp.zeros((1, 1280), F32)
    f_small[...] = small_all[...]
    swapped.wait_recv()
    q.share(1)
    p.alone_on()
    o.alone_end()
    q.arrive(1)
    own.wait()
    columns(q.regions[1][1:])
    columns(q.alone)
    q.arrive(0)
    q.alone_share()
    f.alone_on()
    columns(q.regions[0][1:])
    f.widen(0)
    o.pass_on(0)
    p.alone_end()
    q.share_last(1)
    wait_all(sent)
    fwd.start()
    f.widen(1)
    q.share_last(0)
    fwd.take(0)
    p.pass_on(0)
    p.pass_on(1)
    p.share(0)
    fwd.head(0, 0)
    p.alone_share()
    o.share(0)
    f.pass_on(0)
    fwd.head(1, 1)
    o.arrive(0)
    o.alone_share()
    o.share_last(0)
    fwd.give(0)
    q.finish()
    p.share(1)
    keep = pltpu.make_async_copy(v_qkv, f_qkv, lsem.at[0])
    keep.start()
    f.pass_on(1)
    f.share(1)
    fwd.take(1)
    f.alone_end()
    f.alone_share()
    f.share(0)
    fwd.head(2, 0)
    fwd.head(3, 1)
    fwd.give(1)
    fwd.take(2)
    fwd.head(4, 0)
    f.arrive(0)
    p.arrive(0)
    f.share_last(0)
    fwd.give(2)
    p.arrive(1)
    p.share_last(0)
    f.arrive(1)
    f.share_last(1)
    o.finish()
    p.share_last(1)
    f.finish()
    p.finish()
    fwd.finish()
    att[...] = full[...]
    keep.wait()
    each(local, "wait")
    net.finish()


FRONT_SEMS = 340


def front(tokens, small, w_qkv, w_out, w_fc, w_proj):
    vm, anys = pl.BlockSpec(memory_space=pltpu.VMEM), pl.BlockSpec(memory_space=pl.ANY)
    weights = (w_qkv, w_out, w_fc, w_proj)
    return pl.pallas_call(
        front_kernel,
        name="front",
        out_shape=[jax.ShapeDtypeStruct((4,) + w.shape, BF16) for w in weights]
        + [
            jax.ShapeDtypeStruct((4, 8, 1280), F32),
            jax.ShapeDtypeStruct((2, 256, 1280), BF16),
            jax.ShapeDtypeStruct((256, 1280), BF16),
            jax.ShapeDtypeStruct((3, 5, 1024, 64), BF16),
            jax.ShapeDtypeStruct((1024, 128), F32),
        ],
        in_specs=[vm] * 2 + [anys] * 4,
        out_specs=[anys] * 4 + [vm] * 5,
        scratch_shapes=[
            pltpu.VMEM((4, 320, 3840), BF16),
            pltpu.VMEM((320, 1280), BF16),
            pltpu.VMEM((320, 5120), BF16),
            pltpu.VMEM((1280, 1280), BF16),
            pltpu.VMEM((4, 8, 1280), F32),
            pltpu.VMEM((8, 3840), F32),
            pltpu.VMEM((256, 3840), BF16),
            pltpu.VMEM((256, 3840), BF16),
            pltpu.VMEM((256, 1280), BF16),
            pltpu.VMEM((2, 3, 4, 256, 128), BF16),
            pltpu.VMEM((4, 256, 256), BF16),
            pltpu.VMEM((4, 256, 256), BF16),
            pltpu.VMEM((2, 1024, 64), BF16),
            pltpu.VMEM((4, 1, 2, 256, 128), BF16),
            pltpu.VMEM((4, 256, 128), BF16),
            pltpu.VMEM((4, 256, 128), BF16),
            pltpu.SemaphoreType.DMA((FRONT_SEMS,)),
            pltpu.SemaphoreType.DMA((FRONT_SEMS,)),
            pltpu.SemaphoreType.DMA((4,)),
        ],
        compiler_params=pltpu.CompilerParams(collective_id=0, has_side_effects=True, vmem_limit_bytes=56 << 20),
    )(tokens, small, *weights)


GELU_A, GELU_B = 0.7978845608028654, 0.044715
FF_STEP = 640


def mlp_kernel(
    tokens, att, cot, small, w_out, w_fc, w_proj,
    block_out, grad_mid, datt, n2t_c, attt_c, cot_c, actt_c, gp_c, gb_c, small_c,
    n2, middle, out_acc, grad_acc, bias, n2t, attt, actt, gp, gb, small_grad, ssem, rsem, lsem,
):
    t = Torus()
    j = pl.program_id(0)
    sib, c = t.sibling(), t.c
    low, high = pl.ds(0, 256), pl.ds(256, 256)

    def keep(k, src, dst):
        return pltpu.make_async_copy(src, dst, lsem.at[k])

    def give(k, src, dst):
        return pltpu.make_async_remote_copy(
            src_ref=src, dst_ref=dst, send_sem=ssem.at[k], recv_sem=rsem.at[k], device_id=sib, device_id_type=MESH
        )

    half = [pl.ds(pl.multiple_of(k * 640, 128), 640) for k in (c, 1 - c)]
    whole = [
        (keep(0, n2t, n2t_c.at[:, low]), give(0, n2t, n2t_c.at[:, high])),
        (keep(1, attt, attt_c.at[:, low]), give(1, attt, attt_c.at[:, high])),
        (keep(2, cot, cot_c.at[low]), give(2, cot, cot_c.at[high])),
        (keep(3, gb.at[:, half[0]], gb_c.at[low]), give(3, gb.at[:, half[1]], gb_c.at[high])),
        (keep(4, small_grad, small_c.at[0]), give(4, small_grad, small_c.at[1])),
    ]

    def strip(s, kept):
        n = 2 * s + (c if kept else 1 - c)
        rows = pl.ds(pl.multiple_of(s * 640, 16), 640)
        if kept:
            return [
                keep(5 + s, actt.at[n], actt_c.at[rows, low]),
                keep(9 + s, gp.at[n], gp_c.at[s, low]),
            ]
        return [
            give(5 + s, actt.at[n], actt_c.at[rows, high]),
            give(9 + s, gp.at[n], gp_c.at[s, high]),
        ]

    @pl.when(j == 0)
    def _():
        greet([sib])
        for copy in whole[2]:
            copy.start()
        attt[...] = att[...].T
        for copy in whole[1]:
            copy.start()
        mid = tokens[...].astype(F32) + dot(att[...], w_out[...]) + whole_vector(small, "out_bias")
        middle[...] = mid
        hat, _ = norm(mid)
        n2[...] = (hat * whole_vector(small, "ln2_gain") + whole_vector(small, "ln2_bias")).astype(BF16)
        n2t[...] = n2[...].T
        for copy in whole[0]:
            copy.start()
        out_acc[...] = mid + whole_vector(small, "proj_bias")
        grad_acc[...] = jnp.zeros_like(grad_acc)
        k = VECTORS.index("fc_bias")
        for x in range(4):
            for h in range(2):
                bias[2 * x + h, 0:1, :] = small[x, k : k + 1, 640 * h : 640 * (h + 1)]

    pre = dot(n2[...], w_fc[...]) + bias[j, 0:1, :]
    square = pre * pre
    bend = jnp.tanh(GELU_A * (pre + GELU_B * pre * square))
    act = (0.5 * pre * (1.0 + bend)).astype(BF16)
    actt[j] = act.T
    out_acc[...] += dot(act, w_proj[...])
    slope = 0.5 * (1.0 + bend) + (0.5 * GELU_A) * pre * (1.0 - bend * bend) * (1.0 + 3.0 * GELU_B * square)
    grad = (dot_t(cot[...], w_proj[...]) * slope).astype(BF16)
    gp[j] = grad
    grad_acc[...] += dot_t(grad, w_fc[...])
    column_sums = jnp.sum(grad.astype(F32), axis=0, keepdims=True)
    for n in range(8):
        @pl.when(j == n)
        def _():
            small_grad[4 + n // 2 : 5 + n // 2, 640 * (n % 2) : 640 * (n % 2 + 1)] = column_sums

    @pl.when(lax.rem(j, 2) == c)
    def _():
        for copy in strip(j // 2, True):
            copy.start()

    @pl.when(lax.rem(j, 2) != c)
    def _():
        for copy in strip(j // 2, False):
            copy.start()

    @pl.when(j == pl.num_programs(0) - 1)
    def _():
        hat, scale = norm(middle[...])
        g = grad_acc[...]
        cot_rows = cot[...].astype(F32)
        mid = cot_rows + norm_back(g, hat, scale, whole_vector(small, "ln2_gain"))
        grad_mid[...] = mid
        branch = mid.astype(BF16)
        gb[...] = branch
        for copy in whole[3]:
            copy.start()
        small_grad[0:1, :] = jnp.sum(g * hat, axis=0, keepdims=True)
        small_grad[1:2, :] = jnp.sum(g, axis=0, keepdims=True)
        small_grad[2:3, :] = jnp.sum(cot_rows, axis=0, keepdims=True)
        small_grad[3:4, :] = jnp.sum(branch.astype(F32), axis=0, keepdims=True)
        for copy in whole[4]:
            copy.start()
        datt[...] = dot_t(branch, w_out[...]).astype(BF16)
        block_out[...] = out_acc[...].astype(BF16)
        for own, other in whole:
            own.wait()
            other.wait()
        for s in range(4):
            for copy in strip(s, True) + strip(s, False):
                copy.wait()


def mlp(tokens, att, cot, small, w_out, w_fc, w_proj):
    rows = pl.BlockSpec((256, 1280), lambda j: (0, 0))
    anys = pl.BlockSpec(memory_space=pl.ANY)
    return pl.pallas_call(
        mlp_kernel,
        name="mlp",
        grid=(5120 // FF_STEP,),
        out_shape=[
            jax.ShapeDtypeStruct((256, 1280), BF16),
            jax.ShapeDtypeStruct((256, 1280), F32),
            jax.ShapeDtypeStruct((256, 1280), BF16),
            jax.ShapeDtypeStruct((1280, 512), BF16),
            jax.ShapeDtypeStruct((1280, 512), BF16),
            jax.ShapeDtypeStruct((512, 1280), BF16),
            jax.ShapeDtypeStruct((2560, 512), BF16),
            jax.ShapeDtypeStruct((4, 512, 640), BF16),
            jax.ShapeDtypeStruct((512, 640), BF16),
            jax.ShapeDtypeStruct((2, 8, 1280), F32),
        ],
        in_specs=[
            rows,
            rows,
            rows,
            pl.BlockSpec((4, 8, 1280), lambda j: (0, 0, 0)),
            pl.BlockSpec((1280, 1280), lambda j: (0, 0)),
            pl.BlockSpec((1280, FF_STEP), lambda j: (0, j)),
            pl.BlockSpec((FF_STEP, 1280), lambda j: (j, 0)),
        ],
        out_specs=[rows] * 3 + [anys] * 7,
        scratch_shapes=[
            pltpu.VMEM((256, 1280), BF16),
            pltpu.VMEM((256, 1280), F32),
            pltpu.VMEM((256, 1280), F32),
            pltpu.VMEM((256, 1280), F32),
            pltpu.VMEM((8, 8, 640), F32),
            pltpu.VMEM((1280, 256), BF16),
            pltpu.VMEM((1280, 256), BF16),
            pltpu.VMEM((8, 640, 256), BF16),
            pltpu.VMEM((8, 256, 640), BF16),
            pltpu.VMEM((256, 1280), BF16),
            pltpu.VMEM((8, 1280), F32),
            pltpu.SemaphoreType.DMA((13,)),
            pltpu.SemaphoreType.DMA((13,)),
            pltpu.SemaphoreType.DMA((13,)),
        ],
        compiler_params=pltpu.CompilerParams(
            collective_id=3, has_side_effects=True, vmem_limit_bytes=48 << 20, dimension_semantics=("arbitrary",)
        ),
    )(tokens, att, cot, small, w_out, w_fc, w_proj)


def view(ref, axes, chosen, rows):
    return ref.at[tuple(chosen.get(a, slice(None)) for a in axes) + (pl.ds(*rows),)]


def leading(ref):
    return ref.shape[:-2]


def add_into(dst, *srcs):
    lead = leading(dst)
    count = 1
    for n in lead:
        count *= n

    def slab(i):
        index = []
        for n in reversed(lead):
            index.append(lax.rem(i, n))
            i = i // n
        return tuple(reversed(index))

    def body(i, _):
        at = slab(i)
        total = dst[at].astype(F32)
        for s in srcs:
            total = total + s[at].astype(F32)
        dst[at] = total.astype(BF16)
        return 0

    if count == 1 and not lead:
        total = dst[...].astype(F32)
        for s in srcs:
            total = total + s[...].astype(F32)
        dst[...] = total.astype(BF16)
    else:
        lax.fori_loop(0, count, body, 0)


def inbox_shapes(classes, phases):
    out = []
    for order, _, n in classes:
        if 0 in phases:
            half = [2 if a == order[1] else 4 for a in "xyz" if a != order[0]]
            out += [half + [n, 128]] * 2 + [[4, 4, n, 128]] * 2
        if 1 in phases:
            out += [[2, n, 128]] * 2 + [[4, n, 128]] * 2
        if 2 in phases:
            out += [[3, n, 128]]
    return [pltpu.VMEM(tuple(s), BF16) for s in out]


def inboxes(refs, phases):
    refs, out = list(refs), []
    while refs:
        mine = {}
        for phase in phases:
            n = 1 if phase == 2 else 4
            mine[phase], refs = refs[:n], refs[n:]
        out.append(mine)
    return out


class Lane:
    def __init__(self, net, torus, acc, axes, inbox, order, row, n):
        self.net, self.t, self.acc, self.axes, self.inbox, self.order = net, torus, acc, axes, inbox, order
        self.rows, self.base = (row, n), 0
        self.fixed = {}
        self.got = {}

    def part(self, phase):
        axis = self.order[phase]
        return view(self.acc, self.axes, {**self.fixed, axis: self.t.pos(axis)}, self.rows)

    def held(self):
        return view(self.acc, self.axes, self.fixed, self.rows)

    def halves(self, phase):
        a = self.order[phase + 1]
        return [{a: pl.ds(0, 2)}, {a: pl.ds(2, 2)}]

    def box_half(self, box, phase, half):
        if phase == 1:
            return box.at[pl.ds(2 * half, 2)]
        left = [a for a in "xyz" if a != self.order[0]]
        cut = left.index(self.order[1])
        return box.at[(slice(None),) * cut + (pl.ds(2 * half, 2),)]

    def first(self, phase):
        axis = self.order[phase]
        p = self.t.pos(axis)
        h = self.halves(phase)
        b = self.inbox[phase]
        at = lambda shift, cut: view(self.acc, self.axes, {**self.fixed, axis: wrap(p + shift), **cut}, self.rows)
        up, down = self.t.at(axis, 1), self.t.at(axis, 3)
        far = [self.net.send(at(2, h[0]), b[0], up), self.net.send(at(2, h[1]), b[1], down)]
        near = [
            self.net.send(at(1, h[1]), self.box_half(b[2], phase, 1), up),
            self.net.send(at(3, h[0]), self.box_half(b[3], phase, 0), down),
        ]
        self.got[phase] = (far, near)

    def second(self, phase, side):
        axis = self.order[phase]
        p = self.t.pos(axis)
        b = self.inbox[phase]
        far, near = self.got[phase]
        step = 3 if side else 1
        chosen = {**self.fixed, axis: wrap(p + step), **self.halves(phase)[side]}
        here = view(self.acc, self.axes, chosen, self.rows)
        far[side].wait_recv()
        add_into(here, b[side])
        near.append(self.net.send(here, self.box_half(b[2 + side], phase, side), self.t.at(axis, step)))

    def third(self, phase):
        axis = self.order[phase]
        p = self.t.pos(axis)
        b = self.inbox[phase]
        for copy in self.got[phase][1]:
            copy.wait_recv()
        self.fixed[axis] = p
        add_into(self.held(), b[2], b[3])

    def last(self):
        axis = self.order[2]
        p = self.t.pos(axis)
        box = self.inbox[2][0]
        self.got[2] = [
            self.net.send(view(self.acc, self.axes, {**self.fixed, axis: wrap(p + s)}, self.rows), box.at[s - 1], self.t.at(axis, s))
            for s in (1, 3, 2)
        ]

    def done(self):
        axis = self.order[2]
        for copy in self.got[2]:
            copy.wait_recv()
        self.fixed[axis] = self.t.pos(axis)
        box = self.inbox[2][0]
        add_into(self.held(), box.at[0], box.at[1], box.at[2])


class Spread:
    def __init__(self, lane, out, order, row, n, sem):
        self.net, self.t, self.out, self.order, self.rows, self.sem = lane.net, lane.t, out, order, (row, n), sem
        chosen = {a: lane.t.pos(a) for a in lane.axes}
        self.own = view(lane.acc, lane.axes, chosen, (row - lane.base, n))

    def place(self, y, z):
        return self.out.at[self.t.c, y, z, pl.ds(*self.rows)]

    def band(self, v, b=slice(None)):
        y, z = (b, v) if self.order == "yz" else (v, b)
        return self.place(y, z)

    def start(self):
        t = self.t
        here = self.place(t.y, t.z)
        self.keep = pltpu.make_async_copy(self.own, here, self.sem)
        self.keep.start()
        self.first = [self.net.send(self.own, here, t.at(self.order[0], s)) for s in (1, 3, 2)]

    def second(self):
        t, axis = self.t, self.order[1]
        for copy in self.first:
            copy.wait_recv()
        self.keep.wait()
        here = self.band(t.pos(axis))
        self.near = [self.net.send(here, here, t.at(axis, s)) for s in (1, 3)]

    def third(self):
        t, axis = self.t, self.order[1]
        p = t.pos(axis)
        self.far = []
        for copy, shift, to, b in ((self.near[0], 3, 1, pl.ds(0, 2)), (self.near[1], 1, 3, pl.ds(2, 2))):
            copy.wait_recv()
            there = self.band(wrap(p + shift), b)
            self.far.append(self.net.send(there, there, t.at(axis, to)))

    def share(self):
        for copy in self.far:
            copy.wait_recv()
        whole = self.place(slice(None), slice(None))
        self.core = self.net.send(whole, whole, self.t.sibling())

    def finish(self):
        self.core.wait_recv()


GROUPS = {
    "mlp": ((176, 304, 320), 16, ("xyz", "yzx", "zxy")),
    "attn": ((144, 144, 112), 0, ("xyz", "yxz", "zxy")),
}
SMALL_ROWS = 16


def slab_rows(group):
    return sum(GROUPS[group][0]) + SMALL_ROWS


def classes_of(group):
    rows, extra, orders = GROUPS[group]
    row, out = 0, []
    for k, (order, n) in enumerate(zip(orders, rows)):
        n += extra if k == 2 else 0
        out.append((order, row, n))
        row += n
    return out


def spreads_of(group):
    a, b, c = classes_of(group)
    h = c[2] // 32 * 16
    return [(0, "yz", a[1], a[2]), (1, "zy", b[1], b[2]), (2, "yz", c[1], h), (2, "zy", c[1] + h, c[2] - h)]


def pieces_of(group, first, count):
    rows, out, flat, row = GROUPS[group][0], [], 0, 0
    for n in rows:
        for slab in range(16):
            lo, hi = max(first, flat), min(first + count, flat + n)
            if lo < hi:
                out.append((slab, row + lo - flat, hi - lo, lo - first))
            flat += n
        row += n
    return out


def store_blocks(acc, group, x, first, blocks):
    for k, block in enumerate(blocks):
        for slab, row, n, offset in pieces_of(group, first + 320 * k, 320):
            acc[x, slab // 4, slab % 4, pl.ds(row, n), :] = block[offset : offset + n]


def spreads_for(group, lanes, out, sems):
    return [Spread(lanes[k], out, order, row, n, sems.at[i]) for i, (k, order, row, n) in enumerate(spreads_of(group))]


def row_pieces(ref, row, start, n):
    v = ref[row : row + 1, start : start + n]
    if n % 128:
        v = jnp.concatenate([v, jnp.zeros((1, 128 - n % 128), F32)], axis=1)
    return [v[:, 128 * k : 128 * (k + 1)] for k in range(v.shape[1] // 128)]


def store_small(acc, row, slabs):
    for x in range(4):
        filled = slabs(x)
        for k in range(16):
            pieces = filled[k] if k < len(filled) else []
            if len(pieces) < 16:
                pieces = pieces + [jnp.zeros((16 - len(pieces), 128), F32)]
            acc[x, k // 4, k % 4, pl.ds(row, 16), :] = jnp.concatenate(pieces, axis=0).astype(BF16)


def product(lhs, rhs, acc, group, x, chunk):
    out = dot(lhs, rhs).astype(BF16)
    store_blocks(acc, group, x, 1600 * chunk, [out[:, 128 * t : 128 * (t + 1)] for t in range(5)])


class Backward:
    def __init__(self, net, torus, datt, full, heads, lse, box, single, single_in, do, dkv, grads, res, res_single, res_single_in):
        self.net, self.t, self.datt, self.full, self.heads, self.lse = net, torus, datt, full, heads, lse
        self.box, self.single, self.single_in, self.do, self.dkv, self.grads = box, single, single_in, do, dkv, grads
        self.res, self.res_single, self.res_single_in = res, res_single, res_single_in
        self.swap, self.back = Swap(net, torus, 1), Swap(net, torus, 3)
        self.sent = []

    def start(self):
        t, swap = self.t, self.swap
        self.got = swap.out_pairs(self.datt, self.box)
        swap.pack_single(self.datt, self.single)
        self.got_single = swap.out_single(self.single, self.single_in)
        swap.keep_pairs(self.datt, self.box)
        self.single_in[t.x] = self.single[t.x]

    def take(self, p):
        wait_all(self.got[p] if p < 2 else self.got_single)
        for s in range(4):
            rows = slice(256 * s, 256 * (s + 1))
            if p < 2:
                for j in range(2):
                    self.do[2 * p + j, rows, :] = self.box[p, 0, s, :, 64 * j : 64 * j + 64]
            else:
                self.do[4, rows, :] = self.single_in[s, :, :64]

    def head(self, h, j):
        heads, grads, dkv = self.heads, self.grads, self.dkv
        lane = lax.broadcasted_iota(jnp.int32, (256, 128), 1)
        dkv[...] = jnp.zeros_like(dkv)
        for i in range(4):
            rows = slice(256 * i, 256 * (i + 1))
            n = 256 * (i + 1)
            q, k, v, d = heads[0, h, rows, :], heads[1, h, :n, :], heads[2, h, :n, :], self.do[h, rows, :]
            total = jnp.sum(jnp.where(lane == h, self.lse[rows, :], 0.0), axis=1, keepdims=True)
            p = jnp.exp(causal(dot_t(q, k), i) - total)
            t1 = p * dot_t(d, v)
            inner = jnp.sum(t1, axis=1, keepdims=True)
            ds = (t1 - p * inner).astype(BF16)
            grads[0, j, rows, :] = (dot(ds, k) * 0.125).astype(BF16)
            dkv[0, :, :n] += dot(q.T, ds)
            dkv[1, :, :n] += dot(d.T, p.astype(BF16))
        for k in range(2):
            grads[1 + k, j] = dkv[k].T.astype(BF16)

    def give(self, p):
        grads, back = self.grads, self.back
        for i in range(4):
            rows = slice(256 * i, 256 * (i + 1))
            if p < 2:
                for k in range(3):
                    self.res[i, k, p] = jnp.concatenate([grads[k, 0, rows, :], grads[k, 1, rows, :]], axis=1)
            else:
                cols = [grads[k, 0, rows, :] for k in range(3)] + [jnp.zeros((256, 64), BF16)]
                self.res_single[i] = jnp.concatenate(cols, axis=1)
        if p < 2:
            self.sent += back.back_pair(p, self.res, self.full)
            back.keep_back(p, self.res, self.full)
        else:
            self.sent_single = back.out_single(self.res_single, self.res_single_in)
            self.res_single_in[self.t.x] = self.res_single[self.t.x]

    def finish(self):
        wait_all(self.sent_single)
        self.back.unpack_single(self.res_single_in, self.full)
        wait_all(self.sent)


def back_kernel(
    datt, heads, lse, small, n2t, actt, gp, cot,
    gqkv, part_0, part_1, part_2,
    n2t_v, actt_v, gp_v, cot_v, small_v, full,
    box, single, single_in, do, dkv, grads, res, res_single, res_single_in,
    ssem, rsem, lsem, acc, *inbox,
):
    t = Torus()
    loads = [
        pltpu.make_async_copy(src, dst, lsem.at[k])
        for k, (src, dst) in enumerate(((n2t, n2t_v), (gp, gp_v), (actt, actt_v), (cot, cot_v)))
    ]
    each(loads, "start")
    greet(t.neighbours())
    net = Net(ssem, rsem)
    bwd = Backward(net, t, datt, full, heads, lse, box, single, single_in, do, dkv, grads, res, res_single, res_single_in)
    lanes = [Lane(net, t, acc, "xyz", box_of, *k) for k, box_of in zip(classes_of("mlp"), inboxes(inbox, (0,)))]
    parts = [pltpu.make_async_copy(lane.part(0), part, lsem.at[k]) for k, (lane, part) in enumerate(zip(lanes, (part_0, part_1, part_2)))]

    def fc(s):
        def body(x, _):
            product(n2t_v[pl.ds(pl.multiple_of(x * 320, 16), 320), :], gp_v[s], acc, "mlp", x, s)
            return 0

        lax.fori_loop(0, 4, body, 0)

    def proj(sub):
        def body(x, _):
            lhs = actt_v[pl.ds(pl.multiple_of(x * 640 + sub * 320, 16), 320), :]
            for half in range(2):
                product(lhs, cot_v[:, 640 * half : 640 * (half + 1)], acc, "mlp", x, 4 + 2 * sub + half)
            return 0

        lax.fori_loop(0, 4, body, 0)

    def sums():
        small_v[...] = small[0] + small[1]
        store_small(
            acc, 800,
            lambda x: [
                [row for k in range(4) for row in row_pieces(small_v, k, 320 * x, 320)],
                row_pieces(small_v, 4 + x, 0, 1280),
            ],
        )

    bwd.start()
    each(loads[:2], "wait")
    each(loads[2:], "wait")
    proj(1)
    sums()
    fc(1)
    proj(0)
    lanes[2].first(0)
    fc(0)
    lanes[0].first(0)
    fc(2)
    fc(3)
    lanes[1].first(0)
    bwd.take(0)
    bwd.head(0, 0)
    lanes[0].second(0, 0)
    lanes[0].second(0, 1)
    bwd.head(1, 1)
    lanes[2].second(0, 1)
    bwd.give(0)
    bwd.take(1)
    bwd.head(2, 0)
    lanes[1].second(0, 1)
    lanes[2].second(0, 0)
    bwd.head(3, 1)
    bwd.give(1)
    bwd.take(2)
    lanes[1].second(0, 0)
    bwd.head(4, 0)
    lanes[0].third(0)
    bwd.give(2)
    lanes[2].third(0)
    parts[2].start()
    lanes[1].third(0)
    parts[1].start()
    parts[0].start()
    bwd.finish()
    gqkv[...] = full[...]
    each(parts, "wait")
    net.finish()


BACK_SEMS = 100


def backward(datt, heads, lse, small, n2t, actt, gp, cot):
    vm, anys = pl.BlockSpec(memory_space=pltpu.VMEM), pl.BlockSpec(memory_space=pl.ANY)
    classes = classes_of("mlp")
    return pl.pallas_call(
        back_kernel,
        name="backward",
        out_shape=[jax.ShapeDtypeStruct((256, 3840), BF16)]
        + [jax.ShapeDtypeStruct((4, 4, n, 128), BF16) for _, _, n in classes],
        in_specs=[vm] * 4 + [anys] * 4,
        out_specs=[vm] + [anys] * 3,
        scratch_shapes=[
            pltpu.VMEM((1280, 512), BF16),
            pltpu.VMEM((2560, 512), BF16),
            pltpu.VMEM((4, 512, 640), BF16),
            pltpu.VMEM((512, 1280), BF16),
            pltpu.VMEM((8, 1280), F32),
            pltpu.VMEM((256, 3840), BF16),
            pltpu.VMEM((2, 1, 4, 256, 128), BF16),
            pltpu.VMEM((4, 256, 128), BF16),
            pltpu.VMEM((4, 256, 128), BF16),
            pltpu.VMEM((5, 1024, 64), BF16),
            pltpu.VMEM((2, 64, 1024), F32),
            pltpu.VMEM((3, 2, 1024, 64), BF16),
            pltpu.VMEM((4, 3, 2, 256, 128), BF16),
            pltpu.VMEM((4, 256, 256), BF16),
            pltpu.VMEM((4, 256, 256), BF16),
            pltpu.SemaphoreType.DMA((BACK_SEMS,)),
            pltpu.SemaphoreType.DMA((BACK_SEMS,)),
            pltpu.SemaphoreType.DMA((4,)),
            pltpu.VMEM((4, 4, 4, slab_rows("mlp"), 128), BF16),
        ]
        + inbox_shapes(classes, (0,)),
        compiler_params=pltpu.CompilerParams(collective_id=1, has_side_effects=True, vmem_limit_bytes=60 << 20),
    )(datt, heads, lse, small, n2t, actt, gp, cot)


def last_kernel(
    n1, gqkv, attt, gb, w_qkv, tokens, grad_mid, small_all, part_0, part_1, part_2,
    out_mlp, out_attn, grad_tokens,
    n1_v, n1t, gqkv_v, attt_v, gb_v, w_v, small_v, ssem, rsem, lsem, acc, acc_small, held_0, held_1, held_2, *inbox,
):
    t = Torus()
    helds = (held_0, held_1, held_2)
    moves = [(n1, n1_v), (attt, attt_v), (gb, gb_v), (w_qkv, w_v)] + [*zip((part_0, part_1, part_2), helds)]
    n1_in, att_in, gb_in, w_in, *parts_in = [
        pltpu.make_async_copy(src, dst, lsem.at[k]) for k, (src, dst) in enumerate(moves)
    ]
    each(parts_in, "start")
    each((n1_in, att_in, gb_in, w_in), "start")
    greet(t.neighbours())
    net = Net(ssem, rsem)
    sib, c = t.sibling(), t.c
    m, a = [], []
    boxes = inboxes(inbox[:15], (1, 2))
    for held, box_of, (order, row, n) in zip(helds, boxes, classes_of("mlp")):
        lane = Lane(net, t, held, "".join(v for v in "xyz" if v != order[0]), box_of, order, 0, n)
        lane.base = row
        m.append(lane)
    boxes = inboxes(inbox[15:], (0, 1, 2))
    for box_of, k in zip(boxes, classes_of("attn")):
        a.append(Lane(net, t, acc, "xyz", box_of, *k))
    tiny = Lane(net, t, acc_small, "xyz", boxes[3], "yzx", 0, SMALL_ROWS)
    tiny.base = 400
    ms = spreads_for("mlp", m, out_mlp, lsem.at[pl.ds(7, 4)])
    sp = spreads_for("attn", a, out_attn, lsem.at[pl.ds(11, 4)])
    ts = Spread(tiny, out_attn, "zy", 400, SMALL_ROWS, lsem.at[15])
    got = {}

    def swap():
        for s in range(3):
            theirs = pl.ds(pl.multiple_of((1 - c) * 1920 + s * 640, 128), 640)
            got[s] = net.send(gqkv.at[:, theirs], gqkv_v.at[s, pl.ds(256, 256)], sib)
        for s in range(3):
            gqkv_v[s, 0:256] = gqkv[:, pl.ds(pl.multiple_of(c * 1920 + s * 640, 128), 640)]

    def turn():
        n1_in.wait()
        n1t[:, 0:256] = n1_v[0].T
        n1t[:, 256:512] = n1_v[1].T

    def qkv(s):
        got[s].wait_recv()

        def body(x, _):
            product(n1t[pl.ds(pl.multiple_of(x * 320, 16), 320), :], gqkv_v[s], acc, "attn", x, s)
            return 0

        lax.fori_loop(0, 4, body, 0)

    def outp():
        att_in.wait()
        gb_in.wait()

        def body(x, _):
            product(attt_v[pl.ds(pl.multiple_of(x * 320, 16), 320), :], gb_v[...], acc, "attn", x, 3)
            return 0

        lax.fori_loop(0, 4, body, 0)

    def rows_back():
        w_in.wait()

        def body(n, total):
            cols = pl.ds(pl.multiple_of(n * 640, 128), 640)
            return total + dot_t(gqkv[:, cols], w_v[:, cols])

        grad = lax.fori_loop(0, 6, body, jnp.zeros((256, 1280), F32))
        hat, scale = norm(tokens[...].astype(F32))
        grad_tokens[...] = (grad_mid[...] + norm_back(grad, hat, scale, whole_vector(small_all, "ln1_gain"))).astype(BF16)
        small_v[0, 0:1, :] = jnp.sum(grad * hat, axis=0, keepdims=True)
        small_v[0, 1:2, :] = jnp.sum(grad, axis=0, keepdims=True)
        small_v[0, 2:3, :] = jnp.sum(gqkv[:, :1280].astype(F32), axis=0, keepdims=True)
        small_v[0, 3:4, :] = jnp.sum(gqkv[:, 2560:].astype(F32), axis=0, keepdims=True)
        got["small"] = net.send(small_v.at[0], small_v.at[1], sib)

    def sums():
        got["small"].wait_recv()
        total = small_v.at[2]
        total[...] = small_v[0] + small_v[1]
        store_small(
            acc_small, 0,
            lambda x: [
                [row for k in range(2) for row in row_pieces(total, k, 320 * x, 320)],
                row_pieces(total, 2 + x // 2, 640 * (x % 2), 640),
            ],
        )

    each(parts_in, "wait")
    m[2].first(1)
    swap()
    m[0].first(1)
    turn()
    m[1].first(1)
    qkv(1)
    m[0].second(1, 0)
    m[0].second(1, 1)
    qkv(2)
    a[1].first(0)
    m[2].second(1, 0)
    m[2].second(1, 1)
    qkv(0)
    a[0].first(0)
    m[1].second(1, 1)
    m[0].third(1)
    m[0].last()
    outp()
    a[1].second(0, 1)
    m[1].second(1, 0)
    m[2].third(1)
    a[1].second(0, 0)
    a[2].first(0)
    rows_back()
    m[0].done()
    m[1].third(1)
    a[0].second(0, 1)
    a[0].second(0, 0)
    m[1].last()
    m[2].last()
    ms[0].start()
    a[2].second(0, 1)
    a[2].second(0, 0)
    a[1].third(0)
    sums()
    tiny.first(0)
    m[2].done()
    ms[3].start()
    a[0].third(0)
    a[0].first(1)
    a[1].first(1)
    tiny.second(0, 0)
    ms[2].start()
    m[1].done()
    ms[1].start()
    a[0].second(1, 1)
    a[2].third(0)
    a[0].second(1, 0)
    a[2].first(1)
    tiny.second(0, 1)
    ms[3].second()
    ms[0].second()
    a[1].second(1, 0)
    a[1].second(1, 1)
    ms[1].second()
    a[0].third(1)
    a[0].last()
    a[1].third(1)
    a[2].second(1, 1)
    a[1].last()
    a[2].second(1, 0)
    tiny.third(0)
    tiny.first(1)
    ms[2].second()
    tiny.second(1, 1)
    a[2].third(1)
    a[0].done()
    a[1].done()
    a[2].last()
    sp[0].start()
    ms[3].third()
    tiny.second(1, 0)
    sp[1].start()
    ms[0].third()
    a[2].done()
    tiny.third(1)
    tiny.last()
    ms[2].third()
    sp[2].start()
    sp[3].start()
    ms[1].third()
    sp[0].second()
    ms[0].share()
    ms[0].finish()
    sp[1].second()
    tiny.done()
    ts.start()
    sp[2].second()
    sp[3].second()
    ms[3].share()
    ms[1].share()
    sp[0].third()
    ts.second()
    sp[1].third()
    sp[2].third()
    ms[2].share()
    ts.third()
    sp[0].share()
    ms[1].finish()
    sp[3].third()
    sp[2].share()
    sp[1].share()
    ts.share()
    ms[3].finish()
    sp[3].share()
    ts.finish()
    ms[2].finish()
    sp[2].finish()
    sp[1].finish()
    sp[3].finish()
    sp[0].finish()
    net.finish()


LAST_SEMS = 200


def last(n1, gqkv, attt, gb, w_qkv, tokens, grad_mid, small_all, parts):
    vm, anys = pl.BlockSpec(memory_space=pltpu.VMEM), pl.BlockSpec(memory_space=pl.ANY)
    mlp_classes, attn_classes = classes_of("mlp"), classes_of("attn")
    return pl.pallas_call(
        last_kernel,
        name="last",
        out_shape=[jax.ShapeDtypeStruct((2, 4, 4, slab_rows(g), 128), BF16) for g in ("mlp", "attn")]
        + [jax.ShapeDtypeStruct((256, 1280), BF16)],
        in_specs=[anys, vm, anys, anys, anys, vm, vm, vm] + [anys] * 3,
        out_specs=[anys] * 2 + [vm],
        scratch_shapes=[
            pltpu.VMEM((2, 256, 1280), BF16),
            pltpu.VMEM((1280, 512), BF16),
            pltpu.VMEM((3, 512, 640), BF16),
            pltpu.VMEM((1280, 512), BF16),
            pltpu.VMEM((512, 640), BF16),
            pltpu.VMEM((1280, 3840), BF16),
            pltpu.VMEM((3, 8, 1280), F32),
            pltpu.SemaphoreType.DMA((LAST_SEMS,)),
            pltpu.SemaphoreType.DMA((LAST_SEMS,)),
            pltpu.SemaphoreType.DMA((16,)),
            pltpu.VMEM((4, 4, 4, 400, 128), BF16),
            pltpu.VMEM((4, 4, 4, SMALL_ROWS, 128), BF16),
        ]
        + [pltpu.VMEM((4, 4, n, 128), BF16) for _, _, n in mlp_classes]
        + inbox_shapes(mlp_classes, (1, 2))
        + inbox_shapes(attn_classes + [("yzx", 0, SMALL_ROWS)], (0, 1, 2)),
        compiler_params=pltpu.CompilerParams(collective_id=2, has_side_effects=True, vmem_limit_bytes=60 << 20),
    )(n1, gqkv, attt, gb, w_qkv, tokens, grad_mid, small_all, *parts)


def flat_block(src, core, group, block):
    pieces = [
        src[core, slab // 4, slab % 4, row : row + n, :] for slab, row, n, _ in pieces_of(group, 320 * block, 320)
    ]
    return jnp.concatenate(pieces, axis=0).astype(F32)


def unpack_kernel(packed_mlp, packed_attn, fc, proj, qkv, out, in_0, in_1, stage, in_sem, out_sem):
    loads = []
    for c in range(2):
        loads.append(
            [
                pltpu.make_async_copy(src.at[c], dst.at[c], in_sem.at[2 * c + k])
                for k, (src, dst) in enumerate(((packed_attn, in_1), (packed_mlp, in_0)))
            ]
        )
        each(loads[-1], "start")
    flying = []
    for c in range(2):
        chunks = [(in_1, "attn", q, qkv, 0, 1920 * c + 640 * q) for q in range(3)]
        chunks += [(in_1, "attn", 3, out, 0, 640 * c)]
        chunks += [(in_0, "mlp", q, fc, 0, 1280 * q + 640 * c) for q in range(4)]
        chunks += [(in_0, "mlp", 4 + 2 * sub + h, proj, 640 * c + 320 * sub, 640 * h) for sub in range(2) for h in range(2)]
        for n, (src, group, q, dst, row, col) in enumerate(chunks):
            if n in (0, 4):
                loads[c][n // 4].wait()
            k = len(flying)
            slot = k % STAGES
            if k >= STAGES:
                flying[k - STAGES].wait()
            for t in range(5):
                stage[slot, :, 128 * t : 128 * (t + 1)] = flat_block(src, c, group, 5 * q + t)
            copy = pltpu.make_async_copy(stage.at[slot], dst.at[pl.ds(row, 320), pl.ds(col, 640)], out_sem.at[slot])
            copy.start()
            flying.append(copy)
    for copy in flying[-STAGES:]:
        copy.wait()


STAGES = 8


def unpack(packed_mlp, packed_attn):
    anys = pl.BlockSpec(memory_space=pl.ANY)
    return pl.pallas_call(
        unpack_kernel,
        name="unpack",
        out_shape=[jax.ShapeDtypeStruct(s, F32) for s in ((320, 5120), (1280, 1280), (320, 3840), (320, 1280))],
        in_specs=[anys] * 2,
        out_specs=[anys] * 4,
        scratch_shapes=[
            pltpu.VMEM(packed_mlp.shape, BF16),
            pltpu.VMEM(packed_attn.shape, BF16),
            pltpu.VMEM((STAGES, 320, 640), F32),
            pltpu.SemaphoreType.DMA((4,)),
            pltpu.SemaphoreType.DMA((STAGES,)),
        ],
        compiler_params=pltpu.CompilerParams(vmem_limit_bytes=48 << 20),
    )(packed_mlp, packed_attn)


def small_row(packed, rows, slab, row, n):
    return packed[0, 0, slab, rows + row : rows + row + -(-n // 128), :].astype(F32).reshape(-1)[:n]


def shards(
    tokens,
    cotangent,
    ln1_gain,
    ln1_bias,
    w_qkv,
    qv_bias,
    w_out,
    out_bias,
    ln2_gain,
    ln2_bias,
    w_fc,
    fc_bias,
    w_proj,
    proj_bias,
):
    own = (ln1_gain, ln1_bias, qv_bias, out_bias, ln2_gain, ln2_bias, proj_bias, fc_bias)
    small = jnp.stack([jnp.pad(v.astype(F32), (0, 1280 - v.shape[0])) for v in own])
    f_qkv, f_out, f_fc, f_proj, f_small, normed_one, attended, heads, lse = front(
        tokens[0], small, w_qkv, w_out, w_fc, w_proj
    )
    f_qkv, f_out, f_fc, f_proj = (
        f_qkv.reshape(1280, 3840),
        f_out.reshape(1280, 1280),
        f_fc.reshape(1280, 5120),
        f_proj.reshape(5120, 1280),
    )
    block_out, grad_middle, grad_attended, n2t, attt, cot, actt, grad_pre, grad_branch, small_mlp = mlp(
        tokens[0], attended, cotangent[0], f_small, f_out, f_fc, f_proj
    )
    grad_qkv, *parts = backward(grad_attended, heads, lse, small_mlp, n2t, actt, grad_pre, cot)
    packed_mlp, packed_attn, grad_tokens = last(
        normed_one, grad_qkv, attt, grad_branch, f_qkv, tokens[0], grad_middle, f_small, parts
    )
    g_fc, g_proj, g_qkv, g_out = unpack(packed_mlp, packed_attn)
    return (
        block_out[None],
        grad_tokens[None],
        small_row(packed_attn, 400, 0, 0, 320),
        small_row(packed_attn, 400, 0, 3, 320),
        g_qkv,
        small_row(packed_attn, 400, 1, 0, 640),
        g_out,
        small_row(packed_mlp, 800, 0, 9, 320),
        small_row(packed_mlp, 800, 0, 0, 320),
        small_row(packed_mlp, 800, 0, 3, 320),
        g_fc,
        small_row(packed_mlp, 800, 1, 0, 1280),
        g_proj,
        small_row(packed_mlp, 800, 0, 6, 320),
    )


def solution(mesh):
    vector, matrix, batch = P("shard"), P("shard", None), P("rep", "shard", None)
    placed = (batch, batch, vector, vector, matrix, vector, matrix, vector, vector, vector, matrix, vector, matrix, vector)
    return jax.shard_map(shards, mesh=mesh, in_specs=placed, out_specs=placed, check_vma=False)
```

```python
import jax
import jax.numpy as jnp
from jax import lax
from jax.experimental import pallas as pl
from jax.experimental.pallas import tpu as pltpu
from jax.sharding import PartitionSpec as P

MESH = pl.DeviceIdType.MESH
F32, BF16 = jnp.float32, jnp.bfloat16


def where_am_i():
    rep = lax.axis_index("rep")
    return lax.axis_index("shard"), (rep // 2) % 4, rep // 8, rep % 2


def device_at(x, y, z, c):
    return {"rep": (z * 4 + y) * 2 + c, "shard": x}


def wrap(v):
    return lax.rem(v + 4, 4)


class Net:
    def __init__(self, send_sems, recv_sems):
        self.send_sems, self.recv_sems, self.used = send_sems, recv_sems, 0
        self.all = []

    def send(self, src, dst, target):
        copy = pltpu.make_async_remote_copy(
            src_ref=src, dst_ref=dst,
            send_sem=self.send_sems.at[self.used], recv_sem=self.recv_sems.at[self.used],
            device_id=target, device_id_type=MESH,
        )
        copy.start()
        self.used += 1
        self.all.append(copy)
        return copy

    def finish(self):
        for copy in self.all:
            copy.wait_send()


def wait_all(copies):
    for copy in copies:
        copy.wait_recv()


def each(items, what, *rest):
    for item in items:
        getattr(item, what)(*rest)


class Greeting:
    def __init__(self, targets):
        self.barrier, self.count = pltpu.get_barrier_semaphore(), len(targets)
        for target in targets:
            pl.semaphore_signal(self.barrier, 1, device_id=target, device_id_type=MESH)

    def wait(self):
        pl.semaphore_wait(self.barrier, self.count)


class Torus:
    def __init__(self):
        self.x, self.y, self.z, self.c = where_am_i()

    def at(self, axis, step):
        x, y, z = self.x, self.y, self.z
        if axis == "x":
            x = wrap(x + step)
        elif axis == "y":
            y = wrap(y + step)
        else:
            z = wrap(z + step)
        return device_at(x, y, z, self.c)

    def pos(self, axis):
        return {"x": self.x, "y": self.y, "z": self.z}[axis]

    def sibling(self):
        return device_at(self.x, self.y, self.z, 1 - self.c)

    def neighbours(self, axes="xyz", core=True):
        out = [self.at(a, s) for a in axes for s in (1, 2, 3)]
        return out + ([self.sibling()] if core else [])


PLANS = {
    "qkv": (320, 3840, 4, 8, 3),
    "out": (320, 1280, 4, 0, 1),
    "fc": (320, 5120, 8, 8, 4),
    "proj": (1280, 1280, 2, 2, 1),
}


def rect_of(rows, start, width, order, y, z, stage):
    if rows == 320:
        if stage == 0:
            return y * 80, 80, start + z * (width // 4), width // 4
        if order == "yz":
            return 0, 320, start + z * (width // 4), width // 4
        return y * 80, 80, start, width
    first, second = (y, z) if order == "yz" else (z, y)
    if stage == 0:
        return second * 320 + first * 80, 80, start, width
    return second * 320, 320, start, width


def part(ref, owner, rect):
    r, nr, c, nc = rect
    return ref.at[owner, pl.ds(pl.multiple_of(r, 16), nr), pl.ds(pl.multiple_of(c, 128), nc)]


def own_part(ref, rect):
    r, nr, c, nc = rect
    return ref.at[pl.ds(pl.multiple_of(r, 16), nr), pl.ds(pl.multiple_of(c, 128), nc)]


class Gather:
    def __init__(self, net, torus, name, src, full, lean):
        self.net, self.t, self.src, self.full, self.lean = net, torus, src, full, lean
        self.rows, cols, a, b, d = PLANS[name]
        half = torus.c * (cols // 2)
        self.regions = []
        at = 0
        for order, tiles in (("yz", a), ("zy", b)):
            if tiles:
                self.regions.append((order, half + at * 128, tiles * 128))
            at += tiles
        self.alone = (half + at * 128, d * 128)
        self.others = [wrap(torus.x + k) for k in (1, 2, 3)]
        self.got = {"core": []}

    def rect(self, region, stage, shift=0):
        order, start, width = region
        y, z = self.t.y, self.t.z
        axis = order[stage]
        if axis == "y":
            y = wrap(y + shift)
        else:
            z = wrap(z + shift)
        return rect_of(self.rows, start, width, order, y, z, stage)

    def both(self, what, *rest):
        for i in range(len(self.regions)):
            getattr(self, what)(i, *rest)

    def start(self):
        t, net = self.t, self.net
        for i, region in enumerate(self.regions):
            rect = self.rect(region, 0)
            self.got[i, "x"] = [
                net.send(own_part(self.src, rect), part(self.full, t.x, rect), t.at("x", s)) for s in (1, 3, 2)
            ]

    def start_alone(self):
        t, net = self.t, self.net
        rect = (0, self.rows, *self.alone)
        self.got["alone"] = [
            net.send(own_part(self.src, rect), part(self.full, t.x, rect), t.at("x", s)) for s in (1, 3)
        ]

    def alone_on(self):
        t, net = self.t, self.net
        h = self.rows // 2
        one, two = self.got["alone"]
        start, width = self.alone
        whole = (0, self.rows, start, width)
        one.wait_recv()
        left = wrap(t.x - 1)
        rect = (0, h, start, width)
        a = net.send(part(self.full, left, rect), part(self.full, left, rect), t.at("x", 1))
        two.wait_recv()
        right = wrap(t.x + 1)
        rect = (h, h, start, width)
        b = net.send(part(self.full, right, rect), part(self.full, right, rect), t.at("x", 3))
        self.got["alone2"] = [a, b]
        self.got["core"] += [
            net.send(part(self.full, o, whole), part(self.full, o, whole), t.sibling()) for o in (left, right)
        ]

    def alone_end(self):
        wait_all(self.got["alone2"])

    def alone_share(self):
        o = wrap(self.t.x + 2)
        whole = (0, self.rows, *self.alone)
        self.got["core"].append(self.net.send(part(self.full, o, whole), part(self.full, o, whole), self.t.sibling()))

    def spread(self, i):
        region = self.regions[i]
        wait_all(self.got[i, "x"])
        rect = self.rect(region, 0)
        self.got[i, 0] = [
            self.net.send(part(self.full, o, rect), part(self.full, o, rect), self.t.at(region[0][0], s))
            for s in (1, 3, 2)
            for o in self.others
        ]

    def widen(self, i):
        region = self.regions[i]
        wait_all(self.got[i, 0])
        rect = self.rect(region, 1)
        self.got[i, 1] = [
            [self.net.send(part(self.full, o, rect), part(self.full, o, rect), self.t.at(region[0][1], s)) for o in self.others]
            for s in (1, 3)
        ]

    def pass_on(self, i):
        region = self.regions[i]
        axis = region[0][1]
        cut = 2 if self.lean else 1
        ahead, behind = self.got[i, 1]
        sent = []
        for copies, shift, to, owners in (
            (ahead, -1, 1, self.others[:cut]),
            (behind, 1, 3, self.others[cut:]),
        ):
            wait_all(copies)
            rect = self.rect(region, 1, shift)
            for o in owners:
                sent.append(self.net.send(part(self.full, o, rect), part(self.full, o, rect), self.t.at(axis, to)))
        self.got[i, 2] = sent

    def to_sibling(self, region, shifts):
        for shift in shifts:
            rect = self.rect(region, 1, shift)
            for o in self.others:
                self.got["core"].append(
                    self.net.send(part(self.full, o, rect), part(self.full, o, rect), self.t.sibling())
                )

    def share(self, i):
        self.to_sibling(self.regions[i], (0, -1, 1))

    def arrive(self, i):
        wait_all(self.got[i, 2])

    def share_last(self, i):
        self.to_sibling(self.regions[i], (2,))

    def finish(self):
        wait_all(self.got["core"])


LAG = 0.5


def dot_t(a, b):
    return lax.dot_general(a, b, (((1,), (1,)), ((), ())), preferred_element_type=F32)


def causal(s, i):
    rows = lax.broadcasted_iota(jnp.int32, (256, 256), 0)
    cols = lax.broadcasted_iota(jnp.int32, (256, 256), 1)
    last = jnp.where(cols <= rows, s[:, 256 * i :], -1e30)
    return last if i == 0 else jnp.concatenate([s[:, : 256 * i], last], axis=1)


class Swap:
    def __init__(self, net, torus, parts):
        self.net, self.t, self.parts = net, torus, parts

    def pack_single(self, full, single):
        parts = self.parts
        for d in range(4):
            cols = [full[:, 1280 * k + 1024 + 64 * d : 1280 * k + 1088 + 64 * d] for k in range(parts)]
            if parts % 2:
                cols.append(jnp.zeros((256, 64), BF16))
            single[d] = jnp.concatenate(cols, axis=1)

    def out_pairs(self, full, box):
        t, net, got = self.t, self.net, []
        for p in range(2):
            sent = []
            for s in (1, 3, 2):
                d = wrap(t.x + s)
                for k in range(self.parts):
                    cols = pl.ds(pl.multiple_of(1280 * k + 256 * d + 128 * p, 128), 128)
                    sent.append(net.send(full.at[:, cols], box.at[p, k, t.x], t.at("x", s)))
            got.append(sent)
        return got

    def keep_pairs(self, full, box):
        for p in range(2):
            for k in range(self.parts):
                cols = pl.ds(pl.multiple_of(1280 * k + 256 * self.t.x + 128 * p, 128), 128)
                box[p, k, self.t.x] = full[:, cols]

    def out_single(self, single, box):
        t = self.t
        sent = [self.net.send(single.at[wrap(t.x + s)], box.at[t.x], t.at("x", s)) for s in (1, 3, 2)]
        return sent

    def back_pair(self, p, src, full):
        t, net, sent = self.t, self.net, []
        for s in (1, 3, 2):
            d = wrap(t.x + s)
            for k in range(self.parts):
                cols = pl.ds(pl.multiple_of(1280 * k + 256 * t.x + 128 * p, 128), 128)
                sent.append(net.send(src.at[d, k, p], full.at[:, cols], t.at("x", s)))
        return sent

    def keep_back(self, p, src, full):
        for k in range(self.parts):
            cols = pl.ds(pl.multiple_of(1280 * k + 256 * self.t.x + 128 * p, 128), 128)
            full[:, cols] = src[self.t.x, k, p]

    def unpack_single(self, box, full):
        for k in range(self.parts):
            cols = [box[d, :, 64 * k : 64 * k + 64] for d in range(4)]
            full[:, 1280 * k + 1024 : 1280 * (k + 1)] = jnp.concatenate(cols, axis=1)


EPS = 1e-05
VECTORS = ("ln1_gain", "ln1_bias", "qv_bias", "out_bias", "ln2_gain", "ln2_bias", "proj_bias", "fc_bias")
SIZES = (320, 320, 640, 320, 320, 320, 320, 1280)


def whole_vector(small, name):
    k = VECTORS.index(name)
    return jnp.concatenate([small[x, k : k + 1, : SIZES[k]] for x in range(4)], axis=1)


def dot(a, b):
    return jnp.dot(a, b, preferred_element_type=F32)


def norm(v):
    center = v - jnp.mean(v, axis=-1, keepdims=True)
    scale = lax.rsqrt(jnp.mean(center * center, axis=-1, keepdims=True) + EPS)
    return center * scale, scale


def norm_back(grad, hat, scale, gain):
    inner = grad * gain
    return scale * (
        inner - jnp.mean(inner, axis=-1, keepdims=True) - hat * jnp.mean(inner * hat, axis=-1, keepdims=True)
    )


class Forward:
    def __init__(self, net, torus, qkv, full, heads, lse, box, single, single_in, outs, res, res_single, res_single_in):
        self.net, self.t, self.qkv, self.full, self.heads, self.lse = net, torus, qkv, full, heads, lse
        self.box, self.single, self.single_in, self.outs = box, single, single_in, outs
        self.res, self.res_single, self.res_single_in = res, res_single, res_single_in
        self.swap, self.back = Swap(net, torus, 3), Swap(net, torus, 1)
        self.sent = []

    def start(self):
        t, swap = self.t, self.swap
        self.got = swap.out_pairs(self.qkv, self.box)
        swap.pack_single(self.qkv, self.single)
        self.got_single = swap.out_single(self.single, self.single_in)
        swap.keep_pairs(self.qkv, self.box)
        self.single_in[t.x] = self.single[t.x]
        self.lse[...] = jnp.zeros_like(self.lse)

    def take(self, p):
        heads = self.heads
        if p < 2:
            wait_all(self.got[p])
            for k in range(3):
                for s in range(4):
                    for j in range(2):
                        v = self.box[p, k, s, :, 64 * j : 64 * j + 64]
                        heads[k, 2 * p + j, 256 * s : 256 * (s + 1), :] = v * BF16(0.125) if k == 0 else v
            return
        wait_all(self.got_single)
        for k in range(3):
            for s in range(4):
                v = self.single_in[s, :, 64 * k : 64 * k + 64]
                heads[k, 4, 256 * s : 256 * (s + 1), :] = v * BF16(0.125) if k == 0 else v

    def head(self, h, j):
        heads, lse = self.heads, self.lse
        lane = lax.broadcasted_iota(jnp.int32, (256, 128), 1)
        for i in range(4):
            rows = slice(256 * i, 256 * (i + 1))
            n = 256 * (i + 1)
            s = causal(dot_t(heads[0, h, rows, :], heads[1, h, :n, :]), i)
            top = jnp.max(s, axis=1, keepdims=True)
            p = jnp.exp(s - top)
            total = jnp.sum(p, axis=1, keepdims=True)
            lse[rows, :] = jnp.where(lane == h, top + jnp.log(total), lse[rows, :])
            o = dot(p.astype(BF16), heads[2, h, :n, :])
            self.outs[j, rows, :] = (o / total).astype(BF16)

    def give(self, p):
        back, outs = self.back, self.outs
        for i in range(4):
            rows = slice(256 * i, 256 * (i + 1))
            if p < 2:
                self.res[i, 0, p] = jnp.concatenate([outs[0, rows, :], outs[1, rows, :]], axis=1)
            else:
                self.res_single[i] = jnp.concatenate([outs[0, rows, :], jnp.zeros((256, 64), BF16)], axis=1)
        if p < 2:
            self.sent += back.back_pair(p, self.res, self.full)
            back.keep_back(p, self.res, self.full)
        else:
            self.sent_single = back.out_single(self.res_single, self.res_single_in)
            self.res_single_in[self.t.x] = self.res_single[self.t.x]

    def finish(self):
        wait_all(self.sent_single)
        self.back.unpack_single(self.res_single_in, self.full)
        wait_all(self.sent)


def front_kernel(
    tokens, v_0, v_1, v_2, v_3, v_4, v_5, v_6, v_7, w_qkv, w_out, w_fc, w_proj,
    f_qkv, f_out, f_fc, f_proj, f_small, r_normed, att, r_heads, r_lse,
    normed, heads, lse, tok_v, small, u_0, u_1, u_2, u_3, u_4, u_5, u_6, u_7, v_qkv, h_out, h_fc, h_proj, small_all, bias, qkv, other, full,
    box, single, single_in, outs, res, res_single, res_single_in, ssem, rsem, lsem, vsem,
):
    t = Torus()
    vectors = ((v_0, u_0), (v_1, u_1), (v_2, u_2), (v_3, u_3), (v_4, u_4), (v_5, u_5), (v_6, u_6), (v_7, u_7))
    loads = [pltpu.make_async_copy(src, dst, vsem.at[k]) for k, (src, dst) in enumerate(((tokens, tok_v),) + vectors)]
    greeting = Greeting(t.neighbours())
    each(loads, "start")
    small[...] = jnp.zeros_like(small)
    each(loads, "wait")
    for k, (_, vector) in enumerate(vectors):
        small[k : k + 1, 0 : SIZES[k]] = vector[...].astype(F32).reshape(1, SIZES[k])
    net = Net(ssem, rsem)
    sib, c = t.sibling(), t.c
    q = Gather(net, t, "qkv", w_qkv, v_qkv, 0)
    o = Gather(net, t, "out", w_out, f_out, 1)
    f = Gather(net, t, "fc", w_fc, f_fc, 0)
    p = Gather(net, t, "proj", w_proj, f_proj, 1)
    fwd = Forward(net, t, qkv, full, heads, lse, box, single, single_in, outs, res, res_single, res_single_in)
    own = pltpu.make_async_copy(w_qkv, v_qkv.at[t.x], lsem.at[0])
    own.start()
    held = [(w_out, h_out, f_out), (w_fc, h_fc, f_fc), (w_proj, h_proj, f_proj)]
    local = [pltpu.make_async_copy(s, h, lsem.at[1 + k]) for k, (s, h, _) in enumerate(held)]
    each(local, "start")
    sent = []
    greeting.wait()

    def columns(region):
        start, width = region
        cols = pl.ds(pl.multiple_of(start, 128), width)
        made = dot(normed[...].reshape(512, 1280), v_qkv[:, :, cols].reshape(1280, width)) + bias[0:1, cols]
        made = made.astype(BF16)
        qkv[:, cols] = made[:256]
        other[:, cols] = made[256:]
        sent.append(net.send(other.at[:, cols], qkv.at[:, cols], sib))

    q.start()
    p.start()
    smalls = [net.send(small, small_all.at[t.x], t.at("x", s)) for s in (1, 3, 2)]
    small_all[t.x] = small[...]
    o.start()
    q.start_alone()
    q.spread(0)
    o.start_alone()
    q.spread(1)
    p.spread(0)
    q.widen(0)
    f.start()
    q.widen(1)
    wait_all(smalls)
    hat, _ = norm(tok_v[...].astype(F32))
    gain, shift = whole_vector(small_all, "ln1_gain"), whole_vector(small_all, "ln1_bias")
    normed[0] = (hat * gain + shift).astype(BF16)
    swapped = net.send(normed.at[0], normed.at[1], sib)
    p.spread(1)
    o.alone_on()
    q.alone_on()
    for n, (_, h, full_w) in enumerate(held):
        local[n].wait()
        local[n] = pltpu.make_async_copy(h, full_w.at[t.x], lsem.at[1 + n])
        local[n].start()
    p.widen(0)
    p.start_alone()
    f.start_alone()
    o.spread(0)
    q.alone_end()
    q.pass_on(1)
    f.spread(0)
    q.pass_on(0)
    o.widen(0)
    f.spread(1)
    q.share(0)
    p.widen(1)
    k = VECTORS.index("qv_bias")
    for n in (0, 1, 4, 5):
        row = small_all[n if n < 2 else n - 2, k : k + 1, :640]
        bias[0:1, 640 * n : 640 * (n + 1)] = row
    bias[0:1, 1280:2560] = jnp.zeros((1, 1280), F32)
    f_small[...] = small_all[...]
    swapped.wait_recv()
    q.share(1)
    p.alone_on()
    o.alone_end()
    q.arrive(1)
    own.wait()
    columns(q.regions[1][1:])
    columns(q.alone)
    q.arrive(0)
    q.alone_share()
    f.alone_on()
    columns(q.regions[0][1:])
    f.widen(0)
    o.pass_on(0)
    p.alone_end()
    q.share_last(1)
    wait_all(sent)
    fwd.start()
    f.widen(1)
    q.share_last(0)
    fwd.take(0)
    p.pass_on(0)
    p.pass_on(1)
    p.share(0)
    fwd.head(0, 0)
    p.alone_share()
    o.share(0)
    f.pass_on(0)
    fwd.head(1, 1)
    o.arrive(0)
    o.alone_share()
    o.share_last(0)
    fwd.give(0)
    q.finish()
    p.share(1)
    keep = pltpu.make_async_copy(v_qkv, f_qkv, lsem.at[0])
    keep.start()
    f.pass_on(1)
    f.share(1)
    fwd.take(1)
    f.alone_end()
    f.alone_share()
    f.share(0)
    fwd.head(2, 0)
    fwd.head(3, 1)
    fwd.give(1)
    fwd.take(2)
    fwd.head(4, 0)
    done = [
        pltpu.make_async_copy(src, dst, vsem.at[k])
        for k, (src, dst) in enumerate(((normed, r_normed), (heads, r_heads), (lse, r_lse)))
    ]
    each(done, "start")
    f.arrive(0)
    p.arrive(0)
    f.share_last(0)
    fwd.give(2)
    p.arrive(1)
    p.share_last(0)
    f.arrive(1)
    f.share_last(1)
    o.finish()
    p.share_last(1)
    f.finish()
    p.finish()
    fwd.finish()
    done.append(pltpu.make_async_copy(full, att, vsem.at[3]))
    done[-1].start()
    keep.wait()
    each(local + done, "wait")
    net.finish()


FRONT_SEMS = 340


def front(tokens, vectors, w_qkv, w_out, w_fc, w_proj):
    vm, anys = pl.BlockSpec(memory_space=pltpu.VMEM), pl.BlockSpec(memory_space=pl.ANY)
    weights = (w_qkv, w_out, w_fc, w_proj)
    return pl.pallas_call(
        front_kernel,
        name="front",
        out_shape=[jax.ShapeDtypeStruct((4,) + w.shape, BF16) for w in weights]
        + [
            jax.ShapeDtypeStruct((4, 8, 1280), F32),
            jax.ShapeDtypeStruct((2, 256, 1280), BF16),
            jax.ShapeDtypeStruct((256, 1280), BF16),
            jax.ShapeDtypeStruct((3, 5, 1024, 64), BF16),
            jax.ShapeDtypeStruct((1024, 128), F32),
        ],
        in_specs=[anys] * 13,
        out_specs=[anys] * 4 + [vm] + [anys] * 4,
        scratch_shapes=[
            pltpu.VMEM((2, 256, 1280), BF16),
            pltpu.VMEM((3, 5, 1024, 64), BF16),
            pltpu.VMEM((1024, 128), F32),
            pltpu.VMEM((256, 1280), BF16),
            pltpu.VMEM((8, 1280), F32),
        ]
        + [pltpu.VMEM((n,), BF16) for n in SIZES]
        + [
            pltpu.VMEM((4, 320, 3840), BF16),
            pltpu.VMEM((320, 1280), BF16),
            pltpu.VMEM((320, 5120), BF16),
            pltpu.VMEM((1280, 1280), BF16),
            pltpu.VMEM((4, 8, 1280), F32),
            pltpu.VMEM((8, 3840), F32),
            pltpu.VMEM((256, 3840), BF16),
            pltpu.VMEM((256, 3840), BF16),
            pltpu.VMEM((256, 1280), BF16),
            pltpu.VMEM((2, 3, 4, 256, 128), BF16),
            pltpu.VMEM((4, 256, 256), BF16),
            pltpu.VMEM((4, 256, 256), BF16),
            pltpu.VMEM((2, 1024, 64), BF16),
            pltpu.VMEM((4, 1, 2, 256, 128), BF16),
            pltpu.VMEM((4, 256, 128), BF16),
            pltpu.VMEM((4, 256, 128), BF16),
            pltpu.SemaphoreType.DMA((FRONT_SEMS,)),
            pltpu.SemaphoreType.DMA((FRONT_SEMS,)),
            pltpu.SemaphoreType.DMA((4,)),
            pltpu.SemaphoreType.DMA((9,)),
        ],
        compiler_params=pltpu.CompilerParams(collective_id=0, has_side_effects=True, vmem_limit_bytes=56 << 20),
    )(tokens, *vectors, *weights)


GELU_A, GELU_B = 0.7978845608028654, 0.044715
FF_STEP = 640
FF_STEPS = 8
AHEAD = 2


def mlp_kernel(
    tokens, att, cot, small, w_out, w_fc, w_proj,
    block_out, grad_mid, datt, n2t_c, attt_c, cot_c, actt_c, gp_c, gb_c, small_c,
    tok_v, att_v, cot_v, small_v, wo_v, wf_v, wp_v, n2, middle, out_acc, grad_acc, bias, sums, n2t, attt, actt, gp, gb,
    datt_v, block_v, small_grad, isem, fsem, psem, ssem, rsem, lsem,
):
    t = Torus()
    sib, c = t.sibling(), t.c
    low, high = pl.ds(0, 256), pl.ds(256, 256)
    moves = ((att, att_v), (w_out, wo_v), (tokens, tok_v), (small, small_v), (cot, cot_v))
    loads = [pltpu.make_async_copy(src, dst, isem.at[k]) for k, (src, dst) in enumerate(moves)]
    each(loads, "start")

    def load(j):
        cols = pl.ds(pl.multiple_of(j * FF_STEP, 128), FF_STEP)
        return (
            pltpu.make_async_copy(w_fc.at[:, cols], wf_v.at[j], fsem.at[j]),
            pltpu.make_async_copy(w_proj.at[cols], wp_v.at[j], psem.at[j]),
        )

    for j in range(AHEAD):
        each(load(j), "start")
    greeting = Greeting([sib])

    def keep(k, src, dst):
        return pltpu.make_async_copy(src, dst, lsem.at[k])

    def give(k, src, dst):
        return pltpu.make_async_remote_copy(
            src_ref=src, dst_ref=dst, send_sem=ssem.at[k], recv_sem=rsem.at[k], device_id=sib, device_id_type=MESH
        )

    half = [pl.ds(pl.multiple_of(k * 640, 128), 640) for k in (c, 1 - c)]
    whole = [
        (keep(0, n2t, n2t_c.at[:, low]), give(0, n2t, n2t_c.at[:, high])),
        (keep(1, attt, attt_c.at[:, low]), give(1, attt, attt_c.at[:, high])),
        (keep(2, cot_v, cot_c.at[low]), give(2, cot_v, cot_c.at[high])),
        (keep(3, gb.at[:, half[0]], gb_c.at[low]), give(3, gb.at[:, half[1]], gb_c.at[high])),
        (keep(4, small_grad, small_c.at[0]), give(4, small_grad, small_c.at[1])),
    ]

    def strip(s, kept):
        n = 2 * s + (c if kept else 1 - c)
        rows = pl.ds(pl.multiple_of(s * 640, 16), 640)
        if kept:
            return [
                keep(5 + s, actt.at[n], actt_c.at[rows, low]),
                keep(9 + s, gp.at[n], gp_c.at[s, low]),
            ]
        return [
            give(5 + s, actt.at[n], actt_c.at[rows, high]),
            give(9 + s, gp.at[n], gp_c.at[s, high]),
        ]

    each(loads[:4], "wait")
    mid = tok_v[...].astype(F32) + dot(att_v[...], wo_v[...]) + whole_vector(small_v, "out_bias")
    middle[...] = mid
    hat, _ = norm(mid)
    n2[...] = (hat * whole_vector(small_v, "ln2_gain") + whole_vector(small_v, "ln2_bias")).astype(BF16)
    out_acc[...] = mid + whole_vector(small_v, "proj_bias")
    grad_acc[...] = jnp.zeros_like(grad_acc)
    k = VECTORS.index("fc_bias")
    for n in range(FF_STEPS):
        bias[n, 0:1, :] = small_v[n // 2, k : k + 1, 640 * (n % 2) : 640 * (n % 2 + 1)]
    greeting.wait()
    loads[4].wait()
    each(whole[2], "start")
    n2t[...] = n2[...].T
    each(whole[0], "start")

    def chunk(j, _):
        @pl.when(j + AHEAD < FF_STEPS)
        def _():
            each(load(j + AHEAD), "start")

        each(load(j), "wait")
        pre = dot(n2[...], wf_v[j]) + bias[j, 0:1, :]
        square = pre * pre
        bend = jnp.tanh(GELU_A * (pre + GELU_B * pre * square))
        act = (0.5 * pre * (1.0 + bend)).astype(BF16)
        actt[j] = act.T
        out_acc[...] += dot(act, wp_v[j])
        slope = 0.5 * (1.0 + bend) + (0.5 * GELU_A) * pre * (1.0 - bend * bend) * (1.0 + 3.0 * GELU_B * square)
        grad = (dot_t(cot_v[...], wp_v[j]) * slope).astype(BF16)
        gp[j] = grad
        grad_acc[...] += dot_t(grad, wf_v[j])
        sums[j, 0:1, :] = jnp.sum(grad.astype(F32), axis=0, keepdims=True)

        @pl.when(lax.rem(j, 2) == c)
        def _():
            each(strip(j // 2, True), "start")

        @pl.when(lax.rem(j, 2) != c)
        def _():
            each(strip(j // 2, False), "start")

        return 0

    lax.fori_loop(0, FF_STEPS, chunk, 0)
    hat, scale = norm(middle[...])
    g = grad_acc[...]
    cot_rows = cot_v[...].astype(F32)
    mid = cot_rows + norm_back(g, hat, scale, whole_vector(small_v, "ln2_gain"))
    branch = mid.astype(BF16)
    gb[...] = branch
    each(whole[3], "start")
    small_grad[0:1, :] = jnp.sum(g * hat, axis=0, keepdims=True)
    small_grad[1:2, :] = jnp.sum(g, axis=0, keepdims=True)
    small_grad[2:3, :] = jnp.sum(cot_rows, axis=0, keepdims=True)
    small_grad[3:4, :] = jnp.sum(branch.astype(F32), axis=0, keepdims=True)
    for n in range(FF_STEPS):
        small_grad[4 + n // 2 : 5 + n // 2, 640 * (n % 2) : 640 * (n % 2 + 1)] = sums[n, 0:1, :]
    each(whole[4], "start")
    middle[...] = mid
    block_v[...] = out_acc[...].astype(BF16)
    results = [keep(13, middle, grad_mid), keep(14, block_v, block_out)]
    each(results, "start")
    attt[...] = att_v[...].T
    each(whole[1], "start")
    datt_v[...] = dot_t(branch, wo_v[...]).astype(BF16)
    results.append(keep(15, datt_v, datt))
    results[-1].start()
    for own, other in whole:
        own.wait()
        other.wait()
    for s in range(4):
        each(strip(s, True) + strip(s, False), "wait")
    each(results, "wait")


def mlp(tokens, att, cot, small, w_out, w_fc, w_proj):
    anys = pl.BlockSpec(memory_space=pl.ANY)
    return pl.pallas_call(
        mlp_kernel,
        name="mlp",
        out_shape=[
            jax.ShapeDtypeStruct((256, 1280), BF16),
            jax.ShapeDtypeStruct((256, 1280), F32),
            jax.ShapeDtypeStruct((256, 1280), BF16),
            jax.ShapeDtypeStruct((1280, 512), BF16),
            jax.ShapeDtypeStruct((1280, 512), BF16),
            jax.ShapeDtypeStruct((512, 1280), BF16),
            jax.ShapeDtypeStruct((2560, 512), BF16),
            jax.ShapeDtypeStruct((4, 512, 640), BF16),
            jax.ShapeDtypeStruct((512, 640), BF16),
            jax.ShapeDtypeStruct((2, 8, 1280), F32),
        ],
        in_specs=[anys] * 7,
        out_specs=[anys] * 10,
        scratch_shapes=[pltpu.VMEM((256, 1280), BF16)] * 3
        + [
            pltpu.VMEM((4, 8, 1280), F32),
            pltpu.VMEM((1280, 1280), BF16),
            pltpu.VMEM((FF_STEPS, 1280, FF_STEP), BF16),
            pltpu.VMEM((FF_STEPS, FF_STEP, 1280), BF16),
            pltpu.VMEM((256, 1280), BF16),
            pltpu.VMEM((256, 1280), F32),
            pltpu.VMEM((256, 1280), F32),
            pltpu.VMEM((256, 1280), F32),
            pltpu.VMEM((FF_STEPS, 8, FF_STEP), F32),
            pltpu.VMEM((FF_STEPS, 8, FF_STEP), F32),
            pltpu.VMEM((1280, 256), BF16),
            pltpu.VMEM((1280, 256), BF16),
            pltpu.VMEM((FF_STEPS, FF_STEP, 256), BF16),
            pltpu.VMEM((FF_STEPS, 256, FF_STEP), BF16),
            pltpu.VMEM((256, 1280), BF16),
            pltpu.VMEM((256, 1280), BF16),
            pltpu.VMEM((256, 1280), BF16),
            pltpu.VMEM((8, 1280), F32),
            pltpu.SemaphoreType.DMA((5,)),
            pltpu.SemaphoreType.DMA((FF_STEPS,)),
            pltpu.SemaphoreType.DMA((FF_STEPS,)),
            pltpu.SemaphoreType.DMA((13,)),
            pltpu.SemaphoreType.DMA((13,)),
            pltpu.SemaphoreType.DMA((16,)),
        ],
        compiler_params=pltpu.CompilerParams(collective_id=3, has_side_effects=True, vmem_limit_bytes=60 << 20),
    )(tokens, att, cot, small, w_out, w_fc, w_proj)


def view(ref, axes, chosen, rows):
    return ref.at[tuple(chosen.get(a, slice(None)) for a in axes) + (pl.ds(*rows),)]


def leading(ref):
    return ref.shape[:-2]


def add_into(dst, *srcs):
    lead = leading(dst)
    count = 1
    for n in lead:
        count *= n

    def slab(i):
        index = []
        for n in reversed(lead):
            index.append(lax.rem(i, n))
            i = i // n
        return tuple(reversed(index))

    def body(i, _):
        at = slab(i)
        total = dst[at].astype(F32)
        for s in srcs:
            total = total + s[at].astype(F32)
        dst[at] = total.astype(BF16)
        return 0

    if count == 1 and not lead:
        total = dst[...].astype(F32)
        for s in srcs:
            total = total + s[...].astype(F32)
        dst[...] = total.astype(BF16)
    else:
        lax.fori_loop(0, count, body, 0)


def inbox_shapes(classes, phases):
    out = []
    for order, _, n in classes:
        if 0 in phases:
            half = [2 if a == order[1] else 4 for a in "xyz" if a != order[0]]
            out += [half + [n, 128]] * 2 + [[4, 4, n, 128]] * 2
        if 1 in phases:
            out += [[2, n, 128]] * 2 + [[4, n, 128]] * 2
        if 2 in phases:
            out += [[3, n, 128]]
    return [pltpu.VMEM(tuple(s), BF16) for s in out]


def inboxes(refs, phases):
    refs, out = list(refs), []
    while refs:
        mine = {}
        for phase in phases:
            n = 1 if phase == 2 else 4
            mine[phase], refs = refs[:n], refs[n:]
        out.append(mine)
    return out


class Lane:
    def __init__(self, net, torus, acc, axes, inbox, order, row, n):
        self.net, self.t, self.acc, self.axes, self.inbox, self.order = net, torus, acc, axes, inbox, order
        self.rows, self.base = (row, n), 0
        self.fixed = {}
        self.got = {}

    def part(self, phase):
        axis = self.order[phase]
        return view(self.acc, self.axes, {**self.fixed, axis: self.t.pos(axis)}, self.rows)

    def held(self):
        return view(self.acc, self.axes, self.fixed, self.rows)

    def halves(self, phase):
        a = self.order[phase + 1]
        return [{a: pl.ds(0, 2)}, {a: pl.ds(2, 2)}]

    def box_half(self, box, phase, half):
        if phase == 1:
            return box.at[pl.ds(2 * half, 2)]
        left = [a for a in "xyz" if a != self.order[0]]
        cut = left.index(self.order[1])
        return box.at[(slice(None),) * cut + (pl.ds(2 * half, 2),)]

    def first(self, phase):
        axis = self.order[phase]
        p = self.t.pos(axis)
        h = self.halves(phase)
        b = self.inbox[phase]
        at = lambda shift, cut: view(self.acc, self.axes, {**self.fixed, axis: wrap(p + shift), **cut}, self.rows)
        up, down = self.t.at(axis, 1), self.t.at(axis, 3)
        far = [self.net.send(at(2, h[0]), b[0], up), self.net.send(at(2, h[1]), b[1], down)]
        near = [
            self.net.send(at(1, h[1]), self.box_half(b[2], phase, 1), up),
            self.net.send(at(3, h[0]), self.box_half(b[3], phase, 0), down),
        ]
        self.got[phase] = (far, near)

    def second(self, phase, side):
        axis = self.order[phase]
        p = self.t.pos(axis)
        b = self.inbox[phase]
        far, near = self.got[phase]
        step = 3 if side else 1
        chosen = {**self.fixed, axis: wrap(p + step), **self.halves(phase)[side]}
        here = view(self.acc, self.axes, chosen, self.rows)
        far[side].wait_recv()
        add_into(here, b[side])
        near.append(self.net.send(here, self.box_half(b[2 + side], phase, side), self.t.at(axis, step)))

    def third(self, phase):
        axis = self.order[phase]
        p = self.t.pos(axis)
        b = self.inbox[phase]
        for copy in self.got[phase][1]:
            copy.wait_recv()
        self.fixed[axis] = p
        add_into(self.held(), b[2], b[3])

    def last(self):
        axis = self.order[2]
        p = self.t.pos(axis)
        box = self.inbox[2][0]
        self.got[2] = [
            self.net.send(view(self.acc, self.axes, {**self.fixed, axis: wrap(p + s)}, self.rows), box.at[s - 1], self.t.at(axis, s))
            for s in (1, 3, 2)
        ]

    def done(self):
        axis = self.order[2]
        for copy in self.got[2]:
            copy.wait_recv()
        self.fixed[axis] = self.t.pos(axis)
        box = self.inbox[2][0]
        add_into(self.held(), box.at[0], box.at[1], box.at[2])


class Spread:
    def __init__(self, lane, out, result, order, row, n, sem):
        self.result = result
        self.net, self.t, self.out, self.order, self.rows, self.sem = lane.net, lane.t, out, order, (row, n), sem
        chosen = {a: lane.t.pos(a) for a in lane.axes}
        self.own = view(lane.acc, lane.axes, chosen, (row - lane.base, n))

    def place(self, y, z):
        return self.out.at[self.t.c, y, z, pl.ds(*self.rows)]

    def band(self, v, b=slice(None)):
        y, z = (b, v) if self.order == "yz" else (v, b)
        return self.place(y, z)

    def start(self):
        t = self.t
        here = self.place(t.y, t.z)
        self.keep = pltpu.make_async_copy(self.own, here, self.sem)
        self.keep.start()
        self.first = [self.net.send(self.own, here, t.at(self.order[0], s)) for s in (1, 3, 2)]

    def second(self):
        t, axis = self.t, self.order[1]
        for copy in self.first:
            copy.wait_recv()
        self.keep.wait()
        here = self.band(t.pos(axis))
        self.near = [self.net.send(here, here, t.at(axis, s)) for s in (1, 3)]

    def third(self):
        t, axis = self.t, self.order[1]
        p = t.pos(axis)
        self.far = []
        for copy, shift, to, b in ((self.near[0], 3, 1, pl.ds(0, 2)), (self.near[1], 1, 3, pl.ds(2, 2))):
            copy.wait_recv()
            there = self.band(wrap(p + shift), b)
            self.far.append(self.net.send(there, there, t.at(axis, to)))

    def share(self):
        for copy in self.far:
            copy.wait_recv()
        whole = self.place(slice(None), slice(None))
        self.core = self.net.send(whole, whole, self.t.sibling())

    def finish(self):
        self.core.wait_recv()
        rows = (slice(None),) * 3 + (pl.ds(*self.rows),)
        self.keep = pltpu.make_async_copy(self.out.at[rows], self.result.at[rows], self.sem)
        self.keep.start()

    def end(self):
        self.keep.wait()


GROUPS = {
    "mlp": ((352, 304, 144), 16, ("yxz", "zyx", "xzy")),
    "attn": ((128, 144, 128), 0, ("yxz", "zxy", "xyz")),
}
SMALL_ROWS = 16


def slab_rows(group):
    return sum(GROUPS[group][0]) + SMALL_ROWS


def classes_of(group):
    rows, extra, orders = GROUPS[group]
    row, out = 0, []
    for k, (order, n) in enumerate(zip(orders, rows)):
        n += extra if k == 2 else 0
        out.append((order, row, n))
        row += n
    return out


def spreads_of(group):
    a, b, c = classes_of(group)
    h = c[2] // 32 * 16
    return [(0, "yz", a[1], a[2]), (1, "zy", b[1], b[2]), (2, "yz", c[1], h), (2, "zy", c[1] + h, c[2] - h)]


def pieces_of(group, first, count):
    rows, out, flat, row = GROUPS[group][0], [], 0, 0
    for n in rows:
        for slab in range(16):
            lo, hi = max(first, flat), min(first + count, flat + n)
            if lo < hi:
                out.append((slab, row + lo - flat, hi - lo, lo - first))
            flat += n
        row += n
    return out


def store_blocks(acc, group, x, first, blocks):
    for k, block in enumerate(blocks):
        for slab, row, n, offset in pieces_of(group, first + 320 * k, 320):
            acc[x, slab // 4, slab % 4, pl.ds(row, n), :] = block[offset : offset + n]


def spreads_for(group, lanes, out, result, sems):
    return [Spread(lanes[k], out, result, order, row, n, sems.at[i]) for i, (k, order, row, n) in enumerate(spreads_of(group))]


def row_pieces(ref, row, start, n):
    v = ref[row : row + 1, start : start + n]
    if n % 128:
        v = jnp.concatenate([v, jnp.zeros((1, 128 - n % 128), F32)], axis=1)
    return [v[:, 128 * k : 128 * (k + 1)] for k in range(v.shape[1] // 128)]


def store_small(acc, row, slabs):
    for x in range(4):
        filled = slabs(x)
        for k in range(16):
            pieces = filled[k] if k < len(filled) else []
            if len(pieces) < 16:
                pieces = pieces + [jnp.zeros((16 - len(pieces), 128), F32)]
            acc[x, k // 4, k % 4, pl.ds(row, 16), :] = jnp.concatenate(pieces, axis=0).astype(BF16)


def store_product(lhs, rhs, acc, group, places):
    out = dot(lhs, rhs).astype(BF16)
    for k, (x, chunk) in enumerate(places):
        rows = out[320 * k : 320 * (k + 1)]
        store_blocks(acc, group, x, 1600 * chunk, [rows[:, 128 * t : 128 * (t + 1)] for t in range(5)])


class Backward:
    def __init__(self, net, torus, datt, full, heads, lse, box, single, single_in, do, dkv, grads, res, res_single, res_single_in):
        self.net, self.t, self.datt, self.full, self.heads, self.lse = net, torus, datt, full, heads, lse
        self.box, self.single, self.single_in, self.do, self.dkv, self.grads = box, single, single_in, do, dkv, grads
        self.res, self.res_single, self.res_single_in = res, res_single, res_single_in
        self.swap, self.back = Swap(net, torus, 1), Swap(net, torus, 3)
        self.sent = []

    def start(self):
        t, swap = self.t, self.swap
        self.got = swap.out_pairs(self.datt, self.box)
        swap.pack_single(self.datt, self.single)
        self.got_single = swap.out_single(self.single, self.single_in)
        swap.keep_pairs(self.datt, self.box)
        self.single_in[t.x] = self.single[t.x]

    def take(self, p):
        wait_all(self.got[p] if p < 2 else self.got_single)
        for s in range(4):
            rows = slice(256 * s, 256 * (s + 1))
            if p < 2:
                for j in range(2):
                    self.do[2 * p + j, rows, :] = self.box[p, 0, s, :, 64 * j : 64 * j + 64]
            else:
                self.do[4, rows, :] = self.single_in[s, :, :64]

    def head(self, h, j):
        heads, grads, dkv = self.heads, self.grads, self.dkv
        lane = lax.broadcasted_iota(jnp.int32, (256, 128), 1)
        dkv[...] = jnp.zeros_like(dkv)
        for i in range(4):
            rows = slice(256 * i, 256 * (i + 1))
            n = 256 * (i + 1)
            q, k, v, d = heads[0, h, rows, :], heads[1, h, :n, :], heads[2, h, :n, :], self.do[h, rows, :]
            total = jnp.sum(jnp.where(lane == h, self.lse[rows, :], 0.0), axis=1, keepdims=True)
            p = jnp.exp(causal(dot_t(q, k), i) - total)
            t1 = p * dot_t(d, v)
            inner = jnp.sum(t1, axis=1, keepdims=True)
            ds = (t1 - p * inner).astype(BF16)
            grads[0, j, rows, :] = (dot(ds, k) * 0.125).astype(BF16)
            dkv[0, :, :n] += dot(q.T, ds)
            dkv[1, :, :n] += dot(d.T, p.astype(BF16))
        for k in range(2):
            grads[1 + k, j] = dkv[k].T.astype(BF16)

    def give(self, p):
        grads, back = self.grads, self.back
        for i in range(4):
            rows = slice(256 * i, 256 * (i + 1))
            if p < 2:
                for k in range(3):
                    self.res[i, k, p] = jnp.concatenate([grads[k, 0, rows, :], grads[k, 1, rows, :]], axis=1)
            else:
                cols = [grads[k, 0, rows, :] for k in range(3)] + [jnp.zeros((256, 64), BF16)]
                self.res_single[i] = jnp.concatenate(cols, axis=1)
        if p < 2:
            self.sent += back.back_pair(p, self.res, self.full)
            back.keep_back(p, self.res, self.full)
        else:
            self.sent_single = back.out_single(self.res_single, self.res_single_in)
            self.res_single_in[self.t.x] = self.res_single[self.t.x]

    def finish(self):
        wait_all(self.sent_single)
        self.back.unpack_single(self.res_single_in, self.full)
        wait_all(self.sent)


def back_kernel(
    r_datt, r_heads, r_lse, r_small, n2t, actt, gp, cot,
    gqkv, part_0, part_1, part_2,
    datt, heads, lse, small, n2t_v, actt_v, gp_v, cot_v, small_v, full,
    box, single, single_in, do, dkv, grads, res, res_single, res_single_in,
    ssem, rsem, lsem, acc, *inbox,
):
    t = Torus()
    moves = ((n2t, n2t_v), (gp, gp_v), (r_datt, datt), (r_small, small), (actt, actt_v), (cot, cot_v), (r_heads, heads), (r_lse, lse))
    loads = [pltpu.make_async_copy(src, dst, lsem.at[k]) for k, (src, dst) in enumerate(moves)]
    soon, later = loads[:4], loads[4:]
    each(soon, "start")
    greeting = Greeting(t.neighbours())
    net = Net(ssem, rsem)
    bwd = Backward(net, t, datt, full, heads, lse, box, single, single_in, do, dkv, grads, res, res_single, res_single_in)
    lanes = [Lane(net, t, acc, "xyz", box_of, *k) for k, box_of in zip(classes_of("mlp"), inboxes(inbox, (0,)))]
    parts = [pltpu.make_async_copy(lane.part(0), part, lsem.at[k]) for k, (lane, part) in enumerate(zip(lanes, (part_0, part_1, part_2)))]

    def fc(s):
        store_product(n2t_v[...], gp_v[s], acc, "mlp", [(x, s) for x in range(4)])

    def proj(half):
        def body(x, _):
            lhs = actt_v[pl.ds(pl.multiple_of(x * 640, 16), 640), :]
            places = [(x, 4 + 2 * half), (x, 5 + 2 * half)]
            store_product(lhs, cot_v[:, 640 * half : 640 * (half + 1)], acc, "mlp", places)
            return 0

        lax.fori_loop(0, 4, body, 0)

    def sums():
        small_v[...] = small[0] + small[1]
        store_small(
            acc, 800,
            lambda x: [
                [row for k in range(4) for row in row_pieces(small_v, k, 320 * x, 320)],
                row_pieces(small_v, 4 + x, 0, 1280),
            ],
        )

    each(soon, "wait")
    each(later, "start")
    fc(2)
    fc(3)
    greeting.wait()
    bwd.start()
    fc(1)
    each(later, "wait")
    fc(0)
    lanes[0].first(0)
    proj(1)
    sums()
    lanes[2].first(0)
    proj(0)
    lanes[1].first(0)
    bwd.take(0)
    bwd.head(0, 0)
    lanes[2].second(0, 1)
    bwd.head(1, 1)
    bwd.give(0)
    bwd.take(1)
    lanes[1].second(0, 1)
    lanes[2].second(0, 0)
    bwd.head(2, 0)
    lanes[0].second(0, 0)
    lanes[1].second(0, 0)
    bwd.head(3, 1)
    bwd.give(1)
    lanes[0].second(0, 1)
    bwd.take(2)
    lanes[2].third(0)
    bwd.head(4, 0)
    bwd.give(2)
    lanes[1].third(0)
    parts[2].start()
    lanes[0].third(0)
    parts[0].start()
    parts[1].start()
    bwd.finish()
    gqkv[...] = full[...]
    each(parts, "wait")
    net.finish()


BACK_SEMS = 100


def backward(datt, heads, lse, small, n2t, actt, gp, cot):
    vm, anys = pl.BlockSpec(memory_space=pltpu.VMEM), pl.BlockSpec(memory_space=pl.ANY)
    classes = classes_of("mlp")
    return pl.pallas_call(
        back_kernel,
        name="backward",
        out_shape=[jax.ShapeDtypeStruct((256, 3840), BF16)]
        + [jax.ShapeDtypeStruct((4, 4, n, 128), BF16) for _, _, n in classes],
        in_specs=[anys] * 8,
        out_specs=[vm] + [anys] * 3,
        scratch_shapes=[
            pltpu.VMEM((256, 1280), BF16),
            pltpu.VMEM((3, 5, 1024, 64), BF16),
            pltpu.VMEM((1024, 128), F32),
            pltpu.VMEM((2, 8, 1280), F32),
            pltpu.VMEM((1280, 512), BF16),
            pltpu.VMEM((2560, 512), BF16),
            pltpu.VMEM((4, 512, 640), BF16),
            pltpu.VMEM((512, 1280), BF16),
            pltpu.VMEM((8, 1280), F32),
            pltpu.VMEM((256, 3840), BF16),
            pltpu.VMEM((2, 1, 4, 256, 128), BF16),
            pltpu.VMEM((4, 256, 128), BF16),
            pltpu.VMEM((4, 256, 128), BF16),
            pltpu.VMEM((5, 1024, 64), BF16),
            pltpu.VMEM((2, 64, 1024), F32),
            pltpu.VMEM((3, 2, 1024, 64), BF16),
            pltpu.VMEM((4, 3, 2, 256, 128), BF16),
            pltpu.VMEM((4, 256, 256), BF16),
            pltpu.VMEM((4, 256, 256), BF16),
            pltpu.SemaphoreType.DMA((BACK_SEMS,)),
            pltpu.SemaphoreType.DMA((BACK_SEMS,)),
            pltpu.SemaphoreType.DMA((8,)),
            pltpu.VMEM((4, 4, 4, slab_rows("mlp"), 128), BF16),
        ]
        + inbox_shapes(classes, (0,)),
        compiler_params=pltpu.CompilerParams(collective_id=1, has_side_effects=True, vmem_limit_bytes=60 << 20),
    )(datt, heads, lse, small, n2t, actt, gp, cot)


def last_kernel(
    n1, r_gqkv, attt, gb, w_qkv, r_tokens, r_mid, r_small, part_0, part_1, part_2,
    r_mlp, r_attn, r_grad,
    out_mlp, out_attn, grad_tokens, gqkv, tokens, grad_mid, small_all, n1_v, n1t, gqkv_v, attt_v, gb_v, w_v, small_v, ssem, rsem, lsem, acc, acc_small, held_0, held_1, held_2, *inbox,
):
    t = Torus()
    helds = (held_0, held_1, held_2)
    moves = [(n1, n1_v), (attt, attt_v), (gb, gb_v), (w_qkv, w_v)] + [*zip((part_0, part_1, part_2), helds)]
    moves += [(r_gqkv, gqkv), (r_tokens, tokens), (r_mid, grad_mid), (r_small, small_all)]
    n1_in, att_in, gb_in, w_in, *rest = [
        pltpu.make_async_copy(src, dst, lsem.at[k]) for k, (src, dst) in enumerate(moves)
    ]
    parts_in, rows_in = rest[:3], rest[3:]
    soon, later = rows_in[:1] + [n1_in] + parts_in, [att_in, gb_in] + rows_in[1:] + [w_in]
    each(soon, "start")
    greeting = Greeting(t.neighbours())
    net = Net(ssem, rsem)
    sib, c = t.sibling(), t.c
    m, a = [], []
    boxes = inboxes(inbox[:15], (1, 2))
    for held, box_of, (order, row, n) in zip(helds, boxes, classes_of("mlp")):
        lane = Lane(net, t, held, "".join(v for v in "xyz" if v != order[0]), box_of, order, 0, n)
        lane.base = row
        m.append(lane)
    boxes = inboxes(inbox[15:], (0, 1, 2))
    for box_of, k in zip(boxes, classes_of("attn")):
        a.append(Lane(net, t, acc, "xyz", box_of, *k))
    tiny = Lane(net, t, acc_small, "xyz", boxes[3], "yzx", 0, SMALL_ROWS)
    tiny.base = 400
    ms = spreads_for("mlp", m, out_mlp, r_mlp, lsem.at[pl.ds(11, 4)])
    sp = spreads_for("attn", a, out_attn, r_attn, lsem.at[pl.ds(15, 4)])
    ts = Spread(tiny, out_attn, r_attn, "zy", 400, SMALL_ROWS, lsem.at[19])
    got = {}

    def own():
        rows_in[0].wait()
        for s in range(3):
            gqkv_v[s, 0:256] = gqkv[:, pl.ds(pl.multiple_of(c * 1920 + s * 640, 128), 640)]

    def swap():
        for s in range(3):
            theirs = pl.ds(pl.multiple_of((1 - c) * 1920 + s * 640, 128), 640)
            got[s] = net.send(gqkv.at[:, theirs], gqkv_v.at[s, pl.ds(256, 256)], sib)

    def turn():
        n1_in.wait()
        n1t[:, 0:256] = n1_v[0].T
        n1t[:, 256:512] = n1_v[1].T

    def qkv(s):
        got[s].wait_recv()
        store_product(n1t[...], gqkv_v[s], acc, "attn", [(x, s) for x in range(4)])

    def outp():
        att_in.wait()
        gb_in.wait()
        store_product(attt_v[...], gb_v[...], acc, "attn", [(x, 3) for x in range(4)])

    def rows_back():
        w_in.wait()
        each(rows_in[1:], "wait")

        def body(n, total):
            cols = pl.ds(pl.multiple_of(n * 640, 128), 640)
            return total + dot_t(gqkv[:, cols], w_v[:, cols])

        grad = lax.fori_loop(0, 6, body, jnp.zeros((256, 1280), F32))
        hat, scale = norm(tokens[...].astype(F32))
        grad_tokens[...] = (grad_mid[...] + norm_back(grad, hat, scale, whole_vector(small_all, "ln1_gain"))).astype(BF16)
        small_v[0, 0:1, :] = jnp.sum(grad * hat, axis=0, keepdims=True)
        small_v[0, 1:2, :] = jnp.sum(grad, axis=0, keepdims=True)
        small_v[0, 2:3, :] = jnp.sum(gqkv[:, :1280].astype(F32), axis=0, keepdims=True)
        small_v[0, 3:4, :] = jnp.sum(gqkv[:, 2560:].astype(F32), axis=0, keepdims=True)

    grad_out = pltpu.make_async_copy(grad_tokens, r_grad, lsem.at[20])

    def rows_out():
        grad_out.start()
        got["small"] = net.send(small_v.at[0], small_v.at[1], sib)

    def sums():
        got["small"].wait_recv()
        total = small_v.at[2]
        total[...] = small_v[0] + small_v[1]
        store_small(
            acc_small, 0,
            lambda x: [
                [row for k in range(2) for row in row_pieces(total, k, 320 * x, 320)],
                row_pieces(total, 2 + x // 2, 640 * (x % 2), 640),
            ],
        )

    own()
    each(later, "start")
    each(parts_in, "wait")
    greeting.wait()
    m[1].first(1)
    m[0].first(1)
    swap()
    turn()
    m[2].first(1)
    outp()
    qkv(1)
    qkv(2)
    m[1].second(1, 1)
    a[1].first(0)
    m[1].second(1, 0)
    m[0].second(1, 0)
    m[0].second(1, 1)
    qkv(0)
    a[0].first(0)
    a[2].first(0)
    m[1].third(1)
    m[2].second(1, 1)
    m[2].second(1, 0)
    m[0].third(1)
    rows_back()
    m[0].last()
    a[1].second(0, 0)
    a[1].second(0, 1)
    m[1].last()
    a[0].second(0, 0)
    a[0].second(0, 1)
    m[2].third(1)
    a[2].second(0, 1)
    rows_out()
    a[2].second(0, 0)
    m[0].done()
    m[2].last()
    ms[0].start()
    m[1].done()
    sums()
    tiny.first(0)
    a[0].third(0)
    m[2].done()
    ms[3].start()
    ms[1].start()
    a[0].first(1)
    a[1].third(0)
    a[1].first(1)
    ms[2].start()
    a[2].third(0)
    a[2].first(1)
    ms[0].second()
    tiny.second(0, 0)
    tiny.second(0, 1)
    ms[3].second()
    a[2].second(1, 0)
    a[0].second(1, 0)
    a[2].second(1, 1)
    tiny.third(0)
    a[0].second(1, 1)
    tiny.first(1)
    ms[1].second()
    a[2].third(1)
    a[1].second(1, 0)
    a[2].last()
    a[1].second(1, 1)
    a[0].third(1)
    tiny.second(1, 1)
    a[0].last()
    ms[3].third()
    tiny.second(1, 0)
    ms[2].second()
    a[1].third(1)
    a[2].done()
    a[1].last()
    sp[2].start()
    sp[3].start()
    tiny.third(1)
    a[0].done()
    ms[0].third()
    sp[0].start()
    sp[3].second()
    ms[1].third()
    a[1].done()
    sp[1].start()
    tiny.last()
    ms[2].third()
    ms[3].share()
    tiny.done()
    ms[0].share()
    ts.start()
    sp[0].second()
    sp[1].second()
    ts.second()
    sp[2].second()
    ms[1].share()
    sp[0].third()
    sp[3].third()
    ms[0].finish()
    sp[2].third()
    sp[1].third()
    ms[2].share()
    sp[3].share()
    ts.third()
    sp[0].share()
    ms[3].finish()
    sp[2].share()
    sp[1].share()
    sp[3].finish()
    sp[0].finish()
    ms[2].finish()
    ts.share()
    ms[1].finish()
    sp[2].finish()
    sp[1].finish()
    ts.finish()
    each(ms + sp + [ts], "end")
    grad_out.wait()
    net.finish()


LAST_SEMS = 200


def last(n1, gqkv, attt, gb, w_qkv, tokens, grad_mid, small_all, parts):
    anys = pl.BlockSpec(memory_space=pl.ANY)
    mlp_classes, attn_classes = classes_of("mlp"), classes_of("attn")
    return pl.pallas_call(
        last_kernel,
        name="last",
        out_shape=[jax.ShapeDtypeStruct((2, 4, 4, slab_rows(g), 128), BF16) for g in ("mlp", "attn")]
        + [jax.ShapeDtypeStruct((256, 1280), BF16)],
        in_specs=[anys] * 11,
        out_specs=[anys] * 3,
        scratch_shapes=[pltpu.VMEM((2, 4, 4, slab_rows(g), 128), BF16) for g in ("mlp", "attn")]
        + [
            pltpu.VMEM((256, 1280), BF16),
            pltpu.VMEM((256, 3840), BF16),
            pltpu.VMEM((256, 1280), BF16),
            pltpu.VMEM((256, 1280), F32),
            pltpu.VMEM((4, 8, 1280), F32),
            pltpu.VMEM((2, 256, 1280), BF16),
            pltpu.VMEM((1280, 512), BF16),
            pltpu.VMEM((3, 512, 640), BF16),
            pltpu.VMEM((1280, 512), BF16),
            pltpu.VMEM((512, 640), BF16),
            pltpu.VMEM((1280, 3840), BF16),
            pltpu.VMEM((3, 8, 1280), F32),
            pltpu.SemaphoreType.DMA((LAST_SEMS,)),
            pltpu.SemaphoreType.DMA((LAST_SEMS,)),
            pltpu.SemaphoreType.DMA((21,)),
            pltpu.VMEM((4, 4, 4, 400, 128), BF16),
            pltpu.VMEM((4, 4, 4, SMALL_ROWS, 128), BF16),
        ]
        + [pltpu.VMEM((4, 4, n, 128), BF16) for _, _, n in mlp_classes]
        + inbox_shapes(mlp_classes, (1, 2))
        + inbox_shapes(attn_classes + [("yzx", 0, SMALL_ROWS)], (0, 1, 2)),
        compiler_params=pltpu.CompilerParams(collective_id=2, has_side_effects=True, vmem_limit_bytes=60 << 20),
    )(n1, gqkv, attt, gb, w_qkv, tokens, grad_mid, small_all, *parts)


def flat_block(src, core, group, block):
    pieces = [
        src[core, slab // 4, slab % 4, row : row + n, :] for slab, row, n, _ in pieces_of(group, 320 * block, 320)
    ]
    return jnp.concatenate(pieces, axis=0).astype(F32)


SMALL_PLACES = (
    ("attn", 0, 0, 320),
    ("attn", 0, 3, 320),
    ("attn", 1, 0, 640),
    ("mlp", 0, 9, 320),
    ("mlp", 0, 0, 320),
    ("mlp", 0, 3, 320),
    ("mlp", 1, 0, 1280),
    ("mlp", 0, 6, 320),
)


def unpack_kernel(packed_mlp, packed_attn, block, grad, *refs):
    fc, proj, qkv, out, block_out, grad_out, *smalls = refs[:14]
    in_0, in_1, stage, block_v, grad_v, *rest = refs[14:]
    small_v, (in_sem, out_sem, small_sem) = rest[:8], rest[8:]
    loads = []
    for c in range(2):
        loads.append(
            [
                pltpu.make_async_copy(src.at[c], dst.at[c], in_sem.at[2 * c + k])
                for k, (src, dst) in enumerate(((packed_attn, in_1), (packed_mlp, in_0)))
            ]
        )
        each(loads[-1], "start")
    rows = [pltpu.make_async_copy(block, block_v, in_sem.at[4]), pltpu.make_async_copy(grad, grad_v, in_sem.at[5])]
    each(rows, "start")
    flying, tail = [], []
    for c in range(2):
        chunks = [(in_1, "attn", q, qkv, 0, 1920 * c + 640 * q) for q in range(3)]
        chunks += [(in_1, "attn", 3, out, 0, 640 * c)]
        chunks += [(in_0, "mlp", q, fc, 0, 1280 * q + 640 * c) for q in range(4)]
        chunks += [(in_0, "mlp", 4 + 2 * h + sub, proj, 640 * c + 320 * sub, 640 * h) for h in range(2) for sub in range(2)]
        for n, (src, group, q, dst, row, col) in enumerate(chunks):
            if n in (0, 4):
                loads[c][n // 4].wait()
            k = len(flying)
            slot = k % STAGES
            if k >= STAGES:
                flying[k - STAGES].wait()
            for t in range(5):
                stage[slot, :, 128 * t : 128 * (t + 1)] = flat_block(src, c, group, 5 * q + t)
            copy = pltpu.make_async_copy(stage.at[slot], dst.at[pl.ds(row, 320), pl.ds(col, 640)], out_sem.at[slot])
            copy.start()
            flying.append(copy)
        if c == 0:
            for k, (group, slab, row, n) in enumerate(SMALL_PLACES):
                src = in_1 if group == "attn" else in_0
                first = slab_rows(group) - SMALL_ROWS
                values = src[0, 0, slab, first : first + SMALL_ROWS, :].astype(F32)
                for i in range(0, n, 128):
                    m = min(128, n - i)
                    small_v[k][i : i + m] = values[row + i // 128, :m]
                tail.append(pltpu.make_async_copy(small_v[k], smalls[k], small_sem.at[k]))
                tail[-1].start()
            each(rows, "wait")
            tail.append(pltpu.make_async_copy(block_v, block_out, small_sem.at[8]))
            tail.append(pltpu.make_async_copy(grad_v, grad_out, small_sem.at[9]))
            each(tail[-2:], "start")
    each(flying[-STAGES:] + tail, "wait")


STAGES = 8


def unpack(packed_mlp, packed_attn, block, grad):
    anys = pl.BlockSpec(memory_space=pl.ANY)
    sizes = [n for _, _, _, n in SMALL_PLACES]
    return pl.pallas_call(
        unpack_kernel,
        name="unpack",
        out_shape=[jax.ShapeDtypeStruct(s, F32) for s in ((320, 5120), (1280, 1280), (320, 3840), (320, 1280))]
        + [jax.ShapeDtypeStruct((256, 1280), BF16)] * 2
        + [jax.ShapeDtypeStruct((n,), F32) for n in sizes],
        in_specs=[anys] * 4,
        out_specs=[anys] * 14,
        scratch_shapes=[
            pltpu.VMEM(packed_mlp.shape, BF16),
            pltpu.VMEM(packed_attn.shape, BF16),
            pltpu.VMEM((STAGES, 320, 640), F32),
            pltpu.VMEM((256, 1280), BF16),
            pltpu.VMEM((256, 1280), BF16),
        ]
        + [pltpu.VMEM((n,), F32) for n in sizes]
        + [
            pltpu.SemaphoreType.DMA((6,)),
            pltpu.SemaphoreType.DMA((STAGES,)),
            pltpu.SemaphoreType.DMA((10,)),
        ],
        compiler_params=pltpu.CompilerParams(vmem_limit_bytes=62 << 20),
    )(packed_mlp, packed_attn, block, grad)


def shards(
    tokens,
    cotangent,
    ln1_gain,
    ln1_bias,
    w_qkv,
    qv_bias,
    w_out,
    out_bias,
    ln2_gain,
    ln2_bias,
    w_fc,
    fc_bias,
    w_proj,
    proj_bias,
):
    own = (ln1_gain, ln1_bias, qv_bias, out_bias, ln2_gain, ln2_bias, proj_bias, fc_bias)
    f_qkv, f_out, f_fc, f_proj, f_small, normed_one, attended, heads, lse = front(
        tokens[0], own, w_qkv, w_out, w_fc, w_proj
    )
    f_qkv, f_out, f_fc, f_proj = (
        f_qkv.reshape(1280, 3840),
        f_out.reshape(1280, 1280),
        f_fc.reshape(1280, 5120),
        f_proj.reshape(5120, 1280),
    )
    block_out, grad_middle, grad_attended, n2t, attt, cot, actt, grad_pre, grad_branch, small_mlp = mlp(
        tokens[0], attended, cotangent[0], f_small, f_out, f_fc, f_proj
    )
    grad_qkv, *parts = backward(grad_attended, heads, lse, small_mlp, n2t, actt, grad_pre, cot)
    packed_mlp, packed_attn, grad_tokens = last(
        normed_one, grad_qkv, attt, grad_branch, f_qkv, tokens[0], grad_middle, f_small, parts
    )
    g_fc, g_proj, g_qkv, g_out, block_out, grad_tokens, *vectors = unpack(
        packed_mlp, packed_attn, block_out, grad_tokens
    )
    gain_1, bias_1, bias_qv, bias_out, gain_2, bias_2, bias_fc, bias_proj = vectors
    return (
        block_out[None],
        grad_tokens[None],
        gain_1,
        bias_1,
        g_qkv,
        bias_qv,
        g_out,
        bias_out,
        gain_2,
        bias_2,
        g_fc,
        bias_fc,
        g_proj,
        bias_proj,
    )


def solution(mesh):
    vector, matrix, batch = P("shard"), P("shard", None), P("rep", "shard", None)
    placed = (batch, batch, vector, vector, matrix, vector, matrix, vector, vector, vector, matrix, vector, matrix, vector)
    return jax.shard_map(shards, mesh=mesh, in_specs=placed, out_specs=placed, check_vma=False)
```

```python
import jax
import jax.numpy as jnp
from jax import lax
from jax.experimental import pallas as pl
from jax.experimental.pallas import tpu as pltpu
from jax.sharding import PartitionSpec as P

MESH = pl.DeviceIdType.MESH
F32, BF16 = jnp.float32, jnp.bfloat16


def where_am_i():
    rep = lax.axis_index("rep")
    return lax.axis_index("shard"), (rep // 2) % 4, rep // 8, rep % 2


def device_at(x, y, z, c):
    return {"rep": (z * 4 + y) * 2 + c, "shard": x}


def wrap(v):
    return lax.rem(v + 4, 4)


class Group:
    def __init__(self, sems, whole, target):
        self.sems = sems
        self.all = self.copy(whole, whole, target)

    def copy(self, src, dst, target):
        send_sem, recv_sem = self.sems
        return pltpu.make_async_remote_copy(
            src_ref=src, dst_ref=dst, send_sem=send_sem, recv_sem=recv_sem, device_id=target, device_id_type=MESH
        )

    def send(self, src, dst, target):
        self.copy(src, dst, target).start()

    def wait_recv(self):
        self.all.wait_recv()

    def wait_send(self):
        self.all.wait_send()


class Net:
    def __init__(self, send_sems, recv_sems):
        self.send_sems, self.recv_sems, self.groups = send_sems, recv_sems, []

    def group(self, whole, target):
        k = len(self.groups)
        self.groups.append(Group((self.send_sems.at[k], self.recv_sems.at[k]), whole, target))
        return self.groups[-1]

    def send(self, src, dst, target):
        group = self.group(dst, target)
        group.send(src, dst, target)
        return group

    def finish(self):
        for group in self.groups:
            group.wait_send()


def wait_all(copies):
    for copy in copies:
        copy.wait_recv()


def each(items, what, *rest):
    for item in items:
        getattr(item, what)(*rest)


class Greeting:
    def __init__(self, targets):
        self.barrier, self.count = pltpu.get_barrier_semaphore(), len(targets)
        for target in targets:
            pl.semaphore_signal(self.barrier, 1, device_id=target, device_id_type=MESH)

    def wait(self):
        pl.semaphore_wait(self.barrier, self.count)


class Torus:
    def __init__(self):
        self.x, self.y, self.z, self.c = where_am_i()

    def at(self, axis, step):
        x, y, z = self.x, self.y, self.z
        if axis == "x":
            x = wrap(x + step)
        elif axis == "y":
            y = wrap(y + step)
        else:
            z = wrap(z + step)
        return device_at(x, y, z, self.c)

    def pos(self, axis):
        return {"x": self.x, "y": self.y, "z": self.z}[axis]

    def sibling(self):
        return device_at(self.x, self.y, self.z, 1 - self.c)

    def neighbours(self, axes="xyz", core=True):
        out = [self.at(a, s) for a in axes for s in (1, 2, 3)]
        return out + ([self.sibling()] if core else [])


PLANS = {
    "qkv": (320, 3840, 4, 8, 3),
    "out": (320, 1280, 4, 0, 1),
    "fc": (320, 5120, 8, 8, 4),
    "proj": (1280, 1280, 2, 2, 1),
}


def rect_of(rows, start, width, order, y, z, stage):
    if rows == 320:
        if stage == 0:
            return y * 80, 80, start + z * (width // 4), width // 4
        if order == "yz":
            return 0, 320, start + z * (width // 4), width // 4
        return y * 80, 80, start, width
    first, second = (y, z) if order == "yz" else (z, y)
    if stage == 0:
        return second * 320 + first * 80, 80, start, width
    return second * 320, 320, start, width


def part(ref, owner, rect):
    r, nr, c, nc = rect
    return ref.at[owner, pl.ds(pl.multiple_of(r, 16), nr), pl.ds(pl.multiple_of(c, 128), nc)]


def parts_of(ref, count, rect):
    r, nr, c, nc = rect
    return ref.at[pl.ds(0, count), pl.ds(pl.multiple_of(r, 16), nr), pl.ds(pl.multiple_of(c, 128), nc)]


def own_part(ref, rect):
    r, nr, c, nc = rect
    return ref.at[pl.ds(pl.multiple_of(r, 16), nr), pl.ds(pl.multiple_of(c, 128), nc)]


class Gather:
    def __init__(self, net, torus, name, src, full, lean):
        self.net, self.t, self.src, self.full, self.lean = net, torus, src, full, lean
        self.rows, cols, a, b, d = PLANS[name]
        half = torus.c * (cols // 2)
        self.regions = []
        at = 0
        for order, tiles in (("yz", a), ("zy", b)):
            if tiles:
                self.regions.append((order, half + at * 128, tiles * 128))
            at += tiles
        self.alone = (half + at * 128, d * 128)
        self.others = [wrap(torus.x + k) for k in (1, 2, 3)]
        self.got = {"core": []}

    def rect(self, region, stage, shift=0):
        order, start, width = region
        y, z = self.t.y, self.t.z
        axis = order[stage]
        if axis == "y":
            y = wrap(y + shift)
        else:
            z = wrap(z + shift)
        return rect_of(self.rows, start, width, order, y, z, stage)

    def both(self, what, *rest):
        for i in range(len(self.regions)):
            getattr(self, what)(i, *rest)

    def start(self):
        t, net = self.t, self.net
        for i, region in enumerate(self.regions):
            rect = self.rect(region, 0)
            group = net.group(parts_of(self.full, 3, rect), t.at("x", 1))
            for s in (1, 3, 2):
                group.send(own_part(self.src, rect), part(self.full, t.x, rect), t.at("x", s))
            self.got[i, "x"] = group

    def start_alone(self):
        t, net = self.t, self.net
        rect = (0, self.rows, *self.alone)
        self.got["alone"] = [
            net.send(own_part(self.src, rect), part(self.full, t.x, rect), t.at("x", s)) for s in (1, 3)
        ]

    def alone_on(self):
        t, net = self.t, self.net
        h = self.rows // 2
        start, width = self.alone
        whole = (0, self.rows, start, width)
        left, right = wrap(t.x - 1), wrap(t.x + 1)
        on = net.group(part(self.full, left, whole), t.at("x", 1))
        for copy, owner, row, step in zip(self.got["alone"], (left, right), (0, h), (1, 3)):
            copy.wait_recv()
            half = part(self.full, owner, (row, h, start, width))
            on.send(half, half, t.at("x", step))
        self.got["alone2"] = on
        core = net.group(parts_of(self.full, 2, whole), t.sibling())
        for o in (left, right):
            core.send(part(self.full, o, whole), part(self.full, o, whole), t.sibling())
        self.got["core"].append(core)

    def alone_end(self):
        self.got["alone2"].wait_recv()

    def alone_share(self):
        o = wrap(self.t.x + 2)
        whole = (0, self.rows, *self.alone)
        self.got["core"].append(self.net.send(part(self.full, o, whole), part(self.full, o, whole), self.t.sibling()))

    def to_all(self, rect, target):
        group = self.net.group(parts_of(self.full, 3, rect), target)
        for o in self.others:
            group.send(part(self.full, o, rect), part(self.full, o, rect), target)
        return group

    def spread(self, i):
        region = self.regions[i]
        self.got[i, "x"].wait_recv()
        rect = self.rect(region, 0)
        self.got[i, 0] = [self.to_all(rect, self.t.at(region[0][0], s)) for s in (1, 3, 2)]

    def widen(self, i):
        region = self.regions[i]
        wait_all(self.got[i, 0])
        rect = self.rect(region, 1)
        self.got[i, 1] = [self.to_all(rect, self.t.at(region[0][1], s)) for s in (1, 3)]

    def pass_on(self, i):
        region = self.regions[i]
        axis = region[0][1]
        cut = 2 if self.lean else 1
        ahead, behind = self.got[i, 1]
        group = self.net.group(parts_of(self.full, 3, self.rect(region, 1)), self.t.at(axis, 1))
        for came, shift, to, owners in (
            (ahead, -1, 1, self.others[:cut]),
            (behind, 1, 3, self.others[cut:]),
        ):
            came.wait_recv()
            rect = self.rect(region, 1, shift)
            for o in owners:
                group.send(part(self.full, o, rect), part(self.full, o, rect), self.t.at(axis, to))
        self.got[i, 2] = group

    def to_sibling(self, region, shifts):
        for shift in shifts:
            self.got["core"].append(self.to_all(self.rect(region, 1, shift), self.t.sibling()))

    def share(self, i):
        self.to_sibling(self.regions[i], (0, -1, 1))

    def arrive(self, i):
        self.got[i, 2].wait_recv()

    def share_last(self, i):
        self.to_sibling(self.regions[i], (2,))

    def finish(self):
        wait_all(self.got["core"])


LAG = 0.5


def dot_t(a, b):
    return lax.dot_general(a, b, (((1,), (1,)), ((), ())), preferred_element_type=F32)


def causal(s, i):
    rows = lax.broadcasted_iota(jnp.int32, (256, 256), 0)
    cols = lax.broadcasted_iota(jnp.int32, (256, 256), 1)
    last = jnp.where(cols <= rows, s[:, 256 * i :], -1e30)
    return last if i == 0 else jnp.concatenate([s[:, : 256 * i], last], axis=1)


class Swap:
    def __init__(self, net, torus, parts):
        self.net, self.t, self.parts = net, torus, parts

    def pack_single(self, full, single):
        parts = self.parts
        for d in range(4):
            cols = [full[:, 1280 * k + 1024 + 64 * d : 1280 * k + 1088 + 64 * d] for k in range(parts)]
            if parts % 2:
                cols.append(jnp.zeros((256, 64), BF16))
            single[d] = jnp.concatenate(cols, axis=1)

    def out_pairs(self, full, box):
        t, net, got = self.t, self.net, []
        for p in range(2):
            group = net.group(box.at[p, :, pl.ds(0, 3)], t.at("x", 1))
            for s in (1, 3, 2):
                d = wrap(t.x + s)
                for k in range(self.parts):
                    cols = pl.ds(pl.multiple_of(1280 * k + 256 * d + 128 * p, 128), 128)
                    group.send(full.at[:, cols], box.at[p, k, t.x], t.at("x", s))
            got.append(group)
        return got

    def keep_pairs(self, full, box):
        for p in range(2):
            for k in range(self.parts):
                cols = pl.ds(pl.multiple_of(1280 * k + 256 * self.t.x + 128 * p, 128), 128)
                box[p, k, self.t.x] = full[:, cols]

    def out_single(self, single, box):
        t = self.t
        group = self.net.group(box.at[pl.ds(0, 3)], t.at("x", 1))
        for s in (1, 3, 2):
            group.send(single.at[wrap(t.x + s)], box.at[t.x], t.at("x", s))
        return group

    def back_pair(self, p, src, full):
        t = self.t
        group = self.net.group(src.at[pl.ds(0, 3), :, p], t.at("x", 1))
        for s in (1, 3, 2):
            d = wrap(t.x + s)
            for k in range(self.parts):
                cols = pl.ds(pl.multiple_of(1280 * k + 256 * t.x + 128 * p, 128), 128)
                group.send(src.at[d, k, p], full.at[:, cols], t.at("x", s))
        return group

    def keep_back(self, p, src, full):
        for k in range(self.parts):
            cols = pl.ds(pl.multiple_of(1280 * k + 256 * self.t.x + 128 * p, 128), 128)
            full[:, cols] = src[self.t.x, k, p]

    def unpack_single(self, box, full):
        for k in range(self.parts):
            cols = [box[d, :, 64 * k : 64 * k + 64] for d in range(4)]
            full[:, 1280 * k + 1024 : 1280 * (k + 1)] = jnp.concatenate(cols, axis=1)


EPS = 1e-05
VECTORS = ("ln1_gain", "ln1_bias", "qv_bias", "out_bias", "ln2_gain", "ln2_bias", "proj_bias", "fc_bias")
SIZES = (320, 320, 640, 320, 320, 320, 320, 1280)


def whole_vector(small, name):
    k = VECTORS.index(name)
    return jnp.concatenate([small[x, k : k + 1, : SIZES[k]] for x in range(4)], axis=1)


def dot(a, b):
    return jnp.dot(a, b, preferred_element_type=F32)


def norm(v):
    center = v - jnp.mean(v, axis=-1, keepdims=True)
    scale = lax.rsqrt(jnp.mean(center * center, axis=-1, keepdims=True) + EPS)
    return center * scale, scale


def norm_back(grad, hat, scale, gain):
    inner = grad * gain
    return scale * (
        inner - jnp.mean(inner, axis=-1, keepdims=True) - hat * jnp.mean(inner * hat, axis=-1, keepdims=True)
    )


class Forward:
    def __init__(self, net, torus, qkv, full, heads, lse, box, single, single_in, outs, res, res_single, res_single_in):
        self.net, self.t, self.qkv, self.full, self.heads, self.lse = net, torus, qkv, full, heads, lse
        self.box, self.single, self.single_in, self.outs = box, single, single_in, outs
        self.res, self.res_single, self.res_single_in = res, res_single, res_single_in
        self.swap, self.back = Swap(net, torus, 3), Swap(net, torus, 1)
        self.sent = []

    def start(self):
        t, swap = self.t, self.swap
        self.got = swap.out_pairs(self.qkv, self.box)
        swap.pack_single(self.qkv, self.single)
        self.got_single = swap.out_single(self.single, self.single_in)
        swap.keep_pairs(self.qkv, self.box)
        self.single_in[t.x] = self.single[t.x]
        self.lse[...] = jnp.zeros_like(self.lse)

    def take(self, p):
        heads = self.heads
        if p < 2:
            self.got[p].wait_recv()
            for k in range(3):
                for s in range(4):
                    for j in range(2):
                        v = self.box[p, k, s, :, 64 * j : 64 * j + 64]
                        heads[k, 2 * p + j, 256 * s : 256 * (s + 1), :] = v * BF16(0.125) if k == 0 else v
            return
        self.got_single.wait_recv()
        for k in range(3):
            for s in range(4):
                v = self.single_in[s, :, 64 * k : 64 * k + 64]
                heads[k, 4, 256 * s : 256 * (s + 1), :] = v * BF16(0.125) if k == 0 else v

    def head(self, h, j):
        heads, lse = self.heads, self.lse
        lane = lax.broadcasted_iota(jnp.int32, (256, 128), 1)
        for i in range(4):
            rows = slice(256 * i, 256 * (i + 1))
            n = 256 * (i + 1)
            s = causal(dot_t(heads[0, h, rows, :], heads[1, h, :n, :]), i)
            top = jnp.max(s, axis=1, keepdims=True)
            p = jnp.exp(s - top)
            total = jnp.sum(p, axis=1, keepdims=True)
            lse[rows, :] = jnp.where(lane == h, top + jnp.log(total), lse[rows, :])
            o = dot(p.astype(BF16), heads[2, h, :n, :])
            self.outs[j, rows, :] = (o / total).astype(BF16)

    def give(self, p):
        back, outs = self.back, self.outs
        for i in range(4):
            rows = slice(256 * i, 256 * (i + 1))
            if p < 2:
                self.res[i, 0, p] = jnp.concatenate([outs[0, rows, :], outs[1, rows, :]], axis=1)
            else:
                self.res_single[i] = jnp.concatenate([outs[0, rows, :], jnp.zeros((256, 64), BF16)], axis=1)
        if p < 2:
            self.sent.append(back.back_pair(p, self.res, self.full))
            back.keep_back(p, self.res, self.full)
        else:
            self.sent_single = back.out_single(self.res_single, self.res_single_in)
            self.res_single_in[self.t.x] = self.res_single[self.t.x]

    def finish(self):
        self.sent_single.wait_recv()
        self.back.unpack_single(self.res_single_in, self.full)
        wait_all(self.sent)


def front_kernel(
    tokens, v_0, v_1, v_2, v_3, v_4, v_5, v_6, v_7, w_qkv, w_out, w_fc, w_proj,
    f_qkv, f_out, f_fc, f_proj, f_small, r_normed, att, r_heads, r_lse,
    normed, heads, lse, tok_v, small, u_0, u_1, u_2, u_3, u_4, u_5, u_6, u_7, v_qkv, h_out, h_fc, h_proj, small_all, bias, qkv, other, full,
    box, single, single_in, outs, res, res_single, res_single_in, ssem, rsem, lsem, vsem,
):
    t = Torus()
    vectors = ((v_0, u_0), (v_1, u_1), (v_2, u_2), (v_3, u_3), (v_4, u_4), (v_5, u_5), (v_6, u_6), (v_7, u_7))
    loads = [pltpu.make_async_copy(src, dst, vsem.at[k]) for k, (src, dst) in enumerate(((tokens, tok_v),) + vectors)]
    greeting = Greeting(t.neighbours())
    each(loads, "start")
    small[...] = jnp.zeros_like(small)
    each(loads, "wait")
    for k, (_, vector) in enumerate(vectors):
        small[k : k + 1, 0 : SIZES[k]] = vector[...].astype(F32).reshape(1, SIZES[k])
    net = Net(ssem, rsem)
    sib, c = t.sibling(), t.c
    q = Gather(net, t, "qkv", w_qkv, v_qkv, 0)
    o = Gather(net, t, "out", w_out, f_out, 1)
    f = Gather(net, t, "fc", w_fc, f_fc, 0)
    p = Gather(net, t, "proj", w_proj, f_proj, 1)
    fwd = Forward(net, t, qkv, full, heads, lse, box, single, single_in, outs, res, res_single, res_single_in)
    own = pltpu.make_async_copy(w_qkv, v_qkv.at[t.x], lsem.at[0])
    own.start()
    held = [(w_out, h_out, f_out), (w_fc, h_fc, f_fc), (w_proj, h_proj, f_proj)]
    local = [pltpu.make_async_copy(s, h, lsem.at[1 + k]) for k, (s, h, _) in enumerate(held)]
    each(local, "start")
    sent = []
    greeting.wait()

    def columns(region):
        start, width = region
        cols = pl.ds(pl.multiple_of(start, 128), width)
        made = dot(normed[...].reshape(512, 1280), v_qkv[:, :, cols].reshape(1280, width)) + bias[0:1, cols]
        made = made.astype(BF16)
        qkv[:, cols] = made[:256]
        other[:, cols] = made[256:]
        sent.append(net.send(other.at[:, cols], qkv.at[:, cols], sib))

    q.start()
    p.start()
    smalls = net.group(small_all.at[pl.ds(0, 3)], t.at("x", 1))
    for s in (1, 3, 2):
        smalls.send(small, small_all.at[t.x], t.at("x", s))
    small_all[t.x] = small[...]
    o.start()
    q.start_alone()
    q.spread(0)
    o.start_alone()
    q.spread(1)
    p.spread(0)
    q.widen(0)
    f.start()
    q.widen(1)
    smalls.wait_recv()
    hat, _ = norm(tok_v[...].astype(F32))
    gain, shift = whole_vector(small_all, "ln1_gain"), whole_vector(small_all, "ln1_bias")
    normed[0] = (hat * gain + shift).astype(BF16)
    swapped = net.send(normed.at[0], normed.at[1], sib)
    p.spread(1)
    o.alone_on()
    q.alone_on()
    for n, (_, h, full_w) in enumerate(held):
        local[n].wait()
        local[n] = pltpu.make_async_copy(h, full_w.at[t.x], lsem.at[1 + n])
        local[n].start()
    p.widen(0)
    p.start_alone()
    f.start_alone()
    o.spread(0)
    q.alone_end()
    q.pass_on(1)
    f.spread(0)
    q.pass_on(0)
    o.widen(0)
    f.spread(1)
    q.share(0)
    p.widen(1)
    k = VECTORS.index("qv_bias")
    for n in (0, 1, 4, 5):
        row = small_all[n if n < 2 else n - 2, k : k + 1, :640]
        bias[0:1, 640 * n : 640 * (n + 1)] = row
    bias[0:1, 1280:2560] = jnp.zeros((1, 1280), F32)
    f_small[...] = small_all[...]
    swapped.wait_recv()
    q.share(1)
    p.alone_on()
    o.alone_end()
    q.arrive(1)
    own.wait()
    columns(q.regions[1][1:])
    columns(q.alone)
    q.arrive(0)
    q.alone_share()
    f.alone_on()
    columns(q.regions[0][1:])
    f.widen(0)
    o.pass_on(0)
    p.alone_end()
    q.share_last(1)
    wait_all(sent)
    fwd.start()
    f.widen(1)
    q.share_last(0)
    fwd.take(0)
    p.pass_on(0)
    p.pass_on(1)
    p.share(0)
    fwd.head(0, 0)
    p.alone_share()
    o.share(0)
    f.pass_on(0)
    fwd.head(1, 1)
    o.arrive(0)
    o.alone_share()
    o.share_last(0)
    fwd.give(0)
    q.finish()
    p.share(1)
    keep = pltpu.make_async_copy(v_qkv, f_qkv, lsem.at[0])
    keep.start()
    f.pass_on(1)
    f.share(1)
    fwd.take(1)
    f.alone_end()
    f.alone_share()
    f.share(0)
    fwd.head(2, 0)
    fwd.head(3, 1)
    fwd.give(1)
    fwd.take(2)
    fwd.head(4, 0)
    done = [
        pltpu.make_async_copy(src, dst, vsem.at[k])
        for k, (src, dst) in enumerate(((normed, r_normed), (heads, r_heads), (lse, r_lse)))
    ]
    each(done, "start")
    f.arrive(0)
    p.arrive(0)
    f.share_last(0)
    fwd.give(2)
    p.arrive(1)
    p.share_last(0)
    f.arrive(1)
    f.share_last(1)
    o.finish()
    p.share_last(1)
    f.finish()
    p.finish()
    fwd.finish()
    done.append(pltpu.make_async_copy(full, att, vsem.at[3]))
    done[-1].start()
    keep.wait()
    each(local + done, "wait")
    net.finish()


FRONT_SEMS = 108


def front(tokens, vectors, w_qkv, w_out, w_fc, w_proj):
    vm, anys = pl.BlockSpec(memory_space=pltpu.VMEM), pl.BlockSpec(memory_space=pl.ANY)
    weights = (w_qkv, w_out, w_fc, w_proj)
    return pl.pallas_call(
        front_kernel,
        name="front",
        out_shape=[jax.ShapeDtypeStruct((4,) + w.shape, BF16) for w in weights]
        + [
            jax.ShapeDtypeStruct((4, 8, 1280), F32),
            jax.ShapeDtypeStruct((2, 256, 1280), BF16),
            jax.ShapeDtypeStruct((256, 1280), BF16),
            jax.ShapeDtypeStruct((3, 5, 1024, 64), BF16),
            jax.ShapeDtypeStruct((1024, 128), F32),
        ],
        in_specs=[anys] * 13,
        out_specs=[anys] * 4 + [vm] + [anys] * 4,
        scratch_shapes=[
            pltpu.VMEM((2, 256, 1280), BF16),
            pltpu.VMEM((3, 5, 1024, 64), BF16),
            pltpu.VMEM((1024, 128), F32),
            pltpu.VMEM((256, 1280), BF16),
            pltpu.VMEM((8, 1280), F32),
        ]
        + [pltpu.VMEM((n,), BF16) for n in SIZES]
        + [
            pltpu.VMEM((4, 320, 3840), BF16),
            pltpu.VMEM((320, 1280), BF16),
            pltpu.VMEM((320, 5120), BF16),
            pltpu.VMEM((1280, 1280), BF16),
            pltpu.VMEM((4, 8, 1280), F32),
            pltpu.VMEM((8, 3840), F32),
            pltpu.VMEM((256, 3840), BF16),
            pltpu.VMEM((256, 3840), BF16),
            pltpu.VMEM((256, 1280), BF16),
            pltpu.VMEM((2, 3, 4, 256, 128), BF16),
            pltpu.VMEM((4, 256, 256), BF16),
            pltpu.VMEM((4, 256, 256), BF16),
            pltpu.VMEM((2, 1024, 64), BF16),
            pltpu.VMEM((4, 1, 2, 256, 128), BF16),
            pltpu.VMEM((4, 256, 128), BF16),
            pltpu.VMEM((4, 256, 128), BF16),
            pltpu.SemaphoreType.DMA((FRONT_SEMS,)),
            pltpu.SemaphoreType.DMA((FRONT_SEMS,)),
            pltpu.SemaphoreType.DMA((4,)),
            pltpu.SemaphoreType.DMA((9,)),
        ],
        compiler_params=pltpu.CompilerParams(collective_id=0, has_side_effects=True, vmem_limit_bytes=56 << 20),
    )(tokens, *vectors, *weights)


GELU_A, GELU_B = 0.7978845608028654, 0.044715
FF_STEP = 640
FF_STEPS = 8
AHEAD = 2


def mlp_kernel(
    tokens, att, cot, small, w_out, w_fc, w_proj,
    block_out, grad_mid, datt, n2t_c, attt_c, cot_c, actt_c, gp_c, gb_c, small_c,
    tok_v, att_v, cot_v, small_v, wo_v, wf_v, wp_v, n2, middle, out_acc, grad_acc, bias, sums, n2t, attt, actt, gp, gb,
    datt_v, block_v, small_grad, isem, fsem, psem, ssem, rsem, lsem,
):
    t = Torus()
    sib, c = t.sibling(), t.c
    low, high = pl.ds(0, 256), pl.ds(256, 256)
    moves = ((att, att_v), (w_out, wo_v), (tokens, tok_v), (small, small_v), (cot, cot_v))
    loads = [pltpu.make_async_copy(src, dst, isem.at[k]) for k, (src, dst) in enumerate(moves)]
    each(loads, "start")

    def load(j):
        cols = pl.ds(pl.multiple_of(j * FF_STEP, 128), FF_STEP)
        return (
            pltpu.make_async_copy(w_fc.at[:, cols], wf_v.at[j], fsem.at[j]),
            pltpu.make_async_copy(w_proj.at[cols], wp_v.at[j], psem.at[j]),
        )

    for j in range(AHEAD):
        each(load(j), "start")
    greeting = Greeting([sib])

    def keep(k, src, dst):
        return pltpu.make_async_copy(src, dst, lsem.at[k])

    def give(k, src, dst):
        return pltpu.make_async_remote_copy(
            src_ref=src, dst_ref=dst, send_sem=ssem.at[k], recv_sem=rsem.at[k], device_id=sib, device_id_type=MESH
        )

    half = [pl.ds(pl.multiple_of(k * 640, 128), 640) for k in (c, 1 - c)]
    whole = [
        (keep(0, n2t, n2t_c.at[:, low]), give(0, n2t, n2t_c.at[:, high])),
        (keep(1, attt, attt_c.at[:, low]), give(1, attt, attt_c.at[:, high])),
        (keep(2, cot_v, cot_c.at[low]), give(2, cot_v, cot_c.at[high])),
        (keep(3, gb.at[:, half[0]], gb_c.at[low]), give(3, gb.at[:, half[1]], gb_c.at[high])),
        (keep(4, small_grad, small_c.at[0]), give(4, small_grad, small_c.at[1])),
    ]

    def strip(s, kept):
        n = 2 * s + (c if kept else 1 - c)
        rows = pl.ds(pl.multiple_of(s * 640, 16), 640)
        if kept:
            return [
                keep(5 + s, actt.at[n], actt_c.at[rows, low]),
                keep(9 + s, gp.at[n], gp_c.at[s, low]),
            ]
        return [
            give(5 + s, actt.at[n], actt_c.at[rows, high]),
            give(9 + s, gp.at[n], gp_c.at[s, high]),
        ]

    each(loads[:4], "wait")
    mid = tok_v[...].astype(F32) + dot(att_v[...], wo_v[...]) + whole_vector(small_v, "out_bias")
    middle[...] = mid
    hat, _ = norm(mid)
    n2[...] = (hat * whole_vector(small_v, "ln2_gain") + whole_vector(small_v, "ln2_bias")).astype(BF16)
    out_acc[...] = mid + whole_vector(small_v, "proj_bias")
    grad_acc[...] = jnp.zeros_like(grad_acc)
    k = VECTORS.index("fc_bias")
    for n in range(FF_STEPS):
        bias[n, 0:1, :] = small_v[n // 2, k : k + 1, 640 * (n % 2) : 640 * (n % 2 + 1)]
    greeting.wait()
    loads[4].wait()
    each(whole[2], "start")
    n2t[...] = n2[...].T
    each(whole[0], "start")

    def chunk(j, _):
        @pl.when(j + AHEAD < FF_STEPS)
        def _():
            each(load(j + AHEAD), "start")

        each(load(j), "wait")
        pre = dot(n2[...], wf_v[j]) + bias[j, 0:1, :]
        square = pre * pre
        bend = jnp.tanh(GELU_A * (pre + GELU_B * pre * square))
        act = (0.5 * pre * (1.0 + bend)).astype(BF16)
        actt[j] = act.T
        out_acc[...] += dot(act, wp_v[j])
        slope = 0.5 * (1.0 + bend) + (0.5 * GELU_A) * pre * (1.0 - bend * bend) * (1.0 + 3.0 * GELU_B * square)
        grad = (dot_t(cot_v[...], wp_v[j]) * slope).astype(BF16)
        gp[j] = grad
        grad_acc[...] += dot_t(grad, wf_v[j])
        sums[j, 0:1, :] = jnp.sum(grad.astype(F32), axis=0, keepdims=True)

        @pl.when(lax.rem(j, 2) == c)
        def _():
            each(strip(j // 2, True), "start")

        @pl.when(lax.rem(j, 2) != c)
        def _():
            each(strip(j // 2, False), "start")

        return 0

    lax.fori_loop(0, FF_STEPS, chunk, 0)
    hat, scale = norm(middle[...])
    g = grad_acc[...]
    cot_rows = cot_v[...].astype(F32)
    mid = cot_rows + norm_back(g, hat, scale, whole_vector(small_v, "ln2_gain"))
    branch = mid.astype(BF16)
    gb[...] = branch
    each(whole[3], "start")
    small_grad[0:1, :] = jnp.sum(g * hat, axis=0, keepdims=True)
    small_grad[1:2, :] = jnp.sum(g, axis=0, keepdims=True)
    small_grad[2:3, :] = jnp.sum(cot_rows, axis=0, keepdims=True)
    small_grad[3:4, :] = jnp.sum(branch.astype(F32), axis=0, keepdims=True)
    for n in range(FF_STEPS):
        small_grad[4 + n // 2 : 5 + n // 2, 640 * (n % 2) : 640 * (n % 2 + 1)] = sums[n, 0:1, :]
    each(whole[4], "start")
    middle[...] = mid
    block_v[...] = out_acc[...].astype(BF16)
    results = [keep(13, middle, grad_mid), keep(14, block_v, block_out)]
    each(results, "start")
    attt[...] = att_v[...].T
    each(whole[1], "start")
    datt_v[...] = dot_t(branch, wo_v[...]).astype(BF16)
    results.append(keep(15, datt_v, datt))
    results[-1].start()
    for own, other in whole:
        own.wait()
        other.wait()
    for s in range(4):
        each(strip(s, True) + strip(s, False), "wait")
    each(results, "wait")


def mlp(tokens, att, cot, small, w_out, w_fc, w_proj):
    anys = pl.BlockSpec(memory_space=pl.ANY)
    return pl.pallas_call(
        mlp_kernel,
        name="mlp",
        out_shape=[
            jax.ShapeDtypeStruct((256, 1280), BF16),
            jax.ShapeDtypeStruct((256, 1280), F32),
            jax.ShapeDtypeStruct((256, 1280), BF16),
            jax.ShapeDtypeStruct((1280, 512), BF16),
            jax.ShapeDtypeStruct((1280, 512), BF16),
            jax.ShapeDtypeStruct((512, 1280), BF16),
            jax.ShapeDtypeStruct((2560, 512), BF16),
            jax.ShapeDtypeStruct((4, 512, 640), BF16),
            jax.ShapeDtypeStruct((512, 640), BF16),
            jax.ShapeDtypeStruct((2, 8, 1280), F32),
        ],
        in_specs=[anys] * 7,
        out_specs=[anys] * 10,
        scratch_shapes=[pltpu.VMEM((256, 1280), BF16)] * 3
        + [
            pltpu.VMEM((4, 8, 1280), F32),
            pltpu.VMEM((1280, 1280), BF16),
            pltpu.VMEM((FF_STEPS, 1280, FF_STEP), BF16),
            pltpu.VMEM((FF_STEPS, FF_STEP, 1280), BF16),
            pltpu.VMEM((256, 1280), BF16),
            pltpu.VMEM((256, 1280), F32),
            pltpu.VMEM((256, 1280), F32),
            pltpu.VMEM((256, 1280), F32),
            pltpu.VMEM((FF_STEPS, 8, FF_STEP), F32),
            pltpu.VMEM((FF_STEPS, 8, FF_STEP), F32),
            pltpu.VMEM((1280, 256), BF16),
            pltpu.VMEM((1280, 256), BF16),
            pltpu.VMEM((FF_STEPS, FF_STEP, 256), BF16),
            pltpu.VMEM((FF_STEPS, 256, FF_STEP), BF16),
            pltpu.VMEM((256, 1280), BF16),
            pltpu.VMEM((256, 1280), BF16),
            pltpu.VMEM((256, 1280), BF16),
            pltpu.VMEM((8, 1280), F32),
            pltpu.SemaphoreType.DMA((5,)),
            pltpu.SemaphoreType.DMA((FF_STEPS,)),
            pltpu.SemaphoreType.DMA((FF_STEPS,)),
            pltpu.SemaphoreType.DMA((13,)),
            pltpu.SemaphoreType.DMA((13,)),
            pltpu.SemaphoreType.DMA((16,)),
        ],
        compiler_params=pltpu.CompilerParams(collective_id=3, has_side_effects=True, vmem_limit_bytes=60 << 20),
    )(tokens, att, cot, small, w_out, w_fc, w_proj)


def view(ref, axes, chosen, rows):
    return ref.at[tuple(chosen.get(a, slice(None)) for a in axes) + (pl.ds(*rows),)]


def leading(ref):
    return ref.shape[:-2]


def add_into(dst, *srcs):
    lead = leading(dst)
    count = 1
    for n in lead:
        count *= n

    def slab(i):
        index = []
        for n in reversed(lead):
            index.append(lax.rem(i, n))
            i = i // n
        return tuple(reversed(index))

    def body(i, _):
        at = slab(i)
        total = dst[at].astype(F32)
        for s in srcs:
            total = total + s[at].astype(F32)
        dst[at] = total.astype(BF16)
        return 0

    if count == 1 and not lead:
        total = dst[...].astype(F32)
        for s in srcs:
            total = total + s[...].astype(F32)
        dst[...] = total.astype(BF16)
    else:
        lax.fori_loop(0, count, body, 0)


def inbox_shapes(classes, phases):
    out = []
    for order, _, n in classes:
        if 0 in phases:
            half = [2 if a == order[1] else 4 for a in "xyz" if a != order[0]]
            out += [half + [n, 128]] * 2 + [[4, 4, n, 128]] * 2
        if 1 in phases:
            out += [[2, n, 128]] * 2 + [[4, n, 128]] * 2
        if 2 in phases:
            out += [[3, n, 128]]
    return [pltpu.VMEM(tuple(s), BF16) for s in out]


def inboxes(refs, phases):
    refs, out = list(refs), []
    while refs:
        mine = {}
        for phase in phases:
            n = 1 if phase == 2 else 4
            mine[phase], refs = refs[:n], refs[n:]
        out.append(mine)
    return out


class Lane:
    def __init__(self, net, torus, acc, axes, inbox, order, row, n):
        self.net, self.t, self.acc, self.axes, self.inbox, self.order = net, torus, acc, axes, inbox, order
        self.rows, self.base = (row, n), 0
        self.fixed = {}
        self.got = {}

    def part(self, phase):
        axis = self.order[phase]
        return view(self.acc, self.axes, {**self.fixed, axis: self.t.pos(axis)}, self.rows)

    def held(self):
        return view(self.acc, self.axes, self.fixed, self.rows)

    def halves(self, phase):
        a = self.order[phase + 1]
        return [{a: pl.ds(0, 2)}, {a: pl.ds(2, 2)}]

    def box_half(self, box, phase, half):
        if phase == 1:
            return box.at[pl.ds(2 * half, 2)]
        left = [a for a in "xyz" if a != self.order[0]]
        cut = left.index(self.order[1])
        return box.at[(slice(None),) * cut + (pl.ds(2 * half, 2),)]

    def first(self, phase):
        axis = self.order[phase]
        p = self.t.pos(axis)
        h = self.halves(phase)
        b = self.inbox[phase]
        at = lambda shift, cut: view(self.acc, self.axes, {**self.fixed, axis: wrap(p + shift), **cut}, self.rows)
        up, down = self.t.at(axis, 1), self.t.at(axis, 3)
        far = [self.net.send(at(2, h[0]), b[0], up), self.net.send(at(2, h[1]), b[1], down)]
        near = [self.net.group(b[2], up), self.net.group(b[3], down)]
        near[0].send(at(1, h[1]), self.box_half(b[2], phase, 1), up)
        near[1].send(at(3, h[0]), self.box_half(b[3], phase, 0), down)
        self.got[phase] = (far, near)

    def second(self, phase, side):
        axis = self.order[phase]
        p = self.t.pos(axis)
        b = self.inbox[phase]
        far, near = self.got[phase]
        step = 3 if side else 1
        chosen = {**self.fixed, axis: wrap(p + step), **self.halves(phase)[side]}
        here = view(self.acc, self.axes, chosen, self.rows)
        far[side].wait_recv()
        add_into(here, b[side])
        near[side].send(here, self.box_half(b[2 + side], phase, side), self.t.at(axis, step))

    def third(self, phase):
        axis = self.order[phase]
        p = self.t.pos(axis)
        b = self.inbox[phase]
        for copy in self.got[phase][1]:
            copy.wait_recv()
        self.fixed[axis] = p
        add_into(self.held(), b[2], b[3])

    def last(self):
        axis = self.order[2]
        p = self.t.pos(axis)
        box = self.inbox[2][0]
        self.got[2] = self.net.group(box, self.t.at(axis, 1))
        for s in (1, 3, 2):
            there = view(self.acc, self.axes, {**self.fixed, axis: wrap(p + s)}, self.rows)
            self.got[2].send(there, box.at[s - 1], self.t.at(axis, s))

    def done(self):
        axis = self.order[2]
        self.got[2].wait_recv()
        self.fixed[axis] = self.t.pos(axis)
        box = self.inbox[2][0]
        add_into(self.held(), box.at[0], box.at[1], box.at[2])


class Spread:
    def __init__(self, lane, out, result, order, row, n, sem):
        self.result = result
        self.net, self.t, self.out, self.order, self.rows, self.sem = lane.net, lane.t, out, order, (row, n), sem
        chosen = {a: lane.t.pos(a) for a in lane.axes}
        self.own = view(lane.acc, lane.axes, chosen, (row - lane.base, n))

    def place(self, y, z):
        return self.out.at[self.t.c, y, z, pl.ds(*self.rows)]

    def band(self, v, b=slice(None)):
        y, z = (b, v) if self.order == "yz" else (v, b)
        return self.place(y, z)

    def start(self):
        t = self.t
        here = self.place(t.y, t.z)
        self.keep = pltpu.make_async_copy(self.own, here, self.sem)
        self.keep.start()
        self.first = self.net.group(self.band(0, pl.ds(0, 3)), t.at(self.order[0], 1))
        for s in (1, 3, 2):
            self.first.send(self.own, here, t.at(self.order[0], s))

    def second(self):
        t, axis = self.t, self.order[1]
        self.first.wait_recv()
        self.keep.wait()
        here = self.band(t.pos(axis))
        self.near = [self.net.send(here, here, t.at(axis, s)) for s in (1, 3)]

    def third(self):
        t, axis = self.t, self.order[1]
        p = t.pos(axis)
        self.far = self.net.group(self.band(p), t.at(axis, 1))
        for copy, shift, to, b in ((self.near[0], 3, 1, pl.ds(0, 2)), (self.near[1], 1, 3, pl.ds(2, 2))):
            copy.wait_recv()
            there = self.band(wrap(p + shift), b)
            self.far.send(there, there, t.at(axis, to))

    def share(self):
        self.far.wait_recv()
        whole = self.place(slice(None), slice(None))
        self.core = self.net.send(whole, whole, self.t.sibling())

    def finish(self):
        self.core.wait_recv()
        rows = (slice(None),) * 3 + (pl.ds(*self.rows),)
        self.keep = pltpu.make_async_copy(self.out.at[rows], self.result.at[rows], self.sem)
        self.keep.start()

    def end(self):
        self.keep.wait()


GROUPS = {
    "mlp": ((352, 304, 144), 16, ("yxz", "zyx", "xzy")),
    "attn": ((128, 144, 128), 0, ("yxz", "zxy", "xyz")),
}
SMALL_ROWS = 16


def slab_rows(group):
    return sum(GROUPS[group][0]) + SMALL_ROWS


def classes_of(group):
    rows, extra, orders = GROUPS[group]
    row, out = 0, []
    for k, (order, n) in enumerate(zip(orders, rows)):
        n += extra if k == 2 else 0
        out.append((order, row, n))
        row += n
    return out


def spreads_of(group):
    a, b, c = classes_of(group)
    h = c[2] // 32 * 16
    return [(0, "yz", a[1], a[2]), (1, "zy", b[1], b[2]), (2, "yz", c[1], h), (2, "zy", c[1] + h, c[2] - h)]


def pieces_of(group, first, count):
    rows, out, flat, row = GROUPS[group][0], [], 0, 0
    for n in rows:
        for slab in range(16):
            lo, hi = max(first, flat), min(first + count, flat + n)
            if lo < hi:
                out.append((slab, row + lo - flat, hi - lo, lo - first))
            flat += n
        row += n
    return out


def store_blocks(acc, group, x, first, blocks):
    for k, block in enumerate(blocks):
        for slab, row, n, offset in pieces_of(group, first + 320 * k, 320):
            acc[x, slab // 4, slab % 4, pl.ds(row, n), :] = block[offset : offset + n]


def spreads_for(group, lanes, out, result, sems):
    return [Spread(lanes[k], out, result, order, row, n, sems.at[i]) for i, (k, order, row, n) in enumerate(spreads_of(group))]


def row_pieces(ref, row, start, n):
    v = ref[row : row + 1, start : start + n]
    if n % 128:
        v = jnp.concatenate([v, jnp.zeros((1, 128 - n % 128), F32)], axis=1)
    return [v[:, 128 * k : 128 * (k + 1)] for k in range(v.shape[1] // 128)]


def store_small(acc, row, slabs):
    for x in range(4):
        filled = slabs(x)
        for k in range(16):
            pieces = filled[k] if k < len(filled) else []
            if len(pieces) < 16:
                pieces = pieces + [jnp.zeros((16 - len(pieces), 128), F32)]
            acc[x, k // 4, k % 4, pl.ds(row, 16), :] = jnp.concatenate(pieces, axis=0).astype(BF16)


def store_product(lhs, rhs, acc, group, places):
    out = dot(lhs, rhs).astype(BF16)
    for k, (x, chunk) in enumerate(places):
        rows = out[320 * k : 320 * (k + 1)]
        store_blocks(acc, group, x, 1600 * chunk, [rows[:, 128 * t : 128 * (t + 1)] for t in range(5)])


class Backward:
    def __init__(self, net, torus, datt, full, heads, lse, box, single, single_in, do, dkv, grads, res, res_single, res_single_in):
        self.net, self.t, self.datt, self.full, self.heads, self.lse = net, torus, datt, full, heads, lse
        self.box, self.single, self.single_in, self.do, self.dkv, self.grads = box, single, single_in, do, dkv, grads
        self.res, self.res_single, self.res_single_in = res, res_single, res_single_in
        self.swap, self.back = Swap(net, torus, 1), Swap(net, torus, 3)
        self.sent = []

    def start(self):
        t, swap = self.t, self.swap
        self.got = swap.out_pairs(self.datt, self.box)
        swap.pack_single(self.datt, self.single)
        self.got_single = swap.out_single(self.single, self.single_in)
        swap.keep_pairs(self.datt, self.box)
        self.single_in[t.x] = self.single[t.x]

    def take(self, p):
        (self.got[p] if p < 2 else self.got_single).wait_recv()
        for s in range(4):
            rows = slice(256 * s, 256 * (s + 1))
            if p < 2:
                for j in range(2):
                    self.do[2 * p + j, rows, :] = self.box[p, 0, s, :, 64 * j : 64 * j + 64]
            else:
                self.do[4, rows, :] = self.single_in[s, :, :64]

    def head(self, h, j):
        heads, grads, dkv = self.heads, self.grads, self.dkv
        lane = lax.broadcasted_iota(jnp.int32, (256, 128), 1)
        dkv[...] = jnp.zeros_like(dkv)
        for i in range(4):
            rows = slice(256 * i, 256 * (i + 1))
            n = 256 * (i + 1)
            q, k, v, d = heads[0, h, rows, :], heads[1, h, :n, :], heads[2, h, :n, :], self.do[h, rows, :]
            total = jnp.sum(jnp.where(lane == h, self.lse[rows, :], 0.0), axis=1, keepdims=True)
            p = jnp.exp(causal(dot_t(q, k), i) - total)
            t1 = p * dot_t(d, v)
            inner = jnp.sum(t1, axis=1, keepdims=True)
            ds = (t1 - p * inner).astype(BF16)
            grads[0, j, rows, :] = (dot(ds, k) * 0.125).astype(BF16)
            dkv[0, :, :n] += dot(q.T, ds)
            dkv[1, :, :n] += dot(d.T, p.astype(BF16))
        for k in range(2):
            grads[1 + k, j] = dkv[k].T.astype(BF16)

    def give(self, p):
        grads, back = self.grads, self.back
        for i in range(4):
            rows = slice(256 * i, 256 * (i + 1))
            if p < 2:
                for k in range(3):
                    self.res[i, k, p] = jnp.concatenate([grads[k, 0, rows, :], grads[k, 1, rows, :]], axis=1)
            else:
                cols = [grads[k, 0, rows, :] for k in range(3)] + [jnp.zeros((256, 64), BF16)]
                self.res_single[i] = jnp.concatenate(cols, axis=1)
        if p < 2:
            self.sent.append(back.back_pair(p, self.res, self.full))
            back.keep_back(p, self.res, self.full)
        else:
            self.sent_single = back.out_single(self.res_single, self.res_single_in)
            self.res_single_in[self.t.x] = self.res_single[self.t.x]

    def finish(self):
        self.sent_single.wait_recv()
        self.back.unpack_single(self.res_single_in, self.full)
        wait_all(self.sent)


def back_kernel(
    r_datt, r_heads, r_lse, r_small, n2t, actt, gp, cot,
    gqkv, part_0, part_1, part_2,
    datt, heads, lse, small, n2t_v, actt_v, gp_v, cot_v, small_v, full,
    box, single, single_in, do, dkv, grads, res, res_single, res_single_in,
    ssem, rsem, lsem, acc, *inbox,
):
    t = Torus()
    moves = ((n2t, n2t_v), (gp, gp_v), (r_datt, datt), (r_small, small), (actt, actt_v), (cot, cot_v), (r_heads, heads), (r_lse, lse))
    loads = [pltpu.make_async_copy(src, dst, lsem.at[k]) for k, (src, dst) in enumerate(moves)]
    soon, later = loads[:4], loads[4:]
    each(soon, "start")
    greeting = Greeting(t.neighbours())
    net = Net(ssem, rsem)
    bwd = Backward(net, t, datt, full, heads, lse, box, single, single_in, do, dkv, grads, res, res_single, res_single_in)
    lanes = [Lane(net, t, acc, "xyz", box_of, *k) for k, box_of in zip(classes_of("mlp"), inboxes(inbox, (0,)))]
    parts = [pltpu.make_async_copy(lane.part(0), part, lsem.at[k]) for k, (lane, part) in enumerate(zip(lanes, (part_0, part_1, part_2)))]

    def fc(s):
        store_product(n2t_v[...], gp_v[s], acc, "mlp", [(x, s) for x in range(4)])

    def proj(half):
        def body(x, _):
            lhs = actt_v[pl.ds(pl.multiple_of(x * 640, 16), 640), :]
            places = [(x, 4 + 2 * half), (x, 5 + 2 * half)]
            store_product(lhs, cot_v[:, 640 * half : 640 * (half + 1)], acc, "mlp", places)
            return 0

        lax.fori_loop(0, 4, body, 0)

    def sums():
        small_v[...] = small[0] + small[1]
        store_small(
            acc, 800,
            lambda x: [
                [row for k in range(4) for row in row_pieces(small_v, k, 320 * x, 320)],
                row_pieces(small_v, 4 + x, 0, 1280),
            ],
        )

    each(soon, "wait")
    each(later, "start")
    fc(2)
    fc(3)
    greeting.wait()
    bwd.start()
    fc(1)
    each(later, "wait")
    fc(0)
    lanes[0].first(0)
    proj(1)
    sums()
    lanes[2].first(0)
    proj(0)
    lanes[1].first(0)
    bwd.take(0)
    bwd.head(0, 0)
    lanes[2].second(0, 1)
    bwd.head(1, 1)
    bwd.give(0)
    bwd.take(1)
    lanes[1].second(0, 1)
    lanes[2].second(0, 0)
    bwd.head(2, 0)
    lanes[0].second(0, 0)
    lanes[1].second(0, 0)
    bwd.head(3, 1)
    bwd.give(1)
    lanes[0].second(0, 1)
    bwd.take(2)
    lanes[2].third(0)
    bwd.head(4, 0)
    bwd.give(2)
    lanes[1].third(0)
    parts[2].start()
    lanes[0].third(0)
    parts[0].start()
    parts[1].start()
    bwd.finish()
    gqkv[...] = full[...]
    each(parts, "wait")
    net.finish()


BACK_SEMS = 18


def backward(datt, heads, lse, small, n2t, actt, gp, cot):
    vm, anys = pl.BlockSpec(memory_space=pltpu.VMEM), pl.BlockSpec(memory_space=pl.ANY)
    classes = classes_of("mlp")
    return pl.pallas_call(
        back_kernel,
        name="backward",
        out_shape=[jax.ShapeDtypeStruct((256, 3840), BF16)]
        + [jax.ShapeDtypeStruct((4, 4, n, 128), BF16) for _, _, n in classes],
        in_specs=[anys] * 8,
        out_specs=[vm] + [anys] * 3,
        scratch_shapes=[
            pltpu.VMEM((256, 1280), BF16),
            pltpu.VMEM((3, 5, 1024, 64), BF16),
            pltpu.VMEM((1024, 128), F32),
            pltpu.VMEM((2, 8, 1280), F32),
            pltpu.VMEM((1280, 512), BF16),
            pltpu.VMEM((2560, 512), BF16),
            pltpu.VMEM((4, 512, 640), BF16),
            pltpu.VMEM((512, 1280), BF16),
            pltpu.VMEM((8, 1280), F32),
            pltpu.VMEM((256, 3840), BF16),
            pltpu.VMEM((2, 1, 4, 256, 128), BF16),
            pltpu.VMEM((4, 256, 128), BF16),
            pltpu.VMEM((4, 256, 128), BF16),
            pltpu.VMEM((5, 1024, 64), BF16),
            pltpu.VMEM((2, 64, 1024), F32),
            pltpu.VMEM((3, 2, 1024, 64), BF16),
            pltpu.VMEM((4, 3, 2, 256, 128), BF16),
            pltpu.VMEM((4, 256, 256), BF16),
            pltpu.VMEM((4, 256, 256), BF16),
            pltpu.SemaphoreType.DMA((BACK_SEMS,)),
            pltpu.SemaphoreType.DMA((BACK_SEMS,)),
            pltpu.SemaphoreType.DMA((8,)),
            pltpu.VMEM((4, 4, 4, slab_rows("mlp"), 128), BF16),
        ]
        + inbox_shapes(classes, (0,)),
        compiler_params=pltpu.CompilerParams(collective_id=1, has_side_effects=True, vmem_limit_bytes=60 << 20),
    )(datt, heads, lse, small, n2t, actt, gp, cot)


def last_kernel(
    n1, r_gqkv, attt, gb, w_qkv, r_tokens, r_mid, r_small, part_0, part_1, part_2,
    r_mlp, r_attn, r_grad,
    out_mlp, out_attn, grad_tokens, gqkv, tokens, grad_mid, small_all, n1_v, n1t, gqkv_v, attt_v, gb_v, w_v, small_v, ssem, rsem, lsem, acc, acc_small, held_0, held_1, held_2, *inbox,
):
    t = Torus()
    helds = (held_0, held_1, held_2)
    moves = [(n1, n1_v), (attt, attt_v), (gb, gb_v), (w_qkv, w_v)] + [*zip((part_0, part_1, part_2), helds)]
    moves += [(r_gqkv, gqkv), (r_tokens, tokens), (r_mid, grad_mid), (r_small, small_all)]
    n1_in, att_in, gb_in, w_in, *rest = [
        pltpu.make_async_copy(src, dst, lsem.at[k]) for k, (src, dst) in enumerate(moves)
    ]
    parts_in, rows_in = rest[:3], rest[3:]
    soon, later = rows_in[:1] + [n1_in] + parts_in, [att_in, gb_in] + rows_in[1:] + [w_in]
    each(soon, "start")
    greeting = Greeting(t.neighbours())
    net = Net(ssem, rsem)
    sib, c = t.sibling(), t.c
    m, a = [], []
    boxes = inboxes(inbox[:15], (1, 2))
    for held, box_of, (order, row, n) in zip(helds, boxes, classes_of("mlp")):
        lane = Lane(net, t, held, "".join(v for v in "xyz" if v != order[0]), box_of, order, 0, n)
        lane.base = row
        m.append(lane)
    boxes = inboxes(inbox[15:], (0, 1, 2))
    for box_of, k in zip(boxes, classes_of("attn")):
        a.append(Lane(net, t, acc, "xyz", box_of, *k))
    tiny = Lane(net, t, acc_small, "xyz", boxes[3], "yzx", 0, SMALL_ROWS)
    tiny.base = 400
    ms = spreads_for("mlp", m, out_mlp, r_mlp, lsem.at[pl.ds(11, 4)])
    sp = spreads_for("attn", a, out_attn, r_attn, lsem.at[pl.ds(15, 4)])
    ts = Spread(tiny, out_attn, r_attn, "zy", 400, SMALL_ROWS, lsem.at[19])
    got = {}

    def own():
        rows_in[0].wait()
        for s in range(3):
            gqkv_v[s, 0:256] = gqkv[:, pl.ds(pl.multiple_of(c * 1920 + s * 640, 128), 640)]

    def swap():
        for s in range(3):
            theirs = pl.ds(pl.multiple_of((1 - c) * 1920 + s * 640, 128), 640)
            got[s] = net.send(gqkv.at[:, theirs], gqkv_v.at[s, pl.ds(256, 256)], sib)

    def turn():
        n1_in.wait()
        n1t[:, 0:256] = n1_v[0].T
        n1t[:, 256:512] = n1_v[1].T

    def qkv(s):
        got[s].wait_recv()
        store_product(n1t[...], gqkv_v[s], acc, "attn", [(x, s) for x in range(4)])

    def outp():
        att_in.wait()
        gb_in.wait()
        store_product(attt_v[...], gb_v[...], acc, "attn", [(x, 3) for x in range(4)])

    def rows_back():
        w_in.wait()
        each(rows_in[1:], "wait")

        def body(n, total):
            cols = pl.ds(pl.multiple_of(n * 640, 128), 640)
            return total + dot_t(gqkv[:, cols], w_v[:, cols])

        grad = lax.fori_loop(0, 6, body, jnp.zeros((256, 1280), F32))
        hat, scale = norm(tokens[...].astype(F32))
        grad_tokens[...] = (grad_mid[...] + norm_back(grad, hat, scale, whole_vector(small_all, "ln1_gain"))).astype(BF16)
        small_v[0, 0:1, :] = jnp.sum(grad * hat, axis=0, keepdims=True)
        small_v[0, 1:2, :] = jnp.sum(grad, axis=0, keepdims=True)
        small_v[0, 2:3, :] = jnp.sum(gqkv[:, :1280].astype(F32), axis=0, keepdims=True)
        small_v[0, 3:4, :] = jnp.sum(gqkv[:, 2560:].astype(F32), axis=0, keepdims=True)

    grad_out = pltpu.make_async_copy(grad_tokens, r_grad, lsem.at[20])

    def rows_out():
        grad_out.start()
        got["small"] = net.send(small_v.at[0], small_v.at[1], sib)

    def sums():
        got["small"].wait_recv()
        total = small_v.at[2]
        total[...] = small_v[0] + small_v[1]
        store_small(
            acc_small, 0,
            lambda x: [
                [row for k in range(2) for row in row_pieces(total, k, 320 * x, 320)],
                row_pieces(total, 2 + x // 2, 640 * (x % 2), 640),
            ],
        )

    own()
    each(later, "start")
    each(parts_in, "wait")
    greeting.wait()
    m[1].first(1)
    m[0].first(1)
    swap()
    turn()
    m[2].first(1)
    outp()
    qkv(1)
    qkv(2)
    m[1].second(1, 1)
    a[1].first(0)
    m[1].second(1, 0)
    m[0].second(1, 0)
    m[0].second(1, 1)
    qkv(0)
    a[0].first(0)
    a[2].first(0)
    m[1].third(1)
    m[2].second(1, 1)
    m[2].second(1, 0)
    m[0].third(1)
    rows_back()
    m[0].last()
    a[1].second(0, 0)
    a[1].second(0, 1)
    m[1].last()
    a[0].second(0, 0)
    a[0].second(0, 1)
    m[2].third(1)
    a[2].second(0, 1)
    rows_out()
    a[2].second(0, 0)
    m[0].done()
    m[2].last()
    ms[0].start()
    m[1].done()
    sums()
    tiny.first(0)
    a[0].third(0)
    m[2].done()
    ms[3].start()
    ms[1].start()
    a[0].first(1)
    a[1].third(0)
    a[1].first(1)
    ms[2].start()
    a[2].third(0)
    a[2].first(1)
    ms[0].second()
    tiny.second(0, 0)
    tiny.second(0, 1)
    ms[3].second()
    a[2].second(1, 0)
    a[0].second(1, 0)
    a[2].second(1, 1)
    tiny.third(0)
    a[0].second(1, 1)
    tiny.first(1)
    ms[1].second()
    a[2].third(1)
    a[1].second(1, 0)
    a[2].last()
    a[1].second(1, 1)
    a[0].third(1)
    tiny.second(1, 1)
    a[0].last()
    ms[3].third()
    tiny.second(1, 0)
    ms[2].second()
    a[1].third(1)
    a[2].done()
    a[1].last()
    sp[2].start()
    sp[3].start()
    tiny.third(1)
    a[0].done()
    ms[0].third()
    sp[0].start()
    sp[3].second()
    ms[1].third()
    a[1].done()
    sp[1].start()
    tiny.last()
    ms[2].third()
    ms[3].share()
    tiny.done()
    ms[0].share()
    ts.start()
    sp[0].second()
    sp[1].second()
    ts.second()
    sp[2].second()
    ms[1].share()
    sp[0].third()
    sp[3].third()
    ms[0].finish()
    sp[2].third()
    sp[1].third()
    ms[2].share()
    sp[3].share()
    ts.third()
    sp[0].share()
    ms[3].finish()
    sp[2].share()
    sp[1].share()
    sp[3].finish()
    sp[0].finish()
    ms[2].finish()
    ts.share()
    ms[1].finish()
    sp[2].finish()
    sp[1].finish()
    ts.finish()
    each(ms + sp + [ts], "end")
    grad_out.wait()
    net.finish()


LAST_SEMS = 100


def last(n1, gqkv, attt, gb, w_qkv, tokens, grad_mid, small_all, parts):
    anys = pl.BlockSpec(memory_space=pl.ANY)
    mlp_classes, attn_classes = classes_of("mlp"), classes_of("attn")
    return pl.pallas_call(
        last_kernel,
        name="last",
        out_shape=[jax.ShapeDtypeStruct((2, 4, 4, slab_rows(g), 128), BF16) for g in ("mlp", "attn")]
        + [jax.ShapeDtypeStruct((256, 1280), BF16)],
        in_specs=[anys] * 11,
        out_specs=[anys] * 3,
        scratch_shapes=[pltpu.VMEM((2, 4, 4, slab_rows(g), 128), BF16) for g in ("mlp", "attn")]
        + [
            pltpu.VMEM((256, 1280), BF16),
            pltpu.VMEM((256, 3840), BF16),
            pltpu.VMEM((256, 1280), BF16),
            pltpu.VMEM((256, 1280), F32),
            pltpu.VMEM((4, 8, 1280), F32),
            pltpu.VMEM((2, 256, 1280), BF16),
            pltpu.VMEM((1280, 512), BF16),
            pltpu.VMEM((3, 512, 640), BF16),
            pltpu.VMEM((1280, 512), BF16),
            pltpu.VMEM((512, 640), BF16),
            pltpu.VMEM((1280, 3840), BF16),
            pltpu.VMEM((3, 8, 1280), F32),
            pltpu.SemaphoreType.DMA((LAST_SEMS,)),
            pltpu.SemaphoreType.DMA((LAST_SEMS,)),
            pltpu.SemaphoreType.DMA((21,)),
            pltpu.VMEM((4, 4, 4, 400, 128), BF16),
            pltpu.VMEM((4, 4, 4, SMALL_ROWS, 128), BF16),
        ]
        + [pltpu.VMEM((4, 4, n, 128), BF16) for _, _, n in mlp_classes]
        + inbox_shapes(mlp_classes, (1, 2))
        + inbox_shapes(attn_classes + [("yzx", 0, SMALL_ROWS)], (0, 1, 2)),
        compiler_params=pltpu.CompilerParams(collective_id=2, has_side_effects=True, vmem_limit_bytes=60 << 20),
    )(n1, gqkv, attt, gb, w_qkv, tokens, grad_mid, small_all, *parts)


def flat_block(src, core, group, block):
    pieces = [
        src[core, slab // 4, slab % 4, row : row + n, :] for slab, row, n, _ in pieces_of(group, 320 * block, 320)
    ]
    return jnp.concatenate(pieces, axis=0).astype(F32)


SMALL_PLACES = (
    ("attn", 0, 0, 320),
    ("attn", 0, 3, 320),
    ("attn", 1, 0, 640),
    ("mlp", 0, 9, 320),
    ("mlp", 0, 0, 320),
    ("mlp", 0, 3, 320),
    ("mlp", 1, 0, 1280),
    ("mlp", 0, 6, 320),
)


def unpack_kernel(packed_mlp, packed_attn, block, grad, *refs):
    fc, proj, qkv, out, block_out, grad_out, *smalls = refs[:14]
    in_0, in_1, stage, block_v, grad_v, *rest = refs[14:]
    small_v, (in_sem, out_sem, small_sem) = rest[:8], rest[8:]
    loads = []
    for c in range(2):
        loads.append(
            [
                pltpu.make_async_copy(src.at[c], dst.at[c], in_sem.at[2 * c + k])
                for k, (src, dst) in enumerate(((packed_attn, in_1), (packed_mlp, in_0)))
            ]
        )
        each(loads[-1], "start")
    rows = [pltpu.make_async_copy(block, block_v, in_sem.at[4]), pltpu.make_async_copy(grad, grad_v, in_sem.at[5])]
    each(rows, "start")
    flying, tail = [], []
    for c in range(2):
        chunks = [(in_1, "attn", q, qkv, 0, 1920 * c + 640 * q) for q in range(3)]
        chunks += [(in_1, "attn", 3, out, 0, 640 * c)]
        chunks += [(in_0, "mlp", q, fc, 0, 1280 * q + 640 * c) for q in range(4)]
        chunks += [(in_0, "mlp", 4 + 2 * h + sub, proj, 640 * c + 320 * sub, 640 * h) for h in range(2) for sub in range(2)]
        for n, (src, group, q, dst, row, col) in enumerate(chunks):
            if n in (0, 4):
                loads[c][n // 4].wait()
            k = len(flying)
            slot = k % STAGES
            if k >= STAGES:
                flying[k - STAGES].wait()
            for t in range(5):
                stage[slot, :, 128 * t : 128 * (t + 1)] = flat_block(src, c, group, 5 * q + t)
            copy = pltpu.make_async_copy(stage.at[slot], dst.at[pl.ds(row, 320), pl.ds(col, 640)], out_sem.at[slot])
            copy.start()
            flying.append(copy)
        if c == 0:
            for k, (group, slab, row, n) in enumerate(SMALL_PLACES):
                src = in_1 if group == "attn" else in_0
                first = slab_rows(group) - SMALL_ROWS
                values = src[0, 0, slab, first : first + SMALL_ROWS, :].astype(F32)
                for i in range(0, n, 128):
                    m = min(128, n - i)
                    small_v[k][i : i + m] = values[row + i // 128, :m]
                tail.append(pltpu.make_async_copy(small_v[k], smalls[k], small_sem.at[k]))
                tail[-1].start()
            each(rows, "wait")
            tail.append(pltpu.make_async_copy(block_v, block_out, small_sem.at[8]))
            tail.append(pltpu.make_async_copy(grad_v, grad_out, small_sem.at[9]))
            each(tail[-2:], "start")
    each(flying[-STAGES:] + tail, "wait")


STAGES = 8


def unpack(packed_mlp, packed_attn, block, grad):
    anys = pl.BlockSpec(memory_space=pl.ANY)
    sizes = [n for _, _, _, n in SMALL_PLACES]
    return pl.pallas_call(
        unpack_kernel,
        name="unpack",
        out_shape=[jax.ShapeDtypeStruct(s, F32) for s in ((320, 5120), (1280, 1280), (320, 3840), (320, 1280))]
        + [jax.ShapeDtypeStruct((256, 1280), BF16)] * 2
        + [jax.ShapeDtypeStruct((n,), F32) for n in sizes],
        in_specs=[anys] * 4,
        out_specs=[anys] * 14,
        scratch_shapes=[
            pltpu.VMEM(packed_mlp.shape, BF16),
            pltpu.VMEM(packed_attn.shape, BF16),
            pltpu.VMEM((STAGES, 320, 640), F32),
            pltpu.VMEM((256, 1280), BF16),
            pltpu.VMEM((256, 1280), BF16),
        ]
        + [pltpu.VMEM((n,), F32) for n in sizes]
        + [
            pltpu.SemaphoreType.DMA((6,)),
            pltpu.SemaphoreType.DMA((STAGES,)),
            pltpu.SemaphoreType.DMA((10,)),
        ],
        compiler_params=pltpu.CompilerParams(vmem_limit_bytes=62 << 20),
    )(packed_mlp, packed_attn, block, grad)


def shards(
    tokens,
    cotangent,
    ln1_gain,
    ln1_bias,
    w_qkv,
    qv_bias,
    w_out,
    out_bias,
    ln2_gain,
    ln2_bias,
    w_fc,
    fc_bias,
    w_proj,
    proj_bias,
):
    own = (ln1_gain, ln1_bias, qv_bias, out_bias, ln2_gain, ln2_bias, proj_bias, fc_bias)
    f_qkv, f_out, f_fc, f_proj, f_small, normed_one, attended, heads, lse = front(
        tokens[0], own, w_qkv, w_out, w_fc, w_proj
    )
    f_qkv, f_out, f_fc, f_proj = (
        f_qkv.reshape(1280, 3840),
        f_out.reshape(1280, 1280),
        f_fc.reshape(1280, 5120),
        f_proj.reshape(5120, 1280),
    )
    block_out, grad_middle, grad_attended, n2t, attt, cot, actt, grad_pre, grad_branch, small_mlp = mlp(
        tokens[0], attended, cotangent[0], f_small, f_out, f_fc, f_proj
    )
    grad_qkv, *parts = backward(grad_attended, heads, lse, small_mlp, n2t, actt, grad_pre, cot)
    packed_mlp, packed_attn, grad_tokens = last(
        normed_one, grad_qkv, attt, grad_branch, f_qkv, tokens[0], grad_middle, f_small, parts
    )
    g_fc, g_proj, g_qkv, g_out, block_out, grad_tokens, *vectors = unpack(
        packed_mlp, packed_attn, block_out, grad_tokens
    )
    gain_1, bias_1, bias_qv, bias_out, gain_2, bias_2, bias_fc, bias_proj = vectors
    return (
        block_out[None],
        grad_tokens[None],
        gain_1,
        bias_1,
        g_qkv,
        bias_qv,
        g_out,
        bias_out,
        gain_2,
        bias_2,
        g_fc,
        bias_fc,
        g_proj,
        bias_proj,
    )


def solution(mesh):
    vector, matrix, batch = P("shard"), P("shard", None), P("rep", "shard", None)
    placed = (batch, batch, vector, vector, matrix, vector, matrix, vector, vector, vector, matrix, vector, matrix, vector)
    return jax.shard_map(shards, mesh=mesh, in_specs=placed, out_specs=placed, check_vma=False)
```

```python
import jax
import jax.numpy as jnp
from jax import lax
from jax.experimental import pallas as pl
from jax.experimental.pallas import tpu as pltpu
from jax.sharding import PartitionSpec as P

MESH = pl.DeviceIdType.MESH
F32, BF16 = jnp.float32, jnp.bfloat16


def where_am_i():
    rep = lax.axis_index("rep")
    return lax.axis_index("shard"), (rep // 2) % 4, rep // 8, rep % 2


def device_at(x, y, z, c):
    return {"rep": (z * 4 + y) * 2 + c, "shard": x}


def wrap(v):
    return lax.rem(v + 4, 4)


class Group:
    def __init__(self, sems, whole, target):
        self.sems = sems
        self.all = self.copy(whole, whole, target)

    def copy(self, src, dst, target):
        send_sem, recv_sem = self.sems
        return pltpu.make_async_remote_copy(
            src_ref=src, dst_ref=dst, send_sem=send_sem, recv_sem=recv_sem, device_id=target, device_id_type=MESH
        )

    def send(self, src, dst, target):
        self.copy(src, dst, target).start()

    def wait_recv(self):
        self.all.wait_recv()

    def wait_send(self):
        self.all.wait_send()


class Net:
    def __init__(self, send_sems, recv_sems):
        self.send_sems, self.recv_sems, self.groups = send_sems, recv_sems, []

    def group(self, whole, target):
        k = len(self.groups)
        self.groups.append(Group((self.send_sems.at[k], self.recv_sems.at[k]), whole, target))
        return self.groups[-1]

    def send(self, src, dst, target):
        group = self.group(dst, target)
        group.send(src, dst, target)
        return group

    def finish(self):
        for group in self.groups:
            group.wait_send()


def wait_all(copies):
    for copy in copies:
        copy.wait_recv()


def each(items, what, *rest):
    for item in items:
        getattr(item, what)(*rest)


class Greeting:
    def __init__(self, targets):
        self.barrier, self.count = pltpu.get_barrier_semaphore(), len(targets)
        for target in targets:
            pl.semaphore_signal(self.barrier, 1, device_id=target, device_id_type=MESH)

    def wait(self):
        pl.semaphore_wait(self.barrier, self.count)


class Torus:
    def __init__(self):
        self.x, self.y, self.z, self.c = where_am_i()

    def at(self, axis, step):
        x, y, z = self.x, self.y, self.z
        if axis == "x":
            x = wrap(x + step)
        elif axis == "y":
            y = wrap(y + step)
        else:
            z = wrap(z + step)
        return device_at(x, y, z, self.c)

    def pos(self, axis):
        return {"x": self.x, "y": self.y, "z": self.z}[axis]

    def sibling(self):
        return device_at(self.x, self.y, self.z, 1 - self.c)

    def neighbours(self, axes="xyz", core=True):
        out = [self.at(a, s) for a in axes for s in (1, 2, 3)]
        return out + ([self.sibling()] if core else [])


PLANS = {
    "qkv": (320, 3840, 4, 8, 3),
    "out": (320, 1280, 4, 0, 1),
    "fc": (320, 5120, 8, 8, 4),
    "proj": (1280, 1280, 2, 2, 1),
}


def rect_of(rows, start, width, order, y, z, stage):
    if rows == 320:
        if stage == 0:
            return y * 80, 80, start + z * (width // 4), width // 4
        if order == "yz":
            return 0, 320, start + z * (width // 4), width // 4
        return y * 80, 80, start, width
    first, second = (y, z) if order == "yz" else (z, y)
    if stage == 0:
        return second * 320 + first * 80, 80, start, width
    return second * 320, 320, start, width


def part(ref, owner, rect):
    r, nr, c, nc = rect
    return ref.at[owner, pl.ds(pl.multiple_of(r, 16), nr), pl.ds(pl.multiple_of(c, 128), nc)]


def parts_of(ref, count, rect):
    r, nr, c, nc = rect
    return ref.at[pl.ds(0, count), pl.ds(pl.multiple_of(r, 16), nr), pl.ds(pl.multiple_of(c, 128), nc)]


def own_part(ref, rect):
    r, nr, c, nc = rect
    return ref.at[pl.ds(pl.multiple_of(r, 16), nr), pl.ds(pl.multiple_of(c, 128), nc)]


class Gather:
    def __init__(self, net, torus, name, src, full, lean):
        self.net, self.t, self.src, self.full, self.lean = net, torus, src, full, lean
        self.rows, cols, a, b, d = PLANS[name]
        half = torus.c * (cols // 2)
        self.regions = []
        at = 0
        for order, tiles in (("yz", a), ("zy", b)):
            if tiles:
                self.regions.append((order, half + at * 128, tiles * 128))
            at += tiles
        self.alone = (half + at * 128, d * 128)
        self.others = [wrap(torus.x + k) for k in (1, 2, 3)]
        self.got = {"core": []}

    def rect(self, region, stage, shift=0):
        order, start, width = region
        y, z = self.t.y, self.t.z
        axis = order[stage]
        if axis == "y":
            y = wrap(y + shift)
        else:
            z = wrap(z + shift)
        return rect_of(self.rows, start, width, order, y, z, stage)

    def both(self, what, *rest):
        for i in range(len(self.regions)):
            getattr(self, what)(i, *rest)

    def start(self):
        t, net = self.t, self.net
        for i, region in enumerate(self.regions):
            rect = self.rect(region, 0)
            group = net.group(parts_of(self.full, 3, rect), t.at("x", 1))
            for s in (1, 3, 2):
                group.send(own_part(self.src, rect), part(self.full, t.x, rect), t.at("x", s))
            self.got[i, "x"] = group

    def start_alone(self):
        if not self.alone[1]:
            return
        t, net = self.t, self.net
        rect = (0, self.rows, *self.alone)
        self.got["alone"] = [
            net.send(own_part(self.src, rect), part(self.full, t.x, rect), t.at("x", s)) for s in (1, 3)
        ]

    def alone_on(self):
        if not self.alone[1]:
            return
        t, net = self.t, self.net
        h = self.rows // 2
        start, width = self.alone
        whole = (0, self.rows, start, width)
        left, right = wrap(t.x - 1), wrap(t.x + 1)
        on = net.group(part(self.full, left, whole), t.at("x", 1))
        for copy, owner, row, step in zip(self.got["alone"], (left, right), (0, h), (1, 3)):
            copy.wait_recv()
            half = part(self.full, owner, (row, h, start, width))
            on.send(half, half, t.at("x", step))
        self.got["alone2"] = on
        core = net.group(parts_of(self.full, 2, whole), t.sibling())
        for o in (left, right):
            core.send(part(self.full, o, whole), part(self.full, o, whole), t.sibling())
        self.got["core"].append(core)

    def alone_end(self):
        if not self.alone[1]:
            return
        self.got["alone2"].wait_recv()

    def alone_share(self):
        if not self.alone[1]:
            return
        o = wrap(self.t.x + 2)
        whole = (0, self.rows, *self.alone)
        self.got["core"].append(self.net.send(part(self.full, o, whole), part(self.full, o, whole), self.t.sibling()))

    def to_all(self, rect, target):
        group = self.net.group(parts_of(self.full, 3, rect), target)
        for o in self.others:
            group.send(part(self.full, o, rect), part(self.full, o, rect), target)
        return group

    def spread(self, i):
        region = self.regions[i]
        self.got[i, "x"].wait_recv()
        rect = self.rect(region, 0)
        self.got[i, 0] = [self.to_all(rect, self.t.at(region[0][0], s)) for s in (1, 3, 2)]

    def widen(self, i):
        region = self.regions[i]
        wait_all(self.got[i, 0])
        rect = self.rect(region, 1)
        self.got[i, 1] = [self.to_all(rect, self.t.at(region[0][1], s)) for s in (1, 3)]

    def pass_on(self, i):
        region = self.regions[i]
        axis = region[0][1]
        cut = 2 if self.lean else 1
        ahead, behind = self.got[i, 1]
        group = self.net.group(parts_of(self.full, 3, self.rect(region, 1)), self.t.at(axis, 1))
        for came, shift, to, owners in (
            (ahead, -1, 1, self.others[:cut]),
            (behind, 1, 3, self.others[cut:]),
        ):
            came.wait_recv()
            rect = self.rect(region, 1, shift)
            for o in owners:
                group.send(part(self.full, o, rect), part(self.full, o, rect), self.t.at(axis, to))
        self.got[i, 2] = group

    def to_sibling(self, region, shifts):
        for shift in shifts:
            self.got["core"].append(self.to_all(self.rect(region, 1, shift), self.t.sibling()))

    def share(self, i):
        self.to_sibling(self.regions[i], (0, -1, 1))

    def arrive(self, i):
        self.got[i, 2].wait_recv()

    def share_last(self, i):
        self.to_sibling(self.regions[i], (2,))

    def finish(self):
        wait_all(self.got["core"])


LAG = 0.5


def dot_t(a, b):
    return lax.dot_general(a, b, (((1,), (1,)), ((), ())), preferred_element_type=F32)


def causal(s, i):
    rows = lax.broadcasted_iota(jnp.int32, (256, 256), 0)
    cols = lax.broadcasted_iota(jnp.int32, (256, 256), 1)
    last = jnp.where(cols <= rows, s[:, 256 * i :], -1e30)
    return last if i == 0 else jnp.concatenate([s[:, : 256 * i], last], axis=1)


class Swap:
    def __init__(self, net, torus, parts):
        self.net, self.t, self.parts = net, torus, parts

    def pack_single(self, full, single):
        parts = self.parts
        for d in range(4):
            cols = [full[:, 1280 * k + 1024 + 64 * d : 1280 * k + 1088 + 64 * d] for k in range(parts)]
            if parts % 2:
                cols.append(jnp.zeros((256, 64), BF16))
            single[d] = jnp.concatenate(cols, axis=1)

    def out_pairs(self, full, box):
        t, net, got = self.t, self.net, []
        for p in range(2):
            group = net.group(box.at[p, :, pl.ds(0, 3)], t.at("x", 1))
            for s in (1, 3, 2):
                d = wrap(t.x + s)
                for k in range(self.parts):
                    cols = pl.ds(pl.multiple_of(1280 * k + 256 * d + 128 * p, 128), 128)
                    group.send(full.at[:, cols], box.at[p, k, t.x], t.at("x", s))
            got.append(group)
        return got

    def keep_pairs(self, full, box):
        for p in range(2):
            for k in range(self.parts):
                cols = pl.ds(pl.multiple_of(1280 * k + 256 * self.t.x + 128 * p, 128), 128)
                box[p, k, self.t.x] = full[:, cols]

    def out_single(self, single, box):
        t = self.t
        group = self.net.group(box.at[pl.ds(0, 3)], t.at("x", 1))
        for s in (1, 3, 2):
            group.send(single.at[wrap(t.x + s)], box.at[t.x], t.at("x", s))
        return group

    def back_pair(self, p, src, full):
        t = self.t
        group = self.net.group(src.at[pl.ds(0, 3), :, p], t.at("x", 1))
        for s in (1, 3, 2):
            d = wrap(t.x + s)
            for k in range(self.parts):
                cols = pl.ds(pl.multiple_of(1280 * k + 256 * t.x + 128 * p, 128), 128)
                group.send(src.at[d, k, p], full.at[:, cols], t.at("x", s))
        return group

    def keep_back(self, p, src, full):
        for k in range(self.parts):
            cols = pl.ds(pl.multiple_of(1280 * k + 256 * self.t.x + 128 * p, 128), 128)
            full[:, cols] = src[self.t.x, k, p]

    def unpack_single(self, box, full):
        for k in range(self.parts):
            cols = [box[d, :, 64 * k : 64 * k + 64] for d in range(4)]
            full[:, 1280 * k + 1024 : 1280 * (k + 1)] = jnp.concatenate(cols, axis=1)


EPS = 1e-05
VECTORS = ("ln1_gain", "ln1_bias", "qv_bias", "out_bias", "ln2_gain", "ln2_bias", "proj_bias", "fc_bias")
SIZES = (320, 320, 640, 320, 320, 320, 320, 1280)


def whole_vector(small, name):
    k = VECTORS.index(name)
    return jnp.concatenate([small[x, k : k + 1, : SIZES[k]] for x in range(4)], axis=1)


def dot(a, b):
    return jnp.dot(a, b, preferred_element_type=F32)


def norm(v):
    center = v - jnp.mean(v, axis=-1, keepdims=True)
    scale = lax.rsqrt(jnp.mean(center * center, axis=-1, keepdims=True) + EPS)
    return center * scale, scale


def norm_back(grad, hat, scale, gain):
    inner = grad * gain
    return scale * (
        inner - jnp.mean(inner, axis=-1, keepdims=True) - hat * jnp.mean(inner * hat, axis=-1, keepdims=True)
    )


class Forward:
    def __init__(self, net, torus, qkv, full, heads, lse, box, single, single_in, outs, res, res_single, res_single_in):
        self.net, self.t, self.qkv, self.full, self.heads, self.lse = net, torus, qkv, full, heads, lse
        self.box, self.single, self.single_in, self.outs = box, single, single_in, outs
        self.res, self.res_single, self.res_single_in = res, res_single, res_single_in
        self.swap, self.back = Swap(net, torus, 3), Swap(net, torus, 1)
        self.sent = []

    def start(self):
        t, swap = self.t, self.swap
        self.got = swap.out_pairs(self.qkv, self.box)
        swap.pack_single(self.qkv, self.single)
        self.got_single = swap.out_single(self.single, self.single_in)
        swap.keep_pairs(self.qkv, self.box)
        self.single_in[t.x] = self.single[t.x]
        self.lse[...] = jnp.zeros_like(self.lse)

    def take(self, p):
        heads = self.heads
        if p < 2:
            self.got[p].wait_recv()
            for k in range(3):
                for s in range(4):
                    for j in range(2):
                        v = self.box[p, k, s, :, 64 * j : 64 * j + 64]
                        heads[k, 2 * p + j, 256 * s : 256 * (s + 1), :] = v * BF16(0.125) if k == 0 else v
            return
        self.got_single.wait_recv()
        for k in range(3):
            for s in range(4):
                v = self.single_in[s, :, 64 * k : 64 * k + 64]
                heads[k, 4, 256 * s : 256 * (s + 1), :] = v * BF16(0.125) if k == 0 else v

    def head(self, h, j):
        heads, lse = self.heads, self.lse
        lane = lax.broadcasted_iota(jnp.int32, (256, 128), 1)
        for i in range(4):
            rows = slice(256 * i, 256 * (i + 1))
            n = 256 * (i + 1)
            s = causal(dot_t(heads[0, h, rows, :], heads[1, h, :n, :]), i)
            top = jnp.max(s, axis=1, keepdims=True)
            p = jnp.exp(s - top)
            total = jnp.sum(p, axis=1, keepdims=True)
            lse[rows, :] = jnp.where(lane == h, top + jnp.log(total), lse[rows, :])
            o = dot(p.astype(BF16), heads[2, h, :n, :])
            self.outs[j, rows, :] = (o / total).astype(BF16)

    def give(self, p):
        back, outs = self.back, self.outs
        for i in range(4):
            rows = slice(256 * i, 256 * (i + 1))
            if p < 2:
                self.res[i, 0, p] = jnp.concatenate([outs[0, rows, :], outs[1, rows, :]], axis=1)
            else:
                self.res_single[i] = jnp.concatenate([outs[0, rows, :], jnp.zeros((256, 64), BF16)], axis=1)
        if p < 2:
            self.sent.append(back.back_pair(p, self.res, self.full))
            back.keep_back(p, self.res, self.full)
        else:
            self.sent_single = back.out_single(self.res_single, self.res_single_in)
            self.res_single_in[self.t.x] = self.res_single[self.t.x]

    def finish(self):
        self.sent_single.wait_recv()
        self.back.unpack_single(self.res_single_in, self.full)
        wait_all(self.sent)


def front_kernel(
    tokens, v_0, v_1, v_2, v_3, v_4, v_5, v_6, v_7, w_qkv, w_out, w_fc, w_proj,
    f_qkv, f_out, f_fc, f_proj, f_small, r_normed, att, r_heads, r_lse,
    normed, heads, lse, tok_v, small, u_0, u_1, u_2, u_3, u_4, u_5, u_6, u_7, v_qkv, h_out, h_fc, h_proj, small_all, bias, qkv, other, full,
    box, single, single_in, outs, res, res_single, res_single_in, ssem, rsem, lsem, vsem,
):
    t = Torus()
    vectors = ((v_0, u_0), (v_1, u_1), (v_2, u_2), (v_3, u_3), (v_4, u_4), (v_5, u_5), (v_6, u_6), (v_7, u_7))
    loads = [pltpu.make_async_copy(src, dst, vsem.at[k]) for k, (src, dst) in enumerate(((tokens, tok_v),) + vectors)]
    greeting = Greeting(t.neighbours())
    each(loads, "start")
    small[...] = jnp.zeros_like(small)
    each(loads, "wait")
    for k, (_, vector) in enumerate(vectors):
        small[k : k + 1, 0 : SIZES[k]] = vector[...].astype(F32).reshape(1, SIZES[k])
    net = Net(ssem, rsem)
    sib, c = t.sibling(), t.c
    q = Gather(net, t, "qkv", w_qkv, v_qkv, 0)
    o = Gather(net, t, "out", w_out, f_out, 1)
    f = Gather(net, t, "fc", w_fc, f_fc, 0)
    p = Gather(net, t, "proj", w_proj, f_proj, 1)
    fwd = Forward(net, t, qkv, full, heads, lse, box, single, single_in, outs, res, res_single, res_single_in)
    own = pltpu.make_async_copy(w_qkv, v_qkv.at[t.x], lsem.at[0])
    own.start()
    held = [(w_out, h_out, f_out), (w_fc, h_fc, f_fc), (w_proj, h_proj, f_proj)]
    local = [pltpu.make_async_copy(s, h, lsem.at[1 + k]) for k, (s, h, _) in enumerate(held)]
    each(local, "start")
    sent = []
    greeting.wait()

    def columns(region):
        start, width = region
        cols = pl.ds(pl.multiple_of(start, 128), width)
        made = dot(normed[...].reshape(512, 1280), v_qkv[:, :, cols].reshape(1280, width)) + bias[0:1, cols]
        made = made.astype(BF16)
        qkv[:, cols] = made[:256]
        other[:, cols] = made[256:]
        sent.append(net.send(other.at[:, cols], qkv.at[:, cols], sib))

    q.start()
    p.start()
    smalls = net.group(small_all.at[pl.ds(0, 3)], t.at("x", 1))
    for s in (1, 3, 2):
        smalls.send(small, small_all.at[t.x], t.at("x", s))
    small_all[t.x] = small[...]
    o.start()
    q.start_alone()
    q.spread(0)
    o.start_alone()
    q.spread(1)
    p.spread(0)
    q.widen(0)
    f.start()
    q.widen(1)
    smalls.wait_recv()
    hat, _ = norm(tok_v[...].astype(F32))
    gain, shift = whole_vector(small_all, "ln1_gain"), whole_vector(small_all, "ln1_bias")
    normed[0] = (hat * gain + shift).astype(BF16)
    swapped = net.send(normed.at[0], normed.at[1], sib)
    p.spread(1)
    o.alone_on()
    q.alone_on()
    for n, (_, h, full_w) in enumerate(held):
        local[n].wait()
        local[n] = pltpu.make_async_copy(h, full_w.at[t.x], lsem.at[1 + n])
        local[n].start()
    p.widen(0)
    p.start_alone()
    f.start_alone()
    o.spread(0)
    q.alone_end()
    q.pass_on(1)
    f.spread(0)
    q.pass_on(0)
    o.widen(0)
    f.spread(1)
    q.share(0)
    p.widen(1)
    k = VECTORS.index("qv_bias")
    for n in (0, 1, 4, 5):
        row = small_all[n if n < 2 else n - 2, k : k + 1, :640]
        bias[0:1, 640 * n : 640 * (n + 1)] = row
    bias[0:1, 1280:2560] = jnp.zeros((1, 1280), F32)
    f_small[...] = small_all[...]
    swapped.wait_recv()
    q.share(1)
    p.alone_on()
    o.alone_end()
    q.arrive(1)
    own.wait()
    columns(q.regions[1][1:])
    columns(q.alone)
    q.arrive(0)
    q.alone_share()
    f.alone_on()
    columns(q.regions[0][1:])
    f.widen(0)
    o.pass_on(0)
    p.alone_end()
    q.share_last(1)
    wait_all(sent)
    fwd.start()
    f.widen(1)
    q.share_last(0)
    fwd.take(0)
    p.pass_on(0)
    p.pass_on(1)
    p.share(0)
    fwd.head(0, 0)
    p.alone_share()
    o.share(0)
    f.pass_on(0)
    fwd.head(1, 1)
    o.arrive(0)
    o.alone_share()
    o.share_last(0)
    fwd.give(0)
    q.finish()
    p.share(1)
    keep = pltpu.make_async_copy(v_qkv, f_qkv, lsem.at[0])
    keep.start()
    f.pass_on(1)
    f.share(1)
    fwd.take(1)
    f.alone_end()
    f.alone_share()
    f.share(0)
    fwd.head(2, 0)
    fwd.head(3, 1)
    fwd.give(1)
    fwd.take(2)
    fwd.head(4, 0)
    done = [
        pltpu.make_async_copy(src, dst, vsem.at[k])
        for k, (src, dst) in enumerate(((normed, r_normed), (heads, r_heads), (lse, r_lse)))
    ]
    each(done, "start")
    f.arrive(0)
    p.arrive(0)
    f.share_last(0)
    fwd.give(2)
    p.arrive(1)
    p.share_last(0)
    f.arrive(1)
    f.share_last(1)
    o.finish()
    p.share_last(1)
    f.finish()
    p.finish()
    fwd.finish()
    done.append(pltpu.make_async_copy(full, att, vsem.at[3]))
    done[-1].start()
    keep.wait()
    each(local + done, "wait")
    net.finish()


FRONT_SEMS = 108


def front(tokens, vectors, w_qkv, w_out, w_fc, w_proj):
    vm, anys = pl.BlockSpec(memory_space=pltpu.VMEM), pl.BlockSpec(memory_space=pl.ANY)
    weights = (w_qkv, w_out, w_fc, w_proj)
    return pl.pallas_call(
        front_kernel,
        name="front",
        out_shape=[jax.ShapeDtypeStruct((4,) + w.shape, BF16) for w in weights]
        + [
            jax.ShapeDtypeStruct((4, 8, 1280), F32),
            jax.ShapeDtypeStruct((2, 256, 1280), BF16),
            jax.ShapeDtypeStruct((256, 1280), BF16),
            jax.ShapeDtypeStruct((3, 5, 1024, 64), BF16),
            jax.ShapeDtypeStruct((1024, 128), F32),
        ],
        in_specs=[anys] * 13,
        out_specs=[anys] * 4 + [vm] + [anys] * 4,
        scratch_shapes=[
            pltpu.VMEM((2, 256, 1280), BF16),
            pltpu.VMEM((3, 5, 1024, 64), BF16),
            pltpu.VMEM((1024, 128), F32),
            pltpu.VMEM((256, 1280), BF16),
            pltpu.VMEM((8, 1280), F32),
        ]
        + [pltpu.VMEM((n,), BF16) for n in SIZES]
        + [
            pltpu.VMEM((4, 320, 3840), BF16),
            pltpu.VMEM((320, 1280), BF16),
            pltpu.VMEM((320, 5120), BF16),
            pltpu.VMEM((1280, 1280), BF16),
            pltpu.VMEM((4, 8, 1280), F32),
            pltpu.VMEM((8, 3840), F32),
            pltpu.VMEM((256, 3840), BF16),
            pltpu.VMEM((256, 3840), BF16),
            pltpu.VMEM((256, 1280), BF16),
            pltpu.VMEM((2, 3, 4, 256, 128), BF16),
            pltpu.VMEM((4, 256, 256), BF16),
            pltpu.VMEM((4, 256, 256), BF16),
            pltpu.VMEM((2, 1024, 64), BF16),
            pltpu.VMEM((4, 1, 2, 256, 128), BF16),
            pltpu.VMEM((4, 256, 128), BF16),
            pltpu.VMEM((4, 256, 128), BF16),
            pltpu.SemaphoreType.DMA((FRONT_SEMS,)),
            pltpu.SemaphoreType.DMA((FRONT_SEMS,)),
            pltpu.SemaphoreType.DMA((4,)),
            pltpu.SemaphoreType.DMA((9,)),
        ],
        compiler_params=pltpu.CompilerParams(collective_id=0, has_side_effects=True, vmem_limit_bytes=56 << 20),
    )(tokens, *vectors, *weights)


GELU_A, GELU_B = 0.7978845608028654, 0.044715
FF_STEP = 640
FF_STEPS = 8
AHEAD = 2


def mlp_kernel(
    tokens, att, cot, small, w_out, w_fc, w_proj,
    base, act_c, grad_mid, datt, n2t_c, attt_c, cot_c, actt_c, gp_c, gb_c, small_c,
    tok_v, att_v, cot_v, small_v, wo_v, wf_v, wp_v, n2, middle, base_v, grad_acc, bias, sums, n2t, attt, acts, actt, gp, gb,
    datt_v, small_grad, isem, fsem, psem, ssem, rsem, lsem,
):
    t = Torus()
    sib, c = t.sibling(), t.c
    low, high = pl.ds(0, 256), pl.ds(256, 256)
    moves = ((att, att_v), (w_out, wo_v), (tokens, tok_v), (small, small_v), (cot, cot_v))
    loads = [pltpu.make_async_copy(src, dst, isem.at[k]) for k, (src, dst) in enumerate(moves)]
    each(loads, "start")

    def load(j):
        cols = pl.ds(pl.multiple_of(j * FF_STEP, 128), FF_STEP)
        return (
            pltpu.make_async_copy(w_fc.at[:, cols], wf_v.at[j], fsem.at[j]),
            pltpu.make_async_copy(w_proj.at[cols], wp_v.at[j], psem.at[j]),
        )

    greeting = Greeting([sib])

    def keep(k, src, dst):
        return pltpu.make_async_copy(src, dst, lsem.at[k])

    def give(k, src, dst):
        return pltpu.make_async_remote_copy(
            src_ref=src, dst_ref=dst, send_sem=ssem.at[k], recv_sem=rsem.at[k], device_id=sib, device_id_type=MESH
        )

    half = [pl.ds(pl.multiple_of(k * 640, 128), 640) for k in (c, 1 - c)]
    whole = [
        (keep(0, n2t, n2t_c.at[:, low]), give(0, n2t, n2t_c.at[:, high])),
        (keep(1, attt, attt_c.at[:, low]), give(1, attt, attt_c.at[:, high])),
        (keep(2, cot_v, cot_c.at[low]), give(2, cot_v, cot_c.at[high])),
        (keep(3, gb.at[:, half[0]], gb_c.at[low]), give(3, gb.at[:, half[1]], gb_c.at[high])),
        (keep(4, small_grad, small_c.at[0]), give(4, small_grad, small_c.at[1])),
    ]

    def strip(s, kept):
        n = 2 * s + (c if kept else 1 - c)
        rows = pl.ds(pl.multiple_of(s * 640, 16), 640)
        if kept:
            return [
                keep(5 + s, actt.at[n], actt_c.at[rows, low]),
                keep(9 + s, gp.at[n], gp_c.at[s, low]),
            ]
        return [
            give(5 + s, actt.at[n], actt_c.at[rows, high]),
            give(9 + s, gp.at[n], gp_c.at[s, high]),
        ]

    each(loads[:4], "wait")
    for j in range(AHEAD):
        each(load(j), "start")
    mid = tok_v[...].astype(F32) + dot(att_v[...], wo_v[...]) + whole_vector(small_v, "out_bias")
    middle[...] = mid
    hat, _ = norm(mid)
    n2[...] = (hat * whole_vector(small_v, "ln2_gain") + whole_vector(small_v, "ln2_bias")).astype(BF16)
    base_v[...] = mid + whole_vector(small_v, "proj_bias")
    results = [keep(13, base_v, base)]
    each(results, "start")
    grad_acc[...] = jnp.zeros_like(grad_acc)
    k = VECTORS.index("fc_bias")
    for n in range(FF_STEPS):
        bias[n, 0:1, :] = small_v[n // 2, k : k + 1, 640 * (n % 2) : 640 * (n % 2 + 1)]
    greeting.wait()
    loads[4].wait()
    each(whole[2], "start")
    n2t[...] = n2[...].T
    each(whole[0], "start")

    def chunk(j, _):
        @pl.when(j + AHEAD < FF_STEPS)
        def _():
            each(load(j + AHEAD), "start")

        each(load(j), "wait")
        pre = dot(n2[...], wf_v[j]) + bias[j, 0:1, :]
        square = pre * pre
        bend = jnp.tanh(GELU_A * (pre + GELU_B * pre * square))
        act = (0.5 * pre * (1.0 + bend)).astype(BF16)
        actt[j] = act.T
        acts[j] = act
        slope = 0.5 * (1.0 + bend) + (0.5 * GELU_A) * pre * (1.0 - bend * bend) * (1.0 + 3.0 * GELU_B * square)
        grad = (dot_t(cot_v[...], wp_v[j]) * slope).astype(BF16)
        gp[j] = grad
        grad_acc[...] += dot_t(grad, wf_v[j])
        sums[j, 0:1, :] = jnp.sum(grad.astype(F32), axis=0, keepdims=True)

        @pl.when(lax.rem(j, 2) == c)
        def _():
            each(strip(j // 2, True), "start")

        @pl.when(lax.rem(j, 2) != c)
        def _():
            each(strip(j // 2, False), "start")

        return 0

    lax.fori_loop(0, FF_STEPS, chunk, 0)
    hat, scale = norm(middle[...])
    g = grad_acc[...]
    cot_rows = cot_v[...].astype(F32)
    mid = cot_rows + norm_back(g, hat, scale, whole_vector(small_v, "ln2_gain"))
    branch = mid.astype(BF16)
    gb[...] = branch
    each(whole[3], "start")
    small_grad[0:1, :] = jnp.sum(g * hat, axis=0, keepdims=True)
    small_grad[1:2, :] = jnp.sum(g, axis=0, keepdims=True)
    small_grad[2:3, :] = jnp.sum(cot_rows, axis=0, keepdims=True)
    small_grad[3:4, :] = jnp.sum(branch.astype(F32), axis=0, keepdims=True)
    for n in range(FF_STEPS):
        small_grad[4 + n // 2 : 5 + n // 2, 640 * (n % 2) : 640 * (n % 2 + 1)] = sums[n, 0:1, :]
    each(whole[4], "start")
    middle[...] = mid
    results += [keep(14, middle, grad_mid), keep(16, acts, act_c)]
    each(results[1:], "start")
    attt[...] = att_v[...].T
    each(whole[1], "start")
    datt_v[...] = dot_t(branch, wo_v[...]).astype(BF16)
    results.append(keep(15, datt_v, datt))
    results[-1].start()
    for own, other in whole:
        own.wait()
        other.wait()
    for s in range(4):
        each(strip(s, True) + strip(s, False), "wait")
    each(results, "wait")


def mlp(tokens, att, cot, small, w_out, w_fc, w_proj):
    anys = pl.BlockSpec(memory_space=pl.ANY)
    return pl.pallas_call(
        mlp_kernel,
        name="mlp",
        out_shape=[
            jax.ShapeDtypeStruct((256, 1280), F32),
            jax.ShapeDtypeStruct((FF_STEPS, 256, FF_STEP), BF16),
            jax.ShapeDtypeStruct((256, 1280), F32),
            jax.ShapeDtypeStruct((256, 1280), BF16),
            jax.ShapeDtypeStruct((1280, 512), BF16),
            jax.ShapeDtypeStruct((1280, 512), BF16),
            jax.ShapeDtypeStruct((512, 1280), BF16),
            jax.ShapeDtypeStruct((2560, 512), BF16),
            jax.ShapeDtypeStruct((4, 512, 640), BF16),
            jax.ShapeDtypeStruct((512, 640), BF16),
            jax.ShapeDtypeStruct((2, 8, 1280), F32),
        ],
        in_specs=[anys] * 7,
        out_specs=[anys] * 11,
        scratch_shapes=[pltpu.VMEM((256, 1280), BF16)] * 3
        + [
            pltpu.VMEM((4, 8, 1280), F32),
            pltpu.VMEM((1280, 1280), BF16),
            pltpu.VMEM((FF_STEPS, 1280, FF_STEP), BF16),
            pltpu.VMEM((FF_STEPS, FF_STEP, 1280), BF16),
            pltpu.VMEM((256, 1280), BF16),
            pltpu.VMEM((256, 1280), F32),
            pltpu.VMEM((256, 1280), F32),
            pltpu.VMEM((256, 1280), F32),
            pltpu.VMEM((FF_STEPS, 8, FF_STEP), F32),
            pltpu.VMEM((FF_STEPS, 8, FF_STEP), F32),
            pltpu.VMEM((1280, 256), BF16),
            pltpu.VMEM((1280, 256), BF16),
            pltpu.VMEM((FF_STEPS, 256, FF_STEP), BF16),
            pltpu.VMEM((FF_STEPS, FF_STEP, 256), BF16),
            pltpu.VMEM((FF_STEPS, 256, FF_STEP), BF16),
            pltpu.VMEM((256, 1280), BF16),
            pltpu.VMEM((256, 1280), BF16),
            pltpu.VMEM((8, 1280), F32),
            pltpu.SemaphoreType.DMA((5,)),
            pltpu.SemaphoreType.DMA((FF_STEPS,)),
            pltpu.SemaphoreType.DMA((FF_STEPS,)),
            pltpu.SemaphoreType.DMA((13,)),
            pltpu.SemaphoreType.DMA((13,)),
            pltpu.SemaphoreType.DMA((17,)),
        ],
        compiler_params=pltpu.CompilerParams(collective_id=3, has_side_effects=True, vmem_limit_bytes=60 << 20),
    )(tokens, att, cot, small, w_out, w_fc, w_proj)


def view(ref, axes, chosen, rows):
    return ref.at[tuple(chosen.get(a, slice(None)) for a in axes) + (pl.ds(*rows),)]


def leading(ref):
    return ref.shape[:-2]


def add_into(dst, *srcs):
    lead = leading(dst)
    count = 1
    for n in lead:
        count *= n

    def slab(i):
        index = []
        for n in reversed(lead):
            index.append(lax.rem(i, n))
            i = i // n
        return tuple(reversed(index))

    def body(i, _):
        at = slab(i)
        total = dst[at].astype(F32)
        for s in srcs:
            total = total + s[at].astype(F32)
        dst[at] = total.astype(BF16)
        return 0

    if count == 1 and not lead:
        total = dst[...].astype(F32)
        for s in srcs:
            total = total + s[...].astype(F32)
        dst[...] = total.astype(BF16)
    else:
        lax.fori_loop(0, count, body, 0)


def inbox_shapes(classes, phases):
    out = []
    for order, _, n in classes:
        if 0 in phases:
            half = [2 if a == order[1] else 4 for a in "xyz" if a != order[0]]
            out += [half + [n, 128]] * 2 + [[4, 4, n, 128]] * 2
        if 1 in phases:
            out += [[2, n, 128]] * 2 + [[4, n, 128]] * 2
        if 2 in phases:
            out += [[3, n, 128]]
    return [pltpu.VMEM(tuple(s), BF16) for s in out]


def inboxes(refs, phases):
    refs, out = list(refs), []
    while refs:
        mine = {}
        for phase in phases:
            n = 1 if phase == 2 else 4
            mine[phase], refs = refs[:n], refs[n:]
        out.append(mine)
    return out


class Lane:
    def __init__(self, net, torus, acc, axes, inbox, order, row, n):
        self.net, self.t, self.acc, self.axes, self.inbox, self.order = net, torus, acc, axes, inbox, order
        self.rows, self.base = (row, n), 0
        self.fixed = {}
        self.got = {}

    def part(self, phase):
        axis = self.order[phase]
        return view(self.acc, self.axes, {**self.fixed, axis: self.t.pos(axis)}, self.rows)

    def held(self):
        return view(self.acc, self.axes, self.fixed, self.rows)

    def halves(self, phase):
        a = self.order[phase + 1]
        return [{a: pl.ds(0, 2)}, {a: pl.ds(2, 2)}]

    def box_half(self, box, phase, half):
        if phase == 1:
            return box.at[pl.ds(2 * half, 2)]
        left = [a for a in "xyz" if a != self.order[0]]
        cut = left.index(self.order[1])
        return box.at[(slice(None),) * cut + (pl.ds(2 * half, 2),)]

    def first(self, phase):
        axis = self.order[phase]
        p = self.t.pos(axis)
        h = self.halves(phase)
        b = self.inbox[phase]
        at = lambda shift, cut: view(self.acc, self.axes, {**self.fixed, axis: wrap(p + shift), **cut}, self.rows)
        up, down = self.t.at(axis, 1), self.t.at(axis, 3)
        far = [self.net.send(at(2, h[0]), b[0], up), self.net.send(at(2, h[1]), b[1], down)]
        near = [self.net.group(b[2], up), self.net.group(b[3], down)]
        near[0].send(at(1, h[1]), self.box_half(b[2], phase, 1), up)
        near[1].send(at(3, h[0]), self.box_half(b[3], phase, 0), down)
        self.got[phase] = (far, near)

    def second(self, phase, side):
        axis = self.order[phase]
        p = self.t.pos(axis)
        b = self.inbox[phase]
        far, near = self.got[phase]
        step = 3 if side else 1
        chosen = {**self.fixed, axis: wrap(p + step), **self.halves(phase)[side]}
        here = view(self.acc, self.axes, chosen, self.rows)
        far[side].wait_recv()
        add_into(here, b[side])
        near[side].send(here, self.box_half(b[2 + side], phase, side), self.t.at(axis, step))

    def third(self, phase):
        axis = self.order[phase]
        p = self.t.pos(axis)
        b = self.inbox[phase]
        for copy in self.got[phase][1]:
            copy.wait_recv()
        self.fixed[axis] = p
        add_into(self.held(), b[2], b[3])

    def last(self):
        axis = self.order[2]
        p = self.t.pos(axis)
        box = self.inbox[2][0]
        self.got[2] = self.net.group(box, self.t.at(axis, 1))
        for s in (1, 3, 2):
            there = view(self.acc, self.axes, {**self.fixed, axis: wrap(p + s)}, self.rows)
            self.got[2].send(there, box.at[s - 1], self.t.at(axis, s))

    def done(self):
        axis = self.order[2]
        self.got[2].wait_recv()
        self.fixed[axis] = self.t.pos(axis)
        box = self.inbox[2][0]
        add_into(self.held(), box.at[0], box.at[1], box.at[2])


class Spread:
    def __init__(self, lane, out, result, order, row, n, sem):
        self.result = result
        self.net, self.t, self.out, self.order, self.rows, self.sem = lane.net, lane.t, out, order, (row, n), sem
        chosen = {a: lane.t.pos(a) for a in lane.axes}
        self.own = view(lane.acc, lane.axes, chosen, (row - lane.base, n))

    def place(self, y, z):
        return self.out.at[self.t.c, y, z, pl.ds(*self.rows)]

    def band(self, v, b=slice(None)):
        y, z = (b, v) if self.order == "yz" else (v, b)
        return self.place(y, z)

    def start(self):
        t = self.t
        here = self.place(t.y, t.z)
        self.keep = pltpu.make_async_copy(self.own, here, self.sem)
        self.keep.start()
        self.first = self.net.group(self.band(0, pl.ds(0, 3)), t.at(self.order[0], 1))
        for s in (1, 3, 2):
            self.first.send(self.own, here, t.at(self.order[0], s))

    def second(self):
        t, axis = self.t, self.order[1]
        self.first.wait_recv()
        self.keep.wait()
        here = self.band(t.pos(axis))
        self.near = [self.net.send(here, here, t.at(axis, s)) for s in (1, 3)]

    def third(self):
        t, axis = self.t, self.order[1]
        p = t.pos(axis)
        self.far = self.net.group(self.band(p), t.at(axis, 1))
        for copy, shift, to, b in ((self.near[0], 3, 1, pl.ds(0, 2)), (self.near[1], 1, 3, pl.ds(2, 2))):
            copy.wait_recv()
            there = self.band(wrap(p + shift), b)
            self.far.send(there, there, t.at(axis, to))

    def share(self):
        self.far.wait_recv()
        whole = self.place(slice(None), slice(None))
        self.core = self.net.send(whole, whole, self.t.sibling())

    def finish(self):
        self.core.wait_recv()
        rows = (slice(None),) * 3 + (pl.ds(*self.rows),)
        self.keep = pltpu.make_async_copy(self.out.at[rows], self.result.at[rows], self.sem)
        self.keep.start()

    def end(self):
        self.keep.wait()


GROUPS = {
    "mlp": ((352, 304, 144), 0, ("yzx", "zxy", "xyz")),
    "attn": ((128, 144, 128), 0, ("yxz", "zxy", "xyz")),
}
SMALL_ROWS = 16


def slab_rows(group):
    return sum(GROUPS[group][0]) + (SMALL_ROWS if group == "attn" else 0)


def classes_of(group):
    rows, extra, orders = GROUPS[group]
    row, out = 0, []
    for k, (order, n) in enumerate(zip(orders, rows)):
        n += extra if k == 2 else 0
        out.append((order, row, n))
        row += n
    return out


def spreads_of(group):
    a, b, c = classes_of(group)
    h = c[2] // 32 * 16
    return [(0, "yz", a[1], a[2]), (1, "zy", b[1], b[2]), (2, "yz", c[1], h), (2, "zy", c[1] + h, c[2] - h)]


def pieces_of(group, first, count):
    rows, out, flat, row = GROUPS[group][0], [], 0, 0
    for n in rows:
        for slab in range(16):
            lo, hi = max(first, flat), min(first + count, flat + n)
            if lo < hi:
                out.append((slab, row + lo - flat, hi - lo, lo - first))
            flat += n
        row += n
    return out


def store_blocks(acc, group, x, first, blocks):
    for k, block in enumerate(blocks):
        for slab, row, n, offset in pieces_of(group, first + 320 * k, 320):
            acc[x, slab // 4, slab % 4, pl.ds(row, n), :] = block[offset : offset + n]


def spreads_for(group, lanes, out, result, sems):
    return [Spread(lanes[k], out, result, order, row, n, sems.at[i]) for i, (k, order, row, n) in enumerate(spreads_of(group))]


def row_pieces(ref, row, start, n):
    v = ref[row : row + 1, start : start + n]
    if n % 128:
        v = jnp.concatenate([v, jnp.zeros((1, 128 - n % 128), F32)], axis=1)
    return [v[:, 128 * k : 128 * (k + 1)] for k in range(v.shape[1] // 128)]


def store_small(acc, row, slabs):
    for x in range(4):
        filled = slabs(x)
        for k in range(16):
            pieces = filled[k] if k < len(filled) else []
            if len(pieces) < 16:
                pieces = pieces + [jnp.zeros((16 - len(pieces), 128), F32)]
            acc[x, k // 4, k % 4, pl.ds(row, 16), :] = jnp.concatenate(pieces, axis=0).astype(BF16)


def store_product(lhs, rhs, acc, group, places):
    out = dot(lhs, rhs).astype(BF16)
    for k, (x, chunk) in enumerate(places):
        rows = out[320 * k : 320 * (k + 1)]
        store_blocks(acc, group, x, 1600 * chunk, [rows[:, 128 * t : 128 * (t + 1)] for t in range(5)])


class Backward:
    def __init__(self, net, torus, datt, full, heads, lse, box, single, single_in, do, dkv, grads, res, res_single, res_single_in):
        self.net, self.t, self.datt, self.full, self.heads, self.lse = net, torus, datt, full, heads, lse
        self.box, self.single, self.single_in, self.do, self.dkv, self.grads = box, single, single_in, do, dkv, grads
        self.res, self.res_single, self.res_single_in = res, res_single, res_single_in
        self.swap, self.back = Swap(net, torus, 1), Swap(net, torus, 3)
        self.sent = []

    def start(self):
        t, swap = self.t, self.swap
        self.got = swap.out_pairs(self.datt, self.box)
        swap.pack_single(self.datt, self.single)
        self.got_single = swap.out_single(self.single, self.single_in)
        swap.keep_pairs(self.datt, self.box)
        self.single_in[t.x] = self.single[t.x]

    def take(self, p):
        (self.got[p] if p < 2 else self.got_single).wait_recv()
        for s in range(4):
            rows = slice(256 * s, 256 * (s + 1))
            if p < 2:
                for j in range(2):
                    self.do[2 * p + j, rows, :] = self.box[p, 0, s, :, 64 * j : 64 * j + 64]
            else:
                self.do[4, rows, :] = self.single_in[s, :, :64]

    def head(self, h, j):
        heads, grads, dkv = self.heads, self.grads, self.dkv
        lane = lax.broadcasted_iota(jnp.int32, (256, 128), 1)
        dkv[...] = jnp.zeros_like(dkv)
        for i in range(4):
            rows = slice(256 * i, 256 * (i + 1))
            n = 256 * (i + 1)
            q, k, v, d = heads[0, h, rows, :], heads[1, h, :n, :], heads[2, h, :n, :], self.do[h, rows, :]
            total = jnp.sum(jnp.where(lane == h, self.lse[rows, :], 0.0), axis=1, keepdims=True)
            p = jnp.exp(causal(dot_t(q, k), i) - total)
            t1 = p * dot_t(d, v)
            inner = jnp.sum(t1, axis=1, keepdims=True)
            ds = (t1 - p * inner).astype(BF16)
            grads[0, j, rows, :] = (dot(ds, k) * 0.125).astype(BF16)
            dkv[0, :, :n] += dot(q.T, ds)
            dkv[1, :, :n] += dot(d.T, p.astype(BF16))
        for k in range(2):
            grads[1 + k, j] = dkv[k].T.astype(BF16)

    def give(self, p):
        grads, back = self.grads, self.back
        for i in range(4):
            rows = slice(256 * i, 256 * (i + 1))
            if p < 2:
                for k in range(3):
                    self.res[i, k, p] = jnp.concatenate([grads[k, 0, rows, :], grads[k, 1, rows, :]], axis=1)
            else:
                cols = [grads[k, 0, rows, :] for k in range(3)] + [jnp.zeros((256, 64), BF16)]
                self.res_single[i] = jnp.concatenate(cols, axis=1)
        if p < 2:
            self.sent.append(back.back_pair(p, self.res, self.full))
            back.keep_back(p, self.res, self.full)
        else:
            self.sent_single = back.out_single(self.res_single, self.res_single_in)
            self.res_single_in[self.t.x] = self.res_single[self.t.x]

    def finish(self):
        self.sent_single.wait_recv()
        self.back.unpack_single(self.res_single_in, self.full)
        wait_all(self.sent)


def back_kernel(
    r_datt, r_heads, r_lse, n2t, actt, gp, cot,
    gqkv, part_0, part_1, part_2,
    datt, heads, lse, n2t_v, actt_v, gp_v, cot_v, full,
    box, single, single_in, do, dkv, grads, res, res_single, res_single_in,
    ssem, rsem, lsem, acc, *inbox,
):
    t = Torus()
    moves = ((n2t, n2t_v), (gp, gp_v), (r_datt, datt), (actt, actt_v), (cot, cot_v), (r_heads, heads), (r_lse, lse))
    loads = [pltpu.make_async_copy(src, dst, lsem.at[k]) for k, (src, dst) in enumerate(moves)]
    soon, later = loads[:3], loads[3:]
    each(soon, "start")
    greeting = Greeting(t.neighbours())
    net = Net(ssem, rsem)
    bwd = Backward(net, t, datt, full, heads, lse, box, single, single_in, do, dkv, grads, res, res_single, res_single_in)
    lanes = [Lane(net, t, acc, "xyz", box_of, *k) for k, box_of in zip(classes_of("mlp"), inboxes(inbox, (0,)))]
    parts = [pltpu.make_async_copy(lane.part(0), part, lsem.at[k]) for k, (lane, part) in enumerate(zip(lanes, (part_0, part_1, part_2)))]

    def fc(s):
        store_product(n2t_v[...], gp_v[s], acc, "mlp", [(x, s) for x in range(4)])

    def proj(half):
        def body(x, _):
            lhs = actt_v[pl.ds(pl.multiple_of(x * 640, 16), 640), :]
            places = [(x, 4 + 2 * half), (x, 5 + 2 * half)]
            store_product(lhs, cot_v[:, 640 * half : 640 * (half + 1)], acc, "mlp", places)
            return 0

        lax.fori_loop(0, 4, body, 0)

    each(soon, "wait")
    fc(3)
    each(later, "start")
    fc(0)
    fc(2)
    greeting.wait()
    bwd.start()
    fc(1)
    lanes[0].first(0)
    each(later, "wait")
    proj(0)
    proj(1)
    lanes[1].first(0)
    bwd.take(0)
    lanes[2].first(0)
    bwd.head(0, 0)
    bwd.head(1, 1)
    lanes[2].second(0, 0)
    bwd.give(0)
    bwd.take(1)
    bwd.head(2, 0)
    lanes[0].second(0, 0)
    bwd.head(3, 1)
    lanes[0].second(0, 1)
    lanes[1].second(0, 0)
    lanes[2].second(0, 1)
    bwd.give(1)
    bwd.take(2)
    lanes[1].second(0, 1)
    bwd.head(4, 0)
    bwd.give(2)
    lanes[1].third(0)
    lanes[2].third(0)
    parts[2].start()
    parts[1].start()
    lanes[0].third(0)
    parts[0].start()
    bwd.finish()
    gqkv[...] = full[...]
    each(parts, "wait")
    net.finish()


BACK_SEMS = 18


def backward(datt, heads, lse, n2t, actt, gp, cot):
    vm, anys = pl.BlockSpec(memory_space=pltpu.VMEM), pl.BlockSpec(memory_space=pl.ANY)
    classes = classes_of("mlp")
    return pl.pallas_call(
        back_kernel,
        name="backward",
        out_shape=[jax.ShapeDtypeStruct((256, 3840), BF16)]
        + [jax.ShapeDtypeStruct((4, 4, n, 128), BF16) for _, _, n in classes],
        in_specs=[anys] * 7,
        out_specs=[vm] + [anys] * 3,
        scratch_shapes=[
            pltpu.VMEM((256, 1280), BF16),
            pltpu.VMEM((3, 5, 1024, 64), BF16),
            pltpu.VMEM((1024, 128), F32),
            pltpu.VMEM((1280, 512), BF16),
            pltpu.VMEM((2560, 512), BF16),
            pltpu.VMEM((4, 512, 640), BF16),
            pltpu.VMEM((512, 1280), BF16),
            pltpu.VMEM((256, 3840), BF16),
            pltpu.VMEM((2, 1, 4, 256, 128), BF16),
            pltpu.VMEM((4, 256, 128), BF16),
            pltpu.VMEM((4, 256, 128), BF16),
            pltpu.VMEM((5, 1024, 64), BF16),
            pltpu.VMEM((2, 64, 1024), F32),
            pltpu.VMEM((3, 2, 1024, 64), BF16),
            pltpu.VMEM((4, 3, 2, 256, 128), BF16),
            pltpu.VMEM((4, 256, 256), BF16),
            pltpu.VMEM((4, 256, 256), BF16),
            pltpu.SemaphoreType.DMA((BACK_SEMS,)),
            pltpu.SemaphoreType.DMA((BACK_SEMS,)),
            pltpu.SemaphoreType.DMA((8,)),
            pltpu.VMEM((4, 4, 4, slab_rows("mlp"), 128), BF16),
        ]
        + inbox_shapes(classes, (0,)),
        compiler_params=pltpu.CompilerParams(collective_id=1, has_side_effects=True, vmem_limit_bytes=60 << 20),
    )(datt, heads, lse, n2t, actt, gp, cot)


def last_kernel(
    n1, r_gqkv, attt, gb, w_qkv, r_tokens, r_mid, r_small, r_sums, base, acts, w_proj, part_0, part_1, part_2,
    r_mlp, r_attn, r_grad, r_block,
    out_mlp, out_attn, grad_tokens, gqkv, tokens, grad_mid, small_all, mlp_sums, acts_v, block_v, n1_v, n1t, gqkv_v, attt_v, gb_v, w_v, small_v, ssem, rsem, lsem, acc, acc_small, held_0, held_1, held_2, *inbox,
):
    t = Torus()
    helds = (held_0, held_1, held_2)
    moves = [(n1, n1_v), (attt, attt_v), (gb, gb_v), (w_qkv, w_v)] + [*zip((part_0, part_1, part_2), helds)]
    moves += [(r_gqkv, gqkv), (r_tokens, tokens), (r_mid, grad_mid), (r_small, small_all), (r_sums, mlp_sums)]
    n1_in, att_in, gb_in, w_in, *rest = [
        pltpu.make_async_copy(src, dst, lsem.at[k]) for k, (src, dst) in enumerate(moves)
    ]
    parts_in, rows_in = rest[:3], rest[3:]
    soon, later = rows_in[:1] + [n1_in] + parts_in, [att_in, gb_in] + rows_in[1:] + [w_in]
    each(soon, "start")
    greeting = Greeting(t.neighbours())
    net = Net(ssem, rsem)
    sib, c = t.sibling(), t.c
    m, a = [], []
    boxes = inboxes(inbox[:15], (1, 2))
    for held, box_of, (order, row, n) in zip(helds, boxes, classes_of("mlp")):
        lane = Lane(net, t, held, "".join(v for v in "xyz" if v != order[0]), box_of, order, 0, n)
        lane.base = row
        m.append(lane)
    boxes = inboxes(inbox[15:], (0, 1, 2))
    for box_of, k in zip(boxes, classes_of("attn")):
        a.append(Lane(net, t, acc, "xyz", box_of, *k))
    tiny = Lane(net, t, acc_small, "xyz", boxes[3], "yzx", 0, SMALL_ROWS)
    tiny.base = 400
    ms = spreads_for("mlp", m, out_mlp, r_mlp, lsem.at[pl.ds(12, 4)])
    sp = spreads_for("attn", a, out_attn, r_attn, lsem.at[pl.ds(16, 4)])
    ts = Spread(tiny, out_attn, r_attn, "zy", 400, SMALL_ROWS, lsem.at[20])
    got = {}

    def own():
        rows_in[0].wait()
        for s in range(3):
            gqkv_v[s, 0:256] = gqkv[:, pl.ds(pl.multiple_of(c * 1920 + s * 640, 128), 640)]

    def swap():
        for s in range(3):
            theirs = pl.ds(pl.multiple_of((1 - c) * 1920 + s * 640, 128), 640)
            got[s] = net.send(gqkv.at[:, theirs], gqkv_v.at[s, pl.ds(256, 256)], sib)

    def turn():
        n1_in.wait()
        n1t[:, 0:256] = n1_v[0].T
        n1t[:, 256:512] = n1_v[1].T

    def qkv(s):
        got[s].wait_recv()
        store_product(n1t[...], gqkv_v[s], acc, "attn", [(x, s) for x in range(4)])

    def outp():
        att_in.wait()
        gb_in.wait()
        store_product(attt_v[...], gb_v[...], acc, "attn", [(x, 3) for x in range(4)])

    def rows_back():
        w_in.wait()
        each(rows_in[1:], "wait")

        def body(n, total):
            cols = pl.ds(pl.multiple_of(n * 640, 128), 640)
            return total + dot_t(gqkv[:, cols], w_v[:, cols])

        grad = lax.fori_loop(0, 6, body, jnp.zeros((256, 1280), F32))
        hat, scale = norm(tokens[...].astype(F32))
        grad_tokens[...] = (grad_mid[...] + norm_back(grad, hat, scale, whole_vector(small_all, "ln1_gain"))).astype(BF16)
        small_v[0, 0:1, :] = jnp.sum(grad * hat, axis=0, keepdims=True)
        small_v[0, 1:2, :] = jnp.sum(grad, axis=0, keepdims=True)
        small_v[0, 2:3, :] = jnp.sum(gqkv[:, :1280].astype(F32), axis=0, keepdims=True)
        small_v[0, 3:4, :] = jnp.sum(gqkv[:, 2560:].astype(F32), axis=0, keepdims=True)

    grad_out = pltpu.make_async_copy(grad_tokens, r_grad, lsem.at[21])

    def rows_out():
        grad_out.start()
        got["small"] = net.send(small_v.at[0], small_v.at[1], sib)

    def sums():
        got["small"].wait_recv()
        total, other = small_v.at[2], small_v.at[3]
        total[...] = small_v[0] + small_v[1]
        other[...] = mlp_sums[0] + mlp_sums[1]
        store_small(
            acc_small, 0,
            lambda x: [
                [row for k in range(2) for row in row_pieces(total, k, 320 * x, 320)],
                row_pieces(total, 2 + x // 2, 640 * (x % 2), 640),
                [row for k in range(4) for row in row_pieces(other, k, 320 * x, 320)],
                row_pieces(other, 4 + x, 0, 1280),
            ],
        )

    more = [pltpu.make_async_copy(base, grad_mid, lsem.at[22]), pltpu.make_async_copy(acts, acts_v, lsem.at[23])]
    block_out = pltpu.make_async_copy(block_v, r_block, lsem.at[24])

    def slot(j):
        return w_v.at[pl.ds(640 * (j % 2), 640), pl.ds(1280 * (j // 2 % 3), 1280)]

    def chunk(j):
        return pltpu.make_async_copy(w_proj.at[pl.ds(FF_STEP * j, FF_STEP)], slot(j), lsem.at[25 + j])

    def block(j):
        if j == 0:
            each(more, "start")
            each([chunk(k) for k in range(6)], "start")
            each(more, "wait")
        chunk(j).wait()
        grad_mid[...] += dot(acts_v[j], slot(j)[...])
        if j < 2:
            chunk(6 + j).start()
        if j == FF_STEPS - 1:
            block_v[...] = grad_mid[...].astype(BF16)
            block_out.start()

    each(parts_in, "wait")
    own()
    greeting.wait()
    m[1].first(1)
    m[0].first(1)
    swap()
    m[2].first(1)
    turn()
    each(later, "start")
    qkv(0)
    qkv(1)
    a[0].first(0)
    qkv(2)
    m[1].second(1, 0)
    m[1].second(1, 1)
    a[1].first(0)
    m[2].second(1, 0)
    outp()
    a[2].first(0)
    m[0].second(1, 1)
    m[0].second(1, 0)
    rows_back()
    m[1].third(1)
    m[2].second(1, 1)
    rows_out()
    m[1].last()
    block(0)
    sums()
    tiny.first(0)
    m[2].third(1)
    a[2].second(0, 0)
    a[0].second(0, 0)
    a[2].second(0, 1)
    m[2].last()
    a[0].second(0, 1)
    block(1)
    a[1].second(0, 1)
    a[1].second(0, 0)
    tiny.second(0, 1)
    m[1].done()
    tiny.second(0, 0)
    m[0].third(1)
    m[0].last()
    a[2].third(0)
    a[2].first(1)
    a[0].third(0)
    m[2].done()
    ms[1].start()
    tiny.third(0)
    ms[2].start()
    tiny.first(1)
    a[0].first(1)
    a[2].second(1, 0)
    a[2].second(1, 1)
    m[0].done()
    ms[0].start()
    a[1].third(0)
    a[0].second(1, 1)
    a[0].second(1, 0)
    ms[3].start()
    a[1].first(1)
    ms[2].second()
    a[2].third(1)
    a[2].last()
    tiny.second(1, 0)
    ms[1].second()
    tiny.second(1, 1)
    a[0].third(1)
    a[0].last()
    ms[0].second()
    a[1].second(1, 1)
    a[1].second(1, 0)
    a[2].done()
    block(2)
    tiny.third(1)
    a[1].third(1)
    a[1].last()
    ms[3].second()
    a[0].done()
    sp[2].start()
    tiny.last()
    sp[3].start()
    sp[0].start()
    block(3)
    ms[1].third()
    a[1].done()
    sp[1].start()
    ms[0].third()
    sp[3].second()
    sp[1].second()
    sp[0].second()
    tiny.done()
    ms[1].share()
    block(4)
    ts.start()
    ms[2].third()
    sp[3].third()
    sp[2].second()
    block(5)
    ms[0].share()
    ms[3].third()
    sp[0].third()
    ts.second()
    sp[1].third()
    block(6)
    sp[3].share()
    ms[0].finish()
    ms[2].share()
    ms[3].share()
    sp[2].third()
    ts.third()
    ms[1].finish()
    block(7)
    sp[0].share()
    sp[1].share()
    ts.share()
    ms[2].finish()
    sp[2].share()
    sp[0].finish()
    sp[1].finish()
    ts.finish()
    sp[3].finish()
    ms[3].finish()
    sp[2].finish()
    each(ms + sp + [ts], "end")
    grad_out.wait()
    block_out.wait()
    net.finish()


LAST_SEMS = 100


def last(n1, gqkv, attt, gb, w_qkv, tokens, grad_mid, small_all, sums, base, acts, w_proj, parts):
    anys = pl.BlockSpec(memory_space=pl.ANY)
    mlp_classes, attn_classes = classes_of("mlp"), classes_of("attn")
    return pl.pallas_call(
        last_kernel,
        name="last",
        out_shape=[jax.ShapeDtypeStruct((2, 4, 4, slab_rows(g), 128), BF16) for g in ("mlp", "attn")]
        + [jax.ShapeDtypeStruct((256, 1280), BF16)] * 2,
        in_specs=[anys] * 15,
        out_specs=[anys] * 4,
        scratch_shapes=[pltpu.VMEM((2, 4, 4, slab_rows(g), 128), BF16) for g in ("mlp", "attn")]
        + [
            pltpu.VMEM((256, 1280), BF16),
            pltpu.VMEM((256, 3840), BF16),
            pltpu.VMEM((256, 1280), BF16),
            pltpu.VMEM((256, 1280), F32),
            pltpu.VMEM((4, 8, 1280), F32),
            pltpu.VMEM((2, 8, 1280), F32),
            pltpu.VMEM((FF_STEPS, 256, FF_STEP), BF16),
            pltpu.VMEM((256, 1280), BF16),
            pltpu.VMEM((2, 256, 1280), BF16),
            pltpu.VMEM((1280, 512), BF16),
            pltpu.VMEM((3, 512, 640), BF16),
            pltpu.VMEM((1280, 512), BF16),
            pltpu.VMEM((512, 640), BF16),
            pltpu.VMEM((1280, 3840), BF16),
            pltpu.VMEM((4, 8, 1280), F32),
            pltpu.SemaphoreType.DMA((LAST_SEMS,)),
            pltpu.SemaphoreType.DMA((LAST_SEMS,)),
            pltpu.SemaphoreType.DMA((33,)),
            pltpu.VMEM((4, 4, 4, 400, 128), BF16),
            pltpu.VMEM((4, 4, 4, SMALL_ROWS, 128), BF16),
        ]
        + [pltpu.VMEM((4, 4, n, 128), BF16) for _, _, n in mlp_classes]
        + inbox_shapes(mlp_classes, (1, 2))
        + inbox_shapes(attn_classes + [("yzx", 0, SMALL_ROWS)], (0, 1, 2)),
        compiler_params=pltpu.CompilerParams(collective_id=2, has_side_effects=True, vmem_limit_bytes=60 << 20),
    )(n1, gqkv, attt, gb, w_qkv, tokens, grad_mid, small_all, sums, base, acts, w_proj, *parts)


def flat_block(src, core, group, block):
    pieces = [
        src[core, slab // 4, slab % 4, row : row + n, :] for slab, row, n, _ in pieces_of(group, 320 * block, 320)
    ]
    return jnp.concatenate(pieces, axis=0).astype(F32)


SMALL_PLACES = (
    (0, 0, 320),
    (0, 3, 320),
    (1, 0, 640),
    (2, 9, 320),
    (2, 0, 320),
    (2, 3, 320),
    (3, 0, 1280),
    (2, 6, 320),
)


def unpack_kernel(packed_mlp, packed_attn, block, grad, *refs):
    fc, proj, qkv, out, block_out, grad_out, *smalls = refs[:14]
    in_0, in_1, stage, block_v, grad_v, *rest = refs[14:]
    small_v, (in_sem, out_sem, small_sem) = rest[:8], rest[8:]
    loads = []
    for c in range(2):
        loads.append(
            [
                pltpu.make_async_copy(src.at[c], dst.at[c], in_sem.at[2 * c + k])
                for k, (src, dst) in enumerate(((packed_attn, in_1), (packed_mlp, in_0)))
            ]
        )
        each(loads[-1], "start")
    rows = [pltpu.make_async_copy(block, block_v, in_sem.at[4]), pltpu.make_async_copy(grad, grad_v, in_sem.at[5])]
    each(rows, "start")
    flying, tail = [], []
    for c in range(2):
        chunks = [(in_1, "attn", q, qkv, 0, 1920 * c + 640 * q) for q in range(3)]
        chunks += [(in_1, "attn", 3, out, 0, 640 * c)]
        chunks += [(in_0, "mlp", q, fc, 0, 1280 * q + 640 * c) for q in range(4)]
        chunks += [(in_0, "mlp", 4 + 2 * h + sub, proj, 640 * c + 320 * sub, 640 * h) for h in range(2) for sub in range(2)]
        for n, (src, group, q, dst, row, col) in enumerate(chunks):
            if n in (0, 4):
                loads[c][n // 4].wait()
            k = len(flying)
            slot = k % STAGES
            if k >= STAGES:
                flying[k - STAGES].wait()
            for t in range(5):
                stage[slot, :, 128 * t : 128 * (t + 1)] = flat_block(src, c, group, 5 * q + t)
            copy = pltpu.make_async_copy(stage.at[slot], dst.at[pl.ds(row, 320), pl.ds(col, 640)], out_sem.at[slot])
            copy.start()
            flying.append(copy)
        if c == 0:
            for k, (slab, row, n) in enumerate(SMALL_PLACES):
                first = slab_rows("attn") - SMALL_ROWS
                values = in_1[0, 0, slab, first : first + SMALL_ROWS, :].astype(F32)
                for i in range(0, n, 128):
                    m = min(128, n - i)
                    small_v[k][i : i + m] = values[row + i // 128, :m]
                tail.append(pltpu.make_async_copy(small_v[k], smalls[k], small_sem.at[k]))
                tail[-1].start()
            each(rows, "wait")
            tail.append(pltpu.make_async_copy(block_v, block_out, small_sem.at[8]))
            tail.append(pltpu.make_async_copy(grad_v, grad_out, small_sem.at[9]))
            each(tail[-2:], "start")
    each(flying[-STAGES:] + tail, "wait")


STAGES = 8


def unpack(packed_mlp, packed_attn, block, grad):
    anys = pl.BlockSpec(memory_space=pl.ANY)
    sizes = [n for _, _, n in SMALL_PLACES]
    return pl.pallas_call(
        unpack_kernel,
        name="unpack",
        out_shape=[jax.ShapeDtypeStruct(s, F32) for s in ((320, 5120), (1280, 1280), (320, 3840), (320, 1280))]
        + [jax.ShapeDtypeStruct((256, 1280), BF16)] * 2
        + [jax.ShapeDtypeStruct((n,), F32) for n in sizes],
        in_specs=[anys] * 4,
        out_specs=[anys] * 14,
        scratch_shapes=[
            pltpu.VMEM(packed_mlp.shape, BF16),
            pltpu.VMEM(packed_attn.shape, BF16),
            pltpu.VMEM((STAGES, 320, 640), F32),
            pltpu.VMEM((256, 1280), BF16),
            pltpu.VMEM((256, 1280), BF16),
        ]
        + [pltpu.VMEM((n,), F32) for n in sizes]
        + [
            pltpu.SemaphoreType.DMA((6,)),
            pltpu.SemaphoreType.DMA((STAGES,)),
            pltpu.SemaphoreType.DMA((10,)),
        ],
        compiler_params=pltpu.CompilerParams(vmem_limit_bytes=62 << 20),
    )(packed_mlp, packed_attn, block, grad)


def shards(
    tokens,
    cotangent,
    ln1_gain,
    ln1_bias,
    w_qkv,
    qv_bias,
    w_out,
    out_bias,
    ln2_gain,
    ln2_bias,
    w_fc,
    fc_bias,
    w_proj,
    proj_bias,
):
    own = (ln1_gain, ln1_bias, qv_bias, out_bias, ln2_gain, ln2_bias, proj_bias, fc_bias)
    f_qkv, f_out, f_fc, f_proj, f_small, normed_one, attended, heads, lse = front(
        tokens[0], own, w_qkv, w_out, w_fc, w_proj
    )
    f_qkv, f_out, f_fc, f_proj = (
        f_qkv.reshape(1280, 3840),
        f_out.reshape(1280, 1280),
        f_fc.reshape(1280, 5120),
        f_proj.reshape(5120, 1280),
    )
    base, acts, grad_middle, grad_attended, n2t, attt, cot, actt, grad_pre, grad_branch, small_mlp = mlp(
        tokens[0], attended, cotangent[0], f_small, f_out, f_fc, f_proj
    )
    grad_qkv, *parts = backward(grad_attended, heads, lse, n2t, actt, grad_pre, cot)
    packed_mlp, packed_attn, grad_tokens, block_out = last(
        normed_one, grad_qkv, attt, grad_branch, f_qkv, tokens[0], grad_middle, f_small,
        small_mlp, base, acts, f_proj, parts,
    )
    g_fc, g_proj, g_qkv, g_out, block_out, grad_tokens, *vectors = unpack(
        packed_mlp, packed_attn, block_out, grad_tokens
    )
    gain_1, bias_1, bias_qv, bias_out, gain_2, bias_2, bias_fc, bias_proj = vectors
    return (
        block_out[None],
        grad_tokens[None],
        gain_1,
        bias_1,
        g_qkv,
        bias_qv,
        g_out,
        bias_out,
        gain_2,
        bias_2,
        g_fc,
        bias_fc,
        g_proj,
        bias_proj,
    )


def solution(mesh):
    vector, matrix, batch = P("shard"), P("shard", None), P("rep", "shard", None)
    placed = (batch, batch, vector, vector, matrix, vector, matrix, vector, vector, vector, matrix, vector, matrix, vector)
    return jax.shard_map(shards, mesh=mesh, in_specs=placed, out_specs=placed, check_vma=False)
```

```python
import jax
import jax.numpy as jnp
from jax import lax
from jax.experimental import pallas as pl
from jax.experimental.pallas import tpu as pltpu
from jax.sharding import PartitionSpec as P

MESH = pl.DeviceIdType.MESH
F32, BF16 = jnp.float32, jnp.bfloat16


def where_am_i():
    rep = lax.axis_index("rep")
    return lax.axis_index("shard"), (rep // 2) % 4, rep // 8, rep % 2


def device_at(x, y, z, c):
    return {"rep": (z * 4 + y) * 2 + c, "shard": x}


def wrap(v):
    return lax.rem(v + 4, 4)


class Group:
    def __init__(self, sems, whole, target):
        self.sems = sems
        self.all = self.copy(whole, whole, target)

    def copy(self, src, dst, target):
        send_sem, recv_sem = self.sems
        return pltpu.make_async_remote_copy(
            src_ref=src, dst_ref=dst, send_sem=send_sem, recv_sem=recv_sem, device_id=target, device_id_type=MESH
        )

    def send(self, src, dst, target):
        self.copy(src, dst, target).start()

    def wait_recv(self):
        self.all.wait_recv()

    def wait_send(self):
        self.all.wait_send()


class Net:
    def __init__(self, send_sems, recv_sems):
        self.send_sems, self.recv_sems, self.groups = send_sems, recv_sems, []

    def group(self, whole, target):
        k = len(self.groups)
        self.groups.append(Group((self.send_sems.at[k], self.recv_sems.at[k]), whole, target))
        return self.groups[-1]

    def send(self, src, dst, target):
        group = self.group(dst, target)
        group.send(src, dst, target)
        return group

    def finish(self):
        for group in self.groups:
            group.wait_send()


def wait_all(copies):
    for copy in copies:
        copy.wait_recv()


def each(items, what, *rest):
    for item in items:
        getattr(item, what)(*rest)


class Greeting:
    def __init__(self, targets):
        self.barrier, self.count = pltpu.get_barrier_semaphore(), len(targets)
        for target in targets:
            pl.semaphore_signal(self.barrier, 1, device_id=target, device_id_type=MESH)

    def wait(self):
        pl.semaphore_wait(self.barrier, self.count)


class Torus:
    def __init__(self):
        self.x, self.y, self.z, self.c = where_am_i()

    def at(self, axis, step):
        x, y, z = self.x, self.y, self.z
        if axis == "x":
            x = wrap(x + step)
        elif axis == "y":
            y = wrap(y + step)
        else:
            z = wrap(z + step)
        return device_at(x, y, z, self.c)

    def pos(self, axis):
        return {"x": self.x, "y": self.y, "z": self.z}[axis]

    def sibling(self):
        return device_at(self.x, self.y, self.z, 1 - self.c)

    def neighbours(self, axes="xyz", core=True):
        out = [self.at(a, s) for a in axes for s in (1, 2, 3)]
        return out + ([self.sibling()] if core else [])


PLANS = {
    "qkv": (320, 3840, 4, 8, 3),
    "out": (320, 1280, 4, 0, 1),
    "fc": (320, 5120, 8, 8, 4),
    "proj": (1280, 1280, 2, 2, 1),
}


def rect_of(rows, start, width, order, y, z, stage):
    if rows == 320:
        if stage == 0:
            return y * 80, 80, start + z * (width // 4), width // 4
        if order == "yz":
            return 0, 320, start + z * (width // 4), width // 4
        return y * 80, 80, start, width
    first, second = (y, z) if order == "yz" else (z, y)
    if stage == 0:
        return second * 320 + first * 80, 80, start, width
    return second * 320, 320, start, width


def part(ref, owner, rect):
    r, nr, c, nc = rect
    return ref.at[owner, pl.ds(pl.multiple_of(r, 16), nr), pl.ds(pl.multiple_of(c, 128), nc)]


def parts_of(ref, count, rect):
    r, nr, c, nc = rect
    return ref.at[pl.ds(0, count), pl.ds(pl.multiple_of(r, 16), nr), pl.ds(pl.multiple_of(c, 128), nc)]


def own_part(ref, rect):
    r, nr, c, nc = rect
    return ref.at[pl.ds(pl.multiple_of(r, 16), nr), pl.ds(pl.multiple_of(c, 128), nc)]


class Gather:
    def __init__(self, net, torus, name, src, full, lean):
        self.net, self.t, self.src, self.full, self.lean = net, torus, src, full, lean
        self.ring = name != "qkv"
        self.rows, cols, a, b, d = PLANS[name]
        half = torus.c * (cols // 2)
        self.regions = []
        at = 0
        for order, tiles in (("yz", a), ("zy", b)):
            if tiles:
                self.regions.append((order, half + at * 128, tiles * 128))
            at += tiles
        self.alone = (half + at * 128, d * 128)
        self.others = [wrap(torus.x + k) for k in (1, 2, 3)]
        self.got = {"core": []}

    def rect(self, region, stage, shift=0):
        order, start, width = region
        y, z = self.t.y, self.t.z
        axis = order[stage]
        if axis == "y":
            y = wrap(y + shift)
        else:
            z = wrap(z + shift)
        return rect_of(self.rows, start, width, order, y, z, stage)

    def both(self, what, *rest):
        for i in range(len(self.regions)):
            getattr(self, what)(i, *rest)

    def start(self):
        t, net = self.t, self.net
        for i, region in enumerate(self.regions):
            rect = self.rect(region, 0)
            if self.ring:
                self.got[i, "near"] = [
                    net.send(own_part(self.src, rect), part(self.full, t.x, rect), t.at("x", s)) for s in (1, 3)
                ]
                continue
            group = net.group(parts_of(self.full, 3, rect), t.at("x", 1))
            for s in (1, 3, 2):
                group.send(own_part(self.src, rect), part(self.full, t.x, rect), t.at("x", s))
            self.got[i, "x"] = group

    def hop(self, i):
        t = self.t
        row, n, start, width = self.rect(self.regions[i], 0)
        left, right = wrap(t.x - 1), wrap(t.x + 1)
        group = self.net.group(part(self.full, left, (row, n, start, width)), t.at("x", 1))
        cut = n // 32 * 16
        for copy, owner, first, m, step in zip(
            self.got[i, "near"], (left, right), (0, cut), (cut, n - cut), (1, 3)
        ):
            copy.wait_recv()
            rows = part(self.full, owner, (row + first, m, start, width))
            group.send(rows, rows, t.at("x", step))
        self.got[i, "x"] = group

    def start_alone(self):
        if not self.alone[1]:
            return
        t, net = self.t, self.net
        rect = (0, self.rows, *self.alone)
        self.got["alone"] = [
            net.send(own_part(self.src, rect), part(self.full, t.x, rect), t.at("x", s)) for s in (1, 3)
        ]

    def alone_on(self):
        if not self.alone[1]:
            return
        t, net = self.t, self.net
        h = self.rows // 2
        start, width = self.alone
        whole = (0, self.rows, start, width)
        left, right = wrap(t.x - 1), wrap(t.x + 1)
        on = net.group(part(self.full, left, whole), t.at("x", 1))
        for copy, owner, row, step in zip(self.got["alone"], (left, right), (0, h), (1, 3)):
            copy.wait_recv()
            half = part(self.full, owner, (row, h, start, width))
            on.send(half, half, t.at("x", step))
        self.got["alone2"] = on
        core = net.group(parts_of(self.full, 2, whole), t.sibling())
        for o in (left, right):
            core.send(part(self.full, o, whole), part(self.full, o, whole), t.sibling())
        self.got["core"].append(core)

    def alone_end(self):
        if not self.alone[1]:
            return
        self.got["alone2"].wait_recv()

    def alone_share(self):
        if not self.alone[1]:
            return
        o = wrap(self.t.x + 2)
        whole = (0, self.rows, *self.alone)
        self.got["core"].append(self.net.send(part(self.full, o, whole), part(self.full, o, whole), self.t.sibling()))

    def to_all(self, rect, target):
        group = self.net.group(parts_of(self.full, 3, rect), target)
        for o in self.others:
            group.send(part(self.full, o, rect), part(self.full, o, rect), target)
        return group

    def spread(self, i):
        region = self.regions[i]
        self.got[i, "x"].wait_recv()
        rect = self.rect(region, 0)
        self.got[i, 0] = [self.to_all(rect, self.t.at(region[0][0], s)) for s in (1, 3, 2)]

    def widen(self, i):
        region = self.regions[i]
        wait_all(self.got[i, 0])
        rect = self.rect(region, 1)
        self.got[i, 1] = [self.to_all(rect, self.t.at(region[0][1], s)) for s in (1, 3)]

    def pass_on(self, i):
        region = self.regions[i]
        axis = region[0][1]
        cut = 2 if self.lean else 1
        ahead, behind = self.got[i, 1]
        group = self.net.group(parts_of(self.full, 3, self.rect(region, 1)), self.t.at(axis, 1))
        for came, shift, to, owners in (
            (ahead, -1, 1, self.others[:cut]),
            (behind, 1, 3, self.others[cut:]),
        ):
            came.wait_recv()
            rect = self.rect(region, 1, shift)
            for o in owners:
                group.send(part(self.full, o, rect), part(self.full, o, rect), self.t.at(axis, to))
        self.got[i, 2] = group

    def to_sibling(self, region, shifts):
        for shift in shifts:
            self.got["core"].append(self.to_all(self.rect(region, 1, shift), self.t.sibling()))

    def share(self, i):
        self.to_sibling(self.regions[i], (0, -1, 1))

    def arrive(self, i):
        self.got[i, 2].wait_recv()

    def share_last(self, i):
        self.to_sibling(self.regions[i], (2,))

    def finish(self):
        wait_all(self.got["core"])


LAG = 0.5


def dot_t(a, b):
    return lax.dot_general(a, b, (((1,), (1,)), ((), ())), preferred_element_type=F32)


def causal(s, i):
    rows = lax.broadcasted_iota(jnp.int32, (256, 256), 0)
    cols = lax.broadcasted_iota(jnp.int32, (256, 256), 1)
    last = jnp.where(cols <= rows, s[:, 256 * i :], -1e30)
    return last if i == 0 else jnp.concatenate([s[:, : 256 * i], last], axis=1)


class Swap:
    def __init__(self, net, torus, parts):
        self.net, self.t, self.parts = net, torus, parts

    def pack_single(self, full, single):
        parts = self.parts
        for d in range(4):
            cols = [full[:, 1280 * k + 1024 + 64 * d : 1280 * k + 1088 + 64 * d] for k in range(parts)]
            if parts % 2:
                cols.append(jnp.zeros((256, 64), BF16))
            single[d] = jnp.concatenate(cols, axis=1)

    def out_pairs(self, full, box):
        t, net, got = self.t, self.net, []
        for p in range(2):
            group = net.group(box.at[p, :, pl.ds(0, 3)], t.at("x", 1))
            for s in (1, 3, 2):
                d = wrap(t.x + s)
                for k in range(self.parts):
                    cols = pl.ds(pl.multiple_of(1280 * k + 256 * d + 128 * p, 128), 128)
                    group.send(full.at[:, cols], box.at[p, k, t.x], t.at("x", s))
            got.append(group)
        return got

    def keep_pairs(self, full, box):
        for p in range(2):
            for k in range(self.parts):
                cols = pl.ds(pl.multiple_of(1280 * k + 256 * self.t.x + 128 * p, 128), 128)
                box[p, k, self.t.x] = full[:, cols]

    def out_single(self, single, box):
        t = self.t
        group = self.net.group(box.at[pl.ds(0, 3)], t.at("x", 1))
        for s in (1, 3, 2):
            group.send(single.at[wrap(t.x + s)], box.at[t.x], t.at("x", s))
        return group

    def back_pair(self, p, src, full):
        t = self.t
        group = self.net.group(src.at[pl.ds(0, 3), :, p], t.at("x", 1))
        for s in (1, 3, 2):
            d = wrap(t.x + s)
            for k in range(self.parts):
                cols = pl.ds(pl.multiple_of(1280 * k + 256 * t.x + 128 * p, 128), 128)
                group.send(src.at[d, k, p], full.at[:, cols], t.at("x", s))
        return group

    def keep_back(self, p, src, full):
        for k in range(self.parts):
            cols = pl.ds(pl.multiple_of(1280 * k + 256 * self.t.x + 128 * p, 128), 128)
            full[:, cols] = src[self.t.x, k, p]

    def unpack_single(self, box, full):
        for k in range(self.parts):
            cols = [box[d, :, 64 * k : 64 * k + 64] for d in range(4)]
            full[:, 1280 * k + 1024 : 1280 * (k + 1)] = jnp.concatenate(cols, axis=1)


EPS = 1e-05
VECTORS = ("ln1_gain", "ln1_bias", "qv_bias", "out_bias", "ln2_gain", "ln2_bias", "proj_bias", "fc_bias")
SIZES = (320, 320, 640, 320, 320, 320, 320, 1280)


def whole_vector(small, name):
    k = VECTORS.index(name)
    return jnp.concatenate([small[x, k : k + 1, : SIZES[k]] for x in range(4)], axis=1)


def dot(a, b):
    return jnp.dot(a, b, preferred_element_type=F32)


def norm(v):
    center = v - jnp.mean(v, axis=-1, keepdims=True)
    scale = lax.rsqrt(jnp.mean(center * center, axis=-1, keepdims=True) + EPS)
    return center * scale, scale


def norm_back(grad, hat, scale, gain):
    inner = grad * gain
    return scale * (
        inner - jnp.mean(inner, axis=-1, keepdims=True) - hat * jnp.mean(inner * hat, axis=-1, keepdims=True)
    )


class Forward:
    def __init__(self, net, torus, qkv, full, heads, lse, box, single, single_in, outs, res, res_single, res_single_in):
        self.net, self.t, self.qkv, self.full, self.heads, self.lse = net, torus, qkv, full, heads, lse
        self.box, self.single, self.single_in, self.outs = box, single, single_in, outs
        self.res, self.res_single, self.res_single_in = res, res_single, res_single_in
        self.swap, self.back = Swap(net, torus, 3), Swap(net, torus, 1)
        self.sent = []

    def start(self):
        t, swap = self.t, self.swap
        self.got = swap.out_pairs(self.qkv, self.box)
        swap.pack_single(self.qkv, self.single)
        self.got_single = swap.out_single(self.single, self.single_in)
        swap.keep_pairs(self.qkv, self.box)
        self.single_in[t.x] = self.single[t.x]
        self.lse[...] = jnp.zeros_like(self.lse)

    def take(self, p):
        heads = self.heads
        if p < 2:
            self.got[p].wait_recv()
            for k in range(3):
                for s in range(4):
                    for j in range(2):
                        v = self.box[p, k, s, :, 64 * j : 64 * j + 64]
                        heads[k, 2 * p + j, 256 * s : 256 * (s + 1), :] = v * BF16(0.125) if k == 0 else v
            return
        self.got_single.wait_recv()
        for k in range(3):
            for s in range(4):
                v = self.single_in[s, :, 64 * k : 64 * k + 64]
                heads[k, 4, 256 * s : 256 * (s + 1), :] = v * BF16(0.125) if k == 0 else v

    def head(self, h, j):
        heads, lse = self.heads, self.lse
        lane = lax.broadcasted_iota(jnp.int32, (256, 128), 1)
        for i in range(4):
            rows = slice(256 * i, 256 * (i + 1))
            n = 256 * (i + 1)
            s = causal(dot_t(heads[0, h, rows, :], heads[1, h, :n, :]), i)
            top = jnp.max(s, axis=1, keepdims=True)
            p = jnp.exp(s - top)
            total = jnp.sum(p, axis=1, keepdims=True)
            lse[rows, :] = jnp.where(lane == h, top + jnp.log(total), lse[rows, :])
            o = dot(p.astype(BF16), heads[2, h, :n, :])
            self.outs[j, rows, :] = (o / total).astype(BF16)

    def give(self, p):
        back, outs = self.back, self.outs
        for i in range(4):
            rows = slice(256 * i, 256 * (i + 1))
            if p < 2:
                self.res[i, 0, p] = jnp.concatenate([outs[0, rows, :], outs[1, rows, :]], axis=1)
            else:
                self.res_single[i] = jnp.concatenate([outs[0, rows, :], jnp.zeros((256, 64), BF16)], axis=1)
        if p < 2:
            self.sent.append(back.back_pair(p, self.res, self.full))
            back.keep_back(p, self.res, self.full)
        else:
            self.sent_single = back.out_single(self.res_single, self.res_single_in)
            self.res_single_in[self.t.x] = self.res_single[self.t.x]

    def finish(self):
        self.sent_single.wait_recv()
        self.back.unpack_single(self.res_single_in, self.full)
        wait_all(self.sent)


def front_kernel(
    tokens, v_0, v_1, v_2, v_3, v_4, v_5, v_6, v_7, w_qkv, w_out, w_fc, w_proj,
    f_qkv, f_out, f_fc, f_proj, f_small, r_normed, att, r_heads, r_lse,
    normed, heads, lse, tok_v, small, u_0, u_1, u_2, u_3, u_4, u_5, u_6, u_7, v_qkv, h_out, h_fc, h_proj, small_all, bias, qkv, other, full,
    box, single, single_in, outs, res, res_single, res_single_in, ssem, rsem, lsem, vsem,
):
    t = Torus()
    vectors = ((v_0, u_0), (v_1, u_1), (v_2, u_2), (v_3, u_3), (v_4, u_4), (v_5, u_5), (v_6, u_6), (v_7, u_7))
    loads = [pltpu.make_async_copy(src, dst, vsem.at[k]) for k, (src, dst) in enumerate(((tokens, tok_v),) + vectors)]
    greeting = Greeting(t.neighbours())
    each(loads, "start")
    small[...] = jnp.zeros_like(small)
    each(loads, "wait")
    for k, (_, vector) in enumerate(vectors):
        small[k : k + 1, 0 : SIZES[k]] = vector[...].astype(F32).reshape(1, SIZES[k])
    net = Net(ssem, rsem)
    sib, c = t.sibling(), t.c
    q = Gather(net, t, "qkv", w_qkv, v_qkv, 0)
    o = Gather(net, t, "out", w_out, f_out, 1)
    f = Gather(net, t, "fc", w_fc, f_fc, 0)
    p = Gather(net, t, "proj", w_proj, f_proj, 1)
    fwd = Forward(net, t, qkv, full, heads, lse, box, single, single_in, outs, res, res_single, res_single_in)
    own = pltpu.make_async_copy(w_qkv, v_qkv.at[t.x], lsem.at[0])
    own.start()
    held = [(w_out, h_out, f_out), (w_fc, h_fc, f_fc), (w_proj, h_proj, f_proj)]
    local = [pltpu.make_async_copy(s, h, lsem.at[1 + k]) for k, (s, h, _) in enumerate(held)]
    each(local, "start")
    sent = []
    greeting.wait()

    def columns(region):
        start, width = region
        cols = pl.ds(pl.multiple_of(start, 128), width)
        made = dot(normed[...].reshape(512, 1280), v_qkv[:, :, cols].reshape(1280, width)) + bias[0:1, cols]
        made = made.astype(BF16)
        qkv[:, cols] = made[:256]
        other[:, cols] = made[256:]
        sent.append(net.send(other.at[:, cols], qkv.at[:, cols], sib))

    q.start()
    p.start()
    q.spread(0)
    f.start()
    p.hop(0)
    o.start()
    q.spread(1)
    smalls = net.group(small_all.at[pl.ds(0, 3)], t.at("x", 1))
    for s in (1, 3, 2):
        smalls.send(small, small_all.at[t.x], t.at("x", s))
    small_all[t.x] = small[...]
    p.hop(1)
    q.start_alone()
    p.spread(0)
    o.hop(0)
    f.start_alone()
    q.widen(0)
    f.hop(0)
    q.widen(1)
    f.hop(1)
    p.spread(1)
    o.spread(0)
    q.pass_on(0)
    p.widen(0)
    q.alone_on()
    smalls.wait_recv()
    hat, _ = norm(tok_v[...].astype(F32))
    gain, shift = whole_vector(small_all, "ln1_gain"), whole_vector(small_all, "ln1_bias")
    normed[0] = (hat * gain + shift).astype(BF16)
    swapped = net.send(normed.at[0], normed.at[1], sib)
    k = VECTORS.index("qv_bias")
    for n in (0, 1, 4, 5):
        row = small_all[n if n < 2 else n - 2, k : k + 1, :640]
        bias[0:1, 640 * n : 640 * (n + 1)] = row
    bias[0:1, 1280:2560] = jnp.zeros((1, 1280), F32)
    f_small[...] = small_all[...]
    p.start_alone()
    q.pass_on(1)
    f.alone_on()
    q.arrive(0)
    swapped.wait_recv()
    q.alone_end()
    f.spread(0)
    o.start_alone()
    f.spread(1)
    own.wait()
    columns(q.regions[0][1:])
    columns(q.alone)
    q.share(1)
    p.alone_on()
    o.widen(0)
    q.alone_share()
    for n, (_, h, full_w) in enumerate(held):
        local[n].wait()
        local[n] = pltpu.make_async_copy(h, full_w.at[t.x], lsem.at[1 + n])
        local[n].start()
    p.widen(1)
    q.arrive(1)
    columns(q.regions[1][1:])
    o.alone_on()
    wait_all(sent)
    fwd.start()
    f.widen(0)
    f.widen(1)
    p.pass_on(0)
    o.pass_on(0)
    q.share_last(1)
    q.share(0)
    fwd.take(0)
    p.pass_on(1)
    f.alone_end()
    q.share_last(0)
    fwd.head(0, 0)
    p.alone_end()
    o.alone_end()
    o.share(0)
    p.share(0)
    fwd.head(1, 1)
    q.finish()
    p.alone_share()
    p.share(1)
    fwd.give(0)
    f.pass_on(0)
    fwd.take(1)
    fwd.head(2, 0)
    f.pass_on(1)
    f.share(0)
    fwd.head(3, 1)
    f.share(1)
    keep = pltpu.make_async_copy(v_qkv, f_qkv, lsem.at[0])
    keep.start()
    p.arrive(0)
    f.alone_share()
    fwd.give(1)
    fwd.take(2)
    p.arrive(1)
    fwd.head(4, 0)
    done = [
        pltpu.make_async_copy(src, dst, vsem.at[k])
        for k, (src, dst) in enumerate(((normed, r_normed), (heads, r_heads), (lse, r_lse)))
    ]
    each(done, "start")
    o.arrive(0)
    fwd.give(2)
    p.share_last(1)
    o.alone_share()
    p.share_last(0)
    f.arrive(0)
    f.share_last(0)
    o.share_last(0)
    f.arrive(1)
    f.share_last(1)
    o.finish()
    p.finish()
    fwd.finish()
    f.finish()
    done.append(pltpu.make_async_copy(full, att, vsem.at[3]))
    done[-1].start()
    keep.wait()
    each(local + done, "wait")
    net.finish()


FRONT_SEMS = 118


def front(tokens, vectors, w_qkv, w_out, w_fc, w_proj):
    vm, anys = pl.BlockSpec(memory_space=pltpu.VMEM), pl.BlockSpec(memory_space=pl.ANY)
    weights = (w_qkv, w_out, w_fc, w_proj)
    return pl.pallas_call(
        front_kernel,
        name="front",
        out_shape=[jax.ShapeDtypeStruct((4,) + w.shape, BF16) for w in weights]
        + [
            jax.ShapeDtypeStruct((4, 8, 1280), F32),
            jax.ShapeDtypeStruct((2, 256, 1280), BF16),
            jax.ShapeDtypeStruct((256, 1280), BF16),
            jax.ShapeDtypeStruct((3, 5, 1024, 64), BF16),
            jax.ShapeDtypeStruct((1024, 128), F32),
        ],
        in_specs=[anys] * 13,
        out_specs=[anys] * 4 + [vm] + [anys] * 4,
        scratch_shapes=[
            pltpu.VMEM((2, 256, 1280), BF16),
            pltpu.VMEM((3, 5, 1024, 64), BF16),
            pltpu.VMEM((1024, 128), F32),
            pltpu.VMEM((256, 1280), BF16),
            pltpu.VMEM((8, 1280), F32),
        ]
        + [pltpu.VMEM((n,), BF16) for n in SIZES]
        + [
            pltpu.VMEM((4, 320, 3840), BF16),
            pltpu.VMEM((320, 1280), BF16),
            pltpu.VMEM((320, 5120), BF16),
            pltpu.VMEM((1280, 1280), BF16),
            pltpu.VMEM((4, 8, 1280), F32),
            pltpu.VMEM((8, 3840), F32),
            pltpu.VMEM((256, 3840), BF16),
            pltpu.VMEM((256, 3840), BF16),
            pltpu.VMEM((256, 1280), BF16),
            pltpu.VMEM((2, 3, 4, 256, 128), BF16),
            pltpu.VMEM((4, 256, 256), BF16),
            pltpu.VMEM((4, 256, 256), BF16),
            pltpu.VMEM((2, 1024, 64), BF16),
            pltpu.VMEM((4, 1, 2, 256, 128), BF16),
            pltpu.VMEM((4, 256, 128), BF16),
            pltpu.VMEM((4, 256, 128), BF16),
            pltpu.SemaphoreType.DMA((FRONT_SEMS,)),
            pltpu.SemaphoreType.DMA((FRONT_SEMS,)),
            pltpu.SemaphoreType.DMA((4,)),
            pltpu.SemaphoreType.DMA((9,)),
        ],
        compiler_params=pltpu.CompilerParams(collective_id=0, has_side_effects=True, vmem_limit_bytes=56 << 20),
    )(tokens, *vectors, *weights)


GELU_A, GELU_B = 0.7978845608028654, 0.044715
FF_STEP = 640
FF_STEPS = 8
AHEAD = 2


def mlp_kernel(
    tokens, att, cot, small, w_out, w_fc, w_proj,
    base, act_c, grad_mid, datt, n2t_c, attt_c, cot_c, actt_c, gp_c, gb_c, small_c,
    tok_v, att_v, cot_v, small_v, wo_v, wf_v, wp_v, n2, middle, base_v, grad_acc, bias, sums, n2t, attt, acts, actt, gp, gb,
    datt_v, small_grad, isem, fsem, psem, ssem, rsem, lsem,
):
    t = Torus()
    sib, c = t.sibling(), t.c
    low, high = pl.ds(0, 256), pl.ds(256, 256)
    moves = ((att, att_v), (w_out, wo_v), (tokens, tok_v), (small, small_v), (cot, cot_v))
    loads = [pltpu.make_async_copy(src, dst, isem.at[k]) for k, (src, dst) in enumerate(moves)]
    each(loads, "start")

    def load(j):
        cols = pl.ds(pl.multiple_of(j * FF_STEP, 128), FF_STEP)
        return (
            pltpu.make_async_copy(w_fc.at[:, cols], wf_v.at[j], fsem.at[j]),
            pltpu.make_async_copy(w_proj.at[cols], wp_v.at[j], psem.at[j]),
        )

    greeting = Greeting([sib])

    def keep(k, src, dst):
        return pltpu.make_async_copy(src, dst, lsem.at[k])

    def give(k, src, dst):
        return pltpu.make_async_remote_copy(
            src_ref=src, dst_ref=dst, send_sem=ssem.at[k], recv_sem=rsem.at[k], device_id=sib, device_id_type=MESH
        )

    half = [pl.ds(pl.multiple_of(k * 640, 128), 640) for k in (c, 1 - c)]
    whole = [
        (keep(0, n2t, n2t_c.at[:, low]), give(0, n2t, n2t_c.at[:, high])),
        (keep(1, attt, attt_c.at[:, low]), give(1, attt, attt_c.at[:, high])),
        (keep(2, cot_v, cot_c.at[low]), give(2, cot_v, cot_c.at[high])),
        (keep(3, gb.at[:, half[0]], gb_c.at[low]), give(3, gb.at[:, half[1]], gb_c.at[high])),
        (keep(4, small_grad, small_c.at[0]), give(4, small_grad, small_c.at[1])),
    ]

    def strip(s, kept):
        n = 2 * s + (c if kept else 1 - c)
        rows = pl.ds(pl.multiple_of(s * 640, 16), 640)
        if kept:
            return [
                keep(5 + s, actt.at[n], actt_c.at[rows, low]),
                keep(9 + s, gp.at[n], gp_c.at[s, low]),
            ]
        return [
            give(5 + s, actt.at[n], actt_c.at[rows, high]),
            give(9 + s, gp.at[n], gp_c.at[s, high]),
        ]

    each(loads[:4], "wait")
    for j in range(AHEAD):
        each(load(j), "start")
    mid = tok_v[...].astype(F32) + dot(att_v[...], wo_v[...]) + whole_vector(small_v, "out_bias")
    middle[...] = mid
    hat, _ = norm(mid)
    n2[...] = (hat * whole_vector(small_v, "ln2_gain") + whole_vector(small_v, "ln2_bias")).astype(BF16)
    base_v[...] = mid + whole_vector(small_v, "proj_bias")
    results = [keep(13, base_v, base)]
    each(results, "start")
    grad_acc[...] = jnp.zeros_like(grad_acc)
    k = VECTORS.index("fc_bias")
    for n in range(FF_STEPS):
        bias[n, 0:1, :] = small_v[n // 2, k : k + 1, 640 * (n % 2) : 640 * (n % 2 + 1)]
    greeting.wait()
    loads[4].wait()
    each(whole[2], "start")
    n2t[...] = n2[...].T
    each(whole[0], "start")

    def chunk(j, _, back=True):
        @pl.when(j + AHEAD < FF_STEPS)
        def _():
            each(load(j + AHEAD), "start")

        each(load(j), "wait")
        pre = dot(n2[...], wf_v[j]) + bias[j, 0:1, :]
        if back:
            grad_acc[...] += dot_t(gp[j - 1], wf_v[j - 1])
        raw = dot_t(cot_v[...], wp_v[j])
        square = pre * pre
        bend = jnp.tanh(GELU_A * (pre + GELU_B * pre * square))
        act = (0.5 * pre * (1.0 + bend)).astype(BF16)
        actt[j] = act.T
        acts[j] = act
        slope = 0.5 * (1.0 + bend) + (0.5 * GELU_A) * pre * (1.0 - bend * bend) * (1.0 + 3.0 * GELU_B * square)
        grad = (raw * slope).astype(BF16)
        gp[j] = grad
        sums[j, 0:1, :] = jnp.sum(grad.astype(F32), axis=0, keepdims=True)

        @pl.when(lax.rem(j, 2) == c)
        def _():
            each(strip(j // 2, True), "start")

        @pl.when(lax.rem(j, 2) != c)
        def _():
            each(strip(j // 2, False), "start")

        return 0

    chunk(0, 0, False)
    lax.fori_loop(1, FF_STEPS, chunk, 0)
    grad_acc[...] += dot_t(gp[FF_STEPS - 1], wf_v[FF_STEPS - 1])
    hat, scale = norm(middle[...])
    g = grad_acc[...]
    cot_rows = cot_v[...].astype(F32)
    mid = cot_rows + norm_back(g, hat, scale, whole_vector(small_v, "ln2_gain"))
    branch = mid.astype(BF16)
    gb[...] = branch
    each(whole[3], "start")
    small_grad[0:1, :] = jnp.sum(g * hat, axis=0, keepdims=True)
    small_grad[1:2, :] = jnp.sum(g, axis=0, keepdims=True)
    small_grad[2:3, :] = jnp.sum(cot_rows, axis=0, keepdims=True)
    small_grad[3:4, :] = jnp.sum(branch.astype(F32), axis=0, keepdims=True)
    for n in range(FF_STEPS):
        small_grad[4 + n // 2 : 5 + n // 2, 640 * (n % 2) : 640 * (n % 2 + 1)] = sums[n, 0:1, :]
    each(whole[4], "start")
    middle[...] = mid
    results += [keep(14, middle, grad_mid), keep(16, acts, act_c)]
    each(results[1:], "start")
    attt[...] = att_v[...].T
    each(whole[1], "start")
    datt_v[...] = dot_t(branch, wo_v[...]).astype(BF16)
    results.append(keep(15, datt_v, datt))
    results[-1].start()
    for own, other in whole:
        own.wait()
        other.wait()
    for s in range(4):
        each(strip(s, True) + strip(s, False), "wait")
    each(results, "wait")


def mlp(tokens, att, cot, small, w_out, w_fc, w_proj):
    anys = pl.BlockSpec(memory_space=pl.ANY)
    return pl.pallas_call(
        mlp_kernel,
        name="mlp",
        out_shape=[
            jax.ShapeDtypeStruct((256, 1280), F32),
            jax.ShapeDtypeStruct((FF_STEPS, 256, FF_STEP), BF16),
            jax.ShapeDtypeStruct((256, 1280), F32),
            jax.ShapeDtypeStruct((256, 1280), BF16),
            jax.ShapeDtypeStruct((1280, 512), BF16),
            jax.ShapeDtypeStruct((1280, 512), BF16),
            jax.ShapeDtypeStruct((512, 1280), BF16),
            jax.ShapeDtypeStruct((2560, 512), BF16),
            jax.ShapeDtypeStruct((4, 512, 640), BF16),
            jax.ShapeDtypeStruct((512, 640), BF16),
            jax.ShapeDtypeStruct((2, 8, 1280), F32),
        ],
        in_specs=[anys] * 7,
        out_specs=[anys] * 11,
        scratch_shapes=[pltpu.VMEM((256, 1280), BF16)] * 3
        + [
            pltpu.VMEM((4, 8, 1280), F32),
            pltpu.VMEM((1280, 1280), BF16),
            pltpu.VMEM((FF_STEPS, 1280, FF_STEP), BF16),
            pltpu.VMEM((FF_STEPS, FF_STEP, 1280), BF16),
            pltpu.VMEM((256, 1280), BF16),
            pltpu.VMEM((256, 1280), F32),
            pltpu.VMEM((256, 1280), F32),
            pltpu.VMEM((256, 1280), F32),
            pltpu.VMEM((FF_STEPS, 8, FF_STEP), F32),
            pltpu.VMEM((FF_STEPS, 8, FF_STEP), F32),
            pltpu.VMEM((1280, 256), BF16),
            pltpu.VMEM((1280, 256), BF16),
            pltpu.VMEM((FF_STEPS, 256, FF_STEP), BF16),
            pltpu.VMEM((FF_STEPS, FF_STEP, 256), BF16),
            pltpu.VMEM((FF_STEPS, 256, FF_STEP), BF16),
            pltpu.VMEM((256, 1280), BF16),
            pltpu.VMEM((256, 1280), BF16),
            pltpu.VMEM((8, 1280), F32),
            pltpu.SemaphoreType.DMA((5,)),
            pltpu.SemaphoreType.DMA((FF_STEPS,)),
            pltpu.SemaphoreType.DMA((FF_STEPS,)),
            pltpu.SemaphoreType.DMA((13,)),
            pltpu.SemaphoreType.DMA((13,)),
            pltpu.SemaphoreType.DMA((17,)),
        ],
        compiler_params=pltpu.CompilerParams(collective_id=3, has_side_effects=True, vmem_limit_bytes=60 << 20),
    )(tokens, att, cot, small, w_out, w_fc, w_proj)


def view(ref, axes, chosen, rows):
    return ref.at[tuple(chosen.get(a, slice(None)) for a in axes) + (pl.ds(*rows),)]


def leading(ref):
    return ref.shape[:-2]


def add_into(dst, *srcs):
    lead = leading(dst)
    count = 1
    for n in lead:
        count *= n

    def slab(i):
        index = []
        for n in reversed(lead):
            index.append(lax.rem(i, n))
            i = i // n
        return tuple(reversed(index))

    def body(i, _):
        at = slab(i)
        total = dst[at].astype(F32)
        for s in srcs:
            total = total + s[at].astype(F32)
        dst[at] = total.astype(BF16)
        return 0

    if count == 1 and not lead:
        total = dst[...].astype(F32)
        for s in srcs:
            total = total + s[...].astype(F32)
        dst[...] = total.astype(BF16)
    else:
        lax.fori_loop(0, count, body, 0)


def inbox_shapes(classes, phases):
    out = []
    for order, _, n in classes:
        if 0 in phases:
            half = [2 if a == order[1] else 4 for a in "xyz" if a != order[0]]
            out += [half + [n, 128]] * 2 + [[4, 4, n, 128]] * 2
        if 1 in phases:
            out += [[2, n, 128]] * 2 + [[4, n, 128]] * 2
        if 2 in phases:
            out += [[3, n, 128]]
    return [pltpu.VMEM(tuple(s), BF16) for s in out]


def inboxes(refs, phases):
    refs, out = list(refs), []
    while refs:
        mine = {}
        for phase in phases:
            n = 1 if phase == 2 else 4
            mine[phase], refs = refs[:n], refs[n:]
        out.append(mine)
    return out


class Lane:
    def __init__(self, net, torus, acc, axes, inbox, order, row, n):
        self.net, self.t, self.acc, self.axes, self.inbox, self.order = net, torus, acc, axes, inbox, order
        self.rows, self.base = (row, n), 0
        self.fixed = {}
        self.got = {}

    def part(self, phase):
        axis = self.order[phase]
        return view(self.acc, self.axes, {**self.fixed, axis: self.t.pos(axis)}, self.rows)

    def held(self):
        return view(self.acc, self.axes, self.fixed, self.rows)

    def halves(self, phase):
        a = self.order[phase + 1]
        return [{a: pl.ds(0, 2)}, {a: pl.ds(2, 2)}]

    def box_half(self, box, phase, half):
        if phase == 1:
            return box.at[pl.ds(2 * half, 2)]
        left = [a for a in "xyz" if a != self.order[0]]
        cut = left.index(self.order[1])
        return box.at[(slice(None),) * cut + (pl.ds(2 * half, 2),)]

    def first(self, phase):
        axis = self.order[phase]
        p = self.t.pos(axis)
        h = self.halves(phase)
        b = self.inbox[phase]
        at = lambda shift, cut: view(self.acc, self.axes, {**self.fixed, axis: wrap(p + shift), **cut}, self.rows)
        up, down = self.t.at(axis, 1), self.t.at(axis, 3)
        far = [self.net.send(at(2, h[0]), b[0], up), self.net.send(at(2, h[1]), b[1], down)]
        near = [self.net.group(b[2], up), self.net.group(b[3], down)]
        near[0].send(at(1, h[1]), self.box_half(b[2], phase, 1), up)
        near[1].send(at(3, h[0]), self.box_half(b[3], phase, 0), down)
        self.got[phase] = (far, near)

    def second(self, phase, side):
        axis = self.order[phase]
        p = self.t.pos(axis)
        b = self.inbox[phase]
        far, near = self.got[phase]
        step = 3 if side else 1
        chosen = {**self.fixed, axis: wrap(p + step), **self.halves(phase)[side]}
        here = view(self.acc, self.axes, chosen, self.rows)
        far[side].wait_recv()
        add_into(here, b[side])
        near[side].send(here, self.box_half(b[2 + side], phase, side), self.t.at(axis, step))

    def third(self, phase):
        axis = self.order[phase]
        p = self.t.pos(axis)
        b = self.inbox[phase]
        for copy in self.got[phase][1]:
            copy.wait_recv()
        self.fixed[axis] = p
        add_into(self.held(), b[2], b[3])

    def last(self):
        axis = self.order[2]
        p = self.t.pos(axis)
        box = self.inbox[2][0]
        self.got[2] = self.net.group(box, self.t.at(axis, 1))
        for s in (1, 3, 2):
            there = view(self.acc, self.axes, {**self.fixed, axis: wrap(p + s)}, self.rows)
            self.got[2].send(there, box.at[s - 1], self.t.at(axis, s))

    def done(self):
        axis = self.order[2]
        self.got[2].wait_recv()
        self.fixed[axis] = self.t.pos(axis)
        box = self.inbox[2][0]
        add_into(self.held(), box.at[0], box.at[1], box.at[2])


class Spread:
    def __init__(self, lane, out, result, order, row, n, sem):
        self.result = result
        self.net, self.t, self.out, self.order, self.rows, self.sem = lane.net, lane.t, out, order, (row, n), sem
        chosen = {a: lane.t.pos(a) for a in lane.axes}
        self.own = view(lane.acc, lane.axes, chosen, (row - lane.base, n))

    def place(self, y, z):
        return self.out.at[self.t.c, y, z, pl.ds(*self.rows)]

    def band(self, v, b=slice(None)):
        y, z = (b, v) if self.order == "yz" else (v, b)
        return self.place(y, z)

    def start(self):
        t = self.t
        here = self.place(t.y, t.z)
        self.keep = pltpu.make_async_copy(self.own, here, self.sem)
        self.keep.start()
        self.first = self.net.group(self.band(0, pl.ds(0, 3)), t.at(self.order[0], 1))
        for s in (1, 3, 2):
            self.first.send(self.own, here, t.at(self.order[0], s))

    def second(self):
        t, axis = self.t, self.order[1]
        self.first.wait_recv()
        self.keep.wait()
        here = self.band(t.pos(axis))
        self.near = [self.net.send(here, here, t.at(axis, s)) for s in (1, 3)]

    def third(self):
        t, axis = self.t, self.order[1]
        p = t.pos(axis)
        self.far = self.net.group(self.band(p), t.at(axis, 1))
        for copy, shift, to, b in ((self.near[0], 3, 1, pl.ds(0, 2)), (self.near[1], 1, 3, pl.ds(2, 2))):
            copy.wait_recv()
            there = self.band(wrap(p + shift), b)
            self.far.send(there, there, t.at(axis, to))

    def share(self):
        self.far.wait_recv()
        whole = self.place(slice(None), slice(None))
        self.core = self.net.send(whole, whole, self.t.sibling())

    def finish(self):
        self.core.wait_recv()
        rows = (slice(None),) * 3 + (pl.ds(*self.rows),)
        self.keep = pltpu.make_async_copy(self.out.at[rows], self.result.at[rows], self.sem)
        self.keep.start()

    def end(self):
        self.keep.wait()


GROUPS = {
    "mlp": ((192, 176, 160, 144, 128), 0, ("yzx", "yzx", "zxy", "zxy", "xyz")),
    "attn": ((128, 144, 128), 0, ("yxz", "zxy", "xyz")),
}
SMALL_ROWS = 16


def slab_rows(group):
    return sum(GROUPS[group][0]) + (SMALL_ROWS if group == "attn" else 0)


def classes_of(group):
    rows, extra, orders = GROUPS[group]
    row, out = 0, []
    for k, (order, n) in enumerate(zip(orders, rows)):
        n += extra if k == 2 else 0
        out.append((order, row, n))
        row += n
    return out


def merged_of(group):
    out = []
    for order, row, n in classes_of(group):
        if out and out[-1][0] == order:
            out[-1] = (order, out[-1][1], out[-1][2] + n)
        else:
            out.append((order, row, n))
    return out


def spreads_of(group):
    a, b, c = merged_of(group)
    h = c[2] // 32 * 16
    return [(0, "yz", a[1], a[2]), (1, "zy", b[1], b[2]), (2, "yz", c[1], h), (2, "zy", c[1] + h, c[2] - h)]


def pieces_of(group, first, count):
    rows, out, flat, row = GROUPS[group][0], [], 0, 0
    for n in rows:
        for slab in range(16):
            lo, hi = max(first, flat), min(first + count, flat + n)
            if lo < hi:
                out.append((slab, row + lo - flat, hi - lo, lo - first))
            flat += n
        row += n
    return out


def store_blocks(acc, group, x, first, blocks):
    for k, block in enumerate(blocks):
        for slab, row, n, offset in pieces_of(group, first + 320 * k, 320):
            acc[x, slab // 4, slab % 4, pl.ds(row, n), :] = block[offset : offset + n]


def spreads_for(group, lanes, out, result, sems):
    return [Spread(lanes[k], out, result, order, row, n, sems.at[i]) for i, (k, order, row, n) in enumerate(spreads_of(group))]


def row_pieces(ref, row, start, n):
    v = ref[row : row + 1, start : start + n]
    if n % 128:
        v = jnp.concatenate([v, jnp.zeros((1, 128 - n % 128), F32)], axis=1)
    return [v[:, 128 * k : 128 * (k + 1)] for k in range(v.shape[1] // 128)]


def store_small(acc, row, slabs):
    for x in range(4):
        filled = slabs(x)
        for k in range(16):
            pieces = filled[k] if k < len(filled) else []
            if len(pieces) < 16:
                pieces = pieces + [jnp.zeros((16 - len(pieces), 128), F32)]
            acc[x, k // 4, k % 4, pl.ds(row, 16), :] = jnp.concatenate(pieces, axis=0).astype(BF16)


def store_product(lhs, rhs, acc, group, places):
    out = dot(lhs, rhs).astype(BF16)
    for k, (x, chunk) in enumerate(places):
        rows = out[320 * k : 320 * (k + 1)]
        store_blocks(acc, group, x, 1600 * chunk, [rows[:, 128 * t : 128 * (t + 1)] for t in range(5)])


class Backward:
    def __init__(self, net, torus, datt, full, heads, lse, box, single, single_in, do, dkv, grads, res, res_single, res_single_in):
        self.net, self.t, self.datt, self.full, self.heads, self.lse = net, torus, datt, full, heads, lse
        self.box, self.single, self.single_in, self.do, self.dkv, self.grads = box, single, single_in, do, dkv, grads
        self.res, self.res_single, self.res_single_in = res, res_single, res_single_in
        self.swap, self.back = Swap(net, torus, 1), Swap(net, torus, 3)
        self.sent = []

    def start(self):
        t, swap = self.t, self.swap
        self.got = swap.out_pairs(self.datt, self.box)
        swap.pack_single(self.datt, self.single)
        self.got_single = swap.out_single(self.single, self.single_in)
        swap.keep_pairs(self.datt, self.box)
        self.single_in[t.x] = self.single[t.x]

    def take(self, p):
        (self.got[p] if p < 2 else self.got_single).wait_recv()
        for s in range(4):
            rows = slice(256 * s, 256 * (s + 1))
            if p < 2:
                for j in range(2):
                    self.do[2 * p + j, rows, :] = self.box[p, 0, s, :, 64 * j : 64 * j + 64]
            else:
                self.do[4, rows, :] = self.single_in[s, :, :64]

    def head(self, h, j):
        heads, grads, dkv = self.heads, self.grads, self.dkv
        lane = lax.broadcasted_iota(jnp.int32, (256, 128), 1)
        dkv[...] = jnp.zeros_like(dkv)
        for i in range(4):
            rows = slice(256 * i, 256 * (i + 1))
            n = 256 * (i + 1)
            q, k, v, d = heads[0, h, rows, :], heads[1, h, :n, :], heads[2, h, :n, :], self.do[h, rows, :]
            total = jnp.sum(jnp.where(lane == h, self.lse[rows, :], 0.0), axis=1, keepdims=True)
            p = jnp.exp(causal(dot_t(q, k), i) - total)
            t1 = p * dot_t(d, v)
            inner = jnp.sum(t1, axis=1, keepdims=True)
            ds = (t1 - p * inner).astype(BF16)
            grads[0, j, rows, :] = (dot(ds, k) * 0.125).astype(BF16)
            dkv[0, :, :n] += dot(q.T, ds)
            dkv[1, :, :n] += dot(d.T, p.astype(BF16))
        for k in range(2):
            grads[1 + k, j] = dkv[k].T.astype(BF16)

    def give(self, p):
        grads, back = self.grads, self.back
        for i in range(4):
            rows = slice(256 * i, 256 * (i + 1))
            if p < 2:
                for k in range(3):
                    self.res[i, k, p] = jnp.concatenate([grads[k, 0, rows, :], grads[k, 1, rows, :]], axis=1)
            else:
                cols = [grads[k, 0, rows, :] for k in range(3)] + [jnp.zeros((256, 64), BF16)]
                self.res_single[i] = jnp.concatenate(cols, axis=1)
        if p < 2:
            self.sent.append(back.back_pair(p, self.res, self.full))
            back.keep_back(p, self.res, self.full)
        else:
            self.sent_single = back.out_single(self.res_single, self.res_single_in)
            self.res_single_in[self.t.x] = self.res_single[self.t.x]

    def finish(self):
        self.sent_single.wait_recv()
        self.back.unpack_single(self.res_single_in, self.full)
        wait_all(self.sent)


def back_kernel(
    r_datt, r_heads, r_lse, n2t, actt, gp, cot,
    gqkv, part_0, part_1, part_2,
    datt, heads, lse, n2t_v, actt_v, gp_v, cot_v, full,
    box, single, single_in, do, dkv, grads, res, res_single, res_single_in,
    ssem, rsem, lsem, acc, *inbox,
):
    t = Torus()
    moves = ((n2t, n2t_v), (gp, gp_v), (r_datt, datt), (actt, actt_v), (cot, cot_v), (r_heads, heads), (r_lse, lse))
    loads = [pltpu.make_async_copy(src, dst, lsem.at[k]) for k, (src, dst) in enumerate(moves)]
    soon, later = loads[:3], loads[3:]
    each(soon, "start")
    greeting = Greeting(t.neighbours())
    net = Net(ssem, rsem)
    bwd = Backward(net, t, datt, full, heads, lse, box, single, single_in, do, dkv, grads, res, res_single, res_single_in)
    lanes = [Lane(net, t, acc, "xyz", box_of, *k) for k, box_of in zip(classes_of("mlp"), inboxes(inbox, (0,)))]
    parts, places = [], {"y": part_0, "z": part_1, "x": part_2}
    first_rows = {order[0]: row for order, row, _ in merged_of("mlp")}
    for k, lane in enumerate(lanes):
        axis, (row, n) = lane.order[0], lane.rows
        place = places[axis].at[:, :, pl.ds(row - first_rows[axis], n)]
        parts.append(pltpu.make_async_copy(lane.part(0), place, lsem.at[k]))

    def fc(s):
        store_product(n2t_v[...], gp_v[s], acc, "mlp", [(x, s) for x in range(4)])

    def proj(half):
        def body(x, _):
            lhs = actt_v[pl.ds(pl.multiple_of(x * 640, 16), 640), :]
            places = [(x, 4 + 2 * half), (x, 5 + 2 * half)]
            store_product(lhs, cot_v[:, 640 * half : 640 * (half + 1)], acc, "mlp", places)
            return 0

        lax.fori_loop(0, 4, body, 0)

    each(soon, "wait")
    each(later, "start")
    fc(1)
    fc(0)
    greeting.wait()
    lanes[0].first(0)
    each(later, "wait")
    bwd.start()
    proj(0)
    fc(2)
    fc(3)
    lanes[2].first(0)
    lanes[1].first(0)
    proj(1)
    lanes[4].first(0)
    bwd.take(0)
    lanes[3].first(0)
    bwd.head(0, 0)
    bwd.head(1, 1)
    bwd.give(0)
    bwd.take(1)
    lanes[4].second(0, 1)
    bwd.head(2, 0)
    bwd.head(3, 1)
    lanes[2].second(0, 1)
    lanes[2].second(0, 0)
    lanes[0].second(0, 0)
    lanes[0].second(0, 1)
    lanes[4].second(0, 0)
    bwd.give(1)
    lanes[1].second(0, 0)
    bwd.take(2)
    bwd.head(4, 0)
    lanes[3].second(0, 1)
    lanes[3].second(0, 0)
    lanes[1].second(0, 1)
    lanes[2].third(0)
    bwd.give(2)
    lanes[4].third(0)
    lanes[3].third(0)
    parts[3].start()
    lanes[0].third(0)
    parts[4].start()
    parts[2].start()
    parts[0].start()
    lanes[1].third(0)
    parts[1].start()
    bwd.finish()
    gqkv[...] = full[...]
    each(parts, "wait")
    net.finish()


BACK_SEMS = 26


def backward(datt, heads, lse, n2t, actt, gp, cot):
    vm, anys = pl.BlockSpec(memory_space=pltpu.VMEM), pl.BlockSpec(memory_space=pl.ANY)
    classes = classes_of("mlp")
    return pl.pallas_call(
        back_kernel,
        name="backward",
        out_shape=[jax.ShapeDtypeStruct((256, 3840), BF16)]
        + [jax.ShapeDtypeStruct((4, 4, n, 128), BF16) for _, _, n in merged_of("mlp")],
        in_specs=[anys] * 7,
        out_specs=[vm] + [anys] * 3,
        scratch_shapes=[
            pltpu.VMEM((256, 1280), BF16),
            pltpu.VMEM((3, 5, 1024, 64), BF16),
            pltpu.VMEM((1024, 128), F32),
            pltpu.VMEM((1280, 512), BF16),
            pltpu.VMEM((2560, 512), BF16),
            pltpu.VMEM((4, 512, 640), BF16),
            pltpu.VMEM((512, 1280), BF16),
            pltpu.VMEM((256, 3840), BF16),
            pltpu.VMEM((2, 1, 4, 256, 128), BF16),
            pltpu.VMEM((4, 256, 128), BF16),
            pltpu.VMEM((4, 256, 128), BF16),
            pltpu.VMEM((5, 1024, 64), BF16),
            pltpu.VMEM((2, 64, 1024), F32),
            pltpu.VMEM((3, 2, 1024, 64), BF16),
            pltpu.VMEM((4, 3, 2, 256, 128), BF16),
            pltpu.VMEM((4, 256, 256), BF16),
            pltpu.VMEM((4, 256, 256), BF16),
            pltpu.SemaphoreType.DMA((BACK_SEMS,)),
            pltpu.SemaphoreType.DMA((BACK_SEMS,)),
            pltpu.SemaphoreType.DMA((8,)),
            pltpu.VMEM((4, 4, 4, slab_rows("mlp"), 128), BF16),
        ]
        + inbox_shapes(classes, (0,)),
        compiler_params=pltpu.CompilerParams(collective_id=1, has_side_effects=True, vmem_limit_bytes=60 << 20),
    )(datt, heads, lse, n2t, actt, gp, cot)


def last_kernel(
    n1, r_gqkv, attt, gb, w_qkv, r_tokens, r_mid, r_small, r_sums, base, acts, w_proj, part_0, part_1, part_2,
    r_mlp, r_attn, r_grad, r_block,
    out_mlp, out_attn, grad_tokens, gqkv, tokens, grad_mid, small_all, mlp_sums, acts_v, block_v, n1_v, n1t, gqkv_v, attt_v, gb_v, w_v, small_v, ssem, rsem, lsem, acc, acc_small, held_0, held_1, held_2, *inbox,
):
    t = Torus()
    helds = (held_0, held_1, held_2)
    moves = [(n1, n1_v), (attt, attt_v), (gb, gb_v), (w_qkv, w_v)] + [*zip((part_0, part_1, part_2), helds)]
    moves += [(r_gqkv, gqkv), (r_tokens, tokens), (r_mid, grad_mid), (r_small, small_all), (r_sums, mlp_sums)]
    n1_in, att_in, gb_in, w_in, *rest = [
        pltpu.make_async_copy(src, dst, lsem.at[k]) for k, (src, dst) in enumerate(moves)
    ]
    parts_in, rows_in = rest[:3], rest[3:]
    soon, later = rows_in[:1] + [n1_in] + parts_in, [att_in, gb_in] + rows_in[1:] + [w_in]
    each(soon, "start")
    greeting = Greeting(t.neighbours())
    net = Net(ssem, rsem)
    sib, c = t.sibling(), t.c
    m, a = [], []
    boxes = inboxes(inbox[:15], (1, 2))
    for held, box_of, (order, row, n) in zip(helds, boxes, merged_of("mlp")):
        lane = Lane(net, t, held, "".join(v for v in "xyz" if v != order[0]), box_of, order, 0, n)
        lane.base = row
        m.append(lane)
    boxes = inboxes(inbox[15:], (0, 1, 2))
    for box_of, k in zip(boxes, classes_of("attn")):
        a.append(Lane(net, t, acc, "xyz", box_of, *k))
    tiny = Lane(net, t, acc_small, "xyz", boxes[3], "yzx", 0, SMALL_ROWS)
    tiny.base = 400
    ms = spreads_for("mlp", m, out_mlp, r_mlp, lsem.at[pl.ds(12, 4)])
    sp = spreads_for("attn", a, out_attn, r_attn, lsem.at[pl.ds(16, 4)])
    ts = Spread(tiny, out_attn, r_attn, "zy", 400, SMALL_ROWS, lsem.at[20])
    got = {}

    def own():
        rows_in[0].wait()
        for s in range(3):
            gqkv_v[s, 0:256] = gqkv[:, pl.ds(pl.multiple_of(c * 1920 + s * 640, 128), 640)]

    def swap():
        for s in range(3):
            theirs = pl.ds(pl.multiple_of((1 - c) * 1920 + s * 640, 128), 640)
            got[s] = net.send(gqkv.at[:, theirs], gqkv_v.at[s, pl.ds(256, 256)], sib)

    def turn():
        n1_in.wait()
        n1t[:, 0:256] = n1_v[0].T
        n1t[:, 256:512] = n1_v[1].T

    def qkv(s):
        got[s].wait_recv()
        store_product(n1t[...], gqkv_v[s], acc, "attn", [(x, s) for x in range(4)])

    def outp():
        att_in.wait()
        gb_in.wait()
        store_product(attt_v[...], gb_v[...], acc, "attn", [(x, 3) for x in range(4)])

    def rows_back():
        w_in.wait()
        each(rows_in[1:], "wait")

        def body(n, total):
            cols = pl.ds(pl.multiple_of(n * 640, 128), 640)
            return total + dot_t(gqkv[:, cols], w_v[:, cols])

        grad = lax.fori_loop(0, 6, body, jnp.zeros((256, 1280), F32))
        hat, scale = norm(tokens[...].astype(F32))
        grad_tokens[...] = (grad_mid[...] + norm_back(grad, hat, scale, whole_vector(small_all, "ln1_gain"))).astype(BF16)
        small_v[0, 0:1, :] = jnp.sum(grad * hat, axis=0, keepdims=True)
        small_v[0, 1:2, :] = jnp.sum(grad, axis=0, keepdims=True)
        small_v[0, 2:3, :] = jnp.sum(gqkv[:, :1280].astype(F32), axis=0, keepdims=True)
        small_v[0, 3:4, :] = jnp.sum(gqkv[:, 2560:].astype(F32), axis=0, keepdims=True)

    grad_out = pltpu.make_async_copy(grad_tokens, r_grad, lsem.at[21])

    def rows_out():
        grad_out.start()
        got["small"] = net.send(small_v.at[0], small_v.at[1], sib)

    def sums():
        got["small"].wait_recv()
        total, other = small_v.at[2], small_v.at[3]
        total[...] = small_v[0] + small_v[1]
        other[...] = mlp_sums[0] + mlp_sums[1]
        store_small(
            acc_small, 0,
            lambda x: [
                [row for k in range(2) for row in row_pieces(total, k, 320 * x, 320)],
                row_pieces(total, 2 + x // 2, 640 * (x % 2), 640),
                [row for k in range(4) for row in row_pieces(other, k, 320 * x, 320)],
                row_pieces(other, 4 + x, 0, 1280),
            ],
        )

    more = [pltpu.make_async_copy(base, grad_mid, lsem.at[22]), pltpu.make_async_copy(acts, acts_v, lsem.at[23])]
    block_out = pltpu.make_async_copy(block_v, r_block, lsem.at[24])

    def slot(j):
        return w_v.at[pl.ds(640 * (j % 2), 640), pl.ds(1280 * (j // 2 % 3), 1280)]

    def chunk(j):
        return pltpu.make_async_copy(w_proj.at[pl.ds(FF_STEP * j, FF_STEP)], slot(j), lsem.at[25 + j])

    def block(j):
        if j == 0:
            each(more, "start")
            each([chunk(k) for k in range(6)], "start")
            each(more, "wait")
        chunk(j).wait()
        grad_mid[...] += dot(acts_v[j], slot(j)[...])
        if j < 2:
            chunk(6 + j).start()
        if j == FF_STEPS - 1:
            block_v[...] = grad_mid[...].astype(BF16)
            block_out.start()

    turn()
    each(parts_in, "wait")
    own()
    greeting.wait()
    m[0].first(1)
    m[1].first(1)
    each(later, "start")
    swap()
    m[2].first(1)
    qkv(0)
    m[2].second(1, 1)
    m[2].second(1, 0)
    qkv(1)
    m[1].second(1, 1)
    a[0].first(0)
    m[1].second(1, 0)
    m[0].second(1, 0)
    m[0].second(1, 1)
    outp()
    qkv(2)
    m[2].third(1)
    m[2].last()
    a[1].first(0)
    a[2].first(0)
    rows_back()
    a[0].second(0, 0)
    rows_out()
    a[0].second(0, 1)
    a[2].second(0, 0)
    a[2].second(0, 1)
    m[2].done()
    m[0].third(1)
    sums()
    block(0)
    a[1].second(0, 0)
    tiny.first(0)
    m[0].last()
    a[1].second(0, 1)
    block(1)
    ms[2].start()
    m[1].third(1)
    m[1].last()
    a[2].third(0)
    a[2].first(1)
    a[0].third(0)
    tiny.second(0, 1)
    tiny.second(0, 0)
    a[0].first(1)
    m[1].done()
    ms[1].start()
    block(2)
    a[2].second(1, 1)
    a[2].second(1, 0)
    m[0].done()
    ms[0].start()
    a[0].second(1, 0)
    a[0].second(1, 1)
    ms[3].start()
    a[1].third(0)
    tiny.third(0)
    a[1].first(1)
    ms[2].second()
    tiny.first(1)
    a[2].third(1)
    block(3)
    a[2].last()
    a[0].third(1)
    ms[1].second()
    a[0].last()
    tiny.second(1, 0)
    a[1].second(1, 0)
    tiny.second(1, 1)
    a[1].second(1, 1)
    ms[0].second()
    tiny.third(1)
    block(4)
    a[1].third(1)
    block(5)
    a[1].last()
    a[2].done()
    a[0].done()
    sp[0].start()
    ms[2].third()
    tiny.last()
    ms[1].third()
    tiny.done()
    ts.start()
    a[1].done()
    sp[1].start()
    block(6)
    sp[2].start()
    sp[3].start()
    ms[0].third()
    ts.second()
    sp[0].second()
    ms[3].second()
    sp[1].second()
    ts.third()
    ms[2].share()
    sp[3].second()
    block(7)
    sp[2].second()
    ms[1].share()
    ms[0].share()
    ms[3].third()
    sp[1].third()
    sp[3].third()
    sp[0].third()
    ms[3].share()
    ts.share()
    sp[2].third()
    ms[0].finish()
    sp[1].share()
    sp[3].share()
    ms[3].finish()
    sp[0].share()
    ms[1].finish()
    ts.finish()
    sp[2].share()
    sp[0].finish()
    sp[1].finish()
    ms[2].finish()
    sp[3].finish()
    sp[2].finish()
    each(ms + sp + [ts], "end")
    grad_out.wait()
    block_out.wait()
    net.finish()


LAST_SEMS = 100


def last(n1, gqkv, attt, gb, w_qkv, tokens, grad_mid, small_all, sums, base, acts, w_proj, parts):
    anys = pl.BlockSpec(memory_space=pl.ANY)
    mlp_classes, attn_classes = merged_of("mlp"), classes_of("attn")
    return pl.pallas_call(
        last_kernel,
        name="last",
        out_shape=[jax.ShapeDtypeStruct((2, 4, 4, slab_rows(g), 128), BF16) for g in ("mlp", "attn")]
        + [jax.ShapeDtypeStruct((256, 1280), BF16)] * 2,
        in_specs=[anys] * 15,
        out_specs=[anys] * 4,
        scratch_shapes=[pltpu.VMEM((2, 4, 4, slab_rows(g), 128), BF16) for g in ("mlp", "attn")]
        + [
            pltpu.VMEM((256, 1280), BF16),
            pltpu.VMEM((256, 3840), BF16),
            pltpu.VMEM((256, 1280), BF16),
            pltpu.VMEM((256, 1280), F32),
            pltpu.VMEM((4, 8, 1280), F32),
            pltpu.VMEM((2, 8, 1280), F32),
            pltpu.VMEM((FF_STEPS, 256, FF_STEP), BF16),
            pltpu.VMEM((256, 1280), BF16),
            pltpu.VMEM((2, 256, 1280), BF16),
            pltpu.VMEM((1280, 512), BF16),
            pltpu.VMEM((3, 512, 640), BF16),
            pltpu.VMEM((1280, 512), BF16),
            pltpu.VMEM((512, 640), BF16),
            pltpu.VMEM((1280, 3840), BF16),
            pltpu.VMEM((4, 8, 1280), F32),
            pltpu.SemaphoreType.DMA((LAST_SEMS,)),
            pltpu.SemaphoreType.DMA((LAST_SEMS,)),
            pltpu.SemaphoreType.DMA((33,)),
            pltpu.VMEM((4, 4, 4, 400, 128), BF16),
            pltpu.VMEM((4, 4, 4, SMALL_ROWS, 128), BF16),
        ]
        + [pltpu.VMEM((4, 4, n, 128), BF16) for _, _, n in mlp_classes]
        + inbox_shapes(mlp_classes, (1, 2))
        + inbox_shapes(attn_classes + [("yzx", 0, SMALL_ROWS)], (0, 1, 2)),
        compiler_params=pltpu.CompilerParams(collective_id=2, has_side_effects=True, vmem_limit_bytes=60 << 20),
    )(n1, gqkv, attt, gb, w_qkv, tokens, grad_mid, small_all, sums, base, acts, w_proj, *parts)


def flat_block(src, core, group, block):
    pieces = [
        src[core, slab // 4, slab % 4, row : row + n, :] for slab, row, n, _ in pieces_of(group, 320 * block, 320)
    ]
    return jnp.concatenate(pieces, axis=0).astype(F32)


SMALL_PLACES = (
    (0, 0, 320),
    (0, 3, 320),
    (1, 0, 640),
    (2, 9, 320),
    (2, 0, 320),
    (2, 3, 320),
    (3, 0, 1280),
    (2, 6, 320),
)


def unpack_kernel(packed_mlp, packed_attn, block, grad, *refs):
    fc, proj, qkv, out, block_out, grad_out, *smalls = refs[:14]
    in_0, in_1, stage, block_v, grad_v, *rest = refs[14:]
    small_v, (in_sem, out_sem, small_sem) = rest[:8], rest[8:]
    loads = []
    for c in range(2):
        loads.append(
            [
                pltpu.make_async_copy(src.at[c], dst.at[c], in_sem.at[2 * c + k])
                for k, (src, dst) in enumerate(((packed_attn, in_1), (packed_mlp, in_0)))
            ]
        )
        each(loads[-1], "start")
    rows = [pltpu.make_async_copy(block, block_v, in_sem.at[4]), pltpu.make_async_copy(grad, grad_v, in_sem.at[5])]
    each(rows, "start")
    flying, tail = [], []
    for c in range(2):
        chunks = [(in_1, "attn", q, qkv, 0, 1920 * c + 640 * q) for q in range(3)]
        chunks += [(in_1, "attn", 3, out, 0, 640 * c)]
        chunks += [(in_0, "mlp", q, fc, 0, 1280 * q + 640 * c) for q in range(4)]
        chunks += [(in_0, "mlp", 4 + 2 * h + sub, proj, 640 * c + 320 * sub, 640 * h) for h in range(2) for sub in range(2)]
        for n, (src, group, q, dst, row, col) in enumerate(chunks):
            if n in (0, 4):
                loads[c][n // 4].wait()
            k = len(flying)
            slot = k % STAGES
            if k >= STAGES:
                flying[k - STAGES].wait()
            for t in range(5):
                stage[slot, :, 128 * t : 128 * (t + 1)] = flat_block(src, c, group, 5 * q + t)
            copy = pltpu.make_async_copy(stage.at[slot], dst.at[pl.ds(row, 320), pl.ds(col, 640)], out_sem.at[slot])
            copy.start()
            flying.append(copy)
        if c == 0:
            for k, (slab, row, n) in enumerate(SMALL_PLACES):
                first = slab_rows("attn") - SMALL_ROWS
                values = in_1[0, 0, slab, first : first + SMALL_ROWS, :].astype(F32)
                for i in range(0, n, 128):
                    m = min(128, n - i)
                    small_v[k][i : i + m] = values[row + i // 128, :m]
                tail.append(pltpu.make_async_copy(small_v[k], smalls[k], small_sem.at[k]))
                tail[-1].start()
            each(rows, "wait")
            tail.append(pltpu.make_async_copy(block_v, block_out, small_sem.at[8]))
            tail.append(pltpu.make_async_copy(grad_v, grad_out, small_sem.at[9]))
            each(tail[-2:], "start")
    each(flying[-STAGES:] + tail, "wait")


STAGES = 8


def unpack(packed_mlp, packed_attn, block, grad):
    anys = pl.BlockSpec(memory_space=pl.ANY)
    sizes = [n for _, _, n in SMALL_PLACES]
    return pl.pallas_call(
        unpack_kernel,
        name="unpack",
        out_shape=[jax.ShapeDtypeStruct(s, F32) for s in ((320, 5120), (1280, 1280), (320, 3840), (320, 1280))]
        + [jax.ShapeDtypeStruct((256, 1280), BF16)] * 2
        + [jax.ShapeDtypeStruct((n,), F32) for n in sizes],
        in_specs=[anys] * 4,
        out_specs=[anys] * 14,
        scratch_shapes=[
            pltpu.VMEM(packed_mlp.shape, BF16),
            pltpu.VMEM(packed_attn.shape, BF16),
            pltpu.VMEM((STAGES, 320, 640), F32),
            pltpu.VMEM((256, 1280), BF16),
            pltpu.VMEM((256, 1280), BF16),
        ]
        + [pltpu.VMEM((n,), F32) for n in sizes]
        + [
            pltpu.SemaphoreType.DMA((6,)),
            pltpu.SemaphoreType.DMA((STAGES,)),
            pltpu.SemaphoreType.DMA((10,)),
        ],
        compiler_params=pltpu.CompilerParams(vmem_limit_bytes=62 << 20),
    )(packed_mlp, packed_attn, block, grad)


def shards(
    tokens,
    cotangent,
    ln1_gain,
    ln1_bias,
    w_qkv,
    qv_bias,
    w_out,
    out_bias,
    ln2_gain,
    ln2_bias,
    w_fc,
    fc_bias,
    w_proj,
    proj_bias,
):
    own = (ln1_gain, ln1_bias, qv_bias, out_bias, ln2_gain, ln2_bias, proj_bias, fc_bias)
    f_qkv, f_out, f_fc, f_proj, f_small, normed_one, attended, heads, lse = front(
        tokens[0], own, w_qkv, w_out, w_fc, w_proj
    )
    f_qkv, f_out, f_fc, f_proj = (
        f_qkv.reshape(1280, 3840),
        f_out.reshape(1280, 1280),
        f_fc.reshape(1280, 5120),
        f_proj.reshape(5120, 1280),
    )
    base, acts, grad_middle, grad_attended, n2t, attt, cot, actt, grad_pre, grad_branch, small_mlp = mlp(
        tokens[0], attended, cotangent[0], f_small, f_out, f_fc, f_proj
    )
    grad_qkv, *parts = backward(grad_attended, heads, lse, n2t, actt, grad_pre, cot)
    packed_mlp, packed_attn, grad_tokens, block_out = last(
        normed_one, grad_qkv, attt, grad_branch, f_qkv, tokens[0], grad_middle, f_small,
        small_mlp, base, acts, f_proj, parts,
    )
    g_fc, g_proj, g_qkv, g_out, block_out, grad_tokens, *vectors = unpack(
        packed_mlp, packed_attn, block_out, grad_tokens
    )
    gain_1, bias_1, bias_qv, bias_out, gain_2, bias_2, bias_fc, bias_proj = vectors
    return (
        block_out[None],
        grad_tokens[None],
        gain_1,
        bias_1,
        g_qkv,
        bias_qv,
        g_out,
        bias_out,
        gain_2,
        bias_2,
        g_fc,
        bias_fc,
        g_proj,
        bias_proj,
    )


def solution(mesh):
    vector, matrix, batch = P("shard"), P("shard", None), P("rep", "shard", None)
    placed = (batch, batch, vector, vector, matrix, vector, matrix, vector, vector, vector, matrix, vector, matrix, vector)
    return jax.shard_map(shards, mesh=mesh, in_specs=placed, out_specs=placed, check_vma=False)
```
